32 devices in a mesh: kpt: 2 (over x), row: 16 (over z, y, core).
Axes of the slice: x: 2, y: 2, z: 4, core: 2. Of those that a mesh axis runs over, the one named last changes fastest.
Arguments:
- orbitals_zero: float32 [32768, 1024], P(('kpt', 'row')), parts along dimension 0, may hold values from -0.046875 to 0.046875
- orbitals_one: float32 [32768, 1024], P(('kpt', 'row')), parts along dimension 0, may hold values from -0.046875 to 0.046875
- correlation_zero: float32 [2048, 1024], P('kpt'), parts along dimension 0, as said below
- correlation_one: float32 [2048, 1024], P('kpt'), parts along dimension 0, as said below
- cotangent: float32 [32768, 1024], P(('kpt', 'row')), parts along dimension 0, may hold values from -6 to 6
Outputs:
- orbital_grad: float32 [32768, 1024], P(('kpt', 'row')), parts along dimension 0
The draws below stay inside these ranges and needn't reach their ends.
There are 2 independent parts, one for each index of `kpt`. The reference program is written for one: setup_inputs(seed, part) draws one part's arguments, and reference() takes and returns one part's arrays. A program takes and returns all parts, laid end to end along the dimension named above; each array names one. Nothing has to cross between parts.
Inputs may be any that keep to these rules, and one draw needn't show every extreme that they name: `correlation_zero`: each correlation matrix is symmetric. `correlation_one`: each correlation matrix is symmetric.
All inputs are finite; a program needn't handle non-finite values.
Results may differ from the reference program's by a relative error of at most 0.000059.
Values sent between devices are 32-bit elements; how exact they have to be, the bound alone decides.
No kernel may reach another device: no remote copies, remote signals or barrier semaphores. Data moves between devices by JAX's collectives and lax.ppermute only.
A program may use at most 128 MiB of HBM per device.

```python
import math
import jax
import jax.numpy as jnp
from jax import lax

K = 1024
ROWS = 16384


def correlation_matrix(key, spread):
    noise_key, shift_key = jax.random.split(key)
    noise = jax.random.normal(noise_key, (K, K), jnp.float32) * (spread / math.sqrt(K))
    diagonal_shift = jax.random.uniform(shift_key, (K,), jnp.float32, -0.3, 0.3)
    return 0.5 * (noise + noise.T) + jnp.diag(1.0 + diagonal_shift)


def draw_correlation_zero(key, part):
    key = jax.random.fold_in(key, 11)
    return correlation_matrix(key, 0.5)


def draw_correlation_one(key, part):
    key = jax.random.fold_in(key, 12)
    return correlation_matrix(key, 0.35)


def shard_levels(rng, extent, shards, least, top_value):
    factor_of = 1.0
    for axis_at, parts in shards:
        heights = jax.random.uniform(jax.random.fold_in(jax.random.fold_in(rng, 6), axis_at), (parts,), jnp.float32, least / len(shards), top_value / len(shards))
        factor_of = factor_of * jnp.repeat(jnp.exp(heights), extent[axis_at] // parts).reshape((-1,) + (1,) * (len(extent) - 1 - axis_at))
    return factor_of


def bell_draw(stream_key, extent, scale, reach, shards=(), dtype=jnp.bfloat16):
    gain = shard_levels(stream_key, extent, shards, -0.22, 0.18) if shards else 1.0
    values = jax.random.normal(stream_key, extent, jnp.float32) * scale * gain
    return jnp.minimum(jnp.maximum(values, -reach), reach).astype(dtype)


def setup_inputs(seed: int = 0, part: int = 0) -> dict:
    streams_of = jax.random.split(jax.random.key(seed), 6)
    part_splits = jax.random.split(jax.random.fold_in(streams_of[5], part), 6)
    orbitals_zero = bell_draw(part_splits[0], (ROWS, K), ROWS ** -0.5, 0.046875, ((0, 16),), jnp.float32)
    orbitals_one = bell_draw(part_splits[1], (ROWS, K), ROWS ** -0.5, 0.046875, ((0, 16),), jnp.float32)
    correlation_zero = draw_correlation_zero(jax.random.fold_in(jax.random.fold_in(streams_of[5], part), 71), part)
    correlation_one = draw_correlation_one(jax.random.fold_in(jax.random.fold_in(streams_of[5], part), 71), part)
    cotangent = bell_draw(part_splits[4], (ROWS, K), 1.0, 6.0, ((0, 16),), jnp.float32)
    return {"orbitals_zero": orbitals_zero, "orbitals_one": orbitals_one, "correlation_zero": correlation_zero, "correlation_one": correlation_one, "cotangent": cotangent}


highest = lax.Precision.HIGHEST


def back_step(orbitals, correlation, incoming):
    direct_term = 1.5 * incoming - 0.5 * jnp.dot(incoming, correlation, precision=highest, preferred_element_type=jnp.float32)
    gram_total = lax.dot_general(orbitals, incoming, (((0,), (0,)), ((), ())), precision=highest, preferred_element_type=jnp.float32)
    symmetric = gram_total + gram_total.T
    return direct_term - 0.5 * jnp.dot(orbitals, symmetric, precision=highest, preferred_element_type=jnp.float32)


def reference(orbitals_zero, orbitals_one, correlation_zero, correlation_one, cotangent):
    middle = back_step(orbitals_one, correlation_one, cotangent)
    return back_step(orbitals_zero, correlation_zero, middle)
```

```python
import jax
import jax.numpy as jnp
from jax import lax
from jax.sharding import PartitionSpec as P

HIGH = lax.Precision.HIGH
B = 128


def mm(a, b):
    return jnp.dot(a, b, precision=HIGH, preferred_element_type=jnp.float32)


def mm_t(a, b):
    return lax.dot_general(
        a, b, (((0,), (0,)), ((), ())), precision=HIGH, preferred_element_type=jnp.float32
    )


def pack(sym):
    n = sym.shape[0] // B
    rows = [sym[i * B:(i + 1) * B, i * B:] for i in range(n)]
    return jnp.concatenate(
        [jnp.concatenate([rows[i], rows[n - 1 - i]], axis=1) for i in range(n // 2)], axis=0
    )


def unpack(packed):
    n = 2 * packed.shape[0] // B
    rows = [None] * n
    for i in range(n // 2):
        line = packed[i * B:(i + 1) * B]
        rows[i] = line[:, :(n - i) * B]
        rows[n - 1 - i] = line[:, (n - i) * B:]
    full = []
    for i in range(n):
        left = [rows[j][:, (i - j) * B:(i - j + 1) * B].T for j in range(i)]
        full.append(jnp.concatenate(left + [rows[i]], axis=1))
    return jnp.concatenate(full, axis=0)


def back_step(orbitals, correlation, incoming):
    gram = mm_t(orbitals, incoming)
    total = lax.psum(pack(gram + gram.T), "row")
    direct = 1.5 * incoming - 0.5 * mm(incoming, correlation)
    return direct - 0.5 * mm(orbitals, unpack(total))


def body(orbitals_zero, orbitals_one, correlation_zero, correlation_one, cotangent):
    middle = back_step(orbitals_one, correlation_one, cotangent)
    return back_step(orbitals_zero, correlation_zero, middle)


def solution(mesh):
    in_specs = (
        P(("kpt", "row"), None),
        P(("kpt", "row"), None),
        P("kpt", None),
        P("kpt", None),
        P(("kpt", "row"), None),
    )
    out_specs = P(("kpt", "row"), None)
    return jax.shard_map(body, mesh=mesh, in_specs=in_specs, out_specs=out_specs, check_vma=False)
```

```python
import functools
import jax
import jax.numpy as jnp
from jax import lax
from jax.experimental import pallas as pl
from jax.experimental.pallas import tpu as pltpu
from jax.sharding import PartitionSpec as P

F32 = jnp.float32
BF16 = jnp.bfloat16
B = 128
TILE = 256
LIMIT = 44 * 1024 * 1024


def split(x):
    hi = x.astype(BF16)
    return hi, (x - hi.astype(F32)).astype(BF16)


def dot3(a, b, dims):
    (ah, al), (bh, bl) = a, b
    one = lambda p, q: lax.dot_general(p, q, (dims, ((), ())), preferred_element_type=F32)
    return one(ah, bh) + (one(ah, bl) + one(al, bh))


NN = ((1,), (0,))
TN = ((0,), (0,))


def params(**kw):
    return pltpu.CompilerParams(vmem_limit_bytes=LIMIT, **kw)


def cost(products, size, arrays):
    return pl.CostEstimate(
        flops=6 * products * size ** 3, bytes_accessed=4 * arrays * size * size, transcendentals=0
    )


def pack_into(g, packed, me, shards):
    size = g.shape[0]
    n = size // B
    rows = size // 2 // shards
    for i in range(n // 2):
        at = 0
        for top in (i, n - 1 - i):
            for j in range(top, n):
                p = slice(top * B, (top + 1) * B)
                q = slice(j * B, (j + 1) * B)
                block = g[p, q] + g[q, p].T
                for s in range(B // rows):
                    slot = (i * (B // rows) + s) ^ me
                    packed[pl.ds(pl.multiple_of(slot * rows, rows), rows), at:at + B] = (
                        block[s * rows:(s + 1) * rows]
                    )
                at += B


def unpack_into(pieces, packed, hi, lo, me, shards):
    size = hi.shape[0]
    n = size // B
    rows = size // 2 // shards
    slot = 0
    for piece in pieces:
        for s in range(piece.shape[0] // rows):
            at = pl.multiple_of((slot ^ me) * rows, rows)
            packed[pl.ds(at, rows), :] = piece[s * rows:(s + 1) * rows, :]
            slot += 1
    for i in range(n // 2):
        at = 0
        for top in (i, n - 1 - i):
            for j in range(top, n):
                p = slice(top * B, (top + 1) * B)
                q = slice(j * B, (j + 1) * B)
                block = packed[i * B:(i + 1) * B, at:at + B]
                hi[p, q], lo[p, q] = split(block)
                if j > top:
                    hi[q, p], lo[q, p] = split(block.T)
                at += B


def gram_kernel(a_ref, b_ref, out_ref):
    @pl.when(pl.program_id(0) == 0)
    def _():
        out_ref[...] = jnp.zeros_like(out_ref)

    out_ref[...] += dot3(split(a_ref[...]), split(b_ref[...]), TN)


def gram(a, b):
    rows, size = a.shape
    block = pl.BlockSpec((TILE, size), lambda r: (r, 0))
    return pl.pallas_call(
        gram_kernel,
        grid=(rows // TILE,),
        in_specs=[block, block],
        out_specs=pl.BlockSpec((size, size), lambda r: (0, 0)),
        out_shape=jax.ShapeDtypeStruct((size, size), F32),
        compiler_params=params(),
        cost_estimate=cost(1, size, 3),
    )(a, b)


def gram_pack_kernel(shards, me_ref, a_ref, b_ref, keep_ref, send_ref, g, packed):
    step = pl.program_id(0)

    @pl.when(step == 0)
    def _():
        g[...] = jnp.zeros_like(g)

    g[...] += dot3(split(a_ref[...]), split(b_ref[...]), TN)

    @pl.when(step == pl.num_programs(0) - 1)
    def _():
        pack_into(g, packed, me_ref[0], shards)
        half = keep_ref.shape[0]
        keep_ref[...] = packed[:half]
        send_ref[...] = packed[half:]


def packed_shape(size):
    return size // 2, size + B


def gram_pack(me, shards, a, b):
    rows, size = a.shape
    height, width = packed_shape(size)
    block = pl.BlockSpec((TILE, size), lambda r: (r, 0))
    half = pl.BlockSpec((height // 2, width), lambda r: (0, 0))
    return pl.pallas_call(
        functools.partial(gram_pack_kernel, shards),
        grid=(rows // TILE,),
        in_specs=[pl.BlockSpec(memory_space=pltpu.SMEM), block, block],
        out_specs=[half, half],
        out_shape=[jax.ShapeDtypeStruct((height // 2, width), F32)] * 2,
        scratch_shapes=[pltpu.VMEM((size, size), F32), pltpu.VMEM((height, width), F32)],
        compiler_params=params(),
        cost_estimate=cost(1, size, 3),
    )(me, a, b)


def affine_kernel(a_ref, b_ref, out_ref, hi, lo):
    @pl.when(pl.program_id(0) == 0)
    def _():
        hi[...], lo[...] = split(b_ref[...])

    a = a_ref[...]
    out_ref[...] = 1.5 * a - 0.5 * dot3(split(a), (hi[...], lo[...]), NN)


def affine(a, b):
    rows, size = a.shape
    block = pl.BlockSpec((TILE, size), lambda r: (r, 0))
    return pl.pallas_call(
        affine_kernel,
        grid=(rows // TILE,),
        in_specs=[block, pl.BlockSpec((size, size), lambda r: (0, 0))],
        out_specs=block,
        out_shape=jax.ShapeDtypeStruct((rows, size), F32),
        scratch_shapes=[pltpu.VMEM((size, size), BF16)] * 2,
        compiler_params=params(),
        cost_estimate=cost(1, size, 3),
    )(a, b)


def second_gram_kernel(shards, count, me_ref, *refs):
    pieces = refs[:count]
    w_ref, p_ref, hi, lo, keep_ref, send_ref, g, packed = refs[count:]
    step = pl.program_id(0)

    @pl.when(step == 0)
    def _():
        unpack_into(pieces, packed, hi, lo, me_ref[0], shards)

    tile = w_ref.shape[0]
    at = pl.multiple_of(step * tile, tile)
    g[pl.ds(at, tile), :] = p_ref[...] - 0.5 * dot3(split(w_ref[...]), (hi[...], lo[...]), NN)

    @pl.when(step == pl.num_programs(0) - 1)
    def _():
        pack_into(g, packed, me_ref[0], shards)
        half = keep_ref.shape[0]
        keep_ref[...] = packed[:half]
        send_ref[...] = packed[half:]


def second_gram(me, shards, pieces, w, p):
    size = w.shape[0]
    height, width = packed_shape(size)
    block = pl.BlockSpec((TILE, size), lambda r: (r, 0))
    whole = lambda x: pl.BlockSpec(x, lambda r: (0, 0))
    return pl.pallas_call(
        functools.partial(second_gram_kernel, shards, len(pieces)),
        grid=(size // TILE,),
        in_specs=[pl.BlockSpec(memory_space=pltpu.SMEM)]
        + [whole(x.shape) for x in pieces]
        + [block, block],
        out_specs=[whole((size, size))] * 2 + [whole((height // 2, width))] * 2,
        out_shape=[jax.ShapeDtypeStruct((size, size), BF16)] * 2
        + [jax.ShapeDtypeStruct((height // 2, width), F32)] * 2,
        scratch_shapes=[pltpu.VMEM((size, size), F32), pltpu.VMEM((height, width), F32)],
        compiler_params=params(),
        cost_estimate=cost(1, size, 5),
    )(me, *pieces, w, p)


def middle_kernel(x_ref, hi_ref, lo_ref, m_ref, s_ref, out_ref, sh, sl):
    @pl.when(pl.program_id(0) == 0)
    def _():
        sh[...], sl[...] = split(s_ref[...])

    mid = m_ref[...] - 0.5 * dot3(split(x_ref[...]), (hi_ref[...], lo_ref[...]), NN)
    out_ref[...] = 1.5 * mid - 0.5 * dot3(split(mid), (sh[...], sl[...]), NN)


def middle_affine(x, hi, lo, m, s):
    rows, size = x.shape
    block = pl.BlockSpec((TILE, size), lambda r: (r, 0))
    whole = pl.BlockSpec((size, size), lambda r: (0, 0))
    return pl.pallas_call(
        middle_kernel,
        grid=(rows // TILE,),
        in_specs=[block, whole, whole, block, whole],
        out_specs=block,
        out_shape=jax.ShapeDtypeStruct((rows, size), F32),
        scratch_shapes=[pltpu.VMEM((size, size), BF16)] * 2,
        compiler_params=params(),
        cost_estimate=cost(2, size, 5),
    )(x, hi, lo, m, s)


def last_kernel(shards, count, me_ref, *refs):
    pieces = refs[:count]
    x_ref, d_ref, out_ref, hi, lo, packed = refs[count:]

    @pl.when(pl.program_id(0) == 0)
    def _():
        unpack_into(pieces, packed, hi, lo, me_ref[0], shards)

    out_ref[...] = d_ref[...] - 0.5 * dot3(split(x_ref[...]), (hi[...], lo[...]), NN)


def last_step(me, shards, pieces, x, d):
    rows, size = x.shape
    block = pl.BlockSpec((TILE, size), lambda r: (r, 0))
    return pl.pallas_call(
        functools.partial(last_kernel, shards, len(pieces)),
        grid=(rows // TILE,),
        in_specs=[pl.BlockSpec(memory_space=pltpu.SMEM)]
        + [pl.BlockSpec(p.shape, lambda r: (0, 0)) for p in pieces]
        + [block, block],
        out_specs=block,
        out_shape=jax.ShapeDtypeStruct((rows, size), F32),
        scratch_shapes=[pltpu.VMEM((size, size), BF16)] * 2
        + [pltpu.VMEM(packed_shape(size), F32)],
        compiler_params=params(),
        cost_estimate=cost(1, size, 4),
    )(me, *pieces, x, d)


def stages_of(count):
    stages, stride = [], 1
    while stride < count:
        left = count // stride
        radix = 2 if stride < 4 or left % 4 else 4
        stages.append((stride, radix))
        stride *= radix
    return stages


def slot_of(index, stages):
    slot = 0
    for stride, radix in stages:
        slot = slot * radix + (index // stride) % radix
    return slot


def swap(x, offset, count):
    return lax.ppermute(x, "row", [(i, i ^ offset) for i in range(count)])


def scatter_sum(keep, send, stages, count):
    stride, radix = stages[0]
    got = [swap(send, stride, count)]
    for at, (stride, radix) in enumerate(stages):
        if at == 0:
            continue
        part = keep.shape[0] // radix
        pick = lambda k: sum((g[k * part:(k + 1) * part] for g in got), keep[k * part:(k + 1) * part])
        sends = [pick(k) for k in range(1, radix)]
        new = [swap(x, stride * (k + 1), count) for k, x in enumerate(sends)]
        keep = pick(0)
        got = new
    return sum(got, keep)


def gather(piece, stages, count):
    pieces = [piece]
    for at, (stride, radix) in reversed(list(enumerate(stages))):
        pieces = pieces + [swap(x, stride * k, count) for k in range(1, radix) for x in pieces]
        if at > 1:
            pieces = [jnp.concatenate(pieces, axis=0)]
    return pieces


def body(count, orbitals_zero, orbitals_one, correlation_zero, correlation_one, cotangent):
    stages = stages_of(count)
    me = slot_of(lax.axis_index("row"), stages).astype(jnp.int32).reshape(1)

    keep, send = gram_pack(me, count, orbitals_one, cotangent)
    direct = affine(cotangent, correlation_one)
    p = gram(orbitals_zero, direct)
    w = gram(orbitals_zero, orbitals_one)
    pieces = gather(scatter_sum(keep, send, stages, count), stages, count)

    hi, lo, keep, send = second_gram(me, count, pieces, w, p)
    direct = middle_affine(orbitals_one, hi, lo, direct, correlation_zero)
    pieces = gather(scatter_sum(keep, send, stages, count), stages, count)

    return last_step(me, count, pieces, orbitals_zero, direct)


def solution(mesh):
    in_specs = (
        P(("kpt", "row"), None),
        P(("kpt", "row"), None),
        P("kpt", None),
        P("kpt", None),
        P(("kpt", "row"), None),
    )
    out_specs = P(("kpt", "row"), None)
    return jax.shard_map(
        functools.partial(body, mesh.shape["row"]),
        mesh=mesh, in_specs=in_specs, out_specs=out_specs, check_vma=False,
    )
```

```python
import functools
import jax
import jax.numpy as jnp
from jax import lax
from jax.experimental import pallas as pl
from jax.experimental.pallas import tpu as pltpu
from jax.sharding import PartitionSpec as P

F32 = jnp.float32
BF16 = jnp.bfloat16
B = 128
MIB = 1024 * 1024


def split(x):
    hi = x.astype(BF16)
    return hi, (x - hi.astype(F32)).astype(BF16)


def mm(a, b):
    (ah, al), (bh, bl) = a, b
    return jnp.dot(
        jnp.concatenate([ah, ah, al], axis=1),
        jnp.concatenate([bh, bl, bh], axis=0),
        preferred_element_type=F32,
    )


def call(kernel, name, out_shape, limit, products, arrays, **kw):
    size = 1024
    return pl.pallas_call(
        kernel,
        name=name,
        out_shape=out_shape,
        compiler_params=pltpu.CompilerParams(vmem_limit_bytes=limit * MIB),
        cost_estimate=pl.CostEstimate(
            flops=int(6 * products * size ** 3),
            bytes_accessed=int(4 * arrays * size * size),
            transcendentals=0,
        ),
        **kw,
    )


def struct(*shape, dtype=F32):
    return jax.ShapeDtypeStruct(shape, dtype)


SMEM = pl.BlockSpec(memory_space=pltpu.SMEM)
VMEM = pl.BlockSpec(memory_space=pltpu.VMEM)


def chunk_lines(size, chunk):
    half = size // B // 4
    return range(chunk * half, (chunk + 1) * half)


def line_blocks(size, i):
    n = size // B
    at = 0
    for top in (i, n - 1 - i):
        for j in range(top, n):
            yield at, slice(top * B, (top + 1) * B), slice(j * B, (j + 1) * B)
            at += B


def pack(g, packed, keep_ref, send_ref, me, shards, chunk):
    size = g.shape[0]
    rows = packed.shape[0] // shards
    per = B // rows
    for line, i in enumerate(chunk_lines(size, chunk)):
        for at, p, q in line_blocks(size, i):
            block = g[p, q] + g[q, p].T
            for s in range(per):
                slot = (line * per + s) ^ me
                packed[pl.ds(pl.multiple_of(slot * rows, rows), rows), at:at + B] = (
                    block[s * rows:(s + 1) * rows]
                )
    half = keep_ref.shape[0]
    keep_ref[...] = packed[:half]
    send_ref[...] = packed[half:]


def unpack(pieces, packed, hi, lo, me, shards, chunk):
    size = hi.shape[0]
    rows = packed.shape[0] // shards
    slot = 0
    for piece in pieces:
        for s in range(piece.shape[0] // rows):
            at = pl.multiple_of((slot ^ me) * rows, rows)
            packed[pl.ds(at, rows), :] = piece[s * rows:(s + 1) * rows, :]
            slot += 1
    for line, i in enumerate(chunk_lines(size, chunk)):
        for at, p, q in line_blocks(size, i):
            block = packed[line * B:(line + 1) * B, at:at + B]
            hi[p, q], lo[p, q] = split(block)
            if p.start != q.start:
                hi[q, p], lo[q, p] = split(block.T)


def packed_scratch(size):
    return pltpu.VMEM((size // 4, size + B), F32)


def halves(size):
    return [struct(size // 8, size + B)] * 2


def first_gram_kernel(shards, chunk, me_ref, a_ref, b_ref, keep_ref, send_ref, at, b3, g, packed):
    size = g.shape[0]
    rows = a_ref.shape[0]
    q = size // 4
    ah, al = split(a_ref[...].T)
    at[:, :rows] = ah
    at[:, rows:2 * rows] = ah
    at[:, 2 * rows:] = al
    bh, bl = split(b_ref[...])
    b3[:rows] = bh
    b3[rows:2 * rows] = bl
    b3[2 * rows:] = bh
    if chunk == 0:
        parts = [(0, q, 0, size), (q, 3 * q, 0, q), (3 * q, size, 0, q), (3 * q, size, 3 * q, size)]
    else:
        parts = [(q, 2 * q, q, size), (2 * q, 3 * q, q, size), (3 * q, size, q, 3 * q)]
    for r0, r1, c0, c1 in parts:
        g[r0:r1, c0:c1] = jnp.dot(at[r0:r1, :], b3[:, c0:c1], preferred_element_type=F32)
    pack(g, packed, keep_ref, send_ref, me_ref[0], shards, chunk)


def first_gram(me, shards, chunk, a, b):
    rows, size = a.shape
    return call(
        functools.partial(first_gram_kernel, shards, chunk), "first_gram", halves(size), 40, 0.5, 3,
        in_specs=[SMEM, VMEM, VMEM],
        out_specs=[VMEM, VMEM],
        scratch_shapes=[
            pltpu.VMEM((size, 3 * rows), BF16), pltpu.VMEM((3 * rows, size), BF16),
            pltpu.VMEM((size, size), F32), packed_scratch(size),
        ],
    )(me, a, b)


def affine_kernel(a_ref, b_ref, out_ref):
    rows, size = a_ref.shape
    tile = min(256, rows)
    b = split(b_ref[...])
    for r in range(0, rows, tile):
        a = a_ref[r:r + tile]
        out_ref[r:r + tile] = 1.5 * a - 0.5 * mm(split(a), b)


def affine(a, b):
    return call(
        affine_kernel, "affine", struct(*a.shape), 32, a.shape[0] / 1024, 3,
        in_specs=[VMEM, VMEM], out_specs=VMEM,
    )(a, b)


def gram_kernel(a_ref, b_ref, out_ref):
    a = split(a_ref[...].T)
    b = split(b_ref[...])
    out_ref[...] = mm(a, b)


def gram(a, b, half):
    rows, size = a.shape
    return call(
        gram_kernel, "gram", struct(size // 2, size), 32, 0.5, 2,
        grid=(1,),
        in_specs=[
            pl.BlockSpec((rows, size // 2), lambda r: (0, half)),
            pl.BlockSpec((rows, size), lambda r: (0, 0)),
        ],
        out_specs=pl.BlockSpec((size // 2, size), lambda r: (0, 0)),
    )(a, b)


def apply_first(a, base, hi, lo):
    size = hi.shape[0]
    q = size // 4
    part = lambda k0, k1, c0, c1: mm(
        (a[0][:, k0:k1], a[1][:, k0:k1]), (hi[k0:k1, c0:c1], lo[k0:k1, c0:c1])
    )
    wide = part(0, q, 0, size)
    left = part(q, size, 0, q)
    corner = part(3 * q, size, 3 * q, size)
    return jnp.concatenate(
        [
            base[:, :q] - 0.5 * (wide[:, :q] + left),
            base[:, q:3 * q] - 0.5 * wide[:, q:3 * q],
            base[:, 3 * q:] - 0.5 * (wide[:, 3 * q:] + corner),
        ],
        axis=1,
    )


def tile_of(refs, at, tile):
    height = refs[0].shape[0]
    return refs[at // height][at % height:at % height + tile]


def partial_kernel(shards, count, lists, me_ref, *refs):
    pieces, refs = refs[:count], refs[count:]
    a_refs, base_refs, (out_ref, hi, lo, packed) = refs[:lists], refs[lists:-4], refs[-4:]
    unpack(pieces, packed, hi, lo, me_ref[0], shards, 0)
    tile = 256
    for r in range(0, out_ref.shape[0], tile):
        out_ref[r:r + tile] = apply_first(
            split(tile_of(a_refs, r, tile)), tile_of(base_refs, r, tile), hi, lo
        )


def partial_apply(me, shards, pieces, a, base):
    size = a[0].shape[1]
    rows = sum(x.shape[0] for x in a)
    return call(
        functools.partial(partial_kernel, shards, len(pieces), len(a)), "partial_apply",
        struct(rows, size), 32, 0.5, 3,
        in_specs=[SMEM] + [VMEM] * (len(pieces) + len(a) + len(base)),
        out_specs=VMEM,
        scratch_shapes=[pltpu.VMEM((size, size), BF16)] * 2 + [packed_scratch(size)],
    )(me, *pieces, *a, *base)


def second_gram_kernel(shards, count, chunk, lists, me_ref, *refs):
    pieces, refs = refs[:count], refs[count:]
    w_refs, (y_ref, keep_ref, send_ref, hi, lo, g, packed) = refs[:lists], refs[lists:]
    unpack(pieces, packed, hi, lo, me_ref[0], shards, 1)
    size = g.shape[0]
    q = size // 4
    height = w_refs[0].shape[0]
    if chunk == 0:
        for r0, r1, c0, c1 in [(0, q, 0, q), (q, size, 0, q)]:
            g[r0:r1, c0:c1] = y_ref[r0:r1, c0:c1]
        parts = [(0, q, q, 3 * q, size), (0, q, 3 * q, size, 3 * q), (3 * q, size, 3 * q, size, 3 * q)]
    else:
        parts = []
        for r in range(q, size, q):
            parts.append((r, r + q, q, 3 * q, size))
            if r + q < size:
                parts.append((r, r + q, 3 * q, size, 3 * q))
    for r0, r1, c0, c1, k1 in parts:
        w = w_refs[r0 // height]
        r = r0 % height
        g[r0:r1, c0:c1] = y_ref[r0:r1, c0:c1] - 0.5 * mm(
            split(w[r:r + r1 - r0, q:k1]), (hi[q:k1, c0:c1], lo[q:k1, c0:c1])
        )
    pack(g, packed, keep_ref, send_ref, me_ref[0], shards, chunk)


def second_gram(me, shards, chunk, pieces, w, y):
    size = y.shape[0]
    return call(
        functools.partial(second_gram_kernel, shards, len(pieces), chunk, len(w)), "second_gram",
        halves(size), 32, 0.4, 3,
        in_specs=[SMEM] + [VMEM] * (len(pieces) + len(w) + 1),
        out_specs=[VMEM, VMEM],
        scratch_shapes=[pltpu.VMEM((size, size), BF16)] * 2
        + [pltpu.VMEM((size, size), F32), packed_scratch(size)],
    )(me, *pieces, *w, y)


def middle_kernel(shards, count, me_ref, *refs):
    first, second, refs = refs[:count], refs[count:2 * count], refs[2 * count:]
    x_ref, m_ref, out_ref, hi, lo, packed = refs
    unpack(first, packed, hi, lo, me_ref[0], shards, 0)
    unpack(second, packed, hi, lo, me_ref[0], shards, 1)
    sym = hi[...], lo[...]
    for r in range(0, x_ref.shape[0], 256):
        out_ref[r:r + 256] = m_ref[r:r + 256] - 0.5 * mm(split(x_ref[r:r + 256]), sym)


def middle_step(me, shards, first, second, x, m):
    rows, size = x.shape
    return call(
        functools.partial(middle_kernel, shards, len(first)), "middle", struct(rows, size), 32, 1, 4,
        in_specs=[SMEM] + [VMEM] * (2 * len(first) + 2),
        out_specs=VMEM,
        scratch_shapes=[pltpu.VMEM((size, size), BF16)] * 2 + [packed_scratch(size)],
    )(me, *first, *second, x, m)


def half_affine(a, b, half):
    rows, size = a.shape
    return call(
        affine_kernel, "half_affine", struct(rows // 2, size), 32, 0.5, 2,
        grid=(1,),
        in_specs=[
            pl.BlockSpec((rows // 2, size), lambda r: (half, 0)),
            pl.BlockSpec((size, size), lambda r: (0, 0)),
        ],
        out_specs=pl.BlockSpec((rows // 2, size), lambda r: (0, 0)),
    )(a, b)


def last_kernel(shards, count, me_ref, *refs):
    pieces = refs[:count]
    x_ref, z_ref, out_ref, hi, lo, packed = refs[count:]
    size = hi.shape[0]
    q = size // 4

    @pl.when(pl.program_id(0) == 0)
    def _():
        unpack(pieces, packed, hi, lo, me_ref[0], shards, 1)

    a = split(x_ref[:, q:])
    out_ref[:, :q] = z_ref[:, :q]
    out_ref[:, q:3 * q] = z_ref[:, q:3 * q] - 0.5 * mm(a, (hi[q:, q:3 * q], lo[q:, q:3 * q]))
    a = (a[0][:, :2 * q], a[1][:, :2 * q])
    out_ref[:, 3 * q:] = z_ref[:, 3 * q:] - 0.5 * mm(a, (hi[q:3 * q, 3 * q:], lo[q:3 * q, 3 * q:]))


def last_step(me, shards, pieces, x, z):
    rows, size = x.shape
    tile = 256
    block = pl.BlockSpec((tile, size), lambda r: (r, 0))
    return call(
        functools.partial(last_kernel, shards, len(pieces)), "last", struct(rows, size), 32, 0.5, 3,
        grid=(rows // tile,),
        in_specs=[SMEM] + [pl.BlockSpec(p.shape, lambda r: (0, 0)) for p in pieces] + [block, block],
        out_specs=block,
        scratch_shapes=[pltpu.VMEM((size, size), BF16)] * 2 + [packed_scratch(size)],
    )(me, *pieces, x, z)


def slot_of(index, strides):
    slot = 0
    for stride in strides:
        slot = slot * 2 + (index // stride) % 2
    return slot


def gate(*values):
    return lax.optimization_barrier(values)


class Sum:
    def __init__(self, count, strides, keep, send):
        self.count, self.strides, self.keep, self.send = count, strides, keep, send

    def swap(self, x, stage):
        offset = self.strides[stage]
        return lax.ppermute(x, "row", [(i, i ^ offset) for i in range(self.count)])

    def scatter(self, stage):
        return self.swap(self.send, stage)

    def add(self, got):
        total = self.keep + got
        half = total.shape[0] // 2
        self.keep, self.send = total[:half], total[half:]

    def finish(self, got):
        self.own = self.keep + got

    def gather(self, stage):
        return self.swap(self.own, stage)

    def join(self, got):
        self.own = jnp.concatenate([self.own, got], axis=0)


def close(env, *got):
    values = lax.optimization_barrier((*got, *env.values()))
    env.update(zip(env, values[len(got):]))
    return values[:len(got)]


def sum_chunks(count, strides, env, first, second, works, late):
    last = len(strides) - 1
    far = range(2, last + 1)
    works = list(works)

    def work():
        if works:
            works.pop(0)(env)

    a = Sum(count, strides, *first)
    got_a = a.scatter(0)
    pair = second(env)
    got_a, *pair = close(env, got_a, *pair)
    b = Sum(count, strides, *pair)

    a.add(got_a)
    got_a, got_b = a.scatter(1), b.scatter(0)
    work()
    got_a, got_b = close(env, got_a, got_b)

    a.add(got_a)
    b.add(got_b)
    got_b = b.scatter(1)
    for stage in far:
        got_a = a.scatter(stage)
        work()
        if stage < last:
            (got_a,) = close(env, got_a)
            a.add(got_a)
    got_a, got_b = close(env, got_a, got_b)
    a.finish(got_a)
    b.add(got_b)

    for stage, back in zip(far, reversed(far)):
        got_a, got_b = a.gather(back), b.scatter(stage)
        work()
        got_a, got_b = close(env, got_a, got_b)
        a.join(got_a)
        if stage < last:
            b.add(got_b)
        else:
            b.finish(got_b)

    got_a, own_a = a.gather(1), a.gather(0)
    for back in reversed(far):
        got_b = b.gather(back)
        work()
        if back > 2:
            (got_b,) = close(env, got_b)
            b.join(got_b)
    got_a, own_a, got_b = close(env, got_a, own_a, got_b)
    b.join(got_b)

    got_b, own_b = b.gather(1), b.gather(0)
    y_a = a.swap(got_a, 0)
    (y_a,) = close(env, y_a)
    pieces_a = [a.own, got_a, own_a, y_a]
    late(env, pieces_a)
    got_b, own_b = close(env, got_b, own_b)
    return pieces_a, [b.own, got_b, own_b, b.swap(got_b, 0)]


def body(count, orbitals_zero, orbitals_one, correlation_zero, correlation_one, cotangent):
    strides = [1 << s for s in range(count.bit_length() - 1)]
    me = slot_of(lax.axis_index("row"), strides).astype(jnp.int32).reshape(1)
    env = dict(
        x0=orbitals_zero, x1=orbitals_one, s0=correlation_zero, s1=correlation_one, c=cotangent
    )

    def direct(env):
        env["m"] = affine(env["c"], env["s1"])

    def put(name, left, right, half):
        def work(env):
            env[name] = gram(env[left], env[right], half)
        return work

    def late_gram(env, pieces):
        env["y"] = partial_apply(
            me, count, pieces, [env["w0"], env["w1"]], [env["p0"], env["p1"]]
        )

    works = [direct, put("p0", "x0", "m", 0), put("p1", "x0", "m", 1),
             put("w0", "x0", "x1", 0), put("w1", "x0", "x1", 1)]
    first = first_gram(me, count, 0, env["x1"], env["c"])
    one_a, one_b = sum_chunks(
        count, strides, env, first,
        lambda env: first_gram(me, count, 1, env["x1"], env["c"]), works, late_gram,
    )

    def middle(env):
        env["mid"] = middle_step(me, count, one_a, one_b, env["x1"], env["m"])

    def top(env):
        env["d0"] = half_affine(env["mid"], env["s0"], 0)

    def bottom(env):
        env["d1"] = half_affine(env["mid"], env["s0"], 1)

    def late_result(env, pieces):
        env["z"] = partial_apply(me, count, pieces, [env["x0"]], [env["d0"], env["d1"]])

    w = [env["w0"], env["w1"]]
    first = second_gram(me, count, 0, one_b, w, env["y"])
    two_a, two_b = sum_chunks(
        count, strides, env, first,
        lambda env: second_gram(me, count, 1, one_b, [env["w0"], env["w1"]], env["y"]),
        [middle, top, bottom], late_result,
    )
    return last_step(me, count, two_b, env["x0"], env["z"])


def solution(mesh):
    in_specs = (
        P(("kpt", "row"), None),
        P(("kpt", "row"), None),
        P("kpt", None),
        P("kpt", None),
        P(("kpt", "row"), None),
    )
    out_specs = P(("kpt", "row"), None)
    return jax.shard_map(
        functools.partial(body, mesh.shape["row"]),
        mesh=mesh, in_specs=in_specs, out_specs=out_specs, check_vma=False,
    )
```

```python
import functools
import jax
import jax.numpy as jnp
from jax import lax
from jax.experimental import pallas as pl
from jax.experimental.pallas import tpu as pltpu
from jax.sharding import PartitionSpec as P

F32 = jnp.float32
BF16 = jnp.bfloat16
B = 128
MIB = 1024 * 1024


def split(x):
    hi = x.astype(BF16)
    return hi, (x - hi.astype(F32)).astype(BF16)


def mm(a, b):
    (ah, al), (bh, bl) = a, b
    return jnp.dot(
        jnp.concatenate([ah, ah, al], axis=1),
        jnp.concatenate([bh, bl, bh], axis=0),
        preferred_element_type=F32,
    )


def call(kernel, name, out_shape, limit, products, arrays, **kw):
    size = 1024
    return pl.pallas_call(
        kernel,
        name=name,
        out_shape=out_shape,
        compiler_params=pltpu.CompilerParams(vmem_limit_bytes=limit * MIB),
        cost_estimate=pl.CostEstimate(
            flops=int(6 * products * size ** 3),
            bytes_accessed=int(4 * arrays * size * size),
            transcendentals=0,
        ),
        **kw,
    )


def struct(*shape, dtype=F32):
    return jax.ShapeDtypeStruct(shape, dtype)


SMEM = pl.BlockSpec(memory_space=pltpu.SMEM)
VMEM = pl.BlockSpec(memory_space=pltpu.VMEM)


def chunk_lines(size, chunk):
    half = size // B // 4
    return range(chunk * half, (chunk + 1) * half)


def line_blocks(size, i):
    n = size // B
    at = 0
    for top in (i, n - 1 - i):
        for j in range(top, n):
            yield at, slice(top * B, (top + 1) * B), slice(j * B, (j + 1) * B)
            at += B


def pack(g, packed, keep_ref, send_ref, me, shards, chunk):
    size = g.shape[0]
    rows = packed.shape[0] // shards
    per = B // rows
    for line, i in enumerate(chunk_lines(size, chunk)):
        for at, p, q in line_blocks(size, i):
            block = g[p, q] + g[q, p].T
            for s in range(per):
                slot = (line * per + s) ^ me
                packed[pl.ds(pl.multiple_of(slot * rows, rows), rows), at:at + B] = (
                    block[s * rows:(s + 1) * rows]
                )
    half = keep_ref.shape[0]
    keep_ref[...] = packed[:half]
    send_ref[...] = packed[half:]


def unpack(pieces, packed, hi, lo, me, shards, chunk):
    size = hi.shape[0]
    rows = packed.shape[0] // shards
    slot = 0
    for piece in pieces:
        for s in range(piece.shape[0] // rows):
            at = pl.multiple_of((slot ^ me) * rows, rows)
            packed[pl.ds(at, rows), :] = piece[s * rows:(s + 1) * rows, :]
            slot += 1
    for line, i in enumerate(chunk_lines(size, chunk)):
        for at, p, q in line_blocks(size, i):
            block = packed[line * B:(line + 1) * B, at:at + B]
            hi[p, q], lo[p, q] = split(block)
            if p.start != q.start:
                hi[q, p], lo[q, p] = split(block.T)


def packed_scratch(size):
    return pltpu.VMEM((size // 4, size + B), F32)


def halves(size):
    return [struct(size // 8, size + B)] * 2


def first_gram_kernel(shards, chunk, me_ref, a_ref, b_ref, keep_ref, send_ref, at, b3, g, packed):
    size = g.shape[0]
    rows = a_ref.shape[0]
    q = size // 4
    ah, al = split(a_ref[...].T)
    at[:, :rows] = ah
    at[:, rows:2 * rows] = ah
    at[:, 2 * rows:] = al
    bh, bl = split(b_ref[...])
    b3[:rows] = bh
    b3[rows:2 * rows] = bl
    b3[2 * rows:] = bh
    if chunk == 0:
        parts = [(0, q, 0, size), (q, 3 * q, 0, q), (3 * q, size, 0, q), (3 * q, size, 3 * q, size)]
    else:
        parts = [(q, 2 * q, q, size), (2 * q, 3 * q, q, size), (3 * q, size, q, 3 * q)]
    for r0, r1, c0, c1 in parts:
        g[r0:r1, c0:c1] = jnp.dot(at[r0:r1, :], b3[:, c0:c1], preferred_element_type=F32)
    pack(g, packed, keep_ref, send_ref, me_ref[0], shards, chunk)


def first_gram(me, shards, chunk, a, b):
    rows, size = a.shape
    return call(
        functools.partial(first_gram_kernel, shards, chunk), "first_gram", halves(size), 40, 0.5, 3,
        in_specs=[SMEM, VMEM, VMEM],
        out_specs=[VMEM, VMEM],
        scratch_shapes=[
            pltpu.VMEM((size, 3 * rows), BF16), pltpu.VMEM((3 * rows, size), BF16),
            pltpu.VMEM((size, size), F32), packed_scratch(size),
        ],
    )(me, a, b)


def affine_kernel(a_ref, b_ref, out_ref):
    rows, size = a_ref.shape
    tile = min(256, rows)
    b = split(b_ref[...])
    for r in range(0, rows, tile):
        a = a_ref[r:r + tile]
        out_ref[r:r + tile] = 1.5 * a - 0.5 * mm(split(a), b)


def affine(a, b):
    return call(
        affine_kernel, "affine", struct(*a.shape), 32, a.shape[0] / 1024, 3,
        in_specs=[VMEM, VMEM], out_specs=VMEM,
    )(a, b)


def gram_kernel(a_ref, b_ref, out_ref):
    a = split(a_ref[...].T)
    b = split(b_ref[...])
    out_ref[...] = mm(a, b)


def gram(a, b, half):
    rows, size = a.shape
    return call(
        gram_kernel, "gram", struct(size // 2, size), 32, 0.5, 2,
        grid=(1,),
        in_specs=[
            pl.BlockSpec((rows, size // 2), lambda r: (0, half)),
            pl.BlockSpec((rows, size), lambda r: (0, 0)),
        ],
        out_specs=pl.BlockSpec((size // 2, size), lambda r: (0, 0)),
    )(a, b)


def apply_first(a, base, hi, lo):
    size = hi.shape[0]
    q = size // 4
    part = lambda k0, k1, c0, c1: mm(
        (a[0][:, k0:k1], a[1][:, k0:k1]), (hi[k0:k1, c0:c1], lo[k0:k1, c0:c1])
    )
    wide = part(0, q, 0, size)
    left = part(q, size, 0, q)
    corner = part(3 * q, size, 3 * q, size)
    return jnp.concatenate(
        [
            base[:, :q] - 0.5 * (wide[:, :q] + left),
            base[:, q:3 * q] - 0.5 * wide[:, q:3 * q],
            base[:, 3 * q:] - 0.5 * (wide[:, 3 * q:] + corner),
        ],
        axis=1,
    )


def tile_of(refs, at, tile):
    height = refs[0].shape[0]
    return refs[at // height][at % height:at % height + tile]


def partial_kernel(shards, count, lists, me_ref, *refs):
    pieces, refs = refs[:count], refs[count:]
    a_refs, base_refs, (out_ref, hi, lo, packed) = refs[:lists], refs[lists:-4], refs[-4:]
    unpack(pieces, packed, hi, lo, me_ref[0], shards, 0)
    tile = 256
    for r in range(0, out_ref.shape[0], tile):
        out_ref[r:r + tile] = apply_first(
            split(tile_of(a_refs, r, tile)), tile_of(base_refs, r, tile), hi, lo
        )


def partial_apply(me, shards, pieces, a, base):
    size = a[0].shape[1]
    rows = sum(x.shape[0] for x in a)
    return call(
        functools.partial(partial_kernel, shards, len(pieces), len(a)), "partial_apply",
        struct(rows, size), 32, 0.5, 3,
        in_specs=[SMEM] + [VMEM] * (len(pieces) + len(a) + len(base)),
        out_specs=VMEM,
        scratch_shapes=[pltpu.VMEM((size, size), BF16)] * 2 + [packed_scratch(size)],
    )(me, *pieces, *a, *base)


def second_gram_kernel(shards, count, chunk, lists, me_ref, *refs):
    pieces, refs = refs[:count], refs[count:]
    w_refs, (y_ref, keep_ref, send_ref, hi, lo, g, packed) = refs[:lists], refs[lists:]
    unpack(pieces, packed, hi, lo, me_ref[0], shards, 1)
    size = g.shape[0]
    q = size // 4
    height = w_refs[0].shape[0]
    if chunk == 0:
        for r0, r1, c0, c1 in [(0, q, 0, q), (q, size, 0, q)]:
            g[r0:r1, c0:c1] = y_ref[r0:r1, c0:c1]
        parts = [(0, q, q, 3 * q, size), (0, q, 3 * q, size, 3 * q), (3 * q, size, 3 * q, size, 3 * q)]
    else:
        parts = []
        for r in range(q, size, q):
            parts.append((r, r + q, q, 3 * q, size))
            if r + q < size:
                parts.append((r, r + q, 3 * q, size, 3 * q))
    for r0, r1, c0, c1, k1 in parts:
        w = w_refs[r0 // height]
        r = r0 % height
        g[r0:r1, c0:c1] = y_ref[r0:r1, c0:c1] - 0.5 * mm(
            split(w[r:r + r1 - r0, q:k1]), (hi[q:k1, c0:c1], lo[q:k1, c0:c1])
        )
    pack(g, packed, keep_ref, send_ref, me_ref[0], shards, chunk)


def second_gram(me, shards, chunk, pieces, w, y):
    size = y.shape[0]
    return call(
        functools.partial(second_gram_kernel, shards, len(pieces), chunk, len(w)), "second_gram",
        halves(size), 32, 0.4, 3,
        in_specs=[SMEM] + [VMEM] * (len(pieces) + len(w) + 1),
        out_specs=[VMEM, VMEM],
        scratch_shapes=[pltpu.VMEM((size, size), BF16)] * 2
        + [pltpu.VMEM((size, size), F32), packed_scratch(size)],
    )(me, *pieces, *w, y)


def middle_kernel(shards, count, me_ref, *refs):
    first, second, refs = refs[:count], refs[count:2 * count], refs[2 * count:]
    x_ref, m_ref, out_ref, hi, lo, packed = refs
    unpack(first, packed, hi, lo, me_ref[0], shards, 0)
    unpack(second, packed, hi, lo, me_ref[0], shards, 1)
    sym = hi[...], lo[...]
    for r in range(0, x_ref.shape[0], 256):
        out_ref[r:r + 256] = m_ref[r:r + 256] - 0.5 * mm(split(x_ref[r:r + 256]), sym)


def middle_step(me, shards, first, second, x, m):
    rows, size = x.shape
    return call(
        functools.partial(middle_kernel, shards, len(first)), "middle", struct(rows, size), 32, 1, 4,
        in_specs=[SMEM] + [VMEM] * (2 * len(first) + 2),
        out_specs=VMEM,
        scratch_shapes=[pltpu.VMEM((size, size), BF16)] * 2 + [packed_scratch(size)],
    )(me, *first, *second, x, m)


def last_kernel(shards, count, me_ref, *refs):
    pieces = refs[:count]
    x_ref, z_ref, out_ref, hi, lo, packed = refs[count:]
    size = hi.shape[0]
    q = size // 4

    @pl.when(pl.program_id(0) == 0)
    def _():
        unpack(pieces, packed, hi, lo, me_ref[0], shards, 1)

    a = split(x_ref[:, q:])
    out_ref[:, :q] = z_ref[:, :q]
    out_ref[:, q:3 * q] = z_ref[:, q:3 * q] - 0.5 * mm(a, (hi[q:, q:3 * q], lo[q:, q:3 * q]))
    a = (a[0][:, :2 * q], a[1][:, :2 * q])
    out_ref[:, 3 * q:] = z_ref[:, 3 * q:] - 0.5 * mm(a, (hi[q:3 * q, 3 * q:], lo[q:3 * q, 3 * q:]))


def last_step(me, shards, pieces, x, z):
    rows, size = x.shape
    tile = 256
    block = pl.BlockSpec((tile, size), lambda r: (r, 0))
    return call(
        functools.partial(last_kernel, shards, len(pieces)), "last", struct(rows, size), 32, 0.5, 3,
        grid=(rows // tile,),
        in_specs=[SMEM] + [pl.BlockSpec(p.shape, lambda r: (0, 0)) for p in pieces] + [block, block],
        out_specs=block,
        scratch_shapes=[pltpu.VMEM((size, size), BF16)] * 2 + [packed_scratch(size)],
    )(me, *pieces, x, z)


CORE = 1
PLANE = (2, 4, 6)
SHARDS = 2 * (1 + len(PLANE))


def slot_of(index):
    return (index % 2) * (SHARDS // 2) + (index // 2) % (SHARDS // 2)


class Sum:
    def __init__(self, count, keep, send):
        self.count, self.keep, self.send = count, keep, send

    def swap(self, x, offset):
        return lax.ppermute(x, "row", [(i, i ^ offset) for i in range(self.count)])

    def core(self):
        return self.swap(self.send, CORE)

    def plane(self, got):
        total = self.keep + got
        part = total.shape[0] // (1 + len(PLANE))
        self.keep, *sends = [total[k * part:(k + 1) * part] for k in range(1 + len(PLANE))]
        return [self.swap(x, offset) for x, offset in zip(sends, PLANE)]

    def own(self, got):
        self.keep = sum(got, self.keep)

    def exchange(self, offset):
        return self.swap(self.keep, offset)

    def gather_plane(self):
        return [self.swap(self.keep, offset) for offset in PLANE]

    def gather_core(self, got):
        self.mine = jnp.concatenate([self.keep, *got], axis=0)
        return self.swap(self.mine, CORE)


def close(env, *got):
    values = lax.optimization_barrier((*got, *env.values()))
    env.update(zip(env, values[len(got):]))
    return values[:len(got)]


def sum_chunks(count, env, first, second, works, late):
    beyond = [1 << s for s in range(3, count.bit_length() - 1)]
    works = list(works)

    def work():
        if works:
            works.pop(0)(env)

    a = Sum(count, *first)
    got_a = a.core()
    pair = second(env)
    got_a, *pair = close(env, got_a, *pair)
    b = Sum(count, *pair)

    got_a, got_b = a.plane(got_a), b.core()
    work()
    *got_a, got_b = close(env, *got_a, got_b)
    a.own(got_a)

    for at, offset in enumerate(beyond):
        got_a = a.exchange(offset)
        got_b = [b.exchange(beyond[at - 1])] if at else b.plane(got_b)
        work()
        got_a, *got_b = close(env, got_a, *got_b)
        a.own([got_a])
        b.own(got_b)

    got_a, got_b = a.gather_plane(), b.exchange(beyond[-1])
    work()
    *got_a, got_b = close(env, *got_a, got_b)
    b.own([got_b])

    got_b = b.gather_plane()
    got_a = a.gather_core(got_a)
    (got_a,) = close(env, got_a)
    pieces_a = [a.mine, got_a]
    late(env, pieces_a)
    got_b = close(env, *got_b)
    got_b = b.gather_core(got_b)
    return pieces_a, [b.mine, got_b]


def body(count, orbitals_zero, orbitals_one, correlation_zero, correlation_one, cotangent):
    me = slot_of(lax.axis_index("row")).astype(jnp.int32).reshape(1)
    env = dict(
        x0=orbitals_zero, x1=orbitals_one, s0=correlation_zero, s1=correlation_one, c=cotangent
    )

    def direct(env):
        env["m"] = affine(env["c"], env["s1"])

    def put(name, left, right):
        def work(env):
            for half in (0, 1):
                env[f"{name}{half}"] = gram(env[left], env[right], half)
        return work

    def late_gram(env, pieces):
        env["y"] = partial_apply(
            me, SHARDS, pieces, [env["w0"], env["w1"]], [env["p0"], env["p1"]]
        )

    works = [direct, put("p", "x0", "m"), put("w", "x0", "x1")]
    first = first_gram(me, SHARDS, 0, env["x1"], env["c"])
    one_a, one_b = sum_chunks(
        count, env, first,
        lambda env: first_gram(me, SHARDS, 1, env["x1"], env["c"]), works, late_gram,
    )

    def middle(env):
        env["mid"] = middle_step(me, SHARDS, one_a, one_b, env["x1"], env["m"])

    def last_direct(env):
        env["d"] = affine(env["mid"], env["s0"])

    def late_result(env, pieces):
        env["z"] = partial_apply(me, SHARDS, pieces, [env["x0"]], [env["d"]])

    w = [env["w0"], env["w1"]]
    first = second_gram(me, SHARDS, 0, one_b, w, env["y"])
    two_a, two_b = sum_chunks(
        count, env, first,
        lambda env: second_gram(me, SHARDS, 1, one_b, [env["w0"], env["w1"]], env["y"]),
        [middle, last_direct], late_result,
    )
    return last_step(me, SHARDS, two_b, env["x0"], env["z"])


def solution(mesh):
    in_specs = (
        P(("kpt", "row"), None),
        P(("kpt", "row"), None),
        P("kpt", None),
        P("kpt", None),
        P(("kpt", "row"), None),
    )
    out_specs = P(("kpt", "row"), None)
    return jax.shard_map(
        functools.partial(body, mesh.shape["row"]),
        mesh=mesh, in_specs=in_specs, out_specs=out_specs, check_vma=False,
    )
```

```python
import functools
import jax
import jax.numpy as jnp
from jax import lax
from jax.experimental import pallas as pl
from jax.experimental.pallas import tpu as pltpu
from jax.sharding import PartitionSpec as P

F32 = jnp.float32
BF16 = jnp.bfloat16
B = 128
MIB = 1024 * 1024


def split(x):
    hi = x.astype(BF16)
    return hi, (x - hi.astype(F32)).astype(BF16)


def mm(a, b):
    (ah, al), (bh, bl) = a, b
    return jnp.dot(
        jnp.concatenate([ah, ah, al], axis=1),
        jnp.concatenate([bh, bl, bh], axis=0),
        preferred_element_type=F32,
    )


def call(kernel, name, out_shape, limit, products, arrays, **kw):
    size = 1024
    return pl.pallas_call(
        kernel,
        name=name,
        out_shape=out_shape,
        compiler_params=pltpu.CompilerParams(vmem_limit_bytes=limit * MIB),
        cost_estimate=pl.CostEstimate(
            flops=int(6 * products * size ** 3),
            bytes_accessed=int(4 * arrays * size * size),
            transcendentals=0,
        ),
        **kw,
    )


def struct(*shape, dtype=F32):
    return jax.ShapeDtypeStruct(shape, dtype)


SMEM = pl.BlockSpec(memory_space=pltpu.SMEM)
VMEM = pl.BlockSpec(memory_space=pltpu.VMEM)


def chunk_lines(size, chunk):
    half = size // B // 4
    return range(chunk * half, (chunk + 1) * half)


def line_blocks(size, i):
    n = size // B
    at = 0
    for top in (i, n - 1 - i):
        for j in range(top, n):
            yield at, slice(top * B, (top + 1) * B), slice(j * B, (j + 1) * B)
            at += B


def pack(g, packed, keep_ref, send_ref, me, shards, chunk):
    size = g.shape[0]
    rows = packed.shape[0] // shards
    per = B // rows
    for line, i in enumerate(chunk_lines(size, chunk)):
        for at, p, q in line_blocks(size, i):
            block = g[p, q] + g[q, p].T
            for s in range(per):
                slot = (line * per + s) ^ me
                packed[pl.ds(pl.multiple_of(slot * rows, rows), rows), at:at + B] = (
                    block[s * rows:(s + 1) * rows]
                )
    half = keep_ref.shape[0]
    keep_ref[...] = packed[:half]
    send_ref[...] = packed[half:]


def unpack(pieces, packed, hi, lo, me, shards, chunk):
    size = hi.shape[0]
    rows = packed.shape[0] // shards
    slot = 0
    for piece in pieces:
        for s in range(piece.shape[0] // rows):
            at = pl.multiple_of((slot ^ me) * rows, rows)
            packed[pl.ds(at, rows), :] = piece[s * rows:(s + 1) * rows, :]
            slot += 1
    for line, i in enumerate(chunk_lines(size, chunk)):
        for at, p, q in line_blocks(size, i):
            block = packed[line * B:(line + 1) * B, at:at + B]
            hi[p, q], lo[p, q] = split(block)
            if p.start != q.start:
                hi[q, p], lo[q, p] = split(block.T)


def packed_scratch(size):
    return pltpu.VMEM((size // 4, size + B), F32)


def halves(size):
    return [struct(size // 8, size + B)] * 2


def parts_of(size, chunk):
    q = size // 4
    if chunk == 0:
        return [(0, q, 0, size), (q, size, 0, q), (3 * q, size, 3 * q, size)]
    return [(q, 3 * q, q, size), (3 * q, size, q, 3 * q)]


def product_parts(g, ah, al, bh, bl, parts):
    for r0, r1, c0, c1 in parts:
        g[r0:r1, c0:c1] = mm((ah[r0:r1, :], al[r0:r1, :]), (bh[:, c0:c1], bl[:, c0:c1]))


def first_gram_kernel(
    shards, me_ref, a_hbm, b_hbm, keep_ref, send_ref, ah, al, bh, bl, a_buf, b_buf, sems, g, packed
):
    rows, size = a_buf.shape
    steps = sems.shape[1]
    tile = rows // steps
    copies = []
    for s in range(steps):
        r = slice(s * tile, (s + 1) * tile)
        pair = [
            pltpu.make_async_copy(src.at[r], dst.at[r], sems.at[k, s])
            for k, (src, dst) in enumerate([(a_hbm, a_buf), (b_hbm, b_buf)])
        ]
        for copy in pair:
            copy.start()
        copies.append((r, pair))
    for r, pair in copies:
        for copy in pair:
            copy.wait()
        ah[:, r], al[:, r] = split(a_buf[r].T)
        bh[r], bl[r] = split(b_buf[r])
    product_parts(g, ah, al, bh, bl, parts_of(size, 0))
    pack(g, packed, keep_ref, send_ref, me_ref[0], shards, 0)


def first_gram(me, shards, a, b):
    rows, size = a.shape
    hbm = pl.BlockSpec(memory_space=pltpu.HBM)
    return call(
        functools.partial(first_gram_kernel, shards), "first_gram",
        halves(size) + [struct(size, rows, dtype=BF16)] * 2 + [struct(rows, size, dtype=BF16)] * 2,
        43, 0.5, 4,
        in_specs=[SMEM, hbm, hbm],
        out_specs=[VMEM] * 6,
        scratch_shapes=[
            pltpu.VMEM((rows, size), F32), pltpu.VMEM((rows, size), F32),
            pltpu.SemaphoreType.DMA((2, 4)),
            pltpu.VMEM((size, size), F32), packed_scratch(size),
        ],
    )(me, a, b)


def other_gram_kernel(shards, me_ref, ah, al, bh, bl, keep_ref, send_ref, g, packed):
    product_parts(g, ah, al, bh, bl, parts_of(g.shape[0], 1))
    pack(g, packed, keep_ref, send_ref, me_ref[0], shards, 1)


def other_gram(me, shards, ah, al, bh, bl):
    size = ah.shape[0]
    return call(
        functools.partial(other_gram_kernel, shards), "other_gram", halves(size), 22, 0.5, 2,
        in_specs=[SMEM] + [VMEM] * 4,
        out_specs=[VMEM, VMEM],
        scratch_shapes=[pltpu.VMEM((size, size), F32), packed_scratch(size)],
    )(me, ah, al, bh, bl)


def affine_kernel(a_ref, b_ref, out_ref):
    rows, size = a_ref.shape
    tile = min(256, rows)
    b = split(b_ref[...])
    for r in range(0, rows, tile):
        a = a_ref[r:r + tile]
        out_ref[r:r + tile] = 1.5 * a - 0.5 * mm(split(a), b)


def affine(a, b, part, parts):
    rows, size = a.shape
    height = rows // parts
    return call(
        affine_kernel, "affine", struct(height, size), 24, 1 / parts, 2,
        grid=(1,),
        in_specs=[
            pl.BlockSpec((height, size), lambda r: (part, 0)),
            pl.BlockSpec((size, size), lambda r: (0, 0)),
        ],
        out_specs=pl.BlockSpec((height, size), lambda r: (0, 0)),
    )(a, b)


def apply_first(a, base, hi, lo):
    size = hi.shape[0]
    q = size // 4
    part = lambda k0, k1, c0, c1: mm(
        (a[0][:, k0:k1], a[1][:, k0:k1]), (hi[k0:k1, c0:c1], lo[k0:k1, c0:c1])
    )
    wide = part(0, q, 0, size)
    left = part(q, size, 0, q)
    corner = part(3 * q, size, 3 * q, size)
    return jnp.concatenate(
        [
            base[:, :q] - 0.5 * (wide[:, :q] + left),
            base[:, q:3 * q] - 0.5 * wide[:, q:3 * q],
            base[:, 3 * q:] - 0.5 * (wide[:, 3 * q:] + corner),
        ],
        axis=1,
    )


def tile_of(refs, at, tile):
    for ref in refs:
        if at < ref.shape[0]:
            return ref[at:at + tile]
        at -= ref.shape[0]


def partial_kernel(shards, count, me_ref, *refs):
    pieces, refs = refs[:count], refs[count:]
    a_ref, base_refs, (out_ref, hi, lo, packed) = refs[0], refs[1:-4], refs[-4:]
    unpack(pieces, packed, hi, lo, me_ref[0], shards, 0)
    tile = 256
    for r in range(0, out_ref.shape[0], tile):
        out_ref[r:r + tile] = apply_first(
            split(a_ref[r:r + tile]), tile_of(base_refs, r, tile), hi, lo
        )


def partial_apply(me, shards, pieces, a, base):
    rows, size = a.shape
    return call(
        functools.partial(partial_kernel, shards, len(pieces)), "partial_apply",
        struct(rows, size), 20, 0.5, 3,
        in_specs=[SMEM] + [VMEM] * (len(pieces) + 1 + len(base)),
        out_specs=VMEM,
        scratch_shapes=[pltpu.VMEM((size, size), BF16)] * 2 + [packed_scratch(size)],
    )(me, *pieces, a, *base)


def early_kernel(shards, count, me_ref, *refs):
    pieces, refs = refs[:count], refs[count:]
    a_ref, base_refs, refs = refs[0], refs[1:-8], refs[-8:]
    x_ref, out_ref, xh, xl, col_ref, hi, lo, packed = refs
    unpack(pieces, packed, hi, lo, me_ref[0], shards, 0)
    tile = 256
    for r in range(0, out_ref.shape[0], tile):
        out_ref[r:r + tile] = apply_first(
            split(a_ref[r:r + tile]), tile_of(base_refs, r, tile), hi, lo
        )
    xh[...], xl[...] = split(x_ref[...].T)
    q = col_ref.shape[1]
    col_ref[...] = mm((xh[...], xl[...]), split(out_ref[:, :q]))


def early_middle(me, shards, pieces, a, base, x):
    rows, size = a.shape
    part = struct(size, rows, dtype=BF16)
    return call(
        functools.partial(early_kernel, shards, len(pieces)), "early_middle",
        [struct(rows, size), part, part, struct(size, size // 4)], 22, 0.75, 5,
        in_specs=[SMEM] + [VMEM] * (len(pieces) + 2 + len(base)),
        out_specs=[VMEM] * 4,
        scratch_shapes=[pltpu.VMEM((size, size), BF16)] * 2 + [packed_scratch(size)],
    )(me, *pieces, a, *base, x)


def apply_second(a, base, hi, lo):
    size = hi.shape[0]
    q = size // 4
    part = lambda k1, c0, c1: mm(
        (a[0][:, q:k1], a[1][:, q:k1]), (hi[q:k1, c0:c1], lo[q:k1, c0:c1])
    )
    return jnp.concatenate(
        [base[:, q:3 * q] - 0.5 * part(size, q, 3 * q), base[:, 3 * q:] - 0.5 * part(3 * q, 3 * q, size)],
        axis=1,
    )


def second_gram_kernel(shards, count, me_ref, *refs):
    pieces, refs = refs[:count], refs[count:]
    a_ref, base_ref, xh, xl, col_ref, refs = refs[0], refs[1], refs[2], refs[3], refs[4], refs[5:]
    keep_ref, send_ref, mid_ref, mh, ml, hi, lo, g, packed = refs
    unpack(pieces, packed, hi, lo, me_ref[0], shards, 1)
    rows, size = a_ref.shape
    q = size // 4
    tile = 256
    mid_ref[:, :q] = base_ref[:, :q]
    for r in range(0, rows, tile):
        t = slice(r, r + tile)
        mid = apply_second(split(a_ref[t]), base_ref[t], hi, lo)
        mid_ref[t, q:] = mid
        mh[t], ml[t] = split(mid)
    g[:, :q] = col_ref[...]
    g[:q, q:] = mm((xh[:q, :], xl[:q, :]), (mh[...], ml[...]))
    g[3 * q:, 3 * q:] = mm((xh[3 * q:, :], xl[3 * q:, :]), (mh[:, 2 * q:], ml[:, 2 * q:]))
    pack(g, packed, keep_ref, send_ref, me_ref[0], shards, 0)


def second_gram(me, shards, pieces, a, base, xh, xl, col):
    rows, size = a.shape
    part = struct(rows, size - size // 4, dtype=BF16)
    return call(
        functools.partial(second_gram_kernel, shards, len(pieces)), "second_gram",
        halves(size) + [struct(rows, size), part, part], 22, 0.8, 5,
        in_specs=[SMEM] + [VMEM] * (len(pieces) + 5),
        out_specs=[VMEM] * 5,
        scratch_shapes=[pltpu.VMEM((size, size), BF16)] * 2
        + [pltpu.VMEM((size, size), F32), packed_scratch(size)],
    )(me, *pieces, a, base, xh, xl, col)


def fourth_gram_kernel(shards, me_ref, xh, xl, mh, ml, keep_ref, send_ref, g, packed):
    size = g.shape[0]
    q = size // 4
    for r0, r1, c0, c1 in parts_of(size, 1):
        g[r0:r1, c0:c1] = mm(
            (xh[r0:r1, :], xl[r0:r1, :]), (mh[:, c0 - q:c1 - q], ml[:, c0 - q:c1 - q])
        )
    pack(g, packed, keep_ref, send_ref, me_ref[0], shards, 1)


def fourth_gram(me, shards, xh, xl, mh, ml):
    size = xh.shape[0]
    return call(
        functools.partial(fourth_gram_kernel, shards), "fourth_gram", halves(size), 22, 0.5, 2,
        in_specs=[SMEM] + [VMEM] * 4,
        out_specs=[VMEM, VMEM],
        scratch_shapes=[pltpu.VMEM((size, size), F32), packed_scratch(size)],
    )(me, xh, xl, mh, ml)


def last_kernel(shards, count, me_ref, *refs):
    pieces = refs[:count]
    x_ref, z_ref, out_ref, hi, lo, packed = refs[count:]
    size = hi.shape[0]
    q = size // 4

    @pl.when(pl.program_id(0) == 0)
    def _():
        unpack(pieces, packed, hi, lo, me_ref[0], shards, 1)

    a = split(x_ref[:, q:])
    out_ref[:, :q] = z_ref[:, :q]
    out_ref[:, q:3 * q] = z_ref[:, q:3 * q] - 0.5 * mm(a, (hi[q:, q:3 * q], lo[q:, q:3 * q]))
    a = (a[0][:, :2 * q], a[1][:, :2 * q])
    out_ref[:, 3 * q:] = z_ref[:, 3 * q:] - 0.5 * mm(a, (hi[q:3 * q, 3 * q:], lo[q:3 * q, 3 * q:]))


def last_step(me, shards, pieces, x, z):
    rows, size = x.shape
    tile = 256
    block = pl.BlockSpec((tile, size), lambda r: (r, 0))
    return call(
        functools.partial(last_kernel, shards, len(pieces)), "last", struct(rows, size), 20, 0.5, 3,
        grid=(rows // tile,),
        in_specs=[SMEM] + [pl.BlockSpec(p.shape, lambda r: (0, 0)) for p in pieces] + [block, block],
        out_specs=block,
        scratch_shapes=[pltpu.VMEM((size, size), BF16)] * 2 + [packed_scratch(size)],
    )(me, *pieces, x, z)


CORE = 1
PLANE = (2, 4, 6)
SHARDS = 2 * (1 + len(PLANE))


def slot_of(index):
    return (index % 2) * (SHARDS // 2) + (index // 2) % (SHARDS // 2)


class Sum:
    def __init__(self, count, keep, send):
        self.count, self.keep, self.send = count, keep, send

    def swap(self, x, offset):
        return lax.ppermute(x, "row", [(i, i ^ offset) for i in range(self.count)])

    def core(self):
        return self.swap(self.send, CORE)

    def plane(self, got):
        total = self.keep + got
        part = total.shape[0] // (1 + len(PLANE))
        self.keep, *sends = [total[k * part:(k + 1) * part] for k in range(1 + len(PLANE))]
        return [self.swap(x, offset) for x, offset in zip(sends, PLANE)]

    def own(self, got):
        self.keep = sum(got, self.keep)

    def exchange(self, offset):
        return self.swap(self.keep, offset)

    def gather_plane(self):
        return [self.swap(self.keep, offset) for offset in PLANE]

    def gather_core(self, got):
        self.mine = jnp.concatenate([self.keep, *got], axis=0)
        return self.swap(self.mine, CORE)


def close(env, *got):
    values = lax.optimization_barrier((*got, *env.values()))
    env.update(zip(env, values[len(got):]))
    return values[:len(got)]


def sum_chunks(count, env, first, second, works, late):
    beyond = [1 << s for s in range(3, count.bit_length() - 1)]
    works = list(works)

    def work():
        if works:
            works.pop(0)(env)

    a = Sum(count, *first)
    got_a = a.core()
    pair = second(env)
    got_a, *pair = close(env, got_a, *pair)
    b = Sum(count, *pair)

    got_a = a.plane(got_a)
    got_b = b.core()
    work()
    (got_b,) = close(env, got_b)

    got_b = b.plane(got_b)
    work()
    a.own(close(env, *got_a))

    for offset in beyond:
        got_a = a.exchange(offset)
        b.own(close(env, *got_b))
        got_b = [b.exchange(offset)]
        a.own(close(env, got_a))

    got_a = a.gather_plane()
    b.own(close(env, *got_b))

    got_b = b.gather_plane()
    work()
    got_a = a.gather_core(close(env, *got_a))
    pieces_a = [a.mine, *close(env, got_a)]
    late(env, pieces_a)
    got_b = b.gather_core(close(env, *got_b))
    return pieces_a, [b.mine, got_b]


def body(count, orbitals_zero, orbitals_one, correlation_zero, correlation_one, cotangent):
    me = slot_of(lax.axis_index("row")).astype(jnp.int32).reshape(1)
    env = dict(
        x0=orbitals_zero, x1=orbitals_one, s0=correlation_zero, s1=correlation_one, c=cotangent
    )

    def thirds(name, left, right):
        def put(at, part, parts):
            def work(env):
                env[f"{name}{at}"] = affine(env[left], env[right], part, parts)
            return work
        return [put(0, 0, 2), put(1, 2, 4), put(2, 3, 4)]

    def three(env, name):
        return [env[f"{name}{at}"] for at in range(3)]

    def early(env, pieces):
        env["mid"], env["xh"], env["xl"], env["col"] = early_middle(
            me, SHARDS, pieces, env["x1"], three(env, "m"), env["x0"]
        )

    keep, send, *parts = first_gram(me, SHARDS, env["x1"], env["c"])
    _, one = sum_chunks(
        count, env, (keep, send), lambda env: other_gram(me, SHARDS, *parts),
        thirds("m", "c", "s1"), early,
    )

    keep, send, env["mid"], mh, ml = second_gram(
        me, SHARDS, one, env["x1"], env["mid"], env["xh"], env["xl"], env["col"]
    )

    def late(env, pieces):
        env["z"] = partial_apply(me, SHARDS, pieces, env["x0"], three(env, "d"))

    _, two = sum_chunks(
        count, env, (keep, send),
        lambda env: fourth_gram(me, SHARDS, env["xh"], env["xl"], mh, ml),
        thirds("d", "mid", "s0"), late,
    )
    return last_step(me, SHARDS, two, env["x0"], env["z"])


def solution(mesh):
    in_specs = (
        P(("kpt", "row"), None),
        P(("kpt", "row"), None),
        P("kpt", None),
        P("kpt", None),
        P(("kpt", "row"), None),
    )
    out_specs = P(("kpt", "row"), None)
    return jax.shard_map(
        functools.partial(body, mesh.shape["row"]),
        mesh=mesh, in_specs=in_specs, out_specs=out_specs, check_vma=False,
    )
```

```python
import functools
import jax
import jax.numpy as jnp
from jax import lax
from jax.experimental import pallas as pl
from jax.experimental.pallas import tpu as pltpu
from jax.sharding import PartitionSpec as P

F32 = jnp.float32
BF16 = jnp.bfloat16
B = 128
MIB = 1024 * 1024


def split(x):
    hi = x.astype(BF16)
    return hi, (x - hi.astype(F32)).astype(BF16)


def mm(a, b):
    (ah, al), (bh, bl) = a, b
    return jnp.dot(
        jnp.concatenate([ah, ah, al], axis=1),
        jnp.concatenate([bh, bl, bh], axis=0),
        preferred_element_type=F32,
    )


def call(kernel, name, out_shape, limit, products, arrays, **kw):
    size = 1024
    return pl.pallas_call(
        kernel,
        name=name,
        out_shape=out_shape,
        compiler_params=pltpu.CompilerParams(vmem_limit_bytes=limit * MIB),
        cost_estimate=pl.CostEstimate(
            flops=int(6 * products * size ** 3),
            bytes_accessed=int(4 * arrays * size * size),
            transcendentals=0,
        ),
        **kw,
    )


def struct(*shape, dtype=F32):
    return jax.ShapeDtypeStruct(shape, dtype)


SMEM = pl.BlockSpec(memory_space=pltpu.SMEM)
VMEM = pl.BlockSpec(memory_space=pltpu.VMEM)


def chunk_lines(size, chunk):
    half = size // B // 4
    return range(chunk * half, (chunk + 1) * half)


def line_blocks(size, i):
    n = size // B
    at = 0
    for top in (i, n - 1 - i):
        for j in range(top, n):
            yield at, slice(top * B, (top + 1) * B), slice(j * B, (j + 1) * B)
            at += B


def pack(g, packed, keep_ref, send_ref, me, shards, chunk):
    size = g.shape[0]
    rows = packed.shape[0] // shards
    per = B // rows
    for line, i in enumerate(chunk_lines(size, chunk)):
        for at, p, q in line_blocks(size, i):
            block = g[p, q] + g[q, p].T
            for s in range(per):
                slot = (line * per + s) ^ me
                packed[pl.ds(pl.multiple_of(slot * rows, rows), rows), at:at + B] = (
                    block[s * rows:(s + 1) * rows]
                )
    half = keep_ref.shape[0]
    keep_ref[...] = packed[:half]
    send_ref[...] = packed[half:]


def unpack(pieces, packed, hi, lo, me, shards, chunk):
    size = hi.shape[0]
    rows = packed.shape[0] // shards
    slot = 0
    for piece in pieces:
        for s in range(piece.shape[0] // rows):
            at = pl.multiple_of((slot ^ me) * rows, rows)
            packed[pl.ds(at, rows), :] = piece[s * rows:(s + 1) * rows, :]
            slot += 1
    for line, i in enumerate(chunk_lines(size, chunk)):
        for at, p, q in line_blocks(size, i):
            block = packed[line * B:(line + 1) * B, at:at + B]
            hi[p, q], lo[p, q] = split(block)
            if p.start != q.start:
                hi[q, p], lo[q, p] = split(block.T)


def packed_scratch(size):
    return pltpu.VMEM((size // 4, size + B), F32)


def halves(size):
    return [struct(size // 8, size + B)] * 2


def first_gram_kernel(
    shards, me_ref, a_hbm, b_hbm, keep_ref, send_ref, ah, al, bh, bl, a_buf, b_buf, sems, g, packed
):
    rows, size = a_buf.shape
    steps = sems.shape[1]
    tile = rows // steps
    copies = []
    for s in range(steps):
        r = slice(s * tile, (s + 1) * tile)
        pair = [
            pltpu.make_async_copy(src.at[r], dst.at[r], sems.at[k, s])
            for k, (src, dst) in enumerate([(a_hbm, a_buf), (b_hbm, b_buf)])
        ]
        for copy in pair:
            copy.start()
        copies.append((r, pair))
    for r, pair in copies:
        for copy in pair:
            copy.wait()
        ah[:, r], al[:, r] = split(a_buf[r].T)
        bh[r], bl[r] = split(b_buf[r])
    q = size // 4
    for r0, r1, c0, c1 in [(0, q, 0, size), (q, size, 0, q), (3 * q, size, 3 * q, size)]:
        g[r0:r1, c0:c1] = mm((ah[r0:r1, :], al[r0:r1, :]), (bh[:, c0:c1], bl[:, c0:c1]))
    pack(g, packed, keep_ref, send_ref, me_ref[0], shards, 0)


def first_gram(me, shards, a, b):
    rows, size = a.shape
    hbm = pl.BlockSpec(memory_space=pltpu.HBM)
    return call(
        functools.partial(first_gram_kernel, shards), "first_gram",
        halves(size) + [struct(size, rows, dtype=BF16)] * 2 + [struct(rows, size, dtype=BF16)] * 2,
        43, 0.5, 4,
        in_specs=[SMEM, hbm, hbm],
        out_specs=[VMEM] * 6,
        scratch_shapes=[
            pltpu.VMEM((rows, size), F32), pltpu.VMEM((rows, size), F32),
            pltpu.SemaphoreType.DMA((2, 4)),
            pltpu.VMEM((size, size), F32), packed_scratch(size),
        ],
    )(me, a, b)


def lower_product(g, ah, al, bh, bl):
    q = g.shape[0] // 4

    def step(r):
        t = pl.ds(pl.multiple_of(q + r.start, r.size), r.size)
        g[t, q:] = mm((ah[t], al[t]), (bh, bl))

    row_tiles(3 * q, q, step)


def other_gram_kernel(shards, me_ref, ah, al, bh, bl, keep_ref, send_ref, g, packed):
    q = g.shape[0] // 4
    lower_product(g, ah, al, bh[:, q:], bl[:, q:])
    pack(g, packed, keep_ref, send_ref, me_ref[0], shards, 1)


def other_gram(me, shards, ah, al, bh, bl):
    size = ah.shape[0]
    return call(
        functools.partial(other_gram_kernel, shards), "other_gram", halves(size), 22, 0.5, 2,
        in_specs=[SMEM] + [VMEM] * 4,
        out_specs=[VMEM, VMEM],
        scratch_shapes=[pltpu.VMEM((size, size), F32), packed_scratch(size)],
    )(me, ah, al, bh, bl)


def row_tiles(rows, tile, step):
    def body(t, _):
        step(pl.ds(pl.multiple_of(t * tile, tile), tile))
        return 0

    lax.fori_loop(0, rows // tile, body, 0)


def affine_kernel(a_ref, b_ref, out_ref, hi, lo):
    hi[...], lo[...] = split(b_ref[...])

    def step(r):
        a = a_ref[r]
        out_ref[r] = 1.5 * a - 0.5 * mm(split(a), (hi[...], lo[...]))

    row_tiles(a_ref.shape[0], 128, step)


def affine(a, b, part, parts):
    rows, size = a.shape
    height = rows // parts
    return call(
        affine_kernel, "affine", struct(height, size), 24, 1 / parts, 2,
        grid=(1,),
        in_specs=[
            pl.BlockSpec((height, size), lambda r: (part, 0)),
            pl.BlockSpec((size, size), lambda r: (0, 0)),
        ],
        out_specs=pl.BlockSpec((height, size), lambda r: (0, 0)),
        scratch_shapes=[pltpu.VMEM((size, size), BF16)] * 2,
    )(a, b)


def apply_first(a, base, hi, lo):
    size = hi.shape[0]
    q = size // 4
    part = lambda k0, k1, c0, c1: mm(
        (a[0][:, k0:k1], a[1][:, k0:k1]), (hi[k0:k1, c0:c1], lo[k0:k1, c0:c1])
    )
    wide = part(0, q, 0, size)
    left = part(q, size, 0, q)
    corner = part(3 * q, size, 3 * q, size)
    return jnp.concatenate(
        [
            base[:, :q] - 0.5 * (wide[:, :q] + left),
            base[:, q:3 * q] - 0.5 * wide[:, q:3 * q],
            base[:, 3 * q:] - 0.5 * (wide[:, 3 * q:] + corner),
        ],
        axis=1,
    )


def apply_parts(a_ref, base_refs, out_ref, hi, lo):
    at = 0
    for base_ref in base_refs:
        start = at

        def step(r):
            t = pl.ds(pl.multiple_of(start + r.start, r.size), r.size)
            out_ref[t] = apply_first(split(a_ref[t]), base_ref[r], hi, lo)

        row_tiles(base_ref.shape[0], 256, step)
        at += base_ref.shape[0]


def partial_kernel(shards, count, me_ref, *refs):
    pieces, refs = refs[:count], refs[count:]
    a_ref, base_refs, (out_ref, hi, lo, packed) = refs[0], refs[1:-4], refs[-4:]
    unpack(pieces, packed, hi, lo, me_ref[0], shards, 0)
    apply_parts(a_ref, base_refs, out_ref, hi, lo)


def partial_apply(me, shards, pieces, a, base):
    rows, size = a.shape
    return call(
        functools.partial(partial_kernel, shards, len(pieces)), "partial_apply",
        struct(rows, size), 20, 0.5, 3,
        in_specs=[SMEM] + [VMEM] * (len(pieces) + 1 + len(base)),
        out_specs=VMEM,
        scratch_shapes=[pltpu.VMEM((size, size), BF16)] * 2 + [packed_scratch(size)],
    )(me, *pieces, a, *base)


def early_kernel(shards, count, me_ref, *refs):
    pieces, refs = refs[:count], refs[count:]
    a_ref, base_refs, refs = refs[0], refs[1:-8], refs[-8:]
    x_ref, out_ref, xh, xl, col_ref, hi, lo, packed = refs
    unpack(pieces, packed, hi, lo, me_ref[0], shards, 0)
    apply_parts(a_ref, base_refs, out_ref, hi, lo)
    xh[...], xl[...] = split(x_ref[...].T)
    q = col_ref.shape[1]
    col = split(out_ref[:, :q])

    def step(r):
        col_ref[r] = mm((xh[r], xl[r]), col)

    row_tiles(col_ref.shape[0], 512, step)


def early_middle(me, shards, pieces, a, base, x):
    rows, size = a.shape
    part = struct(size, rows, dtype=BF16)
    return call(
        functools.partial(early_kernel, shards, len(pieces)), "early_middle",
        [struct(rows, size), part, part, struct(size, size // 4)], 22, 0.75, 5,
        in_specs=[SMEM] + [VMEM] * (len(pieces) + 2 + len(base)),
        out_specs=[VMEM] * 4,
        scratch_shapes=[pltpu.VMEM((size, size), BF16)] * 2 + [packed_scratch(size)],
    )(me, *pieces, a, *base, x)


def apply_second(a, base, hi, lo):
    size = hi.shape[0]
    q = size // 4
    part = lambda k1, c0, c1: mm(
        (a[0][:, q:k1], a[1][:, q:k1]), (hi[q:k1, c0:c1], lo[q:k1, c0:c1])
    )
    return jnp.concatenate(
        [base[:, q:3 * q] - 0.5 * part(size, q, 3 * q), base[:, 3 * q:] - 0.5 * part(3 * q, 3 * q, size)],
        axis=1,
    )


def second_gram_kernel(shards, count, me_ref, *refs):
    pieces, refs = refs[:count], refs[count:]
    a_ref, base_ref, xh, xl, col_ref, refs = refs[0], refs[1], refs[2], refs[3], refs[4], refs[5:]
    keep_ref, send_ref, mid_ref, mh, ml, hi, lo, g, packed = refs
    unpack(pieces, packed, hi, lo, me_ref[0], shards, 1)
    rows, size = a_ref.shape
    q = size // 4
    mid_ref[:, :q] = base_ref[:, :q]

    def step(t):
        mid = apply_second(split(a_ref[t]), base_ref[t], hi, lo)
        mid_ref[t, q:] = mid
        mh[t], ml[t] = split(mid)

    row_tiles(rows, 512, step)
    g[:, :q] = col_ref[...]
    g[:q, q:] = mm((xh[:q, :], xl[:q, :]), (mh[...], ml[...]))
    g[3 * q:, 3 * q:] = mm((xh[3 * q:, :], xl[3 * q:, :]), (mh[:, 2 * q:], ml[:, 2 * q:]))
    pack(g, packed, keep_ref, send_ref, me_ref[0], shards, 0)


def second_gram(me, shards, pieces, a, base, xh, xl, col):
    rows, size = a.shape
    part = struct(rows, size - size // 4, dtype=BF16)
    return call(
        functools.partial(second_gram_kernel, shards, len(pieces)), "second_gram",
        halves(size) + [struct(rows, size), part, part], 22, 0.8, 5,
        in_specs=[SMEM] + [VMEM] * (len(pieces) + 5),
        out_specs=[VMEM] * 5,
        scratch_shapes=[pltpu.VMEM((size, size), BF16)] * 2
        + [pltpu.VMEM((size, size), F32), packed_scratch(size)],
    )(me, *pieces, a, base, xh, xl, col)


def fourth_gram_kernel(shards, me_ref, xh, xl, mh, ml, keep_ref, send_ref, g, packed):
    lower_product(g, xh, xl, mh[...], ml[...])
    pack(g, packed, keep_ref, send_ref, me_ref[0], shards, 1)


def fourth_gram(me, shards, xh, xl, mh, ml):
    size = xh.shape[0]
    return call(
        functools.partial(fourth_gram_kernel, shards), "fourth_gram", halves(size), 22, 0.5, 2,
        in_specs=[SMEM] + [VMEM] * 4,
        out_specs=[VMEM, VMEM],
        scratch_shapes=[pltpu.VMEM((size, size), F32), packed_scratch(size)],
    )(me, xh, xl, mh, ml)


def last_kernel(shards, count, me_ref, *refs):
    pieces = refs[:count]
    x_ref, z_ref, out_ref, hi, lo, packed = refs[count:]
    size = hi.shape[0]
    q = size // 4

    @pl.when(pl.program_id(0) == 0)
    def _():
        unpack(pieces, packed, hi, lo, me_ref[0], shards, 1)

    a = split(x_ref[:, q:])
    out_ref[:, :q] = z_ref[:, :q]
    out_ref[:, q:3 * q] = z_ref[:, q:3 * q] - 0.5 * mm(a, (hi[q:, q:3 * q], lo[q:, q:3 * q]))
    a = (a[0][:, :2 * q], a[1][:, :2 * q])
    out_ref[:, 3 * q:] = z_ref[:, 3 * q:] - 0.5 * mm(a, (hi[q:3 * q, 3 * q:], lo[q:3 * q, 3 * q:]))


def last_step(me, shards, pieces, x, z):
    rows, size = x.shape
    tile = 256
    block = pl.BlockSpec((tile, size), lambda r: (r, 0))
    return call(
        functools.partial(last_kernel, shards, len(pieces)), "last", struct(rows, size), 20, 0.5, 3,
        grid=(rows // tile,),
        in_specs=[SMEM] + [pl.BlockSpec(p.shape, lambda r: (0, 0)) for p in pieces] + [block, block],
        out_specs=block,
        scratch_shapes=[pltpu.VMEM((size, size), BF16)] * 2 + [packed_scratch(size)],
    )(me, *pieces, x, z)


CORE = 1
PLANE = (2, 4, 6)
SHARDS = 2 * (1 + len(PLANE))


def slot_of(index):
    return (index % 2) * (SHARDS // 2) + (index // 2) % (SHARDS // 2)


class Sum:
    def __init__(self, count, keep, send):
        self.count, self.keep, self.send = count, keep, send

    def swap(self, x, offset):
        return lax.ppermute(x, "row", [(i, i ^ offset) for i in range(self.count)])

    def core(self):
        return self.swap(self.send, CORE)

    def plane(self, got):
        total = self.keep + got
        part = total.shape[0] // (1 + len(PLANE))
        self.keep, *sends = [total[k * part:(k + 1) * part] for k in range(1 + len(PLANE))]
        return [self.swap(x, offset) for x, offset in zip(sends, PLANE)]

    def own(self, got):
        self.keep = sum(got, self.keep)

    def exchange(self, offset):
        return self.swap(self.keep, offset)

    def gather_plane(self):
        return [self.swap(self.keep, offset) for offset in PLANE]

    def gather_core(self, got):
        self.mine = jnp.concatenate([self.keep, *got], axis=0)
        return self.swap(self.mine, CORE)


def close(env, *got):
    values = lax.optimization_barrier((*got, *env.values()))
    env.update(zip(env, values[len(got):]))
    return values[:len(got)]


def sum_chunks(count, env, first, second, works, late):
    beyond = [1 << s for s in range(3, count.bit_length() - 1)]
    works = list(works)

    def work():
        if works:
            works.pop(0)(env)

    a = Sum(count, *first)
    got_a = a.core()
    pair = second(env)
    got_a, *pair = close(env, got_a, *pair)
    b = Sum(count, *pair)

    got_a = a.plane(got_a)
    got_b = b.core()
    work()
    (got_b,) = close(env, got_b)

    got_b = b.plane(got_b)
    work()
    a.own(close(env, *got_a))

    for offset in beyond:
        got_a = a.exchange(offset)
        b.own(close(env, *got_b))
        got_b = [b.exchange(offset)]
        a.own(close(env, got_a))

    got_a = a.gather_plane()
    b.own(close(env, *got_b))

    got_b = b.gather_plane()
    work()
    *got_a, got_b[0] = close(env, *got_a, got_b[0])
    got_a = a.gather_core(got_a)
    pieces_a = [a.mine, *close(env, got_a)]
    late(env, pieces_a)
    got_b = b.gather_core(close(env, *got_b))
    return pieces_a, [b.mine, got_b]


def body(count, orbitals_zero, orbitals_one, correlation_zero, correlation_one, cotangent):
    me = slot_of(lax.axis_index("row")).astype(jnp.int32).reshape(1)
    env = dict(
        x0=orbitals_zero, x1=orbitals_one, s0=correlation_zero, s1=correlation_one, c=cotangent
    )

    def thirds(name, left, right):
        def put(at, part, parts):
            def work(env):
                env[f"{name}{at}"] = affine(env[left], env[right], part, parts)
            return work
        return [put(0, 0, 2), put(1, 2, 4), put(2, 3, 4)]

    def three(env, name):
        return [env[f"{name}{at}"] for at in range(3)]

    def early(env, pieces):
        env["mid"], env["xh"], env["xl"], env["col"] = early_middle(
            me, SHARDS, pieces, env["x1"], three(env, "m"), env["x0"]
        )

    keep, send, *parts = first_gram(me, SHARDS, env["x1"], env["c"])
    _, one = sum_chunks(
        count, env, (keep, send), lambda env: other_gram(me, SHARDS, *parts),
        thirds("m", "c", "s1"), early,
    )

    keep, send, env["mid"], mh, ml = second_gram(
        me, SHARDS, one, env["x1"], env["mid"], env["xh"], env["xl"], env["col"]
    )

    def late(env, pieces):
        env["z"] = partial_apply(me, SHARDS, pieces, env["x0"], three(env, "d"))

    _, two = sum_chunks(
        count, env, (keep, send),
        lambda env: fourth_gram(me, SHARDS, env["xh"], env["xl"], mh, ml),
        thirds("d", "mid", "s0"), late,
    )
    return last_step(me, SHARDS, two, env["x0"], env["z"])


def solution(mesh):
    in_specs = (
        P(("kpt", "row"), None),
        P(("kpt", "row"), None),
        P("kpt", None),
        P("kpt", None),
        P(("kpt", "row"), None),
    )
    out_specs = P(("kpt", "row"), None)
    return jax.shard_map(
        functools.partial(body, mesh.shape["row"]),
        mesh=mesh, in_specs=in_specs, out_specs=out_specs, check_vma=False,
    )
```

```python
import functools
import jax
import jax.numpy as jnp
from jax import lax
from jax.experimental import pallas as pl
from jax.experimental.pallas import tpu as pltpu
from jax.sharding import PartitionSpec as P

F32 = jnp.float32
BF16 = jnp.bfloat16
B = 128
MIB = 1024 * 1024


def split(x):
    hi = x.astype(BF16)
    return hi, (x - hi.astype(F32)).astype(BF16)


def mm(a, b):
    (ah, al), (bh, bl) = a, b
    return jnp.dot(
        jnp.concatenate([ah, ah, al], axis=1),
        jnp.concatenate([bh, bl, bh], axis=0),
        preferred_element_type=F32,
    )


def call(kernel, name, out_shape, limit, products, arrays, **kw):
    size = 1024
    return pl.pallas_call(
        kernel,
        name=name,
        out_shape=out_shape,
        compiler_params=pltpu.CompilerParams(vmem_limit_bytes=limit * MIB),
        cost_estimate=pl.CostEstimate(
            flops=int(6 * products * size ** 3),
            bytes_accessed=int(4 * arrays * size * size),
            transcendentals=0,
        ),
        **kw,
    )


def struct(*shape, dtype=F32):
    return jax.ShapeDtypeStruct(shape, dtype)


SMEM = pl.BlockSpec(memory_space=pltpu.SMEM)
VMEM = pl.BlockSpec(memory_space=pltpu.VMEM)


def chunk_lines(size, chunk):
    half = size // B // 4
    return range(chunk * half, (chunk + 1) * half)


def line_blocks(size, i):
    n = size // B
    at = 0
    for top in (i, n - 1 - i):
        for j in range(top, n):
            yield at, slice(top * B, (top + 1) * B), slice(j * B, (j + 1) * B)
            at += B


def pack(g, packed, keep_ref, send_ref, me, shards, chunk):
    size = g.shape[0]
    rows = packed.shape[0] // shards
    per = B // rows
    for line, i in enumerate(chunk_lines(size, chunk)):
        for at, p, q in line_blocks(size, i):
            block = g[p, q] + g[q, p].T
            for s in range(per):
                slot = (line * per + s) ^ me
                packed[pl.ds(pl.multiple_of(slot * rows, rows), rows), at:at + B] = (
                    block[s * rows:(s + 1) * rows]
                )
    half = keep_ref.shape[0]
    keep_ref[...] = packed[:half]
    send_ref[...] = packed[half:]


def unpack(pieces, packed, hi, lo, me, shards, chunk):
    size = hi.shape[0]
    rows = packed.shape[0] // shards
    slot = 0
    for piece in pieces:
        for s in range(piece.shape[0] // rows):
            at = pl.multiple_of((slot ^ me) * rows, rows)
            packed[pl.ds(at, rows), :] = piece[s * rows:(s + 1) * rows, :]
            slot += 1
    for line, i in enumerate(chunk_lines(size, chunk)):
        for at, p, q in line_blocks(size, i):
            block = packed[line * B:(line + 1) * B, at:at + B]
            hi[p, q], lo[p, q] = split(block)
            if p.start != q.start:
                hi[q, p], lo[q, p] = split(block.T)


def packed_scratch(size):
    return pltpu.VMEM((size // 4, size + B), F32)


def halves(size):
    return [struct(size // 8, size + B)] * 2


def first_gram_kernel(
    shards, me_ref, a_hbm, b_hbm, keep_ref, send_ref, ah, al, bh, bl, a_buf, b_buf, sems, g, packed
):
    rows, size = a_buf.shape
    steps = sems.shape[1]
    tile = rows // steps
    copies = []
    for s in range(steps):
        r = slice(s * tile, (s + 1) * tile)
        pair = [
            pltpu.make_async_copy(src.at[r], dst.at[r], sems.at[k, s])
            for k, (src, dst) in enumerate([(a_hbm, a_buf), (b_hbm, b_buf)])
        ]
        for copy in pair:
            copy.start()
        copies.append((r, pair))
    q = size // 4
    for r, pair in copies:
        for copy in pair:
            copy.wait()
        ah[:, r], al[:, r] = split(a_buf[r].T)
        bh[r], bl[r] = split(b_buf[r])
        for r0, r1, c0, c1 in [(0, q, 0, size), (q, size, 0, q), (3 * q, size, 3 * q, size)]:
            product = mm((ah[r0:r1, r], al[r0:r1, r]), (bh[r, c0:c1], bl[r, c0:c1]))
            if r.start:
                product += g[r0:r1, c0:c1]
            g[r0:r1, c0:c1] = product
    pack(g, packed, keep_ref, send_ref, me_ref[0], shards, 0)


def first_gram(me, shards, a, b):
    rows, size = a.shape
    hbm = pl.BlockSpec(memory_space=pltpu.HBM)
    return call(
        functools.partial(first_gram_kernel, shards), "first_gram",
        halves(size) + [struct(size, rows, dtype=BF16)] * 2 + [struct(rows, size, dtype=BF16)] * 2,
        43, 0.5, 4,
        in_specs=[SMEM, hbm, hbm],
        out_specs=[VMEM] * 6,
        scratch_shapes=[
            pltpu.VMEM((rows, size), F32), pltpu.VMEM((rows, size), F32),
            pltpu.SemaphoreType.DMA((2, 4)),
            pltpu.VMEM((size, size), F32), packed_scratch(size),
        ],
    )(me, a, b)


def lower_product(g, ah, al, bh, bl):
    size = g.shape[0]
    q = size // 4
    for r0, r1, c0, c1 in [(q, 3 * q, q, size), (3 * q, size, q, 3 * q)]:
        c = slice(c0 - q, c1 - q)
        g[r0:r1, c0:c1] = mm((ah[r0:r1, :], al[r0:r1, :]), (bh[:, c], bl[:, c]))


def other_gram_kernel(shards, me_ref, ah, al, bh, bl, keep_ref, send_ref, g, packed):
    q = g.shape[0] // 4
    lower_product(g, ah, al, bh[:, q:], bl[:, q:])
    pack(g, packed, keep_ref, send_ref, me_ref[0], shards, 1)


def other_gram(me, shards, ah, al, bh, bl):
    size = ah.shape[0]
    return call(
        functools.partial(other_gram_kernel, shards), "other_gram", halves(size), 22, 0.5, 2,
        in_specs=[SMEM] + [VMEM] * 4,
        out_specs=[VMEM, VMEM],
        scratch_shapes=[pltpu.VMEM((size, size), F32), packed_scratch(size)],
    )(me, ah, al, bh, bl)


def tiles(count, tile, step):
    def body(t, _):
        step(pl.ds(pl.multiple_of(t * tile, tile), tile))
        return 0

    lax.fori_loop(0, count // tile, body, 0)


def affine_kernel(a_ref, b_ref, out_ref, hi, lo):
    hi[...], lo[...] = split(a_ref[...])

    def step(c):
        out_ref[:, c] = 1.5 * a_ref[:, c] - 0.5 * mm((hi[...], lo[...]), split(b_ref[:, c]))

    tiles(out_ref.shape[1], 256, step)


def affine(a, b, part, parts):
    rows, size = a.shape
    height = rows // parts
    return call(
        affine_kernel, "affine", struct(height, size), 24, 1 / parts, 2,
        grid=(1,),
        in_specs=[
            pl.BlockSpec((height, size), lambda r: (part, 0)),
            pl.BlockSpec((size, size), lambda r: (0, 0)),
        ],
        out_specs=pl.BlockSpec((height, size), lambda r: (0, 0)),
        scratch_shapes=[pltpu.VMEM((height, size), BF16)] * 2,
    )(a, b)


SPANS = (
    (((0, 4),), ((0, 1),), ((0, 1),), ((0, 1), (3, 4))),
    ((), ((1, 4),), ((1, 4),), ((1, 3),)),
)


def sym_product(ah, al, hi, lo, chunk, column):
    q = hi.shape[0] // 4
    spans = [slice(k0 * q, k1 * q) for k0, k1 in SPANS[chunk][column]]
    c = slice(column * q, (column + 1) * q)
    a = [ref[:, k] for ref in (ah, ah, al) for k in spans]
    b = [ref[k, c] for ref in (hi, lo, hi) for k in spans]
    return c, jnp.dot(
        jnp.concatenate(a, axis=1), jnp.concatenate(b, axis=0), preferred_element_type=F32
    )


def apply_first(a_ref, base_refs, out_ref, ah, al, hi, lo):
    ah[...], al[...] = split(a_ref[...])
    for column in range(4):
        c, product = sym_product(ah, al, hi, lo, 0, column)
        at = 0
        for base_ref in base_refs:
            end = at + base_ref.shape[0]
            out_ref[at:end, c] = base_ref[:, c] - 0.5 * product[at:end]
            at = end


def sym_scratch(rows, size):
    return (
        [pltpu.VMEM((rows, size), BF16)] * 2
        + [pltpu.VMEM((size, size), BF16)] * 2
        + [packed_scratch(size)]
    )


def partial_kernel(shards, count, me_ref, *refs):
    pieces, refs = refs[:count], refs[count:]
    a_ref, base_refs, (out_ref, ah, al, hi, lo, packed) = refs[0], refs[1:-6], refs[-6:]
    unpack(pieces, packed, hi, lo, me_ref[0], shards, 0)
    apply_first(a_ref, base_refs, out_ref, ah, al, hi, lo)


def partial_apply(me, shards, pieces, a, base):
    rows, size = a.shape
    return call(
        functools.partial(partial_kernel, shards, len(pieces)), "partial_apply",
        struct(rows, size), 22, 0.5, 3,
        in_specs=[SMEM] + [VMEM] * (len(pieces) + 1 + len(base)),
        out_specs=VMEM,
        scratch_shapes=sym_scratch(rows, size),
    )(me, *pieces, a, *base)


def turn_kernel(x_ref, xh, xl):
    xh[...], xl[...] = split(x_ref[...].T)


def turn(x):
    part = struct(*x.shape[::-1], dtype=BF16)
    return call(
        turn_kernel, "turn", [part, part], 16, 0.1, 2, in_specs=[VMEM], out_specs=[VMEM] * 2
    )(x)


def early_kernel(shards, count, me_ref, *refs):
    pieces, refs = refs[:count], refs[count:]
    a_ref, base_refs, refs = refs[0], refs[1:-9], refs[-9:]
    xh, xl, out_ref, col_ref, ah, al, hi, lo, packed = refs
    unpack(pieces, packed, hi, lo, me_ref[0], shards, 0)
    apply_first(a_ref, base_refs, out_ref, ah, al, hi, lo)
    col_ref[...] = mm((xh[...], xl[...]), split(out_ref[:, :col_ref.shape[1]]))


def early_middle(me, shards, pieces, a, base, xh, xl):
    rows, size = a.shape
    return call(
        functools.partial(early_kernel, shards, len(pieces)), "early_middle",
        [struct(rows, size), struct(size, size // 4)], 24, 0.75, 5,
        in_specs=[SMEM] + [VMEM] * (len(pieces) + 3 + len(base)),
        out_specs=[VMEM] * 2,
        scratch_shapes=sym_scratch(rows, size),
    )(me, *pieces, a, *base, xh, xl)


def second_gram_kernel(shards, count, me_ref, *refs):
    pieces, refs = refs[:count], refs[count:]
    a_ref, base_ref, xh, xl, col_ref, refs = refs[0], refs[1], refs[2], refs[3], refs[4], refs[5:]
    keep_ref, send_ref, mid_ref, mh, ml, ah, al, hi, lo, packed, g = refs
    size = g.shape[0]
    q = size // 4
    ah[:, q:], al[:, q:] = split(a_ref[:, q:])
    unpack(pieces, packed, hi, lo, me_ref[0], shards, 1)
    mid_ref[:, :q] = base_ref[:, :q]
    for column in range(1, 4):
        c, product = sym_product(ah, al, hi, lo, 1, column)
        mid = base_ref[:, c] - 0.5 * product
        mid_ref[:, c] = mid
        c = slice(c.start - q, c.stop - q)
        mh[:, c], ml[:, c] = split(mid)
    g[:, :q] = col_ref[...]
    g[:q, q:] = mm((xh[:q, :], xl[:q, :]), (mh[...], ml[...]))
    g[3 * q:, 3 * q:] = mm((xh[3 * q:, :], xl[3 * q:, :]), (mh[:, 2 * q:], ml[:, 2 * q:]))
    pack(g, packed, keep_ref, send_ref, me_ref[0], shards, 0)


def second_gram(me, shards, pieces, a, base, xh, xl, col):
    rows, size = a.shape
    part = struct(rows, size - size // 4, dtype=BF16)
    return call(
        functools.partial(second_gram_kernel, shards, len(pieces)), "second_gram",
        halves(size) + [struct(rows, size), part, part], 26, 0.8, 5,
        in_specs=[SMEM] + [VMEM] * (len(pieces) + 5),
        out_specs=[VMEM] * 5,
        scratch_shapes=sym_scratch(rows, size) + [pltpu.VMEM((size, size), F32)],
    )(me, *pieces, a, base, xh, xl, col)


def fourth_gram_kernel(shards, me_ref, xh, xl, mh, ml, keep_ref, send_ref, g, packed):
    lower_product(g, xh, xl, mh[...], ml[...])
    pack(g, packed, keep_ref, send_ref, me_ref[0], shards, 1)


def fourth_gram(me, shards, xh, xl, mh, ml):
    size = xh.shape[0]
    return call(
        functools.partial(fourth_gram_kernel, shards), "fourth_gram", halves(size), 22, 0.5, 2,
        in_specs=[SMEM] + [VMEM] * 4,
        out_specs=[VMEM, VMEM],
        scratch_shapes=[pltpu.VMEM((size, size), F32), packed_scratch(size)],
    )(me, xh, xl, mh, ml)


def last_kernel(shards, count, me_ref, *refs):
    pieces = refs[:count]
    x_ref, z_ref, out_hbm, ah, al, hi, lo, packed, out, sems = refs[count:]
    q = hi.shape[0] // 4
    copies = []

    def send(src, column):
        c = slice(column * q, (column + 1) * q)
        copy = pltpu.make_async_copy(src.at[:, c], out_hbm.at[:, c], sems.at[column])
        copy.start()
        copies.append(copy)

    send(z_ref, 0)
    ah[:, q:], al[:, q:] = split(x_ref[:, q:])
    unpack(pieces, packed, hi, lo, me_ref[0], shards, 1)
    for column in (1, 2, 3):
        c, product = sym_product(ah, al, hi, lo, 1, column)
        out[:, c] = z_ref[:, c] - 0.5 * product
        send(out, column)
    for copy in copies:
        copy.wait()


def last_step(me, shards, pieces, x, z):
    rows, size = x.shape
    return call(
        functools.partial(last_kernel, shards, len(pieces)), "last", struct(rows, size), 26, 0.5, 3,
        in_specs=[SMEM] + [VMEM] * (len(pieces) + 2),
        out_specs=pl.BlockSpec(memory_space=pltpu.HBM),
        scratch_shapes=sym_scratch(rows, size)
        + [pltpu.VMEM((rows, size), F32), pltpu.SemaphoreType.DMA((4,))],
    )(me, *pieces, x, z)


CORE = 1
PLANE = (2, 4, 6)
SHARDS = 2 * (1 + len(PLANE))


def slot_of(index):
    return (index % 2) * (SHARDS // 2) + (index // 2) % (SHARDS // 2)


class Sum:
    def __init__(self, count, keep, send):
        self.count, self.keep, self.send = count, keep, send

    def swap(self, x, offset):
        return lax.ppermute(x, "row", [(i, i ^ offset) for i in range(self.count)])

    def core(self):
        return self.swap(self.send, CORE)

    def plane(self, got):
        total = self.keep + got
        part = total.shape[0] // (1 + len(PLANE))
        self.keep, *sends = [total[k * part:(k + 1) * part] for k in range(1 + len(PLANE))]
        return [self.swap(x, offset) for x, offset in zip(sends, PLANE)]

    def own(self, got):
        self.keep = sum(got, self.keep)

    def exchange(self, offset):
        return self.swap(self.keep, offset)

    def gather_plane(self):
        return [self.swap(self.keep, offset) for offset in PLANE]

    def gather_core(self, got):
        self.mine = jnp.concatenate([self.keep, *got], axis=0)
        return self.swap(self.mine, CORE)


def close(env, *got):
    values = lax.optimization_barrier((*got, *env.values()))
    env.update(zip(env, values[len(got):]))
    return values[:len(got)]


def sum_chunks(count, env, first, second, works, late):
    beyond = [1 << s for s in range(3, count.bit_length() - 1)]
    works = list(works)

    def work():
        if works:
            works.pop(0)(env)

    a = Sum(count, *first)
    got_a = a.core()
    pair = second(env)
    got_a, *pair = close(env, got_a, *pair)
    b = Sum(count, *pair)

    got_a = a.plane(got_a)
    got_b = b.core()
    work()
    (got_b,) = close(env, got_b)

    got_b = b.plane(got_b)
    work()
    a.own(close(env, *got_a))

    for offset in beyond:
        got_a = a.exchange(offset)
        b.own(close(env, *got_b))
        got_b = [b.exchange(offset)]
        work()
        a.own(close(env, got_a))

    got_a = a.gather_plane()
    b.own(close(env, *got_b))

    got_b = b.gather_plane()
    *got_a, got_b[0] = close(env, *got_a, got_b[0])
    got_a = a.gather_core(got_a)
    pieces_a = [a.mine, *close(env, got_a)]
    late(env, pieces_a)
    got_b = b.gather_core(close(env, *got_b))
    return pieces_a, [b.mine, got_b]


def body(count, orbitals_zero, orbitals_one, correlation_zero, correlation_one, cotangent):
    me = slot_of(lax.axis_index("row")).astype(jnp.int32).reshape(1)
    env = dict(
        x0=orbitals_zero, x1=orbitals_one, s0=correlation_zero, s1=correlation_one, c=cotangent
    )

    def thirds(name, left, right):
        def put(at, part, parts):
            def work(env):
                env[f"{name}{at}"] = affine(env[left], env[right], part, parts)
            return work
        return [put(0, 0, 2), put(1, 2, 4), put(2, 3, 4)]

    def three(env, name):
        return [env[f"{name}{at}"] for at in range(3)]

    def early(env, pieces):
        env["mid"], env["col"] = early_middle(
            me, SHARDS, pieces, env["x1"], three(env, "m"), env["xh"], env["xl"]
        )

    half, quarter, rest = thirds("m", "c", "s1")

    def rest_and_turn(env):
        rest(env)
        env["xh"], env["xl"] = turn(env["x0"])

    keep, send, *parts = first_gram(me, SHARDS, env["x1"], env["c"])
    _, one = sum_chunks(
        count, env, (keep, send), lambda env: other_gram(me, SHARDS, *parts),
        [half, quarter, rest_and_turn], early,
    )

    keep, send, env["mid"], mh, ml = second_gram(
        me, SHARDS, one, env["x1"], env["mid"], env["xh"], env["xl"], env["col"]
    )

    def late(env, pieces):
        env["z"] = partial_apply(me, SHARDS, pieces, env["x0"], three(env, "d"))

    _, two = sum_chunks(
        count, env, (keep, send),
        lambda env: fourth_gram(me, SHARDS, env["xh"], env["xl"], mh, ml),
        thirds("d", "mid", "s0"), late,
    )
    return last_step(me, SHARDS, two, env["x0"], env["z"])


def solution(mesh):
    in_specs = (
        P(("kpt", "row"), None),
        P(("kpt", "row"), None),
        P("kpt", None),
        P("kpt", None),
        P(("kpt", "row"), None),
    )
    out_specs = P(("kpt", "row"), None)
    return jax.shard_map(
        functools.partial(body, mesh.shape["row"]),
        mesh=mesh, in_specs=in_specs, out_specs=out_specs, check_vma=False,
    )
```

```python
import functools
import jax
import jax.numpy as jnp
from jax import lax
from jax.experimental import pallas as pl
from jax.experimental.pallas import tpu as pltpu
from jax.sharding import PartitionSpec as P

F32 = jnp.float32
BF16 = jnp.bfloat16
B = 128
MIB = 1024 * 1024


def split(x):
    hi = x.astype(BF16)
    return hi, (x - hi.astype(F32)).astype(BF16)


def mm(a, b):
    (ah, al), (bh, bl) = a, b
    return jnp.dot(
        jnp.concatenate([ah, ah, al], axis=1),
        jnp.concatenate([bh, bl, bh], axis=0),
        preferred_element_type=F32,
    )


def call(kernel, name, out_shape, limit, products, arrays, **kw):
    size = 1024
    return pl.pallas_call(
        kernel,
        name=name,
        out_shape=out_shape,
        compiler_params=pltpu.CompilerParams(vmem_limit_bytes=limit * MIB),
        cost_estimate=pl.CostEstimate(
            flops=int(6 * products * size ** 3),
            bytes_accessed=int(4 * arrays * size * size),
            transcendentals=0,
        ),
        **kw,
    )


def struct(*shape, dtype=F32):
    return jax.ShapeDtypeStruct(shape, dtype)


SMEM = pl.BlockSpec(memory_space=pltpu.SMEM)
VMEM = pl.BlockSpec(memory_space=pltpu.VMEM)


def chunk_lines(size, chunk):
    half = size // B // 4
    return range(chunk * half, (chunk + 1) * half)


def line_blocks(size, i):
    n = size // B
    at = 0
    for top in (i, n - 1 - i):
        for j in range(top, n):
            yield at, slice(top * B, (top + 1) * B), slice(j * B, (j + 1) * B)
            at += B


def pack(g, packed, keep_ref, send_ref, me, shards, chunk):
    size = g.shape[0]
    rows = packed.shape[0] // shards
    per = B // rows
    for line, i in enumerate(chunk_lines(size, chunk)):
        for at, p, q in line_blocks(size, i):
            block = g[p, q] + g[q, p].T
            for s in range(per):
                slot = (line * per + s) ^ me
                packed[pl.ds(pl.multiple_of(slot * rows, rows), rows), at:at + B] = (
                    block[s * rows:(s + 1) * rows]
                )
    half = keep_ref.shape[0]
    keep_ref[...] = packed[:half]
    send_ref[...] = packed[half:]


def unpack(pieces, packed, hi, lo, me, shards, chunk):
    size = hi.shape[0]
    rows = packed.shape[0] // shards
    slot = 0
    for piece in pieces:
        for s in range(piece.shape[0] // rows):
            at = pl.multiple_of((slot ^ me) * rows, rows)
            packed[pl.ds(at, rows), :] = piece[s * rows:(s + 1) * rows, :]
            slot += 1
    for line, i in enumerate(chunk_lines(size, chunk)):
        for at, p, q in line_blocks(size, i):
            block = packed[line * B:(line + 1) * B, at:at + B]
            hi[p, q], lo[p, q] = split(block)
            if p.start != q.start:
                hi[q, p], lo[q, p] = split(block.T)


def packed_scratch(size):
    return pltpu.VMEM((size // 4, size + B), F32)


def halves(size):
    return [struct(size // 8, size + B)] * 2


def first_gram_kernel(
    shards, me_ref, a_hbm, b_hbm, keep_ref, send_ref, ah, al, bh, bl, a_buf, b_buf, sems, g, packed
):
    rows, size = a_buf.shape
    steps = sems.shape[1]
    tile = rows // steps
    copies = []
    for s in range(steps):
        r = slice(s * tile, (s + 1) * tile)
        pair = [
            pltpu.make_async_copy(src.at[r], dst.at[r], sems.at[k, s])
            for k, (src, dst) in enumerate([(a_hbm, a_buf), (b_hbm, b_buf)])
        ]
        for copy in pair:
            copy.start()
        copies.append((r, pair))
    q = size // 4

    def add_rows(r):
        for r0, r1, c0, c1 in [(0, q, 0, size), (q, size, 0, q), (3 * q, size, 3 * q, size)]:
            product = mm((ah[r0:r1, r], al[r0:r1, r]), (bh[r, c0:c1], bl[r, c0:c1]))
            if r.start:
                product += g[r0:r1, c0:c1]
            g[r0:r1, c0:c1] = product

    before = None
    for r, pair in copies:
        for copy in pair:
            copy.wait()
        if before:
            add_rows(before)
        ah[:, r], al[:, r] = split(a_buf[r].T)
        bh[r], bl[r] = split(b_buf[r])
        before = r
    add_rows(before)
    pack(g, packed, keep_ref, send_ref, me_ref[0], shards, 0)


def first_gram(me, shards, a, b):
    rows, size = a.shape
    hbm = pl.BlockSpec(memory_space=pltpu.HBM)
    return call(
        functools.partial(first_gram_kernel, shards), "first_gram",
        halves(size) + [struct(size, rows, dtype=BF16)] * 2 + [struct(rows, size, dtype=BF16)] * 2,
        43, 0.5, 4,
        in_specs=[SMEM, hbm, hbm],
        out_specs=[VMEM] * 6,
        scratch_shapes=[
            pltpu.VMEM((rows, size), F32), pltpu.VMEM((rows, size), F32),
            pltpu.SemaphoreType.DMA((2, 4)),
            pltpu.VMEM((size, size), F32), packed_scratch(size),
        ],
    )(me, a, b)


def lower_product(g, ah, al, bh, bl):
    size = g.shape[0]
    q = size // 4
    for r0, r1, c0, c1 in [(q, 3 * q, q, size), (3 * q, size, q, 3 * q)]:
        c = slice(c0 - q, c1 - q)
        g[r0:r1, c0:c1] = mm((ah[r0:r1, :], al[r0:r1, :]), (bh[:, c], bl[:, c]))


def other_gram_kernel(shards, me_ref, ah, al, bh, bl, keep_ref, send_ref, g, packed):
    q = g.shape[0] // 4
    lower_product(g, ah, al, bh[:, q:], bl[:, q:])
    pack(g, packed, keep_ref, send_ref, me_ref[0], shards, 1)


def other_gram(me, shards, ah, al, bh, bl):
    size = ah.shape[0]
    return call(
        functools.partial(other_gram_kernel, shards), "other_gram", halves(size), 18, 0.5, 2,
        in_specs=[SMEM] + [VMEM] * 4,
        out_specs=[VMEM, VMEM],
        scratch_shapes=[pltpu.VMEM((size, size), F32), packed_scratch(size)],
    )(me, ah, al, bh, bl)


def tiles(count, tile, step):
    def body(t, _):
        step(pl.ds(pl.multiple_of(t * tile, tile), tile))
        return 0

    lax.fori_loop(0, count // tile, body, 0)


def affine_kernel(a_ref, b_ref, out_ref, hi, lo):
    hi[...], lo[...] = split(a_ref[...])

    def step(c):
        out_ref[:, c] = 1.5 * a_ref[:, c] - 0.5 * mm((hi[...], lo[...]), split(b_ref[:, c]))

    tiles(out_ref.shape[1], 256, step)


def affine(a, b, part, parts):
    rows, size = a.shape
    height = rows // parts
    return call(
        affine_kernel, "affine", struct(height, size), 18, 1 / parts, 2,
        grid=(1,),
        in_specs=[
            pl.BlockSpec((height, size), lambda r: (part, 0)),
            pl.BlockSpec((size, size), lambda r: (0, 0)),
        ],
        out_specs=pl.BlockSpec((height, size), lambda r: (0, 0)),
        scratch_shapes=[pltpu.VMEM((height, size), BF16)] * 2,
    )(a, b)


SPANS = (
    (((0, 4),), ((0, 1),), ((0, 1),), ((0, 1), (3, 4))),
    ((), ((1, 4),), ((1, 4),), ((1, 3),)),
)


def sym_product(ah, al, hi, lo, chunk, column):
    q = hi.shape[0] // 4
    spans = [slice(k0 * q, k1 * q) for k0, k1 in SPANS[chunk][column]]
    c = slice(column * q, (column + 1) * q)
    a = [ref[:, k] for ref in (ah, ah, al) for k in spans]
    b = [ref[k, c] for ref in (hi, lo, hi) for k in spans]
    return c, jnp.dot(
        jnp.concatenate(a, axis=1), jnp.concatenate(b, axis=0), preferred_element_type=F32
    )


def apply_first(base_refs, out_ref, ah, al, hi, lo):
    for column in range(4):
        c, product = sym_product(ah, al, hi, lo, 0, column)
        at = 0
        for base_ref in base_refs:
            end = at + base_ref.shape[0]
            out_ref[at:end, c] = base_ref[:, c] - 0.5 * product[at:end]
            at = end


def sym_scratch(rows, size):
    return (
        [pltpu.VMEM((rows, size), BF16)] * 2
        + [pltpu.VMEM((size, size), BF16)] * 2
        + [packed_scratch(size)]
    )


def partial_kernel(shards, count, me_ref, *refs):
    pieces, refs = refs[:count], refs[count:]
    ah, al, base_refs, (out_ref, hi, lo, packed) = refs[0], refs[1], refs[2:-4], refs[-4:]
    unpack(pieces, packed, hi, lo, me_ref[0], shards, 0)
    apply_first(base_refs, out_ref, ah, al, hi, lo)


def partial_apply(me, shards, pieces, ah, al, base):
    rows, size = ah.shape
    return call(
        functools.partial(partial_kernel, shards, len(pieces)), "partial_apply",
        struct(rows, size), 18, 0.5, 3,
        in_specs=[SMEM] + [VMEM] * (len(pieces) + 2 + len(base)),
        out_specs=VMEM,
        scratch_shapes=sym_scratch(rows, size)[2:],
    )(me, *pieces, ah, al, *base)


def turn_kernel(x_ref, xh, xl):
    xh[...], xl[...] = split(x_ref[...].T)


def turn(x):
    part = struct(*x.shape[::-1], dtype=BF16)
    return call(
        turn_kernel, "turn", [part, part], 16, 0.1, 2, in_specs=[VMEM], out_specs=[VMEM] * 2
    )(x)


def cut_kernel(x_ref, hi, lo):
    hi[...], lo[...] = split(x_ref[...])


def cut(x):
    part = struct(*x.shape, dtype=BF16)
    return call(
        cut_kernel, "cut", [part, part], 16, 0.1, 2, in_specs=[VMEM], out_specs=[VMEM] * 2
    )(x)


def early_kernel(shards, count, me_ref, *refs):
    pieces, refs = refs[:count], refs[count:]
    a_ref, base_refs, refs = refs[0], refs[1:-9], refs[-9:]
    xh, xl, out_ref, col_ref, ah, al, hi, lo, packed = refs
    ah[...], al[...] = split(a_ref[...])
    unpack(pieces, packed, hi, lo, me_ref[0], shards, 0)
    apply_first(base_refs, out_ref, ah, al, hi, lo)
    col_ref[...] = mm((xh[...], xl[...]), split(out_ref[:, :col_ref.shape[1]]))


def early_middle(me, shards, pieces, a, base, xh, xl):
    rows, size = a.shape
    return call(
        functools.partial(early_kernel, shards, len(pieces)), "early_middle",
        [struct(rows, size), struct(size, size // 4)], 20, 0.75, 5,
        in_specs=[SMEM] + [VMEM] * (len(pieces) + 3 + len(base)),
        out_specs=[VMEM] * 2,
        scratch_shapes=sym_scratch(rows, size),
    )(me, *pieces, a, *base, xh, xl)


def second_gram_kernel(shards, count, me_ref, *refs):
    pieces, refs = refs[:count], refs[count:]
    a_ref, base_ref, xh, xl, col_ref, refs = refs[0], refs[1], refs[2], refs[3], refs[4], refs[5:]
    keep_ref, send_ref, mid_ref, mh, ml, ah, al, hi, lo, packed, g = refs
    size = g.shape[0]
    q = size // 4
    ah[:, q:], al[:, q:] = split(a_ref[:, q:])
    unpack(pieces, packed, hi, lo, me_ref[0], shards, 1)
    mid_ref[:, :q] = base_ref[:, :q]
    for column in range(1, 4):
        c, product = sym_product(ah, al, hi, lo, 1, column)
        mid = base_ref[:, c] - 0.5 * product
        mid_ref[:, c] = mid
        c = slice(c.start - q, c.stop - q)
        mh[:, c], ml[:, c] = split(mid)
    g[:, :q] = col_ref[...]
    g[:q, q:] = mm((xh[:q, :], xl[:q, :]), (mh[...], ml[...]))
    g[3 * q:, 3 * q:] = mm((xh[3 * q:, :], xl[3 * q:, :]), (mh[:, 2 * q:], ml[:, 2 * q:]))
    pack(g, packed, keep_ref, send_ref, me_ref[0], shards, 0)


def second_gram(me, shards, pieces, a, base, xh, xl, col):
    rows, size = a.shape
    part = struct(rows, size - size // 4, dtype=BF16)
    return call(
        functools.partial(second_gram_kernel, shards, len(pieces)), "second_gram",
        halves(size) + [struct(rows, size), part, part], 20, 0.8, 5,
        in_specs=[SMEM] + [VMEM] * (len(pieces) + 5),
        out_specs=[VMEM] * 5,
        scratch_shapes=sym_scratch(rows, size) + [pltpu.VMEM((size, size), F32)],
    )(me, *pieces, a, base, xh, xl, col)


def fourth_gram_kernel(shards, me_ref, xh, xl, mh, ml, keep_ref, send_ref, g, packed):
    lower_product(g, xh, xl, mh[...], ml[...])
    pack(g, packed, keep_ref, send_ref, me_ref[0], shards, 1)


def fourth_gram(me, shards, xh, xl, mh, ml):
    size = xh.shape[0]
    return call(
        functools.partial(fourth_gram_kernel, shards), "fourth_gram", halves(size), 18, 0.5, 2,
        in_specs=[SMEM] + [VMEM] * 4,
        out_specs=[VMEM, VMEM],
        scratch_shapes=[pltpu.VMEM((size, size), F32), packed_scratch(size)],
    )(me, xh, xl, mh, ml)


def last_kernel(shards, count, me_ref, *refs):
    pieces = refs[:count]
    ah, al, z_ref, out_hbm, hi, lo, packed, out, sems = refs[count:]
    q = hi.shape[0] // 4
    copies = []

    def send(src, column):
        c = slice(column * q, (column + 1) * q)
        copy = pltpu.make_async_copy(src.at[:, c], out_hbm.at[:, c], sems.at[column])
        copy.start()
        copies.append(copy)

    send(z_ref, 0)
    unpack(pieces, packed, hi, lo, me_ref[0], shards, 1)
    for column in (1, 2, 3):
        c, product = sym_product(ah, al, hi, lo, 1, column)
        out[:, c] = z_ref[:, c] - 0.5 * product
        send(out, column)
    for copy in copies:
        copy.wait()


def last_step(me, shards, pieces, ah, al, z):
    rows, size = z.shape
    return call(
        functools.partial(last_kernel, shards, len(pieces)), "last", struct(rows, size), 22, 0.5, 3,
        in_specs=[SMEM] + [VMEM] * (len(pieces) + 3),
        out_specs=pl.BlockSpec(memory_space=pltpu.HBM),
        scratch_shapes=sym_scratch(rows, size)[2:]
        + [pltpu.VMEM((rows, size), F32), pltpu.SemaphoreType.DMA((4,))],
    )(me, *pieces, ah, al, z)


CORE = 1
PLANE = (2, 4, 6)
SHARDS = 2 * (1 + len(PLANE))


def slot_of(index):
    return (index % 2) * (SHARDS // 2) + (index // 2) % (SHARDS // 2)


class Sum:
    def __init__(self, count, keep, send):
        self.count, self.keep, self.send = count, keep, send

    def swap(self, x, offset):
        return lax.ppermute(x, "row", [(i, i ^ offset) for i in range(self.count)])

    def core(self):
        return self.swap(self.send, CORE)

    def plane(self, got):
        total = self.keep + got
        part = total.shape[0] // (1 + len(PLANE))
        self.keep, *sends = [total[k * part:(k + 1) * part] for k in range(1 + len(PLANE))]
        return [self.swap(x, offset) for x, offset in zip(sends, PLANE)]

    def own(self, got):
        self.keep = sum(got, self.keep)

    def exchange(self, offset):
        return self.swap(self.keep, offset)

    def gather_plane(self):
        return [self.swap(self.keep, offset) for offset in PLANE]

    def gather_core(self, got):
        self.mine = jnp.concatenate([self.keep, *got], axis=0)
        return self.swap(self.mine, CORE)


def close(env, *got):
    values = lax.optimization_barrier((*got, *env.values()))
    env.update(zip(env, values[len(got):]))
    return values[:len(got)]


def sum_chunks(count, env, first, second, works, late):
    beyond = [1 << s for s in range(3, count.bit_length() - 1)]
    works = list(works)

    def work():
        if works:
            works.pop(0)(env)

    a = Sum(count, *first)
    got_a = a.core()
    pair = second(env)
    got_a, *pair = close(env, got_a, *pair)
    b = Sum(count, *pair)

    got_a = a.plane(got_a)
    got_b = b.core()
    work()
    (got_b,) = close(env, got_b)

    got_b = b.plane(got_b)
    work()
    a.own(close(env, *got_a))

    for offset in beyond:
        got_a = a.exchange(offset)
        b.own(close(env, *got_b))
        got_b = [b.exchange(offset)]
        work()
        a.own(close(env, got_a))

    got_a = a.gather_plane()
    b.own(close(env, *got_b))

    got_b = b.gather_plane()
    *got_a, got_b[2] = close(env, *got_a, got_b[2])
    got_a = a.gather_core(got_a)
    pieces_a = [a.mine, *close(env, got_a)]
    late(env, pieces_a)
    got_b = b.gather_core(close(env, *got_b))
    return pieces_a, [b.mine, got_b]


def body(count, orbitals_zero, orbitals_one, correlation_zero, correlation_one, cotangent):
    me = slot_of(lax.axis_index("row")).astype(jnp.int32).reshape(1)
    env = dict(
        x0=orbitals_zero, x1=orbitals_one, s0=correlation_zero, s1=correlation_one, c=cotangent
    )

    def half(name, left, right, part):
        def work(env):
            env[f"{name}{part}"] = affine(env[left], env[right], part, 2)
        return work

    def turned(env):
        env["xh"], env["xl"] = turn(env["x0"])

    def parted(env):
        env["x0h"], env["x0l"] = cut(env["x0"])

    def early(env, pieces):
        env["mid"], env["col"] = early_middle(
            me, SHARDS, pieces, env["x1"], [env["m0"], env["m1"]], env["xh"], env["xl"]
        )

    keep, send, *parts = first_gram(me, SHARDS, env["x1"], env["c"])
    _, one = sum_chunks(
        count, env, (keep, send), lambda env: other_gram(me, SHARDS, *parts),
        [half("m", "c", "s1", 0), turned, half("m", "c", "s1", 1)], early,
    )

    keep, send, env["mid"], mh, ml = second_gram(
        me, SHARDS, one, env["x1"], env["mid"], env["xh"], env["xl"], env["col"]
    )

    def late(env, pieces):
        env["z"] = partial_apply(me, SHARDS, pieces, env["x0h"], env["x0l"], [env["d0"], env["d1"]])

    _, two = sum_chunks(
        count, env, (keep, send),
        lambda env: fourth_gram(me, SHARDS, env["xh"], env["xl"], mh, ml),
        [half("d", "mid", "s0", 0), parted, half("d", "mid", "s0", 1)], late,
    )
    return last_step(me, SHARDS, two, env["x0h"], env["x0l"], env["z"])


def solution(mesh):
    in_specs = (
        P(("kpt", "row"), None),
        P(("kpt", "row"), None),
        P("kpt", None),
        P("kpt", None),
        P(("kpt", "row"), None),
    )
    out_specs = P(("kpt", "row"), None)
    return jax.shard_map(
        functools.partial(body, mesh.shape["row"]),
        mesh=mesh, in_specs=in_specs, out_specs=out_specs, check_vma=False,
    )
```

```python
import functools
import jax
import jax.numpy as jnp
from jax import lax
from jax.experimental import pallas as pl
from jax.experimental.pallas import tpu as pltpu
from jax.sharding import PartitionSpec as P

F32 = jnp.float32
BF16 = jnp.bfloat16
B = 128
MIB = 1024 * 1024


def split(x):
    hi = x.astype(BF16)
    return hi, (x - hi.astype(F32)).astype(BF16)


def mm(a, b):
    (ah, al), (bh, bl) = a, b
    return jnp.dot(
        jnp.concatenate([ah, ah, al], axis=1),
        jnp.concatenate([bh, bl, bh], axis=0),
        preferred_element_type=F32,
    )


def call(kernel, name, out_shape, limit, products, arrays, **kw):
    size = 1024
    return pl.pallas_call(
        kernel,
        name=name,
        out_shape=out_shape,
        compiler_params=pltpu.CompilerParams(vmem_limit_bytes=limit * MIB),
        cost_estimate=pl.CostEstimate(
            flops=int(6 * products * size ** 3),
            bytes_accessed=int(4 * arrays * size * size),
            transcendentals=0,
        ),
        **kw,
    )


def struct(*shape, dtype=F32):
    return jax.ShapeDtypeStruct(shape, dtype)


SMEM = pl.BlockSpec(memory_space=pltpu.SMEM)
VMEM = pl.BlockSpec(memory_space=pltpu.VMEM)


def chunk_lines(size, chunk):
    half = size // B // 4
    return range(chunk * half, (chunk + 1) * half)


def line_blocks(size, i):
    n = size // B
    at = 0
    for top in (i, n - 1 - i):
        for j in range(top, n):
            yield at, slice(top * B, (top + 1) * B), slice(j * B, (j + 1) * B)
            at += B


def pack(g, packed, keep_ref, send_ref, me, shards, chunk):
    size = g.shape[0]
    rows = packed.shape[0] // shards
    per = B // rows
    for line, i in enumerate(chunk_lines(size, chunk)):
        for at, p, q in line_blocks(size, i):
            block = g[p, q] + g[q, p].T
            for s in range(per):
                slot = (line * per + s) ^ me
                packed[pl.ds(pl.multiple_of(slot * rows, rows), rows), at:at + B] = (
                    block[s * rows:(s + 1) * rows]
                )
    half = keep_ref.shape[0]
    keep_ref[...] = packed[:half]
    send_ref[...] = packed[half:]


SLOTS = (range(8), (0, 3, 1, 2, 4, 7, 5, 6))


def unpack(pieces, packed, hi, lo, me, shards, chunk):
    size = hi.shape[0]
    rows = packed.shape[0] // shards
    slots = iter(SLOTS[chunk])
    for piece in pieces:
        for s in range(piece.shape[0] // rows):
            at = pl.multiple_of((next(slots) ^ me) * rows, rows)
            packed[pl.ds(at, rows), :] = piece[s * rows:(s + 1) * rows, :]
    for line, i in enumerate(chunk_lines(size, chunk)):
        for at, p, q in line_blocks(size, i):
            block = packed[line * B:(line + 1) * B, at:at + B]
            hi[p, q], lo[p, q] = split(block)
            if p.start != q.start:
                hi[q, p], lo[q, p] = split(block.T)


def packed_scratch(size):
    return pltpu.VMEM((size // 4, size + B), F32)


def halves(size):
    return [struct(size // 8, size + B)] * 2


def first_gram_kernel(
    shards, me_ref, a_hbm, b_hbm, keep_ref, send_ref, ah, al, bh, bl, a_buf, b_buf, sems, g, packed
):
    rows, size = a_buf.shape
    q = size // 4
    steps = sems.shape[1]
    tile = rows // steps

    def copies(step):
        r = slice(step * tile, (step + 1) * tile)
        return [
            pltpu.make_async_copy(src.at[r], dst.at[r], sems.at[k, step])
            for k, (src, dst) in enumerate([(a_hbm, a_buf), (b_hbm, b_buf)])
        ]

    def start(step):
        for copy in copies(step):
            copy.start()

    start(0)
    start(1)
    for step in range(steps):
        r = slice(step * tile, (step + 1) * tile)
        for copy in copies(step):
            copy.wait()
        if step + 2 < steps:
            start(step + 2)
        ah[:, r], al[:, r] = split(a_buf[r].T)
        bh[r], bl[r] = split(b_buf[r])
        for r0, r1, c0, c1 in [(0, q, 0, size), (q, size, 0, q), (3 * q, size, 3 * q, size)]:
            product = mm((ah[r0:r1, r], al[r0:r1, r]), (bh[r, c0:c1], bl[r, c0:c1]))
            if step:
                product += g[r0:r1, c0:c1]
            g[r0:r1, c0:c1] = product
    pack(g, packed, keep_ref, send_ref, me_ref[0], shards, 0)


def first_gram(me, shards, a, b):
    rows, size = a.shape
    hbm = pl.BlockSpec(memory_space=pltpu.HBM)
    return call(
        functools.partial(first_gram_kernel, shards), "first_gram",
        halves(size) + [struct(size, rows, dtype=BF16)] * 2 + [struct(rows, size, dtype=BF16)] * 2,
        43, 0.5, 4,
        in_specs=[SMEM, hbm, hbm],
        out_specs=[VMEM] * 6,
        scratch_shapes=[
            pltpu.VMEM((rows, size), F32), pltpu.VMEM((rows, size), F32),
            pltpu.SemaphoreType.DMA((2, 4)),
            pltpu.VMEM((size, size), F32), packed_scratch(size),
        ],
    )(me, a, b)


def lower_product(g, ah, al, bh, bl):
    size = g.shape[0]
    q = size // 4
    for r0, r1, c0, c1 in [(q, 3 * q, q, size), (3 * q, size, q, 3 * q)]:
        c = slice(c0 - q, c1 - q)
        g[r0:r1, c0:c1] = mm((ah[r0:r1, :], al[r0:r1, :]), (bh[:, c], bl[:, c]))


def other_gram_kernel(shards, me_ref, ah, al, bh, bl, keep_ref, send_ref, g, packed):
    q = g.shape[0] // 4
    lower_product(g, ah, al, bh[:, q:], bl[:, q:])
    pack(g, packed, keep_ref, send_ref, me_ref[0], shards, 1)


def other_gram(me, shards, ah, al, bh, bl):
    size = ah.shape[0]
    return call(
        functools.partial(other_gram_kernel, shards), "other_gram", halves(size), 18, 0.5, 2,
        in_specs=[SMEM] + [VMEM] * 4,
        out_specs=[VMEM, VMEM],
        scratch_shapes=[pltpu.VMEM((size, size), F32), packed_scratch(size)],
    )(me, ah, al, bh, bl)


def tiles(count, tile, step):
    def body(t, _):
        step(pl.ds(pl.multiple_of(t * tile, tile), tile))
        return 0

    lax.fori_loop(0, count // tile, body, 0)


def affine_kernel(a_ref, b_ref, out_ref, hi, lo):
    hi[...], lo[...] = split(a_ref[...])

    def step(c):
        out_ref[:, c] = 1.5 * a_ref[:, c] - 0.5 * mm((hi[...], lo[...]), split(b_ref[:, c]))

    tiles(out_ref.shape[1], 256, step)


def affine(a, b, part, parts):
    rows, size = a.shape
    height = rows // parts
    return call(
        affine_kernel, "affine", struct(height, size), 18, 1 / parts, 2,
        grid=(1,),
        in_specs=[
            pl.BlockSpec((height, size), lambda r: (part, 0)),
            pl.BlockSpec((size, size), lambda r: (0, 0)),
        ],
        out_specs=pl.BlockSpec((height, size), lambda r: (0, 0)),
        scratch_shapes=[pltpu.VMEM((height, size), BF16)] * 2,
    )(a, b)


SPANS = (
    (((0, 4),), ((0, 1),), ((0, 1),), ((0, 1), (3, 4))),
    ((), ((1, 4),), ((1, 4),), ((1, 3),)),
)


def sym_product(ah, al, hi, lo, chunk, column):
    q = hi.shape[0] // 4
    spans = [slice(k0 * q, k1 * q) for k0, k1 in SPANS[chunk][column]]
    c = slice(column * q, (column + 1) * q)
    a = [ref[:, k] for ref in (ah, ah, al) for k in spans]
    b = [ref[k, c] for ref in (hi, lo, hi) for k in spans]
    return c, jnp.dot(
        jnp.concatenate(a, axis=1), jnp.concatenate(b, axis=0), preferred_element_type=F32
    )


def apply_first(base_refs, out_ref, ah, al, hi, lo):
    for column in range(4):
        c, product = sym_product(ah, al, hi, lo, 0, column)
        at = 0
        for base_ref in base_refs:
            end = at + base_ref.shape[0]
            out_ref[at:end, c] = base_ref[:, c] - 0.5 * product[at:end]
            at = end


def sym_scratch(size):
    return [pltpu.VMEM((size, size), BF16)] * 2 + [packed_scratch(size)]


def partial_kernel(shards, count, me_ref, *refs):
    pieces, refs = refs[:count], refs[count:]
    ah, al, base_refs, (out_ref, hi, lo, packed) = refs[0], refs[1], refs[2:-4], refs[-4:]
    unpack(pieces, packed, hi, lo, me_ref[0], shards, 0)
    apply_first(base_refs, out_ref, ah, al, hi, lo)


def partial_apply(me, shards, pieces, ah, al, base):
    rows, size = ah.shape
    return call(
        functools.partial(partial_kernel, shards, len(pieces)), "partial_apply",
        struct(rows, size), 18, 0.5, 3,
        in_specs=[SMEM] + [VMEM] * (len(pieces) + 2 + len(base)),
        out_specs=VMEM,
        scratch_shapes=sym_scratch(size),
    )(me, *pieces, ah, al, *base)


def turn_kernel(x_ref, xh, xl):
    xh[...], xl[...] = split(x_ref[...].T)


def turn(x):
    part = struct(*x.shape[::-1], dtype=BF16)
    return call(
        turn_kernel, "turn", [part, part], 16, 0.1, 2, in_specs=[VMEM], out_specs=[VMEM] * 2
    )(x)


def cut_kernel(which, x_ref, *out_refs):
    parts = split(x_ref[...])
    for out_ref, k in zip(out_refs, which):
        out_ref[...] = parts[k]


def cut(x, *which):
    count = len(which)
    return call(
        functools.partial(cut_kernel, which), "cut", [struct(*x.shape, dtype=BF16)] * count,
        16, 0.1, 2, in_specs=[VMEM], out_specs=[VMEM] * count,
    )(x)


def early_kernel(shards, count, me_ref, *refs):
    pieces, refs = refs[:count], refs[count:]
    ah, al, base_refs, refs = refs[0], refs[1], refs[2:-7], refs[-7:]
    xh, xl, out_ref, col_ref, hi, lo, packed = refs
    unpack(pieces, packed, hi, lo, me_ref[0], shards, 0)
    apply_first(base_refs, out_ref, ah, al, hi, lo)
    col_ref[...] = mm((xh[...], xl[...]), split(out_ref[:, :col_ref.shape[1]]))


def early_middle(me, shards, pieces, ah, al, base, xh, xl):
    rows, size = ah.shape
    return call(
        functools.partial(early_kernel, shards, len(pieces)), "early_middle",
        [struct(rows, size), struct(size, size // 4)], 20, 0.75, 5,
        in_specs=[SMEM] + [VMEM] * (len(pieces) + 4 + len(base)),
        out_specs=[VMEM] * 2,
        scratch_shapes=sym_scratch(size),
    )(me, *pieces, ah, al, *base, xh, xl)


def second_gram_kernel(shards, count, me_ref, *refs):
    pieces, refs = refs[:count], refs[count:]
    (ah, al, base_ref, xh, xl, col_ref), refs = refs[:6], refs[6:]
    keep_ref, send_ref, mid_ref, mh, ml, hi, lo, packed, g = refs
    size = g.shape[0]
    q = size // 4
    unpack(pieces, packed, hi, lo, me_ref[0], shards, 1)
    mid_ref[:, :q] = base_ref[:, :q]
    for column in range(1, 4):
        c, product = sym_product(ah, al, hi, lo, 1, column)
        mid = base_ref[:, c] - 0.5 * product
        mid_ref[:, c] = mid
        c = slice(c.start - q, c.stop - q)
        mh[:, c], ml[:, c] = split(mid)
    g[:, :q] = col_ref[...]
    g[:q, q:] = mm((xh[:q, :], xl[:q, :]), (mh[...], ml[...]))
    g[3 * q:, 3 * q:] = mm((xh[3 * q:, :], xl[3 * q:, :]), (mh[:, 2 * q:], ml[:, 2 * q:]))
    pack(g, packed, keep_ref, send_ref, me_ref[0], shards, 0)


def second_gram(me, shards, pieces, ah, al, base, xh, xl, col):
    rows, size = ah.shape
    part = struct(rows, size - size // 4, dtype=BF16)
    return call(
        functools.partial(second_gram_kernel, shards, len(pieces)), "second_gram",
        halves(size) + [struct(rows, size), part, part], 20, 0.8, 5,
        in_specs=[SMEM] + [VMEM] * (len(pieces) + 6),
        out_specs=[VMEM] * 5,
        scratch_shapes=sym_scratch(size) + [pltpu.VMEM((size, size), F32)],
    )(me, *pieces, ah, al, base, xh, xl, col)


def fourth_gram_kernel(shards, me_ref, xh, xl, mh, ml, keep_ref, send_ref, g, packed):
    lower_product(g, xh, xl, mh[...], ml[...])
    pack(g, packed, keep_ref, send_ref, me_ref[0], shards, 1)


def fourth_gram(me, shards, xh, xl, mh, ml):
    size = xh.shape[0]
    return call(
        functools.partial(fourth_gram_kernel, shards), "fourth_gram", halves(size), 18, 0.5, 2,
        in_specs=[SMEM] + [VMEM] * 4,
        out_specs=[VMEM, VMEM],
        scratch_shapes=[pltpu.VMEM((size, size), F32), packed_scratch(size)],
    )(me, xh, xl, mh, ml)


def last_kernel(shards, count, me_ref, *refs):
    pieces = refs[:count]
    ah, al, z_ref, out_hbm, hi, lo, packed, out, sems = refs[count:]
    q = hi.shape[0] // 4
    copies = []

    def send(src, column):
        c = slice(column * q, (column + 1) * q)
        copy = pltpu.make_async_copy(src.at[:, c], out_hbm.at[:, c], sems.at[column])
        copy.start()
        copies.append(copy)

    send(z_ref, 0)
    unpack(pieces, packed, hi, lo, me_ref[0], shards, 1)
    for column in (1, 2, 3):
        c, product = sym_product(ah, al, hi, lo, 1, column)
        out[:, c] = z_ref[:, c] - 0.5 * product
        send(out, column)
    for copy in copies:
        copy.wait()


def last_step(me, shards, pieces, ah, al, z):
    rows, size = z.shape
    return call(
        functools.partial(last_kernel, shards, len(pieces)), "last", struct(rows, size), 22, 0.5, 3,
        in_specs=[SMEM] + [VMEM] * (len(pieces) + 3),
        out_specs=pl.BlockSpec(memory_space=pltpu.HBM),
        scratch_shapes=sym_scratch(size)
        + [pltpu.VMEM((rows, size), F32), pltpu.SemaphoreType.DMA((4,))],
    )(me, *pieces, ah, al, z)


CORE = 1
PLANE = (2, 4, 6)
SHARDS = 2 * (1 + len(PLANE))


def slot_of(index):
    return (index % 2) * (SHARDS // 2) + (index // 2) % (SHARDS // 2)


class Sum:
    def __init__(self, count, keep, send):
        self.count, self.keep, self.send = count, keep, send

    def swap(self, x, offset):
        return lax.ppermute(x, "row", [(i, i ^ offset) for i in range(self.count)])

    def core(self):
        return self.swap(self.send, CORE)

    def plane(self, got):
        total = self.keep + got
        part = total.shape[0] // (1 + len(PLANE))
        self.keep, *sends = [total[k * part:(k + 1) * part] for k in range(1 + len(PLANE))]
        return [self.swap(x, offset) for x, offset in zip(sends, PLANE)]

    def own(self, got):
        self.keep = sum(got, self.keep)

    def exchange(self, offset):
        return self.swap(self.keep, offset)

    def gather_plane(self):
        return [self.swap(self.keep, offset) for offset in PLANE]

    def gather_core(self, got):
        self.mine = jnp.concatenate([self.keep, *got], axis=0)
        return self.swap(self.mine, CORE)


def close(env, *got):
    values = lax.optimization_barrier((*got, *env.values()))
    env.update(zip(env, values[len(got):]))
    return values[:len(got)]


def sum_chunks(count, env, first, second, works, late):
    beyond = [1 << s for s in range(3, count.bit_length() - 1)]
    works = list(works)

    def work():
        if works:
            works.pop(0)(env)

    a = Sum(count, *first)
    got_a = a.core()
    pair = second(env)
    got_a, *pair = close(env, got_a, *pair)
    b = Sum(count, *pair)

    got_a = a.plane(got_a)
    got_b = b.core()
    work()
    (got_b,) = close(env, got_b)

    got_b = b.plane(got_b)
    work()
    a.own(close(env, *got_a))

    for offset in beyond:
        got_a = a.exchange(offset)
        work()
        b.own(close(env, *got_b))
        got_b = [b.exchange(offset)]
        a.own(close(env, got_a))

    got_a = a.gather_plane()
    b.own(close(env, *got_b))

    side_b, near_b, diagonal_b = b.gather_plane()
    got_a = a.gather_core(close(env, *got_a))
    work()
    got_a, diagonal_b = close(env, got_a, diagonal_b)
    early_b = jnp.concatenate([b.keep, diagonal_b], axis=0)
    core_b = b.swap(early_b, CORE)
    late(env, [a.mine, got_a])
    side_b, near_b, core_b = close(env, side_b, near_b, core_b)
    late_b = jnp.concatenate([side_b, near_b], axis=0)
    return [early_b, late_b, core_b, b.swap(late_b, CORE)]


def body(count, orbitals_zero, orbitals_one, correlation_zero, correlation_one, cotangent):
    me = slot_of(lax.axis_index("row")).astype(jnp.int32).reshape(1)
    env = dict(
        x0=orbitals_zero, x1=orbitals_one, s0=correlation_zero, s1=correlation_one, c=cotangent
    )

    def half(name, left, right, part):
        def work(env):
            env[f"{name}{part}"] = affine(env[left], env[right], part, 2)
        return work

    def turned(env):
        env["xh"], env["xl"] = turn(env["x0"])

    def cut_one(env):
        env["x1h"], env["x1l"] = cut(env["x1"], 0, 1)

    def high(env):
        (env["x0h"],) = cut(env["x0"], 0)

    def low(env):
        (env["x0l"],) = cut(env["x0"], 1)

    def early(env, pieces):
        env["mid"], env["col"] = early_middle(
            me, SHARDS, pieces, env["x1h"], env["x1l"], [env["m0"], env["m1"]], env["xh"], env["xl"]
        )

    keep, send, *parts = first_gram(me, SHARDS, env["x1"], env["c"])
    one = sum_chunks(
        count, env, (keep, send), lambda env: other_gram(me, SHARDS, *parts),
        [half("m", "c", "s1", 0), turned, half("m", "c", "s1", 1), cut_one], early,
    )

    keep, send, env["mid"], mh, ml = second_gram(
        me, SHARDS, one, env["x1h"], env["x1l"], env["mid"], env["xh"], env["xl"], env["col"]
    )

    def late(env, pieces):
        env["z"] = partial_apply(me, SHARDS, pieces, env["x0h"], env["x0l"], [env["d0"], env["d1"]])

    two = sum_chunks(
        count, env, (keep, send),
        lambda env: fourth_gram(me, SHARDS, env["xh"], env["xl"], mh, ml),
        [half("d", "mid", "s0", 0), high, half("d", "mid", "s0", 1), low], late,
    )
    return last_step(me, SHARDS, two, env["x0h"], env["x0l"], env["z"])


def solution(mesh):
    in_specs = (
        P(("kpt", "row"), None),
        P(("kpt", "row"), None),
        P("kpt", None),
        P("kpt", None),
        P(("kpt", "row"), None),
    )
    out_specs = P(("kpt", "row"), None)
    return jax.shard_map(
        functools.partial(body, mesh.shape["row"]),
        mesh=mesh, in_specs=in_specs, out_specs=out_specs, check_vma=False,
    )
```

```python
import functools
import jax
import jax.numpy as jnp
from jax import lax
from jax.experimental import pallas as pl
from jax.experimental.pallas import tpu as pltpu
from jax.sharding import PartitionSpec as P

F32 = jnp.float32
BF16 = jnp.bfloat16
B = 128
MIB = 1024 * 1024
WEIGHT = 10


def split(x):
    hi = x.astype(BF16)
    return hi, (x - hi.astype(F32)).astype(BF16)


def mm(a, b):
    (ah, al), (bh, bl) = a, b
    return jnp.dot(
        jnp.concatenate([ah, ah, al], axis=1),
        jnp.concatenate([bh, bl, bh], axis=0),
        preferred_element_type=F32,
    )


def call(kernel, name, out_shape, limit, products, arrays, **kw):
    size = 1024
    return pl.pallas_call(
        kernel,
        name=name,
        out_shape=out_shape,
        compiler_params=pltpu.CompilerParams(vmem_limit_bytes=limit * MIB),
        cost_estimate=pl.CostEstimate(
            flops=int(WEIGHT * 6 * products * size ** 3),
            bytes_accessed=int(WEIGHT * 4 * arrays * size * size),
            transcendentals=0,
        ),
        **kw,
    )


def struct(*shape, dtype=F32):
    return jax.ShapeDtypeStruct(shape, dtype)


SMEM = pl.BlockSpec(memory_space=pltpu.SMEM)
VMEM = pl.BlockSpec(memory_space=pltpu.VMEM)


def chunk_lines(size, chunk):
    half = size // B // 4
    return range(chunk * half, (chunk + 1) * half)


def line_blocks(size, i):
    n = size // B
    at = 0
    for top in (i, n - 1 - i):
        for j in range(top, n):
            yield at, slice(top * B, (top + 1) * B), slice(j * B, (j + 1) * B)
            at += B


def pack(g, packed, keep_ref, send_ref, me, shards, chunk):
    size = g.shape[0]
    rows = packed.shape[0] // shards
    per = B // rows
    for line, i in enumerate(chunk_lines(size, chunk)):
        for at, p, q in line_blocks(size, i):
            block = g[p, q] + g[q, p].T
            for s in range(per):
                slot = (line * per + s) ^ me
                packed[pl.ds(pl.multiple_of(slot * rows, rows), rows), at:at + B] = (
                    block[s * rows:(s + 1) * rows]
                )
    half = keep_ref.shape[0]
    keep_ref[...] = packed[:half]
    send_ref[...] = packed[half:]


def unpack(pieces, packed, hi, lo, me, shards, chunk):
    size = hi.shape[0]
    rows = packed.shape[0] // shards
    slots = iter(range(shards))
    for piece in pieces:
        for s in range(piece.shape[0] // rows):
            at = pl.multiple_of((next(slots) ^ me) * rows, rows)
            packed[pl.ds(at, rows), :] = piece[s * rows:(s + 1) * rows, :]
    for line, i in enumerate(chunk_lines(size, chunk)):
        for at, p, q in line_blocks(size, i):
            block = packed[line * B:(line + 1) * B, at:at + B]
            hi[p, q], lo[p, q] = split(block)
            if p.start != q.start:
                hi[q, p], lo[q, p] = split(block.T)


def packed_scratch(size):
    return pltpu.VMEM((size // 4, size + B), F32)


def halves(size):
    return [struct(size // 8, size + B)] * 2


def first_gram_kernel(
    shards, me_ref, a_hbm, b_hbm, keep_ref, send_ref, ah, al, bh, bl, a_buf, b_buf, sems, g, packed
):
    rows, size = a_buf.shape
    q = size // 4
    steps = sems.shape[1]
    tile = rows // steps

    def copies(step):
        r = slice(step * tile, (step + 1) * tile)
        return [
            pltpu.make_async_copy(src.at[r], dst.at[r], sems.at[k, step])
            for k, (src, dst) in enumerate([(a_hbm, a_buf), (b_hbm, b_buf)])
        ]

    def start(step):
        for copy in copies(step):
            copy.start()

    start(0)
    start(1)
    for step in range(steps):
        r = slice(step * tile, (step + 1) * tile)
        for copy in copies(step):
            copy.wait()
        if step + 2 < steps:
            start(step + 2)
        ah[:, r], al[:, r] = split(a_buf[r].T)
        bh[r], bl[r] = split(b_buf[r])
        for r0, r1, c0, c1 in [(0, q, 0, size), (q, size, 0, q), (3 * q, size, 3 * q, size)]:
            product = mm((ah[r0:r1, r], al[r0:r1, r]), (bh[r, c0:c1], bl[r, c0:c1]))
            if step:
                product += g[r0:r1, c0:c1]
            g[r0:r1, c0:c1] = product
    pack(g, packed, keep_ref, send_ref, me_ref[0], shards, 0)


def first_gram(me, shards, a, b):
    rows, size = a.shape
    hbm = pl.BlockSpec(memory_space=pltpu.HBM)
    return call(
        functools.partial(first_gram_kernel, shards), "first_gram",
        halves(size) + [struct(size, rows, dtype=BF16)] * 2 + [struct(rows, size, dtype=BF16)] * 2,
        43, 0.5, 4,
        in_specs=[SMEM, hbm, hbm],
        out_specs=[VMEM] * 6,
        scratch_shapes=[
            pltpu.VMEM((rows, size), F32), pltpu.VMEM((rows, size), F32),
            pltpu.SemaphoreType.DMA((2, 4)),
            pltpu.VMEM((size, size), F32), packed_scratch(size),
        ],
    )(me, a, b)


def lower_product(g, ah, al, bh, bl):
    size = g.shape[0]
    q = size // 4
    for r0, r1, c0, c1 in [(q, 3 * q, q, size), (3 * q, size, q, 3 * q)]:
        c = slice(c0 - q, c1 - q)
        g[r0:r1, c0:c1] = mm((ah[r0:r1, :], al[r0:r1, :]), (bh[:, c], bl[:, c]))


def other_gram_kernel(shards, me_ref, ah, al, bh, bl, keep_ref, send_ref, g, packed):
    q = g.shape[0] // 4
    lower_product(g, ah, al, bh[:, q:], bl[:, q:])
    pack(g, packed, keep_ref, send_ref, me_ref[0], shards, 1)


def other_gram(me, shards, ah, al, bh, bl):
    size = ah.shape[0]
    return call(
        functools.partial(other_gram_kernel, shards), "other_gram", halves(size), 18, 0.5, 2,
        in_specs=[SMEM] + [VMEM] * 4,
        out_specs=[VMEM, VMEM],
        scratch_shapes=[pltpu.VMEM((size, size), F32), packed_scratch(size)],
    )(me, ah, al, bh, bl)


def tiles(count, tile, step):
    def body(t, _):
        step(pl.ds(pl.multiple_of(t * tile, tile), tile))
        return 0

    lax.fori_loop(0, count // tile, body, 0)


def affine_kernel(a_ref, b_ref, out_ref, hi, lo):
    hi[...], lo[...] = split(a_ref[...])

    def step(c):
        out_ref[:, c] = 1.5 * a_ref[:, c] - 0.5 * mm((hi[...], lo[...]), split(b_ref[:, c]))

    tiles(out_ref.shape[1], 256, step)


def affine(a, b, part, parts):
    rows, size = a.shape
    height = rows // parts
    return call(
        affine_kernel, "affine", struct(height, size), 18, 1 / parts, 2,
        grid=(1,),
        in_specs=[
            pl.BlockSpec((height, size), lambda r: (part, 0)),
            pl.BlockSpec((size, size), lambda r: (0, 0)),
        ],
        out_specs=pl.BlockSpec((height, size), lambda r: (0, 0)),
        scratch_shapes=[pltpu.VMEM((height, size), BF16)] * 2,
    )(a, b)


SPANS = (
    (((0, 4),), ((0, 1),), ((0, 1),), ((0, 1), (3, 4))),
    ((), ((1, 4),), ((1, 4),), ((1, 3),)),
)


def sym_product(ah, al, hi, lo, chunk, column):
    q = hi.shape[0] // 4
    spans = [slice(k0 * q, k1 * q) for k0, k1 in SPANS[chunk][column]]
    c = slice(column * q, (column + 1) * q)
    a = [ref[:, k] for ref in (ah, ah, al) for k in spans]
    b = [ref[k, c] for ref in (hi, lo, hi) for k in spans]
    return c, jnp.dot(
        jnp.concatenate(a, axis=1), jnp.concatenate(b, axis=0), preferred_element_type=F32
    )


def apply_first(base_refs, out_ref, ah, al, hi, lo):
    for column in range(4):
        c, product = sym_product(ah, al, hi, lo, 0, column)
        at = 0
        for base_ref in base_refs:
            end = at + base_ref.shape[0]
            out_ref[at:end, c] = base_ref[:, c] - 0.5 * product[at:end]
            at = end


def sym_scratch(size):
    return [pltpu.VMEM((size, size), BF16)] * 2 + [packed_scratch(size)]


def partial_kernel(shards, count, me_ref, *refs):
    pieces, refs = refs[:count], refs[count:]
    ah, al, base_refs, (out_ref, hi, lo, packed) = refs[0], refs[1], refs[2:-4], refs[-4:]
    unpack(pieces, packed, hi, lo, me_ref[0], shards, 0)
    apply_first(base_refs, out_ref, ah, al, hi, lo)


def partial_apply(me, shards, pieces, ah, al, base):
    rows, size = ah.shape
    return call(
        functools.partial(partial_kernel, shards, len(pieces)), "partial_apply",
        struct(rows, size), 18, 0.5, 3,
        in_specs=[SMEM] + [VMEM] * (len(pieces) + 2 + len(base)),
        out_specs=VMEM,
        scratch_shapes=sym_scratch(size),
    )(me, *pieces, ah, al, *base)


def turn_kernel(x_ref, xh, xl):
    xh[...], xl[...] = split(x_ref[...].T)


def turn(x):
    part = struct(*x.shape[::-1], dtype=BF16)
    return call(
        turn_kernel, "turn", [part, part], 16, 0.1, 2, in_specs=[VMEM], out_specs=[VMEM] * 2
    )(x)


def cut_kernel(which, x_ref, *out_refs):
    parts = split(x_ref[...])
    for out_ref, k in zip(out_refs, which):
        out_ref[...] = parts[k]


def cut(x, *which):
    count = len(which)
    return call(
        functools.partial(cut_kernel, which), "cut", [struct(*x.shape, dtype=BF16)] * count,
        16, 0.1, 2, in_specs=[VMEM], out_specs=[VMEM] * count,
    )(x)


def early_kernel(shards, count, me_ref, *refs):
    pieces, refs = refs[:count], refs[count:]
    ah, al, base_refs, refs = refs[0], refs[1], refs[2:-7], refs[-7:]
    xh, xl, out_ref, col_ref, hi, lo, packed = refs
    unpack(pieces, packed, hi, lo, me_ref[0], shards, 0)
    apply_first(base_refs, out_ref, ah, al, hi, lo)
    col_ref[...] = mm((xh[...], xl[...]), split(out_ref[:, :col_ref.shape[1]]))


def early_middle(me, shards, pieces, ah, al, base, xh, xl):
    rows, size = ah.shape
    return call(
        functools.partial(early_kernel, shards, len(pieces)), "early_middle",
        [struct(rows, size), struct(size, size // 4)], 20, 0.75, 5,
        in_specs=[SMEM] + [VMEM] * (len(pieces) + 4 + len(base)),
        out_specs=[VMEM] * 2,
        scratch_shapes=sym_scratch(size),
    )(me, *pieces, ah, al, *base, xh, xl)


def second_gram_kernel(shards, count, me_ref, *refs):
    pieces, refs = refs[:count], refs[count:]
    (ah, al, base_ref, xh, xl, col_ref), refs = refs[:6], refs[6:]
    keep_ref, send_ref, mid_ref, mh, ml, hi, lo, packed, g = refs
    size = g.shape[0]
    q = size // 4
    unpack(pieces, packed, hi, lo, me_ref[0], shards, 1)
    mid_ref[:, :q] = base_ref[:, :q]
    for column in range(1, 4):
        c, product = sym_product(ah, al, hi, lo, 1, column)
        mid = base_ref[:, c] - 0.5 * product
        mid_ref[:, c] = mid
        c = slice(c.start - q, c.stop - q)
        mh[:, c], ml[:, c] = split(mid)
    g[:, :q] = col_ref[...]
    g[:q, q:] = mm((xh[:q, :], xl[:q, :]), (mh[...], ml[...]))
    g[3 * q:, 3 * q:] = mm((xh[3 * q:, :], xl[3 * q:, :]), (mh[:, 2 * q:], ml[:, 2 * q:]))
    pack(g, packed, keep_ref, send_ref, me_ref[0], shards, 0)


def second_gram(me, shards, pieces, ah, al, base, xh, xl, col):
    rows, size = ah.shape
    part = struct(rows, size - size // 4, dtype=BF16)
    return call(
        functools.partial(second_gram_kernel, shards, len(pieces)), "second_gram",
        halves(size) + [struct(rows, size), part, part], 20, 0.8, 5,
        in_specs=[SMEM] + [VMEM] * (len(pieces) + 6),
        out_specs=[VMEM] * 5,
        scratch_shapes=sym_scratch(size) + [pltpu.VMEM((size, size), F32)],
    )(me, *pieces, ah, al, base, xh, xl, col)


def fourth_gram_kernel(shards, me_ref, xh, xl, mh, ml, keep_ref, send_ref, g, packed):
    lower_product(g, xh, xl, mh[...], ml[...])
    pack(g, packed, keep_ref, send_ref, me_ref[0], shards, 1)


def fourth_gram(me, shards, xh, xl, mh, ml):
    size = xh.shape[0]
    return call(
        functools.partial(fourth_gram_kernel, shards), "fourth_gram", halves(size), 18, 0.5, 2,
        in_specs=[SMEM] + [VMEM] * 4,
        out_specs=[VMEM, VMEM],
        scratch_shapes=[pltpu.VMEM((size, size), F32), packed_scratch(size)],
    )(me, xh, xl, mh, ml)


def last_kernel(shards, count, me_ref, *refs):
    pieces = refs[:count]
    ah, al, z_ref, out_hbm, hi, lo, packed, out, sems = refs[count:]
    q = hi.shape[0] // 4
    copies = []

    def send(src, column):
        c = slice(column * q, (column + 1) * q)
        copy = pltpu.make_async_copy(src.at[:, c], out_hbm.at[:, c], sems.at[column])
        copy.start()
        copies.append(copy)

    send(z_ref, 0)
    unpack(pieces, packed, hi, lo, me_ref[0], shards, 1)
    for column in (1, 2, 3):
        c, product = sym_product(ah, al, hi, lo, 1, column)
        out[:, c] = z_ref[:, c] - 0.5 * product
        send(out, column)
    for copy in copies:
        copy.wait()


def last_step(me, shards, pieces, ah, al, z):
    rows, size = z.shape
    return call(
        functools.partial(last_kernel, shards, len(pieces)), "last", struct(rows, size), 22, 0.5, 3,
        in_specs=[SMEM] + [VMEM] * (len(pieces) + 3),
        out_specs=pl.BlockSpec(memory_space=pltpu.HBM),
        scratch_shapes=sym_scratch(size)
        + [pltpu.VMEM((rows, size), F32), pltpu.SemaphoreType.DMA((4,))],
    )(me, *pieces, ah, al, z)


CORE = 1
PLANE = (2, 4, 6)
SHARDS = 2 * (1 + len(PLANE))


def slot_of(index):
    return (index % 2) * (SHARDS // 2) + (index // 2) % (SHARDS // 2)


class Sum:
    def __init__(self, count, keep, send):
        self.count, self.keep, self.send = count, keep, send

    def swap(self, x, offset):
        return lax.ppermute(x, "row", [(i, i ^ offset) for i in range(self.count)])

    def core(self):
        return self.swap(self.send, CORE)

    def plane(self, got):
        total = self.keep + got
        part = total.shape[0] // (1 + len(PLANE))
        self.keep, *sends = [total[k * part:(k + 1) * part] for k in range(1 + len(PLANE))]
        return [self.swap(x, offset) for x, offset in zip(sends, PLANE)]

    def own(self, got):
        self.keep = sum(got, self.keep)

    def exchange(self, offset):
        return self.swap(self.keep, offset)

    def gather_plane(self):
        return [self.swap(self.keep, offset) for offset in PLANE]

    def gather_core(self, got):
        self.mine = jnp.concatenate([self.keep, *got], axis=0)
        return self.swap(self.mine, CORE)


def close(env, *got):
    values = lax.optimization_barrier((*got, *env.values()))
    env.update(zip(env, values[len(got):]))
    return values[:len(got)]


def sum_chunks(count, env, first, second, works, late):
    beyond = [1 << s for s in range(3, count.bit_length() - 1)]
    works = list(works)

    def work():
        if works:
            works.pop(0)(env)

    a = Sum(count, *first)
    got_a = a.core()
    pair = second(env)
    got_a, *pair = close(env, got_a, *pair)
    b = Sum(count, *pair)

    got_a = a.plane(got_a)
    got_b = b.core()
    work()
    (got_b,) = close(env, got_b)

    got_b = b.plane(got_b)
    work()
    a.own(close(env, *got_a))

    for offset in beyond:
        got_a = a.exchange(offset)
        work()
        b.own(close(env, *got_b))
        got_b = [b.exchange(offset)]
        a.own(close(env, got_a))

    got_a = a.gather_plane()
    b.own(close(env, *got_b))

    got_b = b.gather_plane()
    got_a = a.gather_core(close(env, *got_a))
    work()
    (got_a,) = close(env, got_a)
    late(env, [a.mine, got_a])
    got_b = b.gather_core(close(env, *got_b))
    return [b.mine, got_b]


def body(count, orbitals_zero, orbitals_one, correlation_zero, correlation_one, cotangent):
    me = slot_of(lax.axis_index("row")).astype(jnp.int32).reshape(1)
    env = dict(
        x0=orbitals_zero, x1=orbitals_one, s0=correlation_zero, s1=correlation_one, c=cotangent
    )

    def half(name, left, right, part):
        def work(env):
            env[f"{name}{part}"] = affine(env[left], env[right], part, 2)
        return work

    def turned(env):
        env["xh"], env["xl"] = turn(env["x0"])

    def cut_one(env):
        env["x1h"], env["x1l"] = cut(env["x1"], 0, 1)

    def high(env):
        (env["x0h"],) = cut(env["x0"], 0)

    def low(env):
        (env["x0l"],) = cut(env["x0"], 1)

    def early(env, pieces):
        env["mid"], env["col"] = early_middle(
            me, SHARDS, pieces, env["x1h"], env["x1l"], [env["m0"], env["m1"]], env["xh"], env["xl"]
        )

    keep, send, *parts = first_gram(me, SHARDS, env["x1"], env["c"])
    one = sum_chunks(
        count, env, (keep, send), lambda env: other_gram(me, SHARDS, *parts),
        [half("m", "c", "s1", 0), turned, half("m", "c", "s1", 1), cut_one], early,
    )

    keep, send, env["mid"], mh, ml = second_gram(
        me, SHARDS, one, env["x1h"], env["x1l"], env["mid"], env["xh"], env["xl"], env["col"]
    )

    def late(env, pieces):
        env["z"] = partial_apply(me, SHARDS, pieces, env["x0h"], env["x0l"], [env["d0"], env["d1"]])

    two = sum_chunks(
        count, env, (keep, send),
        lambda env: fourth_gram(me, SHARDS, env["xh"], env["xl"], mh, ml),
        [half("d", "mid", "s0", 0), high, half("d", "mid", "s0", 1), low], late,
    )
    return last_step(me, SHARDS, two, env["x0h"], env["x0l"], env["z"])


def solution(mesh):
    in_specs = (
        P(("kpt", "row"), None),
        P(("kpt", "row"), None),
        P("kpt", None),
        P("kpt", None),
        P(("kpt", "row"), None),
    )
    out_specs = P(("kpt", "row"), None)
    return jax.shard_map(
        functools.partial(body, mesh.shape["row"]),
        mesh=mesh, in_specs=in_specs, out_specs=out_specs, check_vma=False,
    )
```

```python
import functools
import jax
import jax.numpy as jnp
from jax import lax
from jax.experimental import pallas as pl
from jax.experimental.pallas import tpu as pltpu
from jax.sharding import PartitionSpec as P

F32 = jnp.float32
BF16 = jnp.bfloat16
B = 128
MIB = 1024 * 1024
WEIGHT = 10


def split(x):
    hi = x.astype(BF16)
    return hi, (x - hi.astype(F32)).astype(BF16)


def mm(a, b):
    (ah, al), (bh, bl) = a, b
    return jnp.dot(
        jnp.concatenate([ah, ah, al], axis=1),
        jnp.concatenate([bh, bl, bh], axis=0),
        preferred_element_type=F32,
    )


def call(kernel, name, out_shape, limit, products, arrays, **kw):
    size = 1024
    return pl.pallas_call(
        kernel,
        name=name,
        out_shape=out_shape,
        compiler_params=pltpu.CompilerParams(vmem_limit_bytes=limit * MIB),
        cost_estimate=pl.CostEstimate(
            flops=int(WEIGHT * 6 * products * size ** 3),
            bytes_accessed=int(WEIGHT * 4 * arrays * size * size),
            transcendentals=0,
        ),
        **kw,
    )


def struct(*shape, dtype=F32):
    return jax.ShapeDtypeStruct(shape, dtype)


SMEM = pl.BlockSpec(memory_space=pltpu.SMEM)
VMEM = pl.BlockSpec(memory_space=pltpu.VMEM)


def chunk_lines(size, chunk):
    half = size // B // 4
    return range(chunk * half, (chunk + 1) * half)


def line_blocks(size, i):
    n = size // B
    block = lambda k: slice(k * B, (k + 1) * B)
    return [(block(top), block(j)) for top in (i, n - 1 - i) for j in range(top + 1, n)]


def diagonal_blocks(size, i):
    n = size // B
    return [slice(k * B, (k + 1) * B) for k in (i, n - 1 - i)]


def part_rows(size, shards):
    return size // 4 // shards


def shard_rows(size, shards):
    return part_rows(size, shards) * (size // B) + 8


def places():
    row = lax.broadcasted_iota(jnp.int32, (B, B), 0)
    column = lax.broadcasted_iota(jnp.int32, (B, B), 1)
    return row, column


def pack(g, packed, keep_ref, send_ref, me, shards, chunk):
    size = g.shape[0]
    rows, height = part_rows(size, shards), shard_rows(size, shards)
    per = B // rows
    row, column = places()
    whole = lambda p, q: g[p, q] + g[q, p].T
    for line, i in enumerate(chunk_lines(size, chunk)):
        starts = [((line * per + s) ^ me) * height for s in range(per)]

        def put(at, s, value):
            start = pl.multiple_of(starts[s] + at, 8)
            packed[pl.ds(start, value.shape[0]), :] = value

        upper, lower = [whole(p, p) for p in diagonal_blocks(size, i)]
        for k, place in enumerate([None] + line_blocks(size, i)):
            block = whole(*place) if place else jnp.where(column >= row, upper, lower)
            for s in range(per):
                put(k * rows, s, block[s * rows:(s + 1) * rows])
        element = jnp.sum(jnp.where(column == row, lower, 0.0), axis=0, keepdims=True)
        for s in range(per):
            put(height - 8, s, jnp.broadcast_to(element, (8, B)))
    half = keep_ref.shape[0]
    keep_ref[...] = packed[:half]
    send_ref[...] = packed[half:]


def unpack(pieces, packed, hi, lo, me, shards, chunk):
    size = hi.shape[0]
    rows, height = part_rows(size, shards), shard_rows(size, shards)
    per = B // rows
    row, column = places()
    slot = 0
    for piece in pieces:
        for s in range(piece.shape[0] // height):
            at = pl.multiple_of((slot ^ me) * height, 8)
            packed[pl.ds(at, height), :] = piece[s * height:(s + 1) * height, :]
            slot += 1

    def put(p, q, block):
        hi[p, q], lo[p, q] = split(block)

    for line, i in enumerate(chunk_lines(size, chunk)):
        start = line * per * height

        def get(k):
            return jnp.concatenate(
                [
                    packed[start + s * height + k * rows:start + s * height + (k + 1) * rows, :]
                    for s in range(per)
                ],
                axis=0,
            )

        first, last = diagonal_blocks(size, i)
        block = get(0)
        turned = block.T
        element = packed[start + height - 8:start + height - 7, :]
        put(first, first, jnp.where(column >= row, block, turned))
        below = jnp.where(column < row, block, turned)
        put(last, last, jnp.where(column == row, jnp.broadcast_to(element, (B, B)), below))
        for k, (p, q) in enumerate(line_blocks(size, i)):
            block = get(k + 1)
            put(p, q, block)
            put(q, p, block.T)


def packed_scratch(size, shards):
    return pltpu.VMEM((shards * shard_rows(size, shards), B), F32)


def halves(size, shards):
    return [struct(shards // 2 * shard_rows(size, shards), B)] * 2


def first_gram_kernel(
    shards, me_ref, a_hbm, b_hbm, keep_ref, send_ref, ah, al, bh, bl, a_buf, b_buf, sems, g, packed
):
    rows, size = a_buf.shape
    q = size // 4
    steps = sems.shape[1]
    tile = rows // steps

    def copies(step):
        r = slice(step * tile, (step + 1) * tile)
        return [
            pltpu.make_async_copy(src.at[r], dst.at[r], sems.at[k, step])
            for k, (src, dst) in enumerate([(a_hbm, a_buf), (b_hbm, b_buf)])
        ]

    def start(step):
        for copy in copies(step):
            copy.start()

    start(0)
    start(1)
    for step in range(steps):
        r = slice(step * tile, (step + 1) * tile)
        for copy in copies(step):
            copy.wait()
        if step + 2 < steps:
            start(step + 2)
        ah[:, r], al[:, r] = split(a_buf[r].T)
        bh[r], bl[r] = split(b_buf[r])
        for r0, r1, c0, c1 in [(0, q, 0, size), (q, size, 0, q), (3 * q, size, 3 * q, size)]:
            product = mm((ah[r0:r1, r], al[r0:r1, r]), (bh[r, c0:c1], bl[r, c0:c1]))
            if step:
                product += g[r0:r1, c0:c1]
            g[r0:r1, c0:c1] = product
    pack(g, packed, keep_ref, send_ref, me_ref[0], shards, 0)


def first_gram(me, shards, a, b):
    rows, size = a.shape
    hbm = pl.BlockSpec(memory_space=pltpu.HBM)
    return call(
        functools.partial(first_gram_kernel, shards), "first_gram",
        halves(size, shards) + [struct(size, rows, dtype=BF16)] * 2 + [struct(rows, size, dtype=BF16)] * 2,
        43, 0.5, 4,
        in_specs=[SMEM, hbm, hbm],
        out_specs=[VMEM] * 6,
        scratch_shapes=[
            pltpu.VMEM((rows, size), F32), pltpu.VMEM((rows, size), F32),
            pltpu.SemaphoreType.DMA((2, 4)),
            pltpu.VMEM((size, size), F32), packed_scratch(size, shards),
        ],
    )(me, a, b)


def lower_product(g, ah, al, bh, bl):
    size = g.shape[0]
    q = size // 4
    for r0, r1, c0, c1 in [(q, 3 * q, q, size), (3 * q, size, q, 3 * q)]:
        c = slice(c0 - q, c1 - q)
        g[r0:r1, c0:c1] = mm((ah[r0:r1, :], al[r0:r1, :]), (bh[:, c], bl[:, c]))


def other_gram_kernel(shards, me_ref, ah, al, bh, bl, keep_ref, send_ref, g, packed):
    q = g.shape[0] // 4
    lower_product(g, ah, al, bh[:, q:], bl[:, q:])
    pack(g, packed, keep_ref, send_ref, me_ref[0], shards, 1)


def other_gram(me, shards, ah, al, bh, bl):
    size = ah.shape[0]
    return call(
        functools.partial(other_gram_kernel, shards), "other_gram", halves(size, shards), 18, 0.5, 2,
        in_specs=[SMEM] + [VMEM] * 4,
        out_specs=[VMEM, VMEM],
        scratch_shapes=[pltpu.VMEM((size, size), F32), packed_scratch(size, shards)],
    )(me, ah, al, bh, bl)


def tiles(count, tile, step):
    def body(t, _):
        step(pl.ds(pl.multiple_of(t * tile, tile), tile))
        return 0

    lax.fori_loop(0, count // tile, body, 0)


def affine_kernel(a_ref, b_ref, out_ref, hi, lo):
    hi[...], lo[...] = split(a_ref[...])

    def step(c):
        out_ref[:, c] = 1.5 * a_ref[:, c] - 0.5 * mm((hi[...], lo[...]), split(b_ref[:, c]))

    tiles(out_ref.shape[1], 256, step)


def affine(a, b, part, parts):
    rows, size = a.shape
    height = rows // parts
    return call(
        affine_kernel, "affine", struct(height, size), 18, 1 / parts, 2,
        grid=(1,),
        in_specs=[
            pl.BlockSpec((height, size), lambda r: (part, 0)),
            pl.BlockSpec((size, size), lambda r: (0, 0)),
        ],
        out_specs=pl.BlockSpec((height, size), lambda r: (0, 0)),
        scratch_shapes=[pltpu.VMEM((height, size), BF16)] * 2,
    )(a, b)


SPANS = (
    (((0, 4),), ((0, 1),), ((0, 1),), ((0, 1), (3, 4))),
    ((), ((1, 4),), ((1, 4),), ((1, 3),)),
)


def sym_product(ah, al, hi, lo, chunk, column):
    q = hi.shape[0] // 4
    spans = [slice(k0 * q, k1 * q) for k0, k1 in SPANS[chunk][column]]
    c = slice(column * q, (column + 1) * q)
    a = [ref[:, k] for ref in (ah, ah, al) for k in spans]
    b = [ref[k, c] for ref in (hi, lo, hi) for k in spans]
    return c, jnp.dot(
        jnp.concatenate(a, axis=1), jnp.concatenate(b, axis=0), preferred_element_type=F32
    )


def apply_first(base_refs, out_ref, ah, al, hi, lo):
    for column in range(4):
        c, product = sym_product(ah, al, hi, lo, 0, column)
        at = 0
        for base_ref in base_refs:
            end = at + base_ref.shape[0]
            out_ref[at:end, c] = base_ref[:, c] - 0.5 * product[at:end]
            at = end


def sym_scratch(size, shards):
    return [pltpu.VMEM((size, size), BF16)] * 2 + [packed_scratch(size, shards)]


def partial_kernel(shards, count, me_ref, *refs):
    pieces, refs = refs[:count], refs[count:]
    ah, al, base_refs, (out_ref, hi, lo, packed) = refs[0], refs[1], refs[2:-4], refs[-4:]
    unpack(pieces, packed, hi, lo, me_ref[0], shards, 0)
    apply_first(base_refs, out_ref, ah, al, hi, lo)


def partial_apply(me, shards, pieces, ah, al, base):
    rows, size = ah.shape
    return call(
        functools.partial(partial_kernel, shards, len(pieces)), "partial_apply",
        struct(rows, size), 18, 0.5, 3,
        in_specs=[SMEM] + [VMEM] * (len(pieces) + 2 + len(base)),
        out_specs=VMEM,
        scratch_shapes=sym_scratch(size, shards),
    )(me, *pieces, ah, al, *base)


def turn_kernel(x_ref, xh, xl):
    xh[...], xl[...] = split(x_ref[...].T)


def turn(x):
    part = struct(*x.shape[::-1], dtype=BF16)
    return call(
        turn_kernel, "turn", [part, part], 16, 0.1, 2, in_specs=[VMEM], out_specs=[VMEM] * 2
    )(x)


def cut_kernel(which, x_ref, *out_refs):
    parts = split(x_ref[...])
    for out_ref, k in zip(out_refs, which):
        out_ref[...] = parts[k]


def cut(x, *which):
    count = len(which)
    return call(
        functools.partial(cut_kernel, which), "cut", [struct(*x.shape, dtype=BF16)] * count,
        16, 0.1, 2, in_specs=[VMEM], out_specs=[VMEM] * count,
    )(x)


def early_kernel(shards, count, me_ref, *refs):
    pieces, refs = refs[:count], refs[count:]
    ah, al, base_refs, refs = refs[0], refs[1], refs[2:-7], refs[-7:]
    xh, xl, out_ref, col_ref, hi, lo, packed = refs
    unpack(pieces, packed, hi, lo, me_ref[0], shards, 0)
    apply_first(base_refs, out_ref, ah, al, hi, lo)
    col_ref[...] = mm((xh[...], xl[...]), split(out_ref[:, :col_ref.shape[1]]))


def early_middle(me, shards, pieces, ah, al, base, xh, xl):
    rows, size = ah.shape
    return call(
        functools.partial(early_kernel, shards, len(pieces)), "early_middle",
        [struct(rows, size), struct(size, size // 4)], 20, 0.75, 5,
        in_specs=[SMEM] + [VMEM] * (len(pieces) + 4 + len(base)),
        out_specs=[VMEM] * 2,
        scratch_shapes=sym_scratch(size, shards),
    )(me, *pieces, ah, al, *base, xh, xl)


def second_gram_kernel(shards, count, me_ref, *refs):
    pieces, refs = refs[:count], refs[count:]
    (ah, al, base_ref, xh, xl, col_ref), refs = refs[:6], refs[6:]
    keep_ref, send_ref, mid_ref, mh, ml, hi, lo, packed, g = refs
    size = g.shape[0]
    q = size // 4
    unpack(pieces, packed, hi, lo, me_ref[0], shards, 1)
    mid_ref[:, :q] = base_ref[:, :q]
    for column in range(1, 4):
        c, product = sym_product(ah, al, hi, lo, 1, column)
        mid = base_ref[:, c] - 0.5 * product
        mid_ref[:, c] = mid
        c = slice(c.start - q, c.stop - q)
        mh[:, c], ml[:, c] = split(mid)
    g[:, :q] = col_ref[...]
    g[:q, q:] = mm((xh[:q, :], xl[:q, :]), (mh[...], ml[...]))
    g[3 * q:, 3 * q:] = mm((xh[3 * q:, :], xl[3 * q:, :]), (mh[:, 2 * q:], ml[:, 2 * q:]))
    pack(g, packed, keep_ref, send_ref, me_ref[0], shards, 0)


def second_gram(me, shards, pieces, ah, al, base, xh, xl, col):
    rows, size = ah.shape
    part = struct(rows, size - size // 4, dtype=BF16)
    return call(
        functools.partial(second_gram_kernel, shards, len(pieces)), "second_gram",
        halves(size, shards) + [struct(rows, size), part, part], 20, 0.8, 5,
        in_specs=[SMEM] + [VMEM] * (len(pieces) + 6),
        out_specs=[VMEM] * 5,
        scratch_shapes=sym_scratch(size, shards) + [pltpu.VMEM((size, size), F32)],
    )(me, *pieces, ah, al, base, xh, xl, col)


def fourth_gram_kernel(shards, me_ref, xh, xl, mh, ml, keep_ref, send_ref, g, packed):
    lower_product(g, xh, xl, mh[...], ml[...])
    pack(g, packed, keep_ref, send_ref, me_ref[0], shards, 1)


def fourth_gram(me, shards, xh, xl, mh, ml):
    size = xh.shape[0]
    return call(
        functools.partial(fourth_gram_kernel, shards), "fourth_gram", halves(size, shards), 18, 0.5, 2,
        in_specs=[SMEM] + [VMEM] * 4,
        out_specs=[VMEM, VMEM],
        scratch_shapes=[pltpu.VMEM((size, size), F32), packed_scratch(size, shards)],
    )(me, xh, xl, mh, ml)


def last_kernel(shards, count, me_ref, *refs):
    pieces = refs[:count]
    ah, al, z_ref, out_hbm, hi, lo, packed, out, sems = refs[count:]
    q = hi.shape[0] // 4
    copies = []

    def send(src, column):
        c = slice(column * q, (column + 1) * q)
        copy = pltpu.make_async_copy(src.at[:, c], out_hbm.at[:, c], sems.at[column])
        copy.start()
        copies.append(copy)

    send(z_ref, 0)
    unpack(pieces, packed, hi, lo, me_ref[0], shards, 1)
    for column in (1, 2, 3):
        c, product = sym_product(ah, al, hi, lo, 1, column)
        out[:, c] = z_ref[:, c] - 0.5 * product
        send(out, column)
    for copy in copies:
        copy.wait()


def last_step(me, shards, pieces, ah, al, z):
    rows, size = z.shape
    return call(
        functools.partial(last_kernel, shards, len(pieces)), "last", struct(rows, size), 22, 0.5, 3,
        in_specs=[SMEM] + [VMEM] * (len(pieces) + 3),
        out_specs=pl.BlockSpec(memory_space=pltpu.HBM),
        scratch_shapes=sym_scratch(size, shards)
        + [pltpu.VMEM((rows, size), F32), pltpu.SemaphoreType.DMA((4,))],
    )(me, *pieces, ah, al, z)


CORE = 1
PLANE = (2, 4, 6)
SHARDS = 2 * (1 + len(PLANE))


def slot_of(index):
    return (index % 2) * (SHARDS // 2) + (index // 2) % (SHARDS // 2)


class Sum:
    def __init__(self, count, keep, send):
        self.count, self.keep, self.send = count, keep, send

    def swap(self, x, offset):
        return lax.ppermute(x, "row", [(i, i ^ offset) for i in range(self.count)])

    def core(self):
        return self.swap(self.send, CORE)

    def plane(self, got):
        total = self.keep + got
        part = total.shape[0] // (1 + len(PLANE))
        self.keep, *sends = [total[k * part:(k + 1) * part] for k in range(1 + len(PLANE))]
        return [self.swap(x, offset) for x, offset in zip(sends, PLANE)]

    def own(self, got):
        self.keep = sum(got, self.keep)

    def exchange(self, offset):
        return self.swap(self.keep, offset)

    def gather_plane(self):
        return [self.swap(self.keep, offset) for offset in PLANE]

    def gather_core(self, got):
        self.mine = jnp.concatenate([self.keep, *got], axis=0)
        return self.swap(self.mine, CORE)


def close(env, *got):
    values = lax.optimization_barrier((*got, *env.values()))
    env.update(zip(env, values[len(got):]))
    return values[:len(got)]


def sum_chunks(count, env, first, second, works, late):
    beyond = [1 << s for s in range(3, count.bit_length() - 1)]
    works = list(works)

    def work():
        if works:
            works.pop(0)(env)

    a = Sum(count, *first)
    got_a = a.core()
    pair = second(env)
    got_a, *pair = close(env, got_a, *pair)
    b = Sum(count, *pair)

    got_a = a.plane(got_a)
    got_b = b.core()
    work()
    (got_b,) = close(env, got_b)

    got_b = b.plane(got_b)
    work()
    a.own(close(env, *got_a))

    for offset in beyond:
        got_a = a.exchange(offset)
        work()
        b.own(close(env, *got_b))
        got_b = [b.exchange(offset)]
        a.own(close(env, got_a))

    got_a = a.gather_plane()
    b.own(close(env, *got_b))

    got_b = b.gather_plane()
    got_a = a.gather_core(close(env, *got_a))
    work()
    (got_a,) = close(env, got_a)
    late(env, [a.mine, got_a])
    got_b = b.gather_core(close(env, *got_b))
    return [b.mine, got_b]


def body(count, orbitals_zero, orbitals_one, correlation_zero, correlation_one, cotangent):
    me = slot_of(lax.axis_index("row")).astype(jnp.int32).reshape(1)
    env = dict(
        x0=orbitals_zero, x1=orbitals_one, s0=correlation_zero, s1=correlation_one, c=cotangent
    )

    def half(name, left, right, part):
        def work(env):
            env[f"{name}{part}"] = affine(env[left], env[right], part, 2)
        return work

    def turned(env):
        env["xh"], env["xl"] = turn(env["x0"])

    def cut_one(env):
        env["x1h"], env["x1l"] = cut(env["x1"], 0, 1)

    def high(env):
        (env["x0h"],) = cut(env["x0"], 0)

    def low(env):
        (env["x0l"],) = cut(env["x0"], 1)

    def early(env, pieces):
        env["mid"], env["col"] = early_middle(
            me, SHARDS, pieces, env["x1h"], env["x1l"], [env["m0"], env["m1"]], env["xh"], env["xl"]
        )

    keep, send, *parts = first_gram(me, SHARDS, env["x1"], env["c"])
    one = sum_chunks(
        count, env, (keep, send), lambda env: other_gram(me, SHARDS, *parts),
        [half("m", "c", "s1", 0), turned, half("m", "c", "s1", 1), cut_one], early,
    )

    keep, send, env["mid"], mh, ml = second_gram(
        me, SHARDS, one, env["x1h"], env["x1l"], env["mid"], env["xh"], env["xl"], env["col"]
    )

    def late(env, pieces):
        env["z"] = partial_apply(me, SHARDS, pieces, env["x0h"], env["x0l"], [env["d0"], env["d1"]])

    two = sum_chunks(
        count, env, (keep, send),
        lambda env: fourth_gram(me, SHARDS, env["xh"], env["xl"], mh, ml),
        [half("d", "mid", "s0", 0), high, half("d", "mid", "s0", 1), low], late,
    )
    return last_step(me, SHARDS, two, env["x0h"], env["x0l"], env["z"])


def solution(mesh):
    in_specs = (
        P(("kpt", "row"), None),
        P(("kpt", "row"), None),
        P("kpt", None),
        P("kpt", None),
        P(("kpt", "row"), None),
    )
    out_specs = P(("kpt", "row"), None)
    return jax.shard_map(
        functools.partial(body, mesh.shape["row"]),
        mesh=mesh, in_specs=in_specs, out_specs=out_specs, check_vma=False,
    )
```

```python
import functools
import jax
import jax.numpy as jnp
from jax import lax
from jax.experimental import pallas as pl
from jax.experimental.pallas import tpu as pltpu
from jax.sharding import PartitionSpec as P

F32 = jnp.float32
BF16 = jnp.bfloat16
B = 128
MIB = 1024 * 1024
WEIGHT = 10


def split(x):
    hi = x.astype(BF16)
    return hi, (x - hi.astype(F32)).astype(BF16)


def mm(a, b):
    (ah, al), (bh, bl) = a, b
    return jnp.dot(
        jnp.concatenate([ah, ah, al], axis=1),
        jnp.concatenate([bh, bl, bh], axis=0),
        preferred_element_type=F32,
    )


def call(kernel, name, out_shape, limit, products, arrays, **kw):
    size = 1024
    return pl.pallas_call(
        kernel,
        name=name,
        out_shape=out_shape,
        compiler_params=pltpu.CompilerParams(vmem_limit_bytes=limit * MIB),
        cost_estimate=pl.CostEstimate(
            flops=int(WEIGHT * 6 * products * size ** 3),
            bytes_accessed=int(WEIGHT * 4 * arrays * size * size),
            transcendentals=0,
        ),
        **kw,
    )


def struct(*shape, dtype=F32):
    return jax.ShapeDtypeStruct(shape, dtype)


SMEM = pl.BlockSpec(memory_space=pltpu.SMEM)
VMEM = pl.BlockSpec(memory_space=pltpu.VMEM)


def chunk_lines(size, chunk):
    half = size // B // 4
    return range(chunk * half, (chunk + 1) * half)


def line_blocks(size, i):
    n = size // B
    block = lambda k: slice(k * B, (k + 1) * B)
    return [(block(top), block(j)) for top in (i, n - 1 - i) for j in range(top + 1, n)]


def diagonal_blocks(size, i):
    n = size // B
    return [slice(k * B, (k + 1) * B) for k in (i, n - 1 - i)]


def part_rows(size, shards):
    return size // 4 // shards


def shard_rows(size, shards):
    return part_rows(size, shards) * (size // B) + 8


def places():
    row = lax.broadcasted_iota(jnp.int32, (B, B), 0)
    column = lax.broadcasted_iota(jnp.int32, (B, B), 1)
    return row, column


def pack(g, packed, keep_ref, send_ref, me, shards, chunk):
    size = g.shape[0]
    rows, height = part_rows(size, shards), shard_rows(size, shards)
    per = B // rows
    row, column = places()
    whole = lambda p, q: g[p, q] + g[q, p].T
    for line, i in enumerate(chunk_lines(size, chunk)):
        starts = [((line * per + s) ^ me) * height for s in range(per)]

        def put(at, s, value):
            start = pl.multiple_of(starts[s] + at, 8)
            packed[pl.ds(start, value.shape[0]), :] = value

        upper, lower = [whole(p, p) for p in diagonal_blocks(size, i)]
        for k, place in enumerate([None] + line_blocks(size, i)):
            block = whole(*place) if place else jnp.where(column >= row, upper, lower)
            for s in range(per):
                put(k * rows, s, block[s * rows:(s + 1) * rows])
        element = jnp.sum(jnp.where(column == row, lower, 0.0), axis=0, keepdims=True)
        for s in range(per):
            put(height - 8, s, jnp.broadcast_to(element, (8, B)))
    half = keep_ref.shape[0]
    keep_ref[...] = packed[:half]
    send_ref[...] = packed[half:]


def unpack(pieces, packed, hi, lo, me, shards, chunk):
    size = hi.shape[0]
    rows, height = part_rows(size, shards), shard_rows(size, shards)
    per = B // rows
    row, column = places()
    slot = 0
    for piece in pieces:
        for s in range(piece.shape[0] // height):
            at = pl.multiple_of((slot ^ me) * height, 8)
            packed[pl.ds(at, height), :] = piece[s * height:(s + 1) * height, :]
            slot += 1

    def put(p, q, block):
        hi[p, q], lo[p, q] = split(block)

    for line, i in enumerate(chunk_lines(size, chunk)):
        start = line * per * height

        def get(k):
            return jnp.concatenate(
                [
                    packed[start + s * height + k * rows:start + s * height + (k + 1) * rows, :]
                    for s in range(per)
                ],
                axis=0,
            )

        first, last = diagonal_blocks(size, i)
        block = get(0)
        turned = block.T
        element = packed[start + height - 8:start + height - 7, :]
        put(first, first, jnp.where(column >= row, block, turned))
        below = jnp.where(column < row, block, turned)
        put(last, last, jnp.where(column == row, jnp.broadcast_to(element, (B, B)), below))
        for k, (p, q) in enumerate(line_blocks(size, i)):
            block = get(k + 1)
            put(p, q, block)
            put(q, p, block.T)


def packed_scratch(size, shards):
    return pltpu.VMEM((shards * shard_rows(size, shards), B), F32)


def halves(size, shards):
    return [struct(shards // 2 * shard_rows(size, shards), B)] * 2


def first_gram_kernel(
    shards, me_ref, a_hbm, b_hbm, keep_ref, send_ref, ah, al, bh, bl, a_buf, b_buf, sems, g, packed
):
    rows, size = a_buf.shape
    q = size // 4
    steps = sems.shape[1]
    tile = rows // steps

    def copies(step):
        r = slice(step * tile, (step + 1) * tile)
        return [
            pltpu.make_async_copy(src.at[r], dst.at[r], sems.at[k, step])
            for k, (src, dst) in enumerate([(a_hbm, a_buf), (b_hbm, b_buf)])
        ]

    def start(step):
        for copy in copies(step):
            copy.start()

    start(0)
    start(1)
    for step in range(steps):
        r = slice(step * tile, (step + 1) * tile)
        for copy in copies(step):
            copy.wait()
        if step + 2 < steps:
            start(step + 2)
        ah[:, r], al[:, r] = split(a_buf[r].T)
        bh[r], bl[r] = split(b_buf[r])
        for r0, r1, c0, c1 in [(0, q, 0, size), (q, size, 0, q), (3 * q, size, 3 * q, size)]:
            product = mm((ah[r0:r1, r], al[r0:r1, r]), (bh[r, c0:c1], bl[r, c0:c1]))
            if step:
                product += g[r0:r1, c0:c1]
            g[r0:r1, c0:c1] = product
    pack(g, packed, keep_ref, send_ref, me_ref[0], shards, 0)


def first_gram(me, shards, a, b):
    rows, size = a.shape
    hbm = pl.BlockSpec(memory_space=pltpu.HBM)
    return call(
        functools.partial(first_gram_kernel, shards), "first_gram",
        halves(size, shards) + [struct(size, rows, dtype=BF16)] * 2 + [struct(rows, size, dtype=BF16)] * 2,
        43, 0.5, 4,
        in_specs=[SMEM, hbm, hbm],
        out_specs=[VMEM] * 6,
        scratch_shapes=[
            pltpu.VMEM((rows, size), F32), pltpu.VMEM((rows, size), F32),
            pltpu.SemaphoreType.DMA((2, 4)),
            pltpu.VMEM((size, size), F32), packed_scratch(size, shards),
        ],
    )(me, a, b)


def lower_product(g, ah, al, bh, bl):
    size = g.shape[0]
    q = size // 4
    for r0, r1, c0, c1 in [(q, 3 * q, q, size), (3 * q, size, q, 3 * q)]:
        c = slice(c0 - q, c1 - q)
        g[r0:r1, c0:c1] = mm((ah[r0:r1, :], al[r0:r1, :]), (bh[:, c], bl[:, c]))


def other_gram_kernel(shards, me_ref, ah, al, bh, bl, keep_ref, send_ref, g, packed):
    q = g.shape[0] // 4
    lower_product(g, ah, al, bh[:, q:], bl[:, q:])
    pack(g, packed, keep_ref, send_ref, me_ref[0], shards, 1)


def other_gram(me, shards, ah, al, bh, bl):
    size = ah.shape[0]
    return call(
        functools.partial(other_gram_kernel, shards), "other_gram", halves(size, shards), 18, 0.5, 2,
        in_specs=[SMEM] + [VMEM] * 4,
        out_specs=[VMEM, VMEM],
        scratch_shapes=[pltpu.VMEM((size, size), F32), packed_scratch(size, shards)],
    )(me, ah, al, bh, bl)


def tiles(count, tile, step):
    def body(t, _):
        step(pl.ds(pl.multiple_of(t * tile, tile), tile))
        return 0

    lax.fori_loop(0, count // tile, body, 0)


def affine_kernel(a_ref, b_ref, out_ref, hi, lo):
    hi[...], lo[...] = split(a_ref[...])

    def step(c):
        out_ref[:, c] = 1.5 * a_ref[:, c] - 0.5 * mm((hi[...], lo[...]), split(b_ref[:, c]))

    tiles(out_ref.shape[1], 256, step)


def affine(a, b, half):
    rows, size = a.shape
    block = lambda at: pl.BlockSpec((rows // 2, size), lambda r: (at, 0))
    return call(
        affine_kernel, "affine", struct(rows // 2, size), 18, 0.5, 2,
        grid=(1,),
        in_specs=[block(half), pl.BlockSpec((size, size), lambda r: (0, 0))],
        out_specs=block(0),
        scratch_shapes=[pltpu.VMEM((rows // 2, size), BF16)] * 2,
    )(a, b)


def affine_parts_kernel(a_ref, ah, al, bh, bl, out_ref):
    def step(c):
        product = mm((ah[...], al[...]), (bh[:, c], bl[:, c]))
        out_ref[:, c] = 1.5 * a_ref[:, c] - 0.5 * product

    tiles(out_ref.shape[1], 256, step)


def affine_parts(a, ah, al, bh, bl, half):
    rows, size = a.shape
    block = lambda at: pl.BlockSpec((rows // 2, size), lambda r: (at, 0))
    whole = pl.BlockSpec((size, size), lambda r: (0, 0))
    return call(
        affine_parts_kernel, "affine_parts", struct(rows // 2, size), 18, 0.5, 2,
        grid=(1,),
        in_specs=[block(half)] * 3 + [whole] * 2,
        out_specs=block(0),
    )(a, ah, al, bh, bl)


SPANS = (
    (((0, 4),), ((0, 1),), ((0, 1),), ((0, 1), (3, 4))),
    ((), ((1, 4),), ((1, 4),), ((1, 3),)),
)


def sym_product(ah, al, hi, lo, chunk, column):
    q = hi.shape[0] // 4
    spans = [slice(k0 * q, k1 * q) for k0, k1 in SPANS[chunk][column]]
    c = slice(column * q, (column + 1) * q)
    a = [ref[:, k] for ref in (ah, ah, al) for k in spans]
    b = [ref[k, c] for ref in (hi, lo, hi) for k in spans]
    return c, jnp.dot(
        jnp.concatenate(a, axis=1), jnp.concatenate(b, axis=0), preferred_element_type=F32
    )


def apply_first(base_refs, out_ref, ah, al, hi, lo, columns):
    q = hi.shape[0] // 4
    for column in columns:
        c, product = sym_product(ah, al, hi, lo, 0, column)
        out = slice(c.start - columns[0] * q, c.stop - columns[0] * q)
        at = 0
        for base_ref in base_refs:
            end = at + base_ref.shape[0]
            out_ref[at:end, out] = base_ref[:, c] - 0.5 * product[at:end]
            at = end


def sym_scratch(size, shards):
    return [pltpu.VMEM((size, size), BF16)] * 2 + [packed_scratch(size, shards)]


def first_part_kernel(shards, count, columns, me_ref, *refs):
    pieces, refs = refs[:count], refs[count:]
    ah, al, base_refs, (out_ref, hi, lo, packed) = refs[0], refs[1], refs[2:-4], refs[-4:]
    unpack(pieces, packed, hi, lo, me_ref[0], shards, 0)
    apply_first(base_refs, out_ref, ah, al, hi, lo, columns)


def first_part(me, shards, pieces, ah, al, base, columns):
    rows, size = ah.shape
    part = struct(size, size, dtype=BF16)
    more = len(columns) < 4
    scratch = sym_scratch(size, shards)
    return call(
        functools.partial(first_part_kernel, shards, len(pieces), columns), "first_part",
        [struct(rows, len(columns) * size // 4)] + [part, part] * more, 18, 0.5, 3,
        in_specs=[SMEM] + [VMEM] * (len(pieces) + 2 + len(base)),
        out_specs=[VMEM] * (1 + 2 * more),
        scratch_shapes=scratch[2 * more:],
    )(me, *pieces, ah, al, *base)


def other_part_kernel(columns, ah, al, hi, lo, *refs):
    apply_first(refs[:-1], refs[-1], ah, al, hi, lo, columns)


def other_part(ah, al, hi, lo, base, columns):
    rows, size = ah.shape
    return call(
        functools.partial(other_part_kernel, columns), "other_part",
        struct(rows, len(columns) * size // 4), 16, 0.25, 3,
        in_specs=[VMEM] * (4 + len(base)),
        out_specs=VMEM,
    )(ah, al, hi, lo, *base)


def column_kernel(xh, xl, mid_ref, col_ref):
    col_ref[...] = mm((xh[...], xl[...]), split(mid_ref[...]))


def column_product(xh, xl, mid):
    size, rows = xh.shape
    block = pl.BlockSpec((rows, size // 4), lambda r: (0, 0))
    whole = pl.BlockSpec((size, rows), lambda r: (0, 0))
    return call(
        column_kernel, "column_product", struct(size, size // 4), 16, 0.25, 2,
        grid=(1,), in_specs=[whole, whole, block], out_specs=block,
    )(xh, xl, mid)


def turn_kernel(x_ref, xh, xl):
    def step(r):
        xh[:, r], xl[:, r] = split(x_ref[r].T)

    tiles(x_ref.shape[0], 256, step)


def turn(x):
    part = struct(*x.shape[::-1], dtype=BF16)
    return call(
        turn_kernel, "turn", [part, part], 16, 0.1, 2, in_specs=[VMEM], out_specs=[VMEM] * 2
    )(x)


def cut_kernel(which, x_ref, *out_refs):
    def step(r):
        parts = split(x_ref[r])
        for out_ref, k in zip(out_refs, which):
            out_ref[r] = parts[k]

    tiles(x_ref.shape[0], 128, step)


def cut(x, *which):
    count = len(which)
    return call(
        functools.partial(cut_kernel, which), "cut", [struct(*x.shape, dtype=BF16)] * count,
        16, 0.1, 2, in_specs=[VMEM], out_specs=[VMEM] * count,
    )(x)


def second_gram_kernel(shards, count, me_ref, *refs):
    pieces, refs = refs[:count], refs[count:]
    (ah, al, base_ref, xh, xl, col_ref), refs = refs[:6], refs[6:]
    keep_ref, send_ref, mid_ref, mh, ml, hi, lo, packed, g = refs
    size = g.shape[0]
    q = size // 4
    unpack(pieces, packed, hi, lo, me_ref[0], shards, 1)
    mid_ref[:, :q] = base_ref[:, :q]
    mh[:, :q], ml[:, :q] = split(base_ref[:, :q])
    for column in range(1, 4):
        c, product = sym_product(ah, al, hi, lo, 1, column)
        mid = base_ref[:, c] - 0.5 * product
        mid_ref[:, c] = mid
        mh[:, c], ml[:, c] = split(mid)
    g[:, :q] = col_ref[...]
    g[:q, q:] = mm((xh[:q, :], xl[:q, :]), (mh[:, q:], ml[:, q:]))
    g[3 * q:, 3 * q:] = mm((xh[3 * q:, :], xl[3 * q:, :]), (mh[:, 3 * q:], ml[:, 3 * q:]))
    pack(g, packed, keep_ref, send_ref, me_ref[0], shards, 0)


def second_gram(me, shards, pieces, ah, al, base, xh, xl, col):
    rows, size = ah.shape
    part = struct(rows, size, dtype=BF16)
    return call(
        functools.partial(second_gram_kernel, shards, len(pieces)), "second_gram",
        halves(size, shards) + [struct(rows, size), part, part], 20, 0.8, 5,
        in_specs=[SMEM] + [VMEM] * (len(pieces) + 6),
        out_specs=[VMEM] * 5,
        scratch_shapes=sym_scratch(size, shards) + [pltpu.VMEM((size, size), F32)],
    )(me, *pieces, ah, al, base, xh, xl, col)


def fourth_gram_kernel(shards, me_ref, xh, xl, mh, ml, keep_ref, send_ref, g, packed):
    q = g.shape[0] // 4
    lower_product(g, xh, xl, mh[:, q:], ml[:, q:])
    pack(g, packed, keep_ref, send_ref, me_ref[0], shards, 1)


def fourth_gram(me, shards, xh, xl, mh, ml):
    size = xh.shape[0]
    return call(
        functools.partial(fourth_gram_kernel, shards), "fourth_gram", halves(size, shards), 18, 0.5, 2,
        in_specs=[SMEM] + [VMEM] * 4,
        out_specs=[VMEM, VMEM],
        scratch_shapes=[pltpu.VMEM((size, size), F32), packed_scratch(size, shards)],
    )(me, xh, xl, mh, ml)


def last_kernel(shards, count, me_ref, *refs):
    pieces = refs[:count]
    ah, al, z_ref, rest_ref, out_hbm, hi, lo, packed, out, sems = refs[count:]
    q = hi.shape[0] // 4
    copies = []

    def send(src, column):
        c = slice(column * q, (column + 1) * q)
        copy = pltpu.make_async_copy(src, out_hbm.at[:, c], sems.at[column])
        copy.start()
        copies.append(copy)

    send(z_ref, 0)
    unpack(pieces, packed, hi, lo, me_ref[0], shards, 1)
    for column in (1, 2, 3):
        c, product = sym_product(ah, al, hi, lo, 1, column)
        out[:, c] = rest_ref[:, c.start - q:c.stop - q] - 0.5 * product
        send(out.at[:, c], column)
    for copy in copies:
        copy.wait()


def last_step(me, shards, pieces, ah, al, z, rest):
    rows, size = ah.shape
    return call(
        functools.partial(last_kernel, shards, len(pieces)), "last", struct(rows, size), 22, 0.5, 3,
        in_specs=[SMEM] + [VMEM] * (len(pieces) + 4),
        out_specs=pl.BlockSpec(memory_space=pltpu.HBM),
        scratch_shapes=sym_scratch(size, shards)
        + [pltpu.VMEM((rows, size), F32), pltpu.SemaphoreType.DMA((4,))],
    )(me, *pieces, ah, al, z, rest)


CORE = 1
PLANE = (2, 4, 6)
SHARDS = 2 * (1 + len(PLANE))


def slot_of(index):
    return (index % 2) * (SHARDS // 2) + (index // 2) % (SHARDS // 2)


class Sum:
    def __init__(self, count, keep, send):
        self.count, self.keep, self.send = count, keep, send

    def swap(self, x, offset):
        return lax.ppermute(x, "row", [(i, i ^ offset) for i in range(self.count)])

    def core(self):
        return self.swap(self.send, CORE)

    def plane(self, got):
        total = self.keep + got
        part = total.shape[0] // (1 + len(PLANE))
        self.keep, *sends = [total[k * part:(k + 1) * part] for k in range(1 + len(PLANE))]
        return [self.swap(x, offset) for x, offset in zip(sends, PLANE)]

    def own(self, got):
        self.keep = sum(got, self.keep)

    def exchange(self, offset):
        return self.swap(self.keep, offset)

    def gather_plane(self):
        return [self.swap(self.keep, offset) for offset in PLANE]

    def gather_core(self, got):
        self.mine = jnp.concatenate([self.keep, *got], axis=0)
        return self.swap(self.mine, CORE)


def close(env, *got):
    values = lax.optimization_barrier((*got, *env.values()))
    env.update(zip(env, values[len(got):]))
    return values[:len(got)]


def sum_chunks(count, env, first, second, works, late):
    beyond = [1 << s for s in range(3, count.bit_length() - 1)]
    works = list(works)

    def work():
        if works:
            works.pop(0)(env)

    a = Sum(count, *first)
    got_a = a.core()
    pair = second(env)
    got_a, *pair = close(env, got_a, *pair)
    b = Sum(count, *pair)

    got_a = a.plane(got_a)
    got_b = b.core()
    work()
    (got_b,) = close(env, got_b)

    got_b = b.plane(got_b)
    work()
    a.own(close(env, *got_a))

    for offset in beyond:
        got_a = a.exchange(offset)
        work()
        b.own(close(env, *got_b))
        got_b = [b.exchange(offset)]
        a.own(close(env, got_a))

    got_a = a.gather_plane()
    b.own(close(env, *got_b))

    got_b = b.gather_plane()
    got_a = a.gather_core(close(env, *got_a))
    work()
    (got_a,) = close(env, got_a)
    late[0](env, [a.mine, got_a])
    got_b = b.gather_core(close(env, *got_b))
    late[1](env)
    (got_b,) = close(env, got_b)
    return [b.mine, got_b]


def body(count, orbitals_zero, orbitals_one, correlation_zero, correlation_one, cotangent):
    me = slot_of(lax.axis_index("row")).astype(jnp.int32).reshape(1)
    env = dict(
        x0=orbitals_zero, x1=orbitals_one, s0=correlation_zero, s1=correlation_one, c=cotangent
    )

    def half(part):
        def work(env):
            env[f"m{part}"] = affine(env["c"], env["s1"], part)
        return work

    def turned(env):
        env["xh"], env["xl"] = turn(env["x0"])

    def cut_two(env):
        env["x1h"], env["x1l"] = cut(env["x1"], 0, 1)
        env["s0h"], env["s0l"] = cut(env["s0"], 0, 1)

    def middle(env, pieces):
        (env["mid"],) = first_part(
            me, SHARDS, pieces, env["x1h"], env["x1l"], [env["m0"], env["m1"]], (0, 1, 2, 3)
        )

    def column(env):
        env["col"] = column_product(env["xh"], env["xl"], env["mid"])

    keep, send, *parts = first_gram(me, SHARDS, env["x1"], env["c"])
    one = sum_chunks(
        count, env, (keep, send), lambda env: other_gram(me, SHARDS, *parts),
        [half(0), turned, half(1), cut_two], [middle, column],
    )

    keep, send, env["mid"], env["mh"], env["ml"] = second_gram(
        me, SHARDS, one, env["x1h"], env["x1l"], env["mid"], env["xh"], env["xl"], env["col"]
    )

    def half_parts(part):
        def work(env):
            env[f"d{part}"] = affine_parts(
                env["mid"], env["mh"], env["ml"], env["s0h"], env["s0l"], part
            )
        return work

    def high(env):
        (env["x0h"],) = cut(env["x0"], 0)

    def low(env):
        (env["x0l"],) = cut(env["x0"], 1)

    def result(env, pieces):
        env["z"], env["symh"], env["syml"] = first_part(
            me, SHARDS, pieces, env["x0h"], env["x0l"], [env["d0"], env["d1"]], (0,)
        )

    def rest(env):
        env["rest"] = other_part(
            env["x0h"], env["x0l"], env["symh"], env["syml"], [env["d0"], env["d1"]], (1, 2, 3)
        )

    two = sum_chunks(
        count, env, (keep, send),
        lambda env: fourth_gram(me, SHARDS, env["xh"], env["xl"], env["mh"], env["ml"]),
        [half_parts(0), high, half_parts(1), low], [result, rest],
    )
    return last_step(me, SHARDS, two, env["x0h"], env["x0l"], env["z"], env["rest"])


def solution(mesh):
    in_specs = (
        P(("kpt", "row"), None),
        P(("kpt", "row"), None),
        P("kpt", None),
        P("kpt", None),
        P(("kpt", "row"), None),
    )
    out_specs = P(("kpt", "row"), None)
    return jax.shard_map(
        functools.partial(body, mesh.shape["row"]),
        mesh=mesh, in_specs=in_specs, out_specs=out_specs, check_vma=False,
    )
```

```python
import functools
import jax
import jax.numpy as jnp
from jax import lax
from jax.experimental import pallas as pl
from jax.experimental.pallas import tpu as pltpu
from jax.sharding import PartitionSpec as P

F32 = jnp.float32
BF16 = jnp.bfloat16
B = 128
MIB = 1024 * 1024
WEIGHT = 10


def split(x):
    hi = x.astype(BF16)
    return hi, (x - hi.astype(F32)).astype(BF16)


def mm(a, b):
    (ah, al), (bh, bl) = a, b
    return jnp.dot(
        jnp.concatenate([ah, ah, al], axis=1),
        jnp.concatenate([bh, bl, bh], axis=0),
        preferred_element_type=F32,
    )


def call(kernel, name, out_shape, limit, products, arrays, **kw):
    size = 1024
    return pl.pallas_call(
        kernel,
        name=name,
        out_shape=out_shape,
        compiler_params=pltpu.CompilerParams(vmem_limit_bytes=limit * MIB),
        cost_estimate=pl.CostEstimate(
            flops=int(WEIGHT * 6 * products * size ** 3),
            bytes_accessed=int(WEIGHT * 4 * arrays * size * size),
            transcendentals=0,
        ),
        **kw,
    )


def struct(*shape, dtype=F32):
    return jax.ShapeDtypeStruct(shape, dtype)


SMEM = pl.BlockSpec(memory_space=pltpu.SMEM)
VMEM = pl.BlockSpec(memory_space=pltpu.VMEM)


def chunk_lines(size, chunk):
    half = size // B // 4
    return range(chunk * half, (chunk + 1) * half)


def line_blocks(size, i):
    n = size // B
    block = lambda k: slice(k * B, (k + 1) * B)
    return [(block(top), block(j)) for top in (i, n - 1 - i) for j in range(top + 1, n)]


def diagonal_blocks(size, i):
    n = size // B
    return [slice(k * B, (k + 1) * B) for k in (i, n - 1 - i)]


def part_rows(size, shards):
    return size // 4 // shards


def shard_rows(size, shards):
    return part_rows(size, shards) * (size // B) + 8


def places():
    row = lax.broadcasted_iota(jnp.int32, (B, B), 0)
    column = lax.broadcasted_iota(jnp.int32, (B, B), 1)
    return row, column


def pack(g, packed, keep_ref, send_ref, me, shards, chunk):
    size = g.shape[0]
    rows, height = part_rows(size, shards), shard_rows(size, shards)
    per = B // rows
    row, column = places()
    whole = lambda p, q: g[p, q] + g[q, p].T
    for line, i in enumerate(chunk_lines(size, chunk)):
        starts = [((line * per + s) ^ me) * height for s in range(per)]

        def put(at, s, value):
            start = pl.multiple_of(starts[s] + at, 8)
            packed[pl.ds(start, value.shape[0]), :] = value

        upper, lower = [whole(p, p) for p in diagonal_blocks(size, i)]
        for k, place in enumerate([None] + line_blocks(size, i)):
            block = whole(*place) if place else jnp.where(column >= row, upper, lower)
            for s in range(per):
                put(k * rows, s, block[s * rows:(s + 1) * rows])
        element = jnp.sum(jnp.where(column == row, lower, 0.0), axis=0, keepdims=True)
        for s in range(per):
            put(height - 8, s, jnp.broadcast_to(element, (8, B)))
    half = keep_ref.shape[0]
    keep_ref[...] = packed[:half]
    send_ref[...] = packed[half:]


def unpack(pieces, packed, hi, lo, me, shards, chunk):
    size = hi.shape[0]
    rows, height = part_rows(size, shards), shard_rows(size, shards)
    per = B // rows
    row, column = places()
    slot = 0
    for piece in pieces:
        for s in range(piece.shape[0] // height):
            at = pl.multiple_of((slot ^ me) * height, 8)
            packed[pl.ds(at, height), :] = piece[s * height:(s + 1) * height, :]
            slot += 1

    def put(p, q, block):
        hi[p, q], lo[p, q] = split(block)

    for line, i in enumerate(chunk_lines(size, chunk)):
        start = line * per * height

        def get(k):
            return jnp.concatenate(
                [
                    packed[start + s * height + k * rows:start + s * height + (k + 1) * rows, :]
                    for s in range(per)
                ],
                axis=0,
            )

        first, last = diagonal_blocks(size, i)
        block = get(0)
        turned = block.T
        element = packed[start + height - 8:start + height - 7, :]
        put(first, first, jnp.where(column >= row, block, turned))
        below = jnp.where(column < row, block, turned)
        put(last, last, jnp.where(column == row, jnp.broadcast_to(element, (B, B)), below))
        for k, (p, q) in enumerate(line_blocks(size, i)):
            block = get(k + 1)
            put(p, q, block)
            put(q, p, block.T)


def packed_scratch(size, shards):
    return pltpu.VMEM((shards * shard_rows(size, shards), B), F32)


def halves(size, shards):
    return [struct(shards // 2 * shard_rows(size, shards), B)] * 2


def first_gram_kernel(
    shards, me_ref, a_hbm, b_hbm, keep_ref, send_ref, ah, al, bh, bl, a_buf, b_buf, sems, g, packed
):
    rows, size = a_buf.shape
    q = size // 4
    steps = sems.shape[1]
    tile = rows // steps

    def copies(step):
        r = slice(step * tile, (step + 1) * tile)
        return [
            pltpu.make_async_copy(src.at[r], dst.at[r], sems.at[k, step])
            for k, (src, dst) in enumerate([(a_hbm, a_buf), (b_hbm, b_buf)])
        ]

    def start(step):
        for copy in copies(step):
            copy.start()

    start(0)
    start(1)
    for step in range(steps):
        r = slice(step * tile, (step + 1) * tile)
        for copy in copies(step):
            copy.wait()
        if step + 2 < steps:
            start(step + 2)
        ah[:, r], al[:, r] = split(a_buf[r].T)
        bh[r], bl[r] = split(b_buf[r])
        for r0, r1, c0, c1 in [(0, q, 0, size), (q, size, 0, q), (3 * q, size, 3 * q, size)]:
            product = mm((ah[r0:r1, r], al[r0:r1, r]), (bh[r, c0:c1], bl[r, c0:c1]))
            if step:
                product += g[r0:r1, c0:c1]
            g[r0:r1, c0:c1] = product
    pack(g, packed, keep_ref, send_ref, me_ref[0], shards, 0)


def first_gram(me, shards, a, b):
    rows, size = a.shape
    hbm = pl.BlockSpec(memory_space=pltpu.HBM)
    return call(
        functools.partial(first_gram_kernel, shards), "first_gram",
        halves(size, shards) + [struct(size, rows, dtype=BF16)] * 2 + [struct(rows, size, dtype=BF16)] * 2,
        43, 0.5, 4,
        in_specs=[SMEM, hbm, hbm],
        out_specs=[VMEM] * 6,
        scratch_shapes=[
            pltpu.VMEM((rows, size), F32), pltpu.VMEM((rows, size), F32),
            pltpu.SemaphoreType.DMA((2, 4)),
            pltpu.VMEM((size, size), F32), packed_scratch(size, shards),
        ],
    )(me, a, b)


def lower_product(g, ah, al, bh, bl):
    size = g.shape[0]
    q = size // 4
    for r0, r1, c0, c1 in [(q, 3 * q, q, size), (3 * q, size, q, 3 * q)]:
        c = slice(c0 - q, c1 - q)
        g[r0:r1, c0:c1] = mm((ah[r0:r1, :], al[r0:r1, :]), (bh[:, c], bl[:, c]))


def other_gram_kernel(shards, me_ref, ah, al, bh, bl, keep_ref, send_ref, g, packed):
    q = g.shape[0] // 4
    lower_product(g, ah, al, bh[:, q:], bl[:, q:])
    pack(g, packed, keep_ref, send_ref, me_ref[0], shards, 1)


def other_gram(me, shards, ah, al, bh, bl):
    size = ah.shape[0]
    return call(
        functools.partial(other_gram_kernel, shards), "other_gram", halves(size, shards), 18, 0.5, 2,
        in_specs=[SMEM] + [VMEM] * 4,
        out_specs=[VMEM, VMEM],
        scratch_shapes=[pltpu.VMEM((size, size), F32), packed_scratch(size, shards)],
    )(me, ah, al, bh, bl)


def tiles(count, tile, step):
    def body(t, _):
        step(pl.ds(pl.multiple_of(t * tile, tile), tile))
        return 0

    lax.fori_loop(0, count // tile, body, 0)


def affine_kernel(a_ref, b_ref, out_ref, hi, lo):
    hi[...], lo[...] = split(a_ref[...])

    def step(c):
        out_ref[:, c] = 1.5 * a_ref[:, c] - 0.5 * mm((hi[...], lo[...]), split(b_ref[:, c]))

    tiles(out_ref.shape[1], 256, step)


def affine(a, b, half):
    rows, size = a.shape
    block = lambda at: pl.BlockSpec((rows // 2, size), lambda r: (at, 0))
    return call(
        affine_kernel, "affine", struct(rows // 2, size), 18, 0.5, 2,
        grid=(1,),
        in_specs=[block(half), pl.BlockSpec((size, size), lambda r: (0, 0))],
        out_specs=block(0),
        scratch_shapes=[pltpu.VMEM((rows // 2, size), BF16)] * 2,
    )(a, b)


def affine_parts_kernel(a_ref, ah, al, bh, bl, out_ref):
    def step(c):
        product = mm((ah[...], al[...]), (bh[:, c], bl[:, c]))
        out_ref[:, c] = 1.5 * a_ref[:, c] - 0.5 * product

    tiles(out_ref.shape[1], 256, step)


def affine_parts(a, ah, al, bh, bl, half):
    rows, size = a.shape
    block = lambda at: pl.BlockSpec((rows // 2, size), lambda r: (at, 0))
    whole = pl.BlockSpec((size, size), lambda r: (0, 0))
    return call(
        affine_parts_kernel, "affine_parts", struct(rows // 2, size), 18, 0.5, 2,
        grid=(1,),
        in_specs=[block(half)] * 3 + [whole] * 2,
        out_specs=block(0),
    )(a, ah, al, bh, bl)


SPANS = (
    (((0, 4),), ((0, 1),), ((0, 1),), ((0, 1), (3, 4))),
    ((), ((1, 4),), ((1, 4),), ((1, 3),)),
)


def sym_product(ah, al, hi, lo, chunk, column):
    q = hi.shape[0] // 4
    spans = [slice(k0 * q, k1 * q) for k0, k1 in SPANS[chunk][column]]
    c = slice(column * q, (column + 1) * q)
    a = [ref[:, k] for ref in (ah, ah, al) for k in spans]
    b = [ref[k, c] for ref in (hi, lo, hi) for k in spans]
    return c, jnp.dot(
        jnp.concatenate(a, axis=1), jnp.concatenate(b, axis=0), preferred_element_type=F32
    )


def apply_first(base_refs, out_ref, ah, al, hi, lo, columns):
    q = hi.shape[0] // 4
    for column in columns:
        c, product = sym_product(ah, al, hi, lo, 0, column)
        out = slice(c.start - columns[0] * q, c.stop - columns[0] * q)
        at = 0
        for base_ref in base_refs:
            end = at + base_ref.shape[0]
            out_ref[at:end, out] = base_ref[:, c] - 0.5 * product[at:end]
            at = end


def sym_scratch(size, shards):
    return [pltpu.VMEM((size, size), BF16)] * 2 + [packed_scratch(size, shards)]


def first_part_kernel(shards, count, columns, me_ref, *refs):
    pieces, refs = refs[:count], refs[count:]
    ah, al, base_refs, (out_ref, hi, lo, packed) = refs[0], refs[1], refs[2:-4], refs[-4:]
    unpack(pieces, packed, hi, lo, me_ref[0], shards, 0)
    apply_first(base_refs, out_ref, ah, al, hi, lo, columns)


def first_part(me, shards, pieces, ah, al, base, columns):
    rows, size = ah.shape
    part = struct(size, size, dtype=BF16)
    more = len(columns) < 4
    scratch = sym_scratch(size, shards)
    return call(
        functools.partial(first_part_kernel, shards, len(pieces), columns), "first_part",
        [struct(rows, len(columns) * size // 4)] + [part, part] * more, 18, 0.5, 3,
        in_specs=[SMEM] + [VMEM] * (len(pieces) + 2 + len(base)),
        out_specs=[VMEM] * (1 + 2 * more),
        scratch_shapes=scratch[2 * more:],
    )(me, *pieces, ah, al, *base)


def other_part_kernel(columns, ah, al, hi, lo, *refs):
    apply_first(refs[:-1], refs[-1], ah, al, hi, lo, columns)


def other_part(ah, al, hi, lo, base, columns):
    rows, size = ah.shape
    return call(
        functools.partial(other_part_kernel, columns), "other_part",
        struct(rows, len(columns) * size // 4), 16, 0.25, 3,
        in_specs=[VMEM] * (4 + len(base)),
        out_specs=VMEM,
    )(ah, al, hi, lo, *base)


def column_kernel(xh, xl, mid_ref, col_ref):
    col_ref[...] = mm((xh[...], xl[...]), split(mid_ref[...]))


def column_product(xh, xl, mid):
    size, rows = xh.shape
    block = pl.BlockSpec((rows, size // 4), lambda r: (0, 0))
    whole = pl.BlockSpec((size, rows), lambda r: (0, 0))
    return call(
        column_kernel, "column_product", struct(size, size // 4), 16, 0.25, 2,
        grid=(1,), in_specs=[whole, whole, block], out_specs=block,
    )(xh, xl, mid)


def turn_kernel(x_ref, xh, xl):
    def step(r):
        xh[:, r], xl[:, r] = split(x_ref[r].T)

    tiles(x_ref.shape[0], 256, step)


def turn(x):
    part = struct(*x.shape[::-1], dtype=BF16)
    return call(
        turn_kernel, "turn", [part, part], 16, 0.1, 2, in_specs=[VMEM], out_specs=[VMEM] * 2
    )(x)


def cut_kernel(which, x_ref, *out_refs):
    def step(r):
        parts = split(x_ref[r])
        for out_ref, k in zip(out_refs, which):
            out_ref[r] = parts[k]

    tiles(x_ref.shape[0], 128, step)


def cut(x, *which):
    count = len(which)
    return call(
        functools.partial(cut_kernel, which), "cut", [struct(*x.shape, dtype=BF16)] * count,
        16, 0.1, 2, in_specs=[VMEM], out_specs=[VMEM] * count,
    )(x)


def second_gram_kernel(shards, count, me_ref, *refs):
    pieces, refs = refs[:count], refs[count:]
    (ah, al, base_ref, xh, xl, col_ref), refs = refs[:6], refs[6:]
    keep_ref, send_ref, mid_ref, mh, ml, hi, lo, packed, g = refs
    size = g.shape[0]
    q = size // 4
    unpack(pieces, packed, hi, lo, me_ref[0], shards, 1)
    mid_ref[:, :q] = base_ref[:, :q]
    mh[:, :q], ml[:, :q] = split(base_ref[:, :q])
    for column in range(1, 4):
        c, product = sym_product(ah, al, hi, lo, 1, column)
        mid = base_ref[:, c] - 0.5 * product
        mid_ref[:, c] = mid
        mh[:, c], ml[:, c] = split(mid)
    g[:, :q] = col_ref[...]
    g[:q, q:] = mm((xh[:q, :], xl[:q, :]), (mh[:, q:], ml[:, q:]))
    g[3 * q:, 3 * q:] = mm((xh[3 * q:, :], xl[3 * q:, :]), (mh[:, 3 * q:], ml[:, 3 * q:]))
    pack(g, packed, keep_ref, send_ref, me_ref[0], shards, 0)


def second_gram(me, shards, pieces, ah, al, base, xh, xl, col):
    rows, size = ah.shape
    part = struct(rows, size, dtype=BF16)
    return call(
        functools.partial(second_gram_kernel, shards, len(pieces)), "second_gram",
        halves(size, shards) + [struct(rows, size), part, part], 20, 0.8, 5,
        in_specs=[SMEM] + [VMEM] * (len(pieces) + 6),
        out_specs=[VMEM] * 5,
        scratch_shapes=sym_scratch(size, shards) + [pltpu.VMEM((size, size), F32)],
    )(me, *pieces, ah, al, base, xh, xl, col)


def fourth_gram_kernel(shards, me_ref, xh, xl, mh, ml, keep_ref, send_ref, g, packed):
    q = g.shape[0] // 4
    lower_product(g, xh, xl, mh[:, q:], ml[:, q:])
    pack(g, packed, keep_ref, send_ref, me_ref[0], shards, 1)


def fourth_gram(me, shards, xh, xl, mh, ml):
    size = xh.shape[0]
    return call(
        functools.partial(fourth_gram_kernel, shards), "fourth_gram", halves(size, shards), 18, 0.5, 2,
        in_specs=[SMEM] + [VMEM] * 4,
        out_specs=[VMEM, VMEM],
        scratch_shapes=[pltpu.VMEM((size, size), F32), packed_scratch(size, shards)],
    )(me, xh, xl, mh, ml)


def last_kernel(shards, count, me_ref, *refs):
    pieces = refs[:count]
    ah, al, z_ref, rest_ref, out_hbm, hi, lo, packed, out, sems = refs[count:]
    q = hi.shape[0] // 4
    copies = []

    def send(src, column):
        c = slice(column * q, (column + 1) * q)
        copy = pltpu.make_async_copy(src, out_hbm.at[:, c], sems.at[column])
        copy.start()
        copies.append(copy)

    send(z_ref, 0)
    unpack(pieces, packed, hi, lo, me_ref[0], shards, 1)
    for column in (1, 2, 3):
        c, product = sym_product(ah, al, hi, lo, 1, column)
        out[:, c] = rest_ref[:, c.start - q:c.stop - q] - 0.5 * product
        send(out.at[:, c], column)
    for copy in copies:
        copy.wait()


def last_step(me, shards, pieces, ah, al, z, rest):
    rows, size = ah.shape
    return call(
        functools.partial(last_kernel, shards, len(pieces)), "last", struct(rows, size), 22, 0.5, 3,
        in_specs=[SMEM] + [VMEM] * (len(pieces) + 4),
        out_specs=pl.BlockSpec(memory_space=pltpu.HBM),
        scratch_shapes=sym_scratch(size, shards)
        + [pltpu.VMEM((rows, size), F32), pltpu.SemaphoreType.DMA((4,))],
    )(me, *pieces, ah, al, z, rest)


CORE = 1
PLANE = (2, 4, 6)
SHARDS = 2 * (1 + len(PLANE))


def slot_of(index):
    return (index % 2) * (SHARDS // 2) + (index // 2) % (SHARDS // 2)


class Sum:
    def __init__(self, count, keep, send):
        self.count, self.keep, self.send = count, keep, send

    def swap(self, x, offset):
        return lax.ppermute(x, "row", [(i, i ^ offset) for i in range(self.count)])

    def swaps(self, values):
        return [self.swap(x, offset) for x, offset in zip(values, PLANE)]

    def core(self):
        return self.swap(self.send, CORE)

    def plane(self, got):
        total = self.keep + got
        part = total.shape[0] // (1 + len(PLANE))
        self.keep, *sends = [total[k * part:(k + 1) * part] for k in range(1 + len(PLANE))]
        return self.swaps(sends)

    def own(self, got):
        self.keep = sum(got, self.keep)

    def exchange(self, offset):
        return self.swap(self.keep, offset)

    def gather_plane(self):
        return self.swaps([self.keep] * len(PLANE))

    def gather_core(self, got):
        self.mine = jnp.concatenate([self.keep, *got], axis=0)
        return self.swap(self.mine, CORE)


def close(env, *got):
    values = lax.optimization_barrier((*env.values(), *got[::-1]))
    env.update(zip(env, values))
    return values[len(env):][::-1]


def sum_chunks(count, env, first, second, works, late):
    beyond = [1 << s for s in range(3, count.bit_length() - 1)]
    works = list(works)

    def work():
        if works:
            works.pop(0)(env)

    a = Sum(count, *first)
    got_a = a.core()
    pair = second(env)
    got_a, *pair = close(env, got_a, *pair)
    b = Sum(count, *pair)

    got_a = a.plane(got_a)
    got_b = b.core()
    work()
    (got_b,) = close(env, got_b)

    got_b = b.plane(got_b)
    work()
    a.own(close(env, *got_a))

    for offset in beyond:
        got_a = a.exchange(offset)
        work()
        b.own(close(env, *got_b))
        got_b = [b.exchange(offset)]
        a.own(close(env, got_a))

    got_a = a.gather_plane()
    b.own(close(env, *got_b))

    got_b = b.gather_plane()
    got_a = a.gather_core(close(env, *got_a))
    work()
    (got_a,) = close(env, got_a)
    late[0](env, [a.mine, got_a])
    got_b = b.gather_core(close(env, *got_b))
    late[1](env)
    (got_b,) = close(env, got_b)
    return [b.mine, got_b]


def body(count, orbitals_zero, orbitals_one, correlation_zero, correlation_one, cotangent):
    me = slot_of(lax.axis_index("row")).astype(jnp.int32).reshape(1)
    env = dict(
        x0=orbitals_zero, x1=orbitals_one, s0=correlation_zero, s1=correlation_one, c=cotangent
    )

    def half(part):
        def work(env):
            env[f"m{part}"] = affine(env["c"], env["s1"], part)
        return work

    def turned(env):
        env["xh"], env["xl"] = turn(env["x0"])

    def half_and_cut(env):
        half(1)(env)
        env["s0h"], env["s0l"] = cut(env["s0"], 0, 1)

    def cut_orbitals(env):
        env["x1h"], env["x1l"] = cut(env["x1"], 0, 1)

    def middle(env, pieces):
        (env["mid"],) = first_part(
            me, SHARDS, pieces, env["x1h"], env["x1l"], [env["m0"], env["m1"]], (0, 1, 2, 3)
        )

    def column(env):
        env["col"] = column_product(env["xh"], env["xl"], env["mid"])

    keep, send, *parts = first_gram(me, SHARDS, env["x1"], env["c"])
    one = sum_chunks(
        count, env, (keep, send), lambda env: other_gram(me, SHARDS, *parts),
        [half(0), turned, half_and_cut, cut_orbitals], [middle, column],
    )

    keep, send, env["mid"], env["mh"], env["ml"] = second_gram(
        me, SHARDS, one, env["x1h"], env["x1l"], env["mid"], env["xh"], env["xl"], env["col"]
    )

    def half_parts(part):
        def work(env):
            env[f"d{part}"] = affine_parts(
                env["mid"], env["mh"], env["ml"], env["s0h"], env["s0l"], part
            )
        return work

    def high(env):
        (env["x0h"],) = cut(env["x0"], 0)

    def low(env):
        (env["x0l"],) = cut(env["x0"], 1)

    def result(env, pieces):
        env["z"], env["symh"], env["syml"] = first_part(
            me, SHARDS, pieces, env["x0h"], env["x0l"], [env["d0"], env["d1"]], (0,)
        )

    def rest(env):
        env["rest"] = other_part(
            env["x0h"], env["x0l"], env["symh"], env["syml"], [env["d0"], env["d1"]], (1, 2, 3)
        )

    two = sum_chunks(
        count, env, (keep, send),
        lambda env: fourth_gram(me, SHARDS, env["xh"], env["xl"], env["mh"], env["ml"]),
        [half_parts(0), high, half_parts(1), low], [result, rest],
    )
    return last_step(me, SHARDS, two, env["x0h"], env["x0l"], env["z"], env["rest"])


def solution(mesh):
    in_specs = (
        P(("kpt", "row"), None),
        P(("kpt", "row"), None),
        P("kpt", None),
        P("kpt", None),
        P(("kpt", "row"), None),
    )
    out_specs = P(("kpt", "row"), None)
    return jax.shard_map(
        functools.partial(body, mesh.shape["row"]),
        mesh=mesh, in_specs=in_specs, out_specs=out_specs, check_vma=False,
    )
```

```python
import functools
import jax
import jax.numpy as jnp
from jax import lax
from jax.experimental import pallas as pl
from jax.experimental.pallas import tpu as pltpu
from jax.sharding import PartitionSpec as P

F32 = jnp.float32
BF16 = jnp.bfloat16
B = 128
MIB = 1024 * 1024
WEIGHT = 10


def split(x):
    hi = x.astype(BF16)
    return hi, (x - hi.astype(F32)).astype(BF16)


def mm(a, b):
    (ah, al), (bh, bl) = a, b
    return jnp.dot(
        jnp.concatenate([ah, ah, al], axis=1),
        jnp.concatenate([bh, bl, bh], axis=0),
        preferred_element_type=F32,
    )


def call(kernel, name, out_shape, limit, products, arrays, **kw):
    size = 1024
    return pl.pallas_call(
        kernel,
        name=name,
        out_shape=out_shape,
        compiler_params=pltpu.CompilerParams(vmem_limit_bytes=limit * MIB),
        cost_estimate=pl.CostEstimate(
            flops=int(WEIGHT * 6 * products * size ** 3),
            bytes_accessed=int(WEIGHT * 4 * arrays * size * size),
            transcendentals=0,
        ),
        **kw,
    )


def struct(*shape, dtype=F32):
    return jax.ShapeDtypeStruct(shape, dtype)


SMEM = pl.BlockSpec(memory_space=pltpu.SMEM)
VMEM = pl.BlockSpec(memory_space=pltpu.VMEM)


def chunk_lines(size, chunk):
    half = size // B // 4
    return range(chunk * half, (chunk + 1) * half)


def line_blocks(size, i):
    n = size // B
    block = lambda k: slice(k * B, (k + 1) * B)
    return [(block(top), block(j)) for top in (i, n - 1 - i) for j in range(top + 1, n)]


def diagonal_blocks(size, i):
    n = size // B
    return [slice(k * B, (k + 1) * B) for k in (i, n - 1 - i)]


def part_rows(size, shards):
    return size // 4 // shards


def shard_rows(size, shards):
    return part_rows(size, shards) * (size // B) + 8


def places():
    row = lax.broadcasted_iota(jnp.int32, (B, B), 0)
    column = lax.broadcasted_iota(jnp.int32, (B, B), 1)
    return row, column


def pack(g, packed, keep_ref, send_ref, me, shards, chunk):
    size = g.shape[0]
    rows, height = part_rows(size, shards), shard_rows(size, shards)
    per = B // rows
    row, column = places()
    whole = lambda p, q: g[p, q] + g[q, p].T
    for line, i in enumerate(chunk_lines(size, chunk)):
        starts = [((line * per + s) ^ me) * height for s in range(per)]

        def put(at, s, value):
            start = pl.multiple_of(starts[s] + at, 8)
            packed[pl.ds(start, value.shape[0]), :] = value

        upper, lower = [whole(p, p) for p in diagonal_blocks(size, i)]
        for k, place in enumerate([None] + line_blocks(size, i)):
            block = whole(*place) if place else jnp.where(column >= row, upper, lower)
            for s in range(per):
                put(k * rows, s, block[s * rows:(s + 1) * rows])
        element = jnp.sum(jnp.where(column == row, lower, 0.0), axis=0, keepdims=True)
        for s in range(per):
            put(height - 8, s, jnp.broadcast_to(element, (8, B)))
    half = keep_ref.shape[0]
    keep_ref[...] = packed[:half]
    send_ref[...] = packed[half:]


def unpack(pieces, packed, hi, lo, me, shards, chunk):
    size = hi.shape[0]
    rows, height = part_rows(size, shards), shard_rows(size, shards)
    per = B // rows
    row, column = places()
    slot = 0
    for piece in pieces:
        for s in range(piece.shape[0] // height):
            at = pl.multiple_of((slot ^ me) * height, 8)
            packed[pl.ds(at, height), :] = piece[s * height:(s + 1) * height, :]
            slot += 1

    def put(p, q, block):
        hi[p, q], lo[p, q] = split(block)

    for line, i in enumerate(chunk_lines(size, chunk)):
        start = line * per * height

        def get(k):
            return jnp.concatenate(
                [
                    packed[start + s * height + k * rows:start + s * height + (k + 1) * rows, :]
                    for s in range(per)
                ],
                axis=0,
            )

        first, last = diagonal_blocks(size, i)
        block = get(0)
        turned = block.T
        element = packed[start + height - 8:start + height - 7, :]
        put(first, first, jnp.where(column >= row, block, turned))
        below = jnp.where(column < row, block, turned)
        put(last, last, jnp.where(column == row, jnp.broadcast_to(element, (B, B)), below))
        for k, (p, q) in enumerate(line_blocks(size, i)):
            block = get(k + 1)
            put(p, q, block)
            put(q, p, block.T)


def packed_scratch(size, shards):
    return pltpu.VMEM((shards * shard_rows(size, shards), B), F32)


def halves(size, shards):
    return [struct(shards // 2 * shard_rows(size, shards), B)] * 2


def first_gram_kernel(
    shards, me_ref, a_hbm, b_hbm, keep_ref, send_ref, ah, al, bh, bl, a_buf, b_buf, sems, g, packed
):
    rows, size = a_buf.shape
    q = size // 4
    steps = sems.shape[1]
    tile = rows // steps

    def copies(step):
        r = slice(step * tile, (step + 1) * tile)
        return [
            pltpu.make_async_copy(src.at[r], dst.at[r], sems.at[k, step])
            for k, (src, dst) in enumerate([(a_hbm, a_buf), (b_hbm, b_buf)])
        ]

    def start(step):
        for copy in copies(step):
            copy.start()

    start(0)
    start(1)
    for step in range(steps):
        r = slice(step * tile, (step + 1) * tile)
        for copy in copies(step):
            copy.wait()
        if step + 2 < steps:
            start(step + 2)
        ah[:, r], al[:, r] = split(a_buf[r].T)
        bh[r], bl[r] = split(b_buf[r])
        for r0, r1, c0, c1 in [(0, q, 0, size), (q, size, 0, q), (3 * q, size, 3 * q, size)]:
            product = mm((ah[r0:r1, r], al[r0:r1, r]), (bh[r, c0:c1], bl[r, c0:c1]))
            if step:
                product += g[r0:r1, c0:c1]
            g[r0:r1, c0:c1] = product
    pack(g, packed, keep_ref, send_ref, me_ref[0], shards, 0)


def first_gram(me, shards, a, b):
    rows, size = a.shape
    hbm = pl.BlockSpec(memory_space=pltpu.HBM)
    return call(
        functools.partial(first_gram_kernel, shards), "first_gram",
        halves(size, shards) + [struct(size, rows, dtype=BF16)] * 2 + [struct(rows, size, dtype=BF16)] * 2,
        43, 0.5, 4,
        in_specs=[SMEM, hbm, hbm],
        out_specs=[VMEM] * 6,
        scratch_shapes=[
            pltpu.VMEM((rows, size), F32), pltpu.VMEM((rows, size), F32),
            pltpu.SemaphoreType.DMA((2, 4)),
            pltpu.VMEM((size, size), F32), packed_scratch(size, shards),
        ],
    )(me, a, b)


def lower_product(g, ah, al, bh, bl):
    size = g.shape[0]
    q = size // 4
    for r0, r1, c0, c1 in [(q, 3 * q, q, size), (3 * q, size, q, 3 * q)]:
        c = slice(c0 - q, c1 - q)
        g[r0:r1, c0:c1] = mm((ah[r0:r1, :], al[r0:r1, :]), (bh[:, c], bl[:, c]))


def other_gram_kernel(shards, me_ref, ah, al, bh, bl, keep_ref, send_ref, g, packed):
    q = g.shape[0] // 4
    lower_product(g, ah, al, bh[:, q:], bl[:, q:])
    pack(g, packed, keep_ref, send_ref, me_ref[0], shards, 1)


def other_gram(me, shards, ah, al, bh, bl):
    size = ah.shape[0]
    return call(
        functools.partial(other_gram_kernel, shards), "other_gram", halves(size, shards), 18, 0.5, 2,
        in_specs=[SMEM] + [VMEM] * 4,
        out_specs=[VMEM, VMEM],
        scratch_shapes=[pltpu.VMEM((size, size), F32), packed_scratch(size, shards)],
    )(me, ah, al, bh, bl)


def tiles(count, tile, step):
    def body(t, _):
        step(pl.ds(pl.multiple_of(t * tile, tile), tile))
        return 0

    lax.fori_loop(0, count // tile, body, 0)


def affine_kernel(a_ref, b_ref, out_ref, hi, lo):
    hi[...], lo[...] = split(a_ref[...])

    def step(c):
        out_ref[:, c] = 1.5 * a_ref[:, c] - 0.5 * mm((hi[...], lo[...]), split(b_ref[:, c]))

    tiles(out_ref.shape[1], 256, step)


THIRDS = ((0, 4), (1, 4), (1, 2))


def row_part(part, rows, size):
    at, parts = THIRDS[part]
    return pl.BlockSpec((rows // parts, size), lambda r: (at, 0))


def affine(a, b, part):
    rows, size = a.shape
    height = rows // THIRDS[part][1]
    return call(
        affine_kernel, "affine", struct(height, size), 18, height / rows, 2,
        grid=(1,),
        in_specs=[row_part(part, rows, size), pl.BlockSpec((size, size), lambda r: (0, 0))],
        out_specs=pl.BlockSpec((height, size), lambda r: (0, 0)),
        scratch_shapes=[pltpu.VMEM((height, size), BF16)] * 2,
    )(a, b)


def affine_parts_kernel(ah, al, b_ref, out_ref):
    def step(c):
        product = mm((ah[...], al[...]), split(b_ref[:, c]))
        out_ref[:, c] = 1.5 * (ah[:, c].astype(F32) + al[:, c].astype(F32)) - 0.5 * product

    tiles(out_ref.shape[1], 256, step)


def affine_parts(ah, al, b, part):
    rows, size = ah.shape
    height = rows // THIRDS[part][1]
    return call(
        affine_parts_kernel, "affine_parts", struct(height, size), 18, height / rows, 2,
        grid=(1,),
        in_specs=[row_part(part, rows, size)] * 2
        + [pl.BlockSpec((size, size), lambda r: (0, 0))],
        out_specs=pl.BlockSpec((height, size), lambda r: (0, 0)),
    )(ah, al, b)


SPANS = (
    (((0, 4),), ((0, 1),), ((0, 1),), ((0, 1), (3, 4))),
    ((), ((1, 4),), ((1, 4),), ((1, 3),)),
)


def sym_product(ah, al, hi, lo, chunk, column):
    q = hi.shape[0] // 4
    spans = [slice(k0 * q, k1 * q) for k0, k1 in SPANS[chunk][column]]
    c = slice(column * q, (column + 1) * q)
    a = [ref[:, k] for ref in (ah, ah, al) for k in spans]
    b = [ref[k, c] for ref in (hi, lo, hi) for k in spans]
    return c, jnp.dot(
        jnp.concatenate(a, axis=1), jnp.concatenate(b, axis=0), preferred_element_type=F32
    )


def apply_first(base_refs, out_ref, ah, al, hi, lo, columns):
    q = hi.shape[0] // 4
    for column in columns:
        c, product = sym_product(ah, al, hi, lo, 0, column)
        out = slice(c.start - columns[0] * q, c.stop - columns[0] * q)
        at = 0
        for base_ref in base_refs:
            end = at + base_ref.shape[0]
            out_ref[at:end, out] = base_ref[:, c] - 0.5 * product[at:end]
            at = end


def sym_scratch(size, shards):
    return [pltpu.VMEM((size, size), BF16)] * 2 + [packed_scratch(size, shards)]


def first_part_kernel(shards, count, columns, me_ref, *refs):
    pieces, refs = refs[:count], refs[count:]
    ah, al, base_refs, (out_ref, hi, lo, packed) = refs[0], refs[1], refs[2:-4], refs[-4:]
    unpack(pieces, packed, hi, lo, me_ref[0], shards, 0)
    apply_first(base_refs, out_ref, ah, al, hi, lo, columns)


def first_part(me, shards, pieces, ah, al, base, columns):
    rows, size = ah.shape
    part = struct(size, size, dtype=BF16)
    more = len(columns) < 4
    scratch = sym_scratch(size, shards)
    return call(
        functools.partial(first_part_kernel, shards, len(pieces), columns), "first_part",
        [struct(rows, len(columns) * size // 4)] + [part, part] * more, 18, 0.5, 3,
        in_specs=[SMEM] + [VMEM] * (len(pieces) + 2 + len(base)),
        out_specs=[VMEM] * (1 + 2 * more),
        scratch_shapes=scratch[2 * more:],
    )(me, *pieces, ah, al, *base)


def other_part_kernel(columns, ah, al, hi, lo, *refs):
    apply_first(refs[:-1], refs[-1], ah, al, hi, lo, columns)


def other_part(ah, al, hi, lo, base, columns):
    rows, size = ah.shape
    return call(
        functools.partial(other_part_kernel, columns), "other_part",
        struct(rows, len(columns) * size // 4), 16, 0.25, 3,
        in_specs=[VMEM] * (4 + len(base)),
        out_specs=VMEM,
    )(ah, al, hi, lo, *base)


def column_kernel(xh, xl, mid_ref, col_ref):
    col_ref[...] = mm((xh[...], xl[...]), split(mid_ref[...]))


def column_product(xh, xl, mid):
    size, rows = xh.shape
    block = pl.BlockSpec((rows, size // 4), lambda r: (0, 0))
    whole = pl.BlockSpec((size, rows), lambda r: (0, 0))
    return call(
        column_kernel, "column_product", struct(size, size // 4), 16, 0.25, 2,
        grid=(1,), in_specs=[whole, whole, block], out_specs=block,
    )(xh, xl, mid)


def turn_kernel(x_ref, xh, xl):
    def step(r):
        xh[:, r], xl[:, r] = split(x_ref[r].T)

    tiles(x_ref.shape[0], 256, step)


def turn(x):
    part = struct(*x.shape[::-1], dtype=BF16)
    return call(
        turn_kernel, "turn", [part, part], 16, 0.1, 2, in_specs=[VMEM], out_specs=[VMEM] * 2
    )(x)


def cut_kernel(x_ref, hi, lo):
    def step(r):
        hi[r], lo[r] = split(x_ref[r])

    tiles(x_ref.shape[0], 128, step)


def cut(x):
    part = struct(*x.shape, dtype=BF16)
    return call(
        cut_kernel, "cut", [part, part], 16, 0.1, 2, in_specs=[VMEM], out_specs=[VMEM] * 2
    )(x)


def second_gram_kernel(shards, count, me_ref, *refs):
    pieces, refs = refs[:count], refs[count:]
    (ah, al, base_ref, xh, xl, col_ref), refs = refs[:6], refs[6:]
    keep_ref, send_ref, mh, ml, hi, lo, packed, g = refs
    size = g.shape[0]
    q = size // 4
    unpack(pieces, packed, hi, lo, me_ref[0], shards, 1)
    mh[:, :q], ml[:, :q] = split(base_ref[:, :q])
    for column in range(1, 4):
        c, product = sym_product(ah, al, hi, lo, 1, column)
        mid = base_ref[:, c] - 0.5 * product
        mh[:, c], ml[:, c] = split(mid)
    g[:, :q] = col_ref[...]
    g[:q, q:] = mm((xh[:q, :], xl[:q, :]), (mh[:, q:], ml[:, q:]))
    g[3 * q:, 3 * q:] = mm((xh[3 * q:, :], xl[3 * q:, :]), (mh[:, 3 * q:], ml[:, 3 * q:]))
    pack(g, packed, keep_ref, send_ref, me_ref[0], shards, 0)


def second_gram(me, shards, pieces, ah, al, base, xh, xl, col):
    rows, size = ah.shape
    part = struct(rows, size, dtype=BF16)
    return call(
        functools.partial(second_gram_kernel, shards, len(pieces)), "second_gram",
        halves(size, shards) + [part, part], 20, 0.8, 5,
        in_specs=[SMEM] + [VMEM] * (len(pieces) + 6),
        out_specs=[VMEM] * 4,
        scratch_shapes=sym_scratch(size, shards) + [pltpu.VMEM((size, size), F32)],
    )(me, *pieces, ah, al, base, xh, xl, col)


def fourth_gram_kernel(shards, me_ref, xh, xl, mh, ml, keep_ref, send_ref, g, packed):
    q = g.shape[0] // 4
    lower_product(g, xh, xl, mh[:, q:], ml[:, q:])
    pack(g, packed, keep_ref, send_ref, me_ref[0], shards, 1)


def fourth_gram(me, shards, xh, xl, mh, ml):
    size = xh.shape[0]
    return call(
        functools.partial(fourth_gram_kernel, shards), "fourth_gram", halves(size, shards), 18, 0.5, 2,
        in_specs=[SMEM] + [VMEM] * 4,
        out_specs=[VMEM, VMEM],
        scratch_shapes=[pltpu.VMEM((size, size), F32), packed_scratch(size, shards)],
    )(me, xh, xl, mh, ml)


def last_kernel(shards, count, me_ref, *refs):
    pieces = refs[:count]
    ah, al, z_ref, rest_ref, out_hbm, hi, lo, packed, out, sems = refs[count:]
    q = hi.shape[0] // 4
    copies = []

    def send(src, column):
        c = slice(column * q, (column + 1) * q)
        copy = pltpu.make_async_copy(src, out_hbm.at[:, c], sems.at[column])
        copy.start()
        copies.append(copy)

    send(z_ref, 0)
    unpack(pieces, packed, hi, lo, me_ref[0], shards, 1)
    for column in (1, 2, 3):
        c, product = sym_product(ah, al, hi, lo, 1, column)
        out[:, c] = rest_ref[:, c.start - q:c.stop - q] - 0.5 * product
        send(out.at[:, c], column)
    for copy in copies:
        copy.wait()


def last_step(me, shards, pieces, ah, al, z, rest):
    rows, size = ah.shape
    return call(
        functools.partial(last_kernel, shards, len(pieces)), "last", struct(rows, size), 22, 0.5, 3,
        in_specs=[SMEM] + [VMEM] * (len(pieces) + 4),
        out_specs=pl.BlockSpec(memory_space=pltpu.HBM),
        scratch_shapes=sym_scratch(size, shards)
        + [pltpu.VMEM((rows, size), F32), pltpu.SemaphoreType.DMA((4,))],
    )(me, *pieces, ah, al, z, rest)


CORE = 1
PLANE = (2, 4, 6)
SHARDS = 2 * (1 + len(PLANE))


def slot_of(index):
    return (index % 2) * (SHARDS // 2) + (index // 2) % (SHARDS // 2)


class Sum:
    def __init__(self, count, keep, send):
        self.count, self.keep, self.send = count, keep, send

    def swap(self, x, offset):
        return lax.ppermute(x, "row", [(i, i ^ offset) for i in range(self.count)])

    def swaps(self, values):
        return [self.swap(x, offset) for x, offset in zip(values, PLANE)]

    def core(self):
        return self.swap(self.send, CORE)

    def plane(self, got):
        total = self.keep + got
        part = total.shape[0] // (1 + len(PLANE))
        self.keep, *sends = [total[k * part:(k + 1) * part] for k in range(1 + len(PLANE))]
        return self.swaps(sends)

    def own(self, got):
        self.keep = sum(got, self.keep)

    def exchange(self, offset):
        return self.swap(self.keep, offset)

    def gather_plane(self):
        return self.swaps([self.keep] * len(PLANE))

    def gather_core(self, got):
        self.mine = jnp.concatenate([self.keep, *got], axis=0)
        return self.swap(self.mine, CORE)


def close(env, *got):
    values = lax.optimization_barrier((*env.values(), *got[::-1]))
    env.update(zip(env, values))
    return values[len(env):][::-1]


def sum_chunks(count, env, first, second, works, late):
    beyond = [1 << s for s in range(3, count.bit_length() - 1)]
    works = list(works)

    def work():
        if works:
            works.pop(0)(env)

    a = Sum(count, *first)
    got_a = a.core()
    pair = second(env)
    got_a, *pair = close(env, got_a, *pair)
    b = Sum(count, *pair)

    got_a = a.plane(got_a)
    got_b = b.core()
    work()
    (got_b,) = close(env, got_b)

    got_b = b.plane(got_b)
    work()
    a.own(close(env, *got_a))

    for offset in beyond:
        got_a = a.exchange(offset)
        work()
        b.own(close(env, *got_b))
        got_b = [b.exchange(offset)]
        a.own(close(env, got_a))

    got_a = a.gather_plane()
    b.own(close(env, *got_b))

    got_b = b.gather_plane()
    got_a = a.gather_core(close(env, *got_a))
    work()
    (got_a,) = close(env, got_a)
    late[0](env, [a.mine, got_a])
    got_b = b.gather_core(close(env, *got_b))
    late[1](env)
    (got_b,) = close(env, got_b)
    return [b.mine, got_b]


def body(count, orbitals_zero, orbitals_one, correlation_zero, correlation_one, cotangent):
    me = slot_of(lax.axis_index("row")).astype(jnp.int32).reshape(1)
    env = dict(
        x0=orbitals_zero, x1=orbitals_one, s0=correlation_zero, s1=correlation_one, c=cotangent
    )

    def direct(part):
        def work(env):
            env[f"m{part}"] = affine(env["c"], env["s1"], part)
        return work

    def direct_and_turn(env):
        direct(2)(env)
        env["xh"], env["xl"] = turn(env["x0"])

    def cut_one(env):
        env["x1h"], env["x1l"] = cut(env["x1"])

    def middle(env, pieces):
        (env["mid"],) = first_part(
            me, SHARDS, pieces, env["x1h"], env["x1l"], [env["m0"], env["m1"], env["m2"]], (0, 1, 2, 3)
        )

    def column(env):
        env["col"] = column_product(env["xh"], env["xl"], env["mid"])

    keep, send, *parts = first_gram(me, SHARDS, env["x1"], env["c"])
    one = sum_chunks(
        count, env, (keep, send), lambda env: other_gram(me, SHARDS, *parts),
        [direct(0), direct(1), direct_and_turn, cut_one], [middle, column],
    )

    keep, send, env["mh"], env["ml"] = second_gram(
        me, SHARDS, one, env["x1h"], env["x1l"], env["mid"], env["xh"], env["xl"], env["col"]
    )

    def last_direct(part):
        def work(env):
            env[f"d{part}"] = affine_parts(env["mh"], env["ml"], env["s0"], part)
        return work

    def cut_zero(env):
        env["x0h"], env["x0l"] = cut(env["x0"])

    def three(name):
        return [env[f"{name}{part}"] for part in range(3)]

    def result(env, pieces):
        env["z"], env["symh"], env["syml"] = first_part(
            me, SHARDS, pieces, env["x0h"], env["x0l"], three("d"), (0,)
        )

    def rest(env):
        env["rest"] = other_part(
            env["x0h"], env["x0l"], env["symh"], env["syml"], three("d"), (1, 2, 3)
        )

    two = sum_chunks(
        count, env, (keep, send),
        lambda env: fourth_gram(me, SHARDS, env["xh"], env["xl"], env["mh"], env["ml"]),
        [last_direct(0), last_direct(1), last_direct(2), cut_zero], [result, rest],
    )
    return last_step(me, SHARDS, two, env["x0h"], env["x0l"], env["z"], env["rest"])


def solution(mesh):
    in_specs = (
        P(("kpt", "row"), None),
        P(("kpt", "row"), None),
        P("kpt", None),
        P("kpt", None),
        P(("kpt", "row"), None),
    )
    out_specs = P(("kpt", "row"), None)
    return jax.shard_map(
        functools.partial(body, mesh.shape["row"]),
        mesh=mesh, in_specs=in_specs, out_specs=out_specs, check_vma=False,
    )
```

```python
import functools
import jax
import jax.numpy as jnp
from jax import lax
from jax.experimental import pallas as pl
from jax.experimental.pallas import tpu as pltpu
from jax.sharding import PartitionSpec as P

F32 = jnp.float32
BF16 = jnp.bfloat16
B = 128
MIB = 1024 * 1024
WEIGHT = 10


def split(x):
    hi = x.astype(BF16)
    return hi, (x - hi.astype(F32)).astype(BF16)


def mm(a, b):
    (ah, al), (bh, bl) = a, b
    return jnp.dot(
        jnp.concatenate([ah, ah, al], axis=1),
        jnp.concatenate([bh, bl, bh], axis=0),
        preferred_element_type=F32,
    )


def call(kernel, name, out_shape, limit, products, arrays, **kw):
    size = 1024
    return pl.pallas_call(
        kernel,
        name=name,
        out_shape=out_shape,
        compiler_params=pltpu.CompilerParams(vmem_limit_bytes=limit * MIB),
        cost_estimate=pl.CostEstimate(
            flops=int(WEIGHT * 6 * products * size ** 3),
            bytes_accessed=int(WEIGHT * 4 * arrays * size * size),
            transcendentals=0,
        ),
        **kw,
    )


def struct(*shape, dtype=F32):
    return jax.ShapeDtypeStruct(shape, dtype)


SMEM = pl.BlockSpec(memory_space=pltpu.SMEM)
VMEM = pl.BlockSpec(memory_space=pltpu.VMEM)


def chunk_lines(size, chunk):
    half = size // B // 4
    return range(chunk * half, (chunk + 1) * half)


def line_blocks(size, i):
    n = size // B
    block = lambda k: slice(k * B, (k + 1) * B)
    return [(block(top), block(j)) for top in (i, n - 1 - i) for j in range(top + 1, n)]


def diagonal_blocks(size, i):
    n = size // B
    return [slice(k * B, (k + 1) * B) for k in (i, n - 1 - i)]


def part_rows(size, shards):
    return size // 4 // shards


def shard_rows(size, shards):
    return part_rows(size, shards) * (size // B) + 8


def places():
    row = lax.broadcasted_iota(jnp.int32, (B, B), 0)
    column = lax.broadcasted_iota(jnp.int32, (B, B), 1)
    return row, column


def pack(g, packed, keep_ref, send_ref, me, shards, chunk):
    size = g.shape[0]
    rows, height = part_rows(size, shards), shard_rows(size, shards)
    per = B // rows
    row, column = places()
    whole = lambda p, q: g[p, q] + g[q, p].T
    for line, i in enumerate(chunk_lines(size, chunk)):
        starts = [((line * per + s) ^ me) * height for s in range(per)]

        def put(at, s, value):
            start = pl.multiple_of(starts[s] + at, 8)
            packed[pl.ds(start, value.shape[0]), :] = value

        upper, lower = [whole(p, p) for p in diagonal_blocks(size, i)]
        for k, place in enumerate([None] + line_blocks(size, i)):
            block = whole(*place) if place else jnp.where(column >= row, upper, lower)
            for s in range(per):
                put(k * rows, s, block[s * rows:(s + 1) * rows])
        element = jnp.sum(jnp.where(column == row, lower, 0.0), axis=0, keepdims=True)
        for s in range(per):
            put(height - 8, s, jnp.broadcast_to(element, (8, B)))
    half = keep_ref.shape[0]
    keep_ref[...] = packed[:half]
    send_ref[...] = packed[half:]


def unpack(pieces, packed, hi, lo, me, shards, chunk):
    size = hi.shape[0]
    rows, height = part_rows(size, shards), shard_rows(size, shards)
    per = B // rows
    row, column = places()
    slot = 0
    for piece in pieces:
        for s in range(piece.shape[0] // height):
            at = pl.multiple_of((slot ^ me) * height, 8)
            packed[pl.ds(at, height), :] = piece[s * height:(s + 1) * height, :]
            slot += 1

    def put(p, q, block):
        hi[p, q], lo[p, q] = split(block)

    for line, i in enumerate(chunk_lines(size, chunk)):
        start = line * per * height

        def get(k):
            return jnp.concatenate(
                [
                    packed[start + s * height + k * rows:start + s * height + (k + 1) * rows, :]
                    for s in range(per)
                ],
                axis=0,
            )

        first, last = diagonal_blocks(size, i)
        block = get(0)
        turned = block.T
        element = packed[start + height - 8:start + height - 7, :]
        put(first, first, jnp.where(column >= row, block, turned))
        below = jnp.where(column < row, block, turned)
        put(last, last, jnp.where(column == row, jnp.broadcast_to(element, (B, B)), below))
        for k, (p, q) in enumerate(line_blocks(size, i)):
            block = get(k + 1)
            put(p, q, block)
            put(q, p, block.T)


def packed_scratch(size, shards):
    return pltpu.VMEM((shards * shard_rows(size, shards), B), F32)


def halves(size, shards):
    return [struct(shards // 2 * shard_rows(size, shards), B)] * 2


def first_gram_kernel(
    shards, me_ref, a_hbm, b_hbm, keep_ref, send_ref, ah, al, bh, bl, a_buf, b_buf, sems, g, packed
):
    rows, size = a_buf.shape
    q = size // 4
    steps = sems.shape[1]
    tile = rows // steps

    def copies(step):
        r = slice(step * tile, (step + 1) * tile)
        return [
            pltpu.make_async_copy(src.at[r], dst.at[r], sems.at[k, step])
            for k, (src, dst) in enumerate([(a_hbm, a_buf), (b_hbm, b_buf)])
        ]

    def start(step):
        for copy in copies(step):
            copy.start()

    start(0)
    start(1)
    for step in range(steps):
        r = slice(step * tile, (step + 1) * tile)
        for copy in copies(step):
            copy.wait()
        if step + 2 < steps:
            start(step + 2)
        ah[:, r], al[:, r] = split(a_buf[r].T)
        bh[r], bl[r] = split(b_buf[r])
        for r0, r1, c0, c1 in [(0, q, 0, size), (q, size, 0, q), (3 * q, size, 3 * q, size)]:
            product = mm((ah[r0:r1, r], al[r0:r1, r]), (bh[r, c0:c1], bl[r, c0:c1]))
            if step:
                product += g[r0:r1, c0:c1]
            g[r0:r1, c0:c1] = product
    pack(g, packed, keep_ref, send_ref, me_ref[0], shards, 0)


def first_gram(me, shards, a, b):
    rows, size = a.shape
    hbm = pl.BlockSpec(memory_space=pltpu.HBM)
    return call(
        functools.partial(first_gram_kernel, shards), "first_gram",
        halves(size, shards) + [struct(size, rows, dtype=BF16)] * 2 + [struct(rows, size, dtype=BF16)] * 2,
        43, 0.5, 4,
        in_specs=[SMEM, hbm, hbm],
        out_specs=[VMEM] * 6,
        scratch_shapes=[
            pltpu.VMEM((rows, size), F32), pltpu.VMEM((rows, size), F32),
            pltpu.SemaphoreType.DMA((2, 4)),
            pltpu.VMEM((size, size), F32), packed_scratch(size, shards),
        ],
    )(me, a, b)


def lower_product(g, ah, al, bh, bl):
    size = g.shape[0]
    q = size // 4
    for r0, r1, c0, c1 in [(q, 3 * q, q, size), (3 * q, size, q, 3 * q)]:
        c = slice(c0 - q, c1 - q)
        g[r0:r1, c0:c1] = mm((ah[r0:r1, :], al[r0:r1, :]), (bh[:, c], bl[:, c]))


def other_gram_kernel(shards, me_ref, ah, al, bh, bl, keep_ref, send_ref, g, packed):
    q = g.shape[0] // 4
    lower_product(g, ah, al, bh[:, q:], bl[:, q:])
    pack(g, packed, keep_ref, send_ref, me_ref[0], shards, 1)


def other_gram(me, shards, ah, al, bh, bl):
    size = ah.shape[0]
    return call(
        functools.partial(other_gram_kernel, shards), "other_gram", halves(size, shards), 18, 0.5, 2,
        in_specs=[SMEM] + [VMEM] * 4,
        out_specs=[VMEM, VMEM],
        scratch_shapes=[pltpu.VMEM((size, size), F32), packed_scratch(size, shards)],
    )(me, ah, al, bh, bl)


def tiles(count, tile, step):
    def body(t, _):
        step(pl.ds(pl.multiple_of(t * tile, tile), tile))
        return 0

    lax.fori_loop(0, count // tile, body, 0)


def affine_kernel(a_ref, b_ref, out_ref, hi, lo):
    hi[...], lo[...] = split(a_ref[...])

    def step(c):
        out_ref[:, c] = 1.5 * a_ref[:, c] - 0.5 * mm((hi[...], lo[...]), split(b_ref[:, c]))

    tiles(out_ref.shape[1], min(512, out_ref.shape[0]), step)


THIRDS = ((0, 4), (1, 4), (1, 2))


def row_part(part, rows, size):
    at, parts = THIRDS[part]
    return pl.BlockSpec((rows // parts, size), lambda r: (at, 0))


def affine(a, b, part):
    rows, size = a.shape
    height = rows // THIRDS[part][1]
    return call(
        affine_kernel, "affine", struct(height, size), 18, height / rows, 2,
        grid=(1,),
        in_specs=[row_part(part, rows, size), pl.BlockSpec((size, size), lambda r: (0, 0))],
        out_specs=pl.BlockSpec((height, size), lambda r: (0, 0)),
        scratch_shapes=[pltpu.VMEM((height, size), BF16)] * 2,
    )(a, b)


def affine_parts_kernel(ah, al, b_ref, out_ref):
    def step(c):
        product = mm((ah[...], al[...]), split(b_ref[:, c]))
        out_ref[:, c] = 1.5 * (ah[:, c].astype(F32) + al[:, c].astype(F32)) - 0.5 * product

    tiles(out_ref.shape[1], min(512, out_ref.shape[0]), step)


def affine_parts(ah, al, b, part):
    rows, size = ah.shape
    height = rows // THIRDS[part][1]
    return call(
        affine_parts_kernel, "affine_parts", struct(height, size), 18, height / rows, 2,
        grid=(1,),
        in_specs=[row_part(part, rows, size)] * 2
        + [pl.BlockSpec((size, size), lambda r: (0, 0))],
        out_specs=pl.BlockSpec((height, size), lambda r: (0, 0)),
    )(ah, al, b)


SPANS = (
    (((0, 4),), ((0, 1),), ((0, 1),), ((0, 1), (3, 4))),
    ((), ((1, 4),), ((1, 4),), ((1, 3),)),
)


def sym_product(ah, al, hi, lo, chunk, column, rows=slice(None)):
    q = hi.shape[0] // 4
    spans = [slice(k0 * q, k1 * q) for k0, k1 in SPANS[chunk][column]]
    c = slice(column * q, (column + 1) * q)
    a = [ref[rows, k] for ref in (ah, ah, al) for k in spans]
    b = [ref[k, c] for ref in (hi, lo, hi) for k in spans]
    return c, jnp.dot(
        jnp.concatenate(a, axis=1), jnp.concatenate(b, axis=0), preferred_element_type=F32
    )


def apply_first(base_refs, out_ref, ah, al, hi, lo, columns):
    q = hi.shape[0] // 4
    for column in columns:
        c, product = sym_product(ah, al, hi, lo, 0, column)
        out = slice(c.start - columns[0] * q, c.stop - columns[0] * q)
        at = 0
        for base_ref in base_refs:
            end = at + base_ref.shape[0]
            out_ref[at:end, out] = base_ref[:, c] - 0.5 * product[at:end]
            at = end


def sym_scratch(size, shards):
    return [pltpu.VMEM((size, size), BF16)] * 2 + [packed_scratch(size, shards)]


def first_part_kernel(shards, count, columns, me_ref, *refs):
    pieces, refs = refs[:count], refs[count:]
    ah, al, base_refs, (out_ref, hi, lo, packed) = refs[0], refs[1], refs[2:-4], refs[-4:]
    unpack(pieces, packed, hi, lo, me_ref[0], shards, 0)
    apply_first(base_refs, out_ref, ah, al, hi, lo, columns)


def first_part(me, shards, pieces, ah, al, base, columns):
    rows, size = ah.shape
    part = struct(size, size, dtype=BF16)
    more = len(columns) < 4
    scratch = sym_scratch(size, shards)
    return call(
        functools.partial(first_part_kernel, shards, len(pieces), columns), "first_part",
        [struct(rows, len(columns) * size // 4)] + [part, part] * more, 18, 0.5, 3,
        in_specs=[SMEM] + [VMEM] * (len(pieces) + 2 + len(base)),
        out_specs=[VMEM] * (1 + 2 * more),
        scratch_shapes=scratch[2 * more:],
    )(me, *pieces, ah, al, *base)


def other_part_kernel(columns, ah, al, hi, lo, *refs):
    apply_first(refs[:-1], refs[-1], ah, al, hi, lo, columns)


def other_part(ah, al, hi, lo, base, columns):
    rows, size = ah.shape
    return call(
        functools.partial(other_part_kernel, columns), "other_part",
        struct(rows, len(columns) * size // 4), 16, 0.25, 3,
        in_specs=[VMEM] * (4 + len(base)),
        out_specs=VMEM,
    )(ah, al, hi, lo, *base)


def column_kernel(xh, xl, mid_ref, col_ref):
    col_ref[...] = mm((xh[...], xl[...]), split(mid_ref[...]))


def column_product(xh, xl, mid):
    size, rows = xh.shape
    block = pl.BlockSpec((rows, size // 4), lambda r: (0, 0))
    whole = pl.BlockSpec((size, rows), lambda r: (0, 0))
    return call(
        column_kernel, "column_product", struct(size, size // 4), 16, 0.25, 2,
        grid=(1,), in_specs=[whole, whole, block], out_specs=block,
    )(xh, xl, mid)


def turn_kernel(x_ref, xh, xl):
    def step(r):
        xh[:, r], xl[:, r] = split(x_ref[r].T)

    tiles(x_ref.shape[0], 256, step)


def turn(x):
    part = struct(*x.shape[::-1], dtype=BF16)
    return call(
        turn_kernel, "turn", [part, part], 16, 0.1, 2, in_specs=[VMEM], out_specs=[VMEM] * 2
    )(x)


def cut_kernel(x_ref, hi, lo):
    def step(r):
        hi[r], lo[r] = split(x_ref[r])

    tiles(x_ref.shape[0], 128, step)


def cut(x):
    part = struct(*x.shape, dtype=BF16)
    return call(
        cut_kernel, "cut", [part, part], 16, 0.1, 2, in_specs=[VMEM], out_specs=[VMEM] * 2
    )(x)


def second_gram_kernel(shards, count, me_ref, *refs):
    pieces, refs = refs[:count], refs[count:]
    (ah, al, base_ref, xh, xl, col_ref), refs = refs[:6], refs[6:]
    keep_ref, send_ref, mh, ml, hi, lo, packed, g = refs
    size = g.shape[0]
    q = size // 4
    unpack(pieces, packed, hi, lo, me_ref[0], shards, 1)
    mh[:, :q], ml[:, :q] = split(base_ref[:, :q])
    for column in range(1, 4):
        c, product = sym_product(ah, al, hi, lo, 1, column)
        mid = base_ref[:, c] - 0.5 * product
        mh[:, c], ml[:, c] = split(mid)
        g[:q, c] = mm((xh[:q, :], xl[:q, :]), (mh[:, c], ml[:, c]))
    g[:, :q] = col_ref[...]
    g[3 * q:, 3 * q:] = mm((xh[3 * q:, :], xl[3 * q:, :]), (mh[:, 3 * q:], ml[:, 3 * q:]))
    pack(g, packed, keep_ref, send_ref, me_ref[0], shards, 0)


def second_gram(me, shards, pieces, ah, al, base, xh, xl, col):
    rows, size = ah.shape
    part = struct(rows, size, dtype=BF16)
    return call(
        functools.partial(second_gram_kernel, shards, len(pieces)), "second_gram",
        halves(size, shards) + [part, part], 20, 0.8, 5,
        in_specs=[SMEM] + [VMEM] * (len(pieces) + 6),
        out_specs=[VMEM] * 4,
        scratch_shapes=sym_scratch(size, shards) + [pltpu.VMEM((size, size), F32)],
    )(me, *pieces, ah, al, base, xh, xl, col)


def fourth_gram_kernel(shards, me_ref, xh, xl, mh, ml, keep_ref, send_ref, g, packed):
    q = g.shape[0] // 4
    lower_product(g, xh, xl, mh[:, q:], ml[:, q:])
    pack(g, packed, keep_ref, send_ref, me_ref[0], shards, 1)


def fourth_gram(me, shards, xh, xl, mh, ml):
    size = xh.shape[0]
    return call(
        functools.partial(fourth_gram_kernel, shards), "fourth_gram", halves(size, shards), 18, 0.5, 2,
        in_specs=[SMEM] + [VMEM] * 4,
        out_specs=[VMEM, VMEM],
        scratch_shapes=[pltpu.VMEM((size, size), F32), packed_scratch(size, shards)],
    )(me, xh, xl, mh, ml)


def last_kernel(shards, count, me_ref, *refs):
    pieces = refs[:count]
    ah, al, z_ref, rest_ref, out_hbm, hi, lo, packed, out, sems = refs[count:]
    q = hi.shape[0] // 4
    copies = []

    def send(src, rows, c):
        copy = pltpu.make_async_copy(src, out_hbm.at[rows, c], sems.at[len(copies)])
        copy.start()
        copies.append(copy)

    count = out.shape[0]
    send(z_ref, slice(0, count), slice(0, q))
    unpack(pieces, packed, hi, lo, me_ref[0], shards, 1)
    for column in (1, 2, 3):
        parts = 2 if column == 3 else 1
        for part in range(parts):
            r = slice(part * count // parts, (part + 1) * count // parts)
            c, product = sym_product(ah, al, hi, lo, 1, column, r)
            out[r, c] = rest_ref[r, c.start - q:c.stop - q] - 0.5 * product
            send(out.at[r, c], r, c)
    for copy in copies:
        copy.wait()


def last_step(me, shards, pieces, ah, al, z, rest):
    rows, size = ah.shape
    return call(
        functools.partial(last_kernel, shards, len(pieces)), "last", struct(rows, size), 22, 0.5, 3,
        in_specs=[SMEM] + [VMEM] * (len(pieces) + 4),
        out_specs=pl.BlockSpec(memory_space=pltpu.HBM),
        scratch_shapes=sym_scratch(size, shards)
        + [pltpu.VMEM((rows, size), F32), pltpu.SemaphoreType.DMA((5,))],
    )(me, *pieces, ah, al, z, rest)


CORE = 1
PLANE = (2, 4, 6)
SHARDS = 2 * (1 + len(PLANE))


def slot_of(index):
    return (index % 2) * (SHARDS // 2) + (index // 2) % (SHARDS // 2)


class Sum:
    def __init__(self, count, keep, send):
        self.count, self.keep, self.send = count, keep, send

    def swap(self, x, offset):
        return lax.ppermute(x, "row", [(i, i ^ offset) for i in range(self.count)])

    def swaps(self, values):
        return [self.swap(x, offset) for x, offset in zip(values, PLANE)]

    def core(self):
        return self.swap(self.send, CORE)

    def plane(self, got):
        total = self.keep + got
        part = total.shape[0] // (1 + len(PLANE))
        self.keep, *sends = [total[k * part:(k + 1) * part] for k in range(1 + len(PLANE))]
        return self.swaps(sends)

    def own(self, got):
        self.keep = sum(got, self.keep)

    def exchange(self, offset):
        return self.swap(self.keep, offset)

    def gather_plane(self):
        return self.swaps([self.keep] * len(PLANE))

    def gather_core(self, got):
        self.mine = jnp.concatenate([self.keep, *got], axis=0)
        return self.swap(self.mine, CORE)


def close(env, *got):
    values = lax.optimization_barrier((*env.values(), *got[::-1]))
    env.update(zip(env, values))
    return values[len(env):][::-1]


def sum_chunks(count, env, first, second, works, late):
    beyond = [1 << s for s in range(3, count.bit_length() - 1)]
    works = list(works)

    def work():
        if works:
            works.pop(0)(env)

    a = Sum(count, *first)
    got_a = a.core()
    pair = second(env)
    got_a, *pair = close(env, got_a, *pair)
    b = Sum(count, *pair)

    got_a = a.plane(got_a)
    got_b = b.core()
    work()
    (got_b,) = close(env, got_b)

    got_b = b.plane(got_b)
    work()
    a.own(close(env, *got_a))

    for offset in beyond:
        got_a = a.exchange(offset)
        work()
        b.own(close(env, *got_b))
        got_b = [b.exchange(offset)]
        a.own(close(env, got_a))

    got_a = a.gather_plane()
    b.own(close(env, *got_b))

    got_b = b.gather_plane()
    got_a = a.gather_core(close(env, *got_a))
    work()
    (got_a,) = close(env, got_a)
    late[0](env, [a.mine, got_a])
    got_b = b.gather_core(close(env, *got_b))
    late[1](env)
    (got_b,) = close(env, got_b)
    return [b.mine, got_b]


def body(count, orbitals_zero, orbitals_one, correlation_zero, correlation_one, cotangent):
    me = slot_of(lax.axis_index("row")).astype(jnp.int32).reshape(1)
    env = dict(
        x0=orbitals_zero, x1=orbitals_one, s0=correlation_zero, s1=correlation_one, c=cotangent
    )

    def direct(part):
        def work(env):
            env[f"m{part}"] = affine(env["c"], env["s1"], part)
        return work

    def direct_and_turn(env):
        direct(2)(env)
        env["xh"], env["xl"] = turn(env["x0"])

    def cut_one(env):
        env["x1h"], env["x1l"] = cut(env["x1"])

    def middle(env, pieces):
        (env["mid"],) = first_part(
            me, SHARDS, pieces, env["x1h"], env["x1l"], [env["m0"], env["m1"], env["m2"]], (0, 1, 2, 3)
        )

    def column(env):
        env["col"] = column_product(env["xh"], env["xl"], env["mid"])

    keep, send, *parts = first_gram(me, SHARDS, env["x1"], env["c"])
    one = sum_chunks(
        count, env, (keep, send), lambda env: other_gram(me, SHARDS, *parts),
        [direct(0), direct(1), direct_and_turn, cut_one], [middle, column],
    )

    keep, send, env["mh"], env["ml"] = second_gram(
        me, SHARDS, one, env["x1h"], env["x1l"], env["mid"], env["xh"], env["xl"], env["col"]
    )

    def last_direct(part):
        def work(env):
            env[f"d{part}"] = affine_parts(env["mh"], env["ml"], env["s0"], part)
        return work

    def cut_zero(env):
        env["x0h"], env["x0l"] = cut(env["x0"])

    def three(name):
        return [env[f"{name}{part}"] for part in range(3)]

    def result(env, pieces):
        env["z"], env["symh"], env["syml"] = first_part(
            me, SHARDS, pieces, env["x0h"], env["x0l"], three("d"), (0,)
        )

    def rest(env):
        env["rest"] = other_part(
            env["x0h"], env["x0l"], env["symh"], env["syml"], three("d"), (1, 2, 3)
        )

    two = sum_chunks(
        count, env, (keep, send),
        lambda env: fourth_gram(me, SHARDS, env["xh"], env["xl"], env["mh"], env["ml"]),
        [last_direct(0), last_direct(1), last_direct(2), cut_zero], [result, rest],
    )
    return last_step(me, SHARDS, two, env["x0h"], env["x0l"], env["z"], env["rest"])


def solution(mesh):
    in_specs = (
        P(("kpt", "row"), None),
        P(("kpt", "row"), None),
        P("kpt", None),
        P("kpt", None),
        P(("kpt", "row"), None),
    )
    out_specs = P(("kpt", "row"), None)
    return jax.shard_map(
        functools.partial(body, mesh.shape["row"]),
        mesh=mesh, in_specs=in_specs, out_specs=out_specs, check_vma=False,
    )
```

```python
import functools
import jax
import jax.numpy as jnp
from jax import lax
from jax.experimental import pallas as pl
from jax.experimental.pallas import tpu as pltpu
from jax.sharding import PartitionSpec as P

F32 = jnp.float32
BF16 = jnp.bfloat16
B = 128
MIB = 1024 * 1024
WEIGHT = 10


def split(x):
    hi = x.astype(BF16)
    return hi, (x - hi.astype(F32)).astype(BF16)


def mm(a, b):
    (ah, al), (bh, bl) = a, b
    return jnp.dot(
        jnp.concatenate([ah, ah, al], axis=1),
        jnp.concatenate([bh, bl, bh], axis=0),
        preferred_element_type=F32,
    )


def call(kernel, name, out_shape, limit, products, arrays, **kw):
    size = 1024
    return pl.pallas_call(
        kernel,
        name=name,
        out_shape=out_shape,
        compiler_params=pltpu.CompilerParams(vmem_limit_bytes=limit * MIB),
        cost_estimate=pl.CostEstimate(
            flops=int(WEIGHT * 6 * products * size ** 3),
            bytes_accessed=int(WEIGHT * 4 * arrays * size * size),
            transcendentals=0,
        ),
        **kw,
    )


def struct(*shape, dtype=F32):
    return jax.ShapeDtypeStruct(shape, dtype)


SMEM = pl.BlockSpec(memory_space=pltpu.SMEM)
VMEM = pl.BlockSpec(memory_space=pltpu.VMEM)


def chunk_lines(size, chunk):
    half = size // B // 4
    return range(chunk * half, (chunk + 1) * half)


def line_blocks(size, i):
    n = size // B
    block = lambda k: slice(k * B, (k + 1) * B)
    return [(block(top), block(j)) for top in (i, n - 1 - i) for j in range(top + 1, n)]


def diagonal_blocks(size, i):
    n = size // B
    return [slice(k * B, (k + 1) * B) for k in (i, n - 1 - i)]


def part_rows(size, shards):
    return size // 4 // shards


def shard_rows(size, shards):
    return part_rows(size, shards) * (size // B) + 8


def places():
    row = lax.broadcasted_iota(jnp.int32, (B, B), 0)
    column = lax.broadcasted_iota(jnp.int32, (B, B), 1)
    return row, column


def pack(g, packed, keep_ref, send_ref, me, shards, chunk):
    size = g.shape[0]
    rows, height = part_rows(size, shards), shard_rows(size, shards)
    per = B // rows
    row, column = places()
    whole = lambda p, q: g[p, q] + g[q, p].T
    for line, i in enumerate(chunk_lines(size, chunk)):
        starts = [((line * per + s) ^ me) * height for s in range(per)]

        def put(at, s, value):
            start = pl.multiple_of(starts[s] + at, 8)
            packed[pl.ds(start, value.shape[0]), :] = value

        upper, lower = [whole(p, p) for p in diagonal_blocks(size, i)]
        for k, place in enumerate([None] + line_blocks(size, i)):
            block = whole(*place) if place else jnp.where(column >= row, upper, lower)
            for s in range(per):
                put(k * rows, s, block[s * rows:(s + 1) * rows])
        element = jnp.sum(jnp.where(column == row, lower, 0.0), axis=0, keepdims=True)
        for s in range(per):
            put(height - 8, s, jnp.broadcast_to(element, (8, B)))
    half = keep_ref.shape[0]
    keep_ref[...] = packed[:half]
    send_ref[...] = packed[half:]


def unpack(pieces, packed, hi, lo, me, shards, chunk):
    size = hi.shape[0]
    rows, height = part_rows(size, shards), shard_rows(size, shards)
    per = B // rows
    row, column = places()
    slot = 0
    for piece in pieces:
        for s in range(piece.shape[0] // height):
            at = pl.multiple_of((slot ^ me) * height, 8)
            packed[pl.ds(at, height), :] = piece[s * height:(s + 1) * height, :]
            slot += 1

    def put(p, q, block):
        hi[p, q], lo[p, q] = split(block)

    for line, i in enumerate(chunk_lines(size, chunk)):
        start = line * per * height

        def get(k):
            return jnp.concatenate(
                [
                    packed[start + s * height + k * rows:start + s * height + (k + 1) * rows, :]
                    for s in range(per)
                ],
                axis=0,
            )

        first, last = diagonal_blocks(size, i)
        block = get(0)
        turned = block.T
        element = packed[start + height - 8:start + height - 7, :]
        put(first, first, jnp.where(column >= row, block, turned))
        below = jnp.where(column < row, block, turned)
        put(last, last, jnp.where(column == row, jnp.broadcast_to(element, (B, B)), below))
        for k, (p, q) in enumerate(line_blocks(size, i)):
            block = get(k + 1)
            put(p, q, block)
            put(q, p, block.T)


def packed_scratch(size, shards):
    return pltpu.VMEM((shards * shard_rows(size, shards), B), F32)


def halves(size, shards):
    return [struct(shards // 2 * shard_rows(size, shards), B)] * 2


def first_gram_kernel(
    shards, me_ref, a_hbm, b_hbm, keep_ref, send_ref, ah, al, bh, bl, a_buf, b_buf, sems, g, packed
):
    rows, size = a_buf.shape
    q = size // 4
    steps = sems.shape[1]
    tile = rows // steps

    def copies(step):
        r = slice(step * tile, (step + 1) * tile)
        return [
            pltpu.make_async_copy(src.at[r], dst.at[r], sems.at[k, step])
            for k, (src, dst) in enumerate([(a_hbm, a_buf), (b_hbm, b_buf)])
        ]

    def start(step):
        for copy in copies(step):
            copy.start()

    start(0)
    start(1)
    for step in range(steps):
        r = slice(step * tile, (step + 1) * tile)
        for copy in copies(step):
            copy.wait()
        if step + 2 < steps:
            start(step + 2)
        ah[:, r], al[:, r] = split(a_buf[r].T)
        bh[r], bl[r] = split(b_buf[r])
        for r0, r1, c0, c1 in [(0, q, 0, size), (q, size, 0, q), (3 * q, size, 3 * q, size)]:
            product = mm((ah[r0:r1, r], al[r0:r1, r]), (bh[r, c0:c1], bl[r, c0:c1]))
            if step:
                product += g[r0:r1, c0:c1]
            g[r0:r1, c0:c1] = product
    pack(g, packed, keep_ref, send_ref, me_ref[0], shards, 0)


def first_gram(me, shards, a, b):
    rows, size = a.shape
    hbm = pl.BlockSpec(memory_space=pltpu.HBM)
    return call(
        functools.partial(first_gram_kernel, shards), "first_gram",
        halves(size, shards) + [struct(size, rows, dtype=BF16)] * 2 + [struct(rows, size, dtype=BF16)] * 2,
        43, 0.5, 4,
        in_specs=[SMEM, hbm, hbm],
        out_specs=[VMEM] * 6,
        scratch_shapes=[
            pltpu.VMEM((rows, size), F32), pltpu.VMEM((rows, size), F32),
            pltpu.SemaphoreType.DMA((2, 4)),
            pltpu.VMEM((size, size), F32), packed_scratch(size, shards),
        ],
    )(me, a, b)


def lower_product(g, ah, al, bh, bl):
    size = g.shape[0]
    q = size // 4
    for r0, r1, c0, c1 in [(q, 3 * q, q, size), (3 * q, size, q, 3 * q)]:
        c = slice(c0 - q, c1 - q)
        g[r0:r1, c0:c1] = mm((ah[r0:r1, :], al[r0:r1, :]), (bh[:, c], bl[:, c]))


def other_gram_kernel(shards, me_ref, ah, al, bh, bl, keep_ref, send_ref, g, packed):
    q = g.shape[0] // 4
    lower_product(g, ah, al, bh[:, q:], bl[:, q:])
    pack(g, packed, keep_ref, send_ref, me_ref[0], shards, 1)


def other_gram(me, shards, ah, al, bh, bl):
    size = ah.shape[0]
    return call(
        functools.partial(other_gram_kernel, shards), "other_gram", halves(size, shards), 18, 0.5, 2,
        in_specs=[SMEM] + [VMEM] * 4,
        out_specs=[VMEM, VMEM],
        scratch_shapes=[pltpu.VMEM((size, size), F32), packed_scratch(size, shards)],
    )(me, ah, al, bh, bl)


def tiles(count, tile, step):
    def body(t, _):
        step(pl.ds(pl.multiple_of(t * tile, tile), tile))
        return 0

    lax.fori_loop(0, count // tile, body, 0)


def affine_kernel(a_ref, b_ref, out_ref, hi, lo):
    hi[...], lo[...] = split(a_ref[...])

    def step(c):
        out_ref[:, c] = 1.5 * a_ref[:, c] - 0.5 * mm((hi[...], lo[...]), split(b_ref[:, c]))

    tiles(out_ref.shape[1], min(512, out_ref.shape[0]), step)


THIRDS = ((0, 4), (1, 4), (1, 2))


def row_part(part, rows, size):
    at, parts = THIRDS[part]
    return pl.BlockSpec((rows // parts, size), lambda r: (at, 0))


def affine(a, b, part):
    rows, size = a.shape
    height = rows // THIRDS[part][1]
    return call(
        affine_kernel, "affine", struct(height, size), 18, height / rows, 2,
        grid=(1,),
        in_specs=[row_part(part, rows, size), pl.BlockSpec((size, size), lambda r: (0, 0))],
        out_specs=pl.BlockSpec((height, size), lambda r: (0, 0)),
        scratch_shapes=[pltpu.VMEM((height, size), BF16)] * 2,
    )(a, b)


def affine_parts_kernel(ah, al, b_ref, out_ref):
    def step(c):
        product = mm((ah[...], al[...]), split(b_ref[:, c]))
        out_ref[:, c] = 1.5 * (ah[:, c].astype(F32) + al[:, c].astype(F32)) - 0.5 * product

    tiles(out_ref.shape[1], min(512, out_ref.shape[0]), step)


def affine_parts(ah, al, b, part):
    rows, size = ah.shape
    height = rows // THIRDS[part][1]
    return call(
        affine_parts_kernel, "affine_parts", struct(height, size), 18, height / rows, 2,
        grid=(1,),
        in_specs=[row_part(part, rows, size)] * 2
        + [pl.BlockSpec((size, size), lambda r: (0, 0))],
        out_specs=pl.BlockSpec((height, size), lambda r: (0, 0)),
    )(ah, al, b)


SPANS = (
    (((0, 4),), ((0, 1),), ((0, 1),), ((0, 1), (3, 4))),
    ((), ((1, 4),), ((1, 4),), ((1, 3),)),
)


def sym_product(ah, al, hi, lo, chunk, column, rows=slice(None)):
    q = hi.shape[0] // 4
    spans = [slice(k0 * q, k1 * q) for k0, k1 in SPANS[chunk][column]]
    c = slice(column * q, (column + 1) * q)
    a = [ref[rows, k] for ref in (ah, ah, al) for k in spans]
    b = [ref[k, c] for ref in (hi, lo, hi) for k in spans]
    return c, jnp.dot(
        jnp.concatenate(a, axis=1), jnp.concatenate(b, axis=0), preferred_element_type=F32
    )


def apply_first(base_refs, out_ref, ah, al, hi, lo, columns):
    q = hi.shape[0] // 4
    for column in columns:
        c, product = sym_product(ah, al, hi, lo, 0, column)
        out = slice(c.start - columns[0] * q, c.stop - columns[0] * q)
        at = 0
        for base_ref in base_refs:
            end = at + base_ref.shape[0]
            out_ref[at:end, out] = base_ref[:, c] - 0.5 * product[at:end]
            at = end


def sym_scratch(size, shards):
    return [pltpu.VMEM((size, size), BF16)] * 2 + [packed_scratch(size, shards)]


def first_part_kernel(shards, count, columns, me_ref, *refs):
    pieces, refs = refs[:count], refs[count:]
    ah, al, base_refs, (out_ref, hi, lo, packed) = refs[0], refs[1], refs[2:-4], refs[-4:]
    unpack(pieces, packed, hi, lo, me_ref[0], shards, 0)
    apply_first(base_refs, out_ref, ah, al, hi, lo, columns)


def first_part(me, shards, pieces, ah, al, base, columns):
    rows, size = ah.shape
    part = struct(size, size, dtype=BF16)
    more = len(columns) < 4
    scratch = sym_scratch(size, shards)
    return call(
        functools.partial(first_part_kernel, shards, len(pieces), columns), "first_part",
        [struct(rows, len(columns) * size // 4)] + [part, part] * more, 18, 0.5, 3,
        in_specs=[SMEM] + [VMEM] * (len(pieces) + 2 + len(base)),
        out_specs=[VMEM] * (1 + 2 * more),
        scratch_shapes=scratch[2 * more:],
    )(me, *pieces, ah, al, *base)


def other_part_kernel(columns, ah, al, hi, lo, *refs):
    apply_first(refs[:-1], refs[-1], ah, al, hi, lo, columns)


def other_part(ah, al, hi, lo, base, columns):
    rows, size = ah.shape
    return call(
        functools.partial(other_part_kernel, columns), "other_part",
        struct(rows, len(columns) * size // 4), 16, 0.25, 3,
        in_specs=[VMEM] * (4 + len(base)),
        out_specs=VMEM,
    )(ah, al, hi, lo, *base)


def column_kernel(xh, xl, mid_ref, col_ref):
    col_ref[...] = mm((xh[...], xl[...]), split(mid_ref[...]))


def column_product(xh, xl, mid):
    size, rows = xh.shape
    block = pl.BlockSpec((rows, size // 4), lambda r: (0, 0))
    whole = pl.BlockSpec((size, rows), lambda r: (0, 0))
    return call(
        column_kernel, "column_product", struct(size, size // 4), 16, 0.25, 2,
        grid=(1,), in_specs=[whole, whole, block], out_specs=block,
    )(xh, xl, mid)


def turn_kernel(x_ref, xh, xl):
    def step(r):
        xh[:, r], xl[:, r] = split(x_ref[r].T)

    tiles(x_ref.shape[0], 256, step)


def turn(x):
    part = struct(*x.shape[::-1], dtype=BF16)
    return call(
        turn_kernel, "turn", [part, part], 16, 0.1, 2, in_specs=[VMEM], out_specs=[VMEM] * 2
    )(x)


def cut_kernel(x_ref, hi, lo):
    def step(r):
        hi[r], lo[r] = split(x_ref[r])

    tiles(x_ref.shape[0], 128, step)


def cut(x):
    part = struct(*x.shape, dtype=BF16)
    return call(
        cut_kernel, "cut", [part, part], 16, 0.1, 2, in_specs=[VMEM], out_specs=[VMEM] * 2
    )(x)


def second_gram_kernel(shards, count, me_ref, *refs):
    pieces, refs = refs[:count], refs[count:]
    (ah, al, base_ref, xh, xl, col_ref), refs = refs[:6], refs[6:]
    keep_ref, send_ref, mh, ml, hi, lo, packed, g = refs
    size = g.shape[0]
    q = size // 4
    unpack(pieces, packed, hi, lo, me_ref[0], shards, 1)
    mh[:, :q], ml[:, :q] = split(base_ref[:, :q])
    for column in range(1, 4):
        c, product = sym_product(ah, al, hi, lo, 1, column)
        mid = base_ref[:, c] - 0.5 * product
        mh[:, c], ml[:, c] = split(mid)
    g[:, :q] = col_ref[...]
    g[:q, q:] = mm((xh[:q, :], xl[:q, :]), (mh[:, q:], ml[:, q:]))
    g[3 * q:, 3 * q:] = mm((xh[3 * q:, :], xl[3 * q:, :]), (mh[:, 3 * q:], ml[:, 3 * q:]))
    pack(g, packed, keep_ref, send_ref, me_ref[0], shards, 0)


def second_gram(me, shards, pieces, ah, al, base, xh, xl, col):
    rows, size = ah.shape
    part = struct(rows, size, dtype=BF16)
    return call(
        functools.partial(second_gram_kernel, shards, len(pieces)), "second_gram",
        halves(size, shards) + [part, part], 20, 0.8, 5,
        in_specs=[SMEM] + [VMEM] * (len(pieces) + 6),
        out_specs=[VMEM] * 4,
        scratch_shapes=sym_scratch(size, shards) + [pltpu.VMEM((size, size), F32)],
    )(me, *pieces, ah, al, base, xh, xl, col)


def fourth_gram_kernel(shards, me_ref, xh, xl, mh, ml, keep_ref, send_ref, g, packed):
    q = g.shape[0] // 4
    lower_product(g, xh, xl, mh[:, q:], ml[:, q:])
    pack(g, packed, keep_ref, send_ref, me_ref[0], shards, 1)


def fourth_gram(me, shards, xh, xl, mh, ml):
    size = xh.shape[0]
    return call(
        functools.partial(fourth_gram_kernel, shards), "fourth_gram", halves(size, shards), 18, 0.5, 2,
        in_specs=[SMEM] + [VMEM] * 4,
        out_specs=[VMEM, VMEM],
        scratch_shapes=[pltpu.VMEM((size, size), F32), packed_scratch(size, shards)],
    )(me, xh, xl, mh, ml)


def last_kernel(shards, count, me_ref, *refs):
    pieces = refs[:count]
    ah, al, z_ref, rest_ref, out_hbm, hi, lo, packed, out, sems = refs[count:]
    q = hi.shape[0] // 4
    copies = []

    def send(src, rows, c):
        copy = pltpu.make_async_copy(src, out_hbm.at[rows, c], sems.at[len(copies)])
        copy.start()
        copies.append(copy)

    count = out.shape[0]
    send(z_ref, slice(0, count), slice(0, q))
    unpack(pieces, packed, hi, lo, me_ref[0], shards, 1)
    for column in (1, 2, 3):
        parts = 2 if column == 3 else 1
        for part in range(parts):
            r = slice(part * count // parts, (part + 1) * count // parts)
            c, product = sym_product(ah, al, hi, lo, 1, column, r)
            out[r, c] = rest_ref[r, c.start - q:c.stop - q] - 0.5 * product
            send(out.at[r, c], r, c)
    for copy in copies:
        copy.wait()


def last_step(me, shards, pieces, ah, al, z, rest):
    rows, size = ah.shape
    return call(
        functools.partial(last_kernel, shards, len(pieces)), "last", struct(rows, size), 22, 0.5, 3,
        in_specs=[SMEM] + [VMEM] * (len(pieces) + 4),
        out_specs=pl.BlockSpec(memory_space=pltpu.HBM),
        scratch_shapes=sym_scratch(size, shards)
        + [pltpu.VMEM((rows, size), F32), pltpu.SemaphoreType.DMA((5,))],
    )(me, *pieces, ah, al, z, rest)


CORE = 1
PLANE = (2, 4, 6)
SHARDS = 2 * (1 + len(PLANE))


def slot_of(index):
    return (index % 2) * (SHARDS // 2) + (index // 2) % (SHARDS // 2)


class Sum:
    def __init__(self, count, keep, send):
        self.count, self.keep, self.send = count, keep, send

    def swap(self, x, offset):
        return lax.ppermute(x, "row", [(i, i ^ offset) for i in range(self.count)])

    def swaps(self, values):
        return [self.swap(x, offset) for x, offset in zip(values, PLANE)]

    def core(self):
        return self.swap(self.send, CORE)

    def plane(self, got):
        total = self.keep + got
        part = total.shape[0] // (1 + len(PLANE))
        self.keep, *sends = [total[k * part:(k + 1) * part] for k in range(1 + len(PLANE))]
        return self.swaps(sends)

    def own(self, got):
        self.keep = sum(got, self.keep)

    def exchange(self, offset):
        return self.swap(self.keep, offset)

    def gather_plane(self):
        return self.swaps([self.keep] * len(PLANE))

    def gather_core(self, got):
        self.mine = jnp.concatenate([self.keep, *got], axis=0)
        return self.swap(self.mine, CORE)


def close(env, *got):
    values = lax.optimization_barrier((*env.values(), *got[::-1]))
    env.update(zip(env, values))
    return values[len(env):][::-1]


def sum_chunks(count, env, first, second, works, late):
    beyond = [1 << s for s in range(3, count.bit_length() - 1)]
    works = list(works)

    def work():
        if works:
            works.pop(0)(env)

    a = Sum(count, *first)
    got_a = a.core()
    pair = second(env)
    got_a, *pair = close(env, got_a, *pair)
    b = Sum(count, *pair)

    got_a = a.plane(got_a)
    got_b = b.core()
    work()
    (got_b,) = close(env, got_b)

    got_b = b.plane(got_b)
    work()
    a.own(close(env, *got_a))

    for offset in beyond:
        got_a = a.exchange(offset)
        work()
        b.own(close(env, *got_b))
        got_b = [b.exchange(offset)]
        a.own(close(env, got_a))

    got_a = a.gather_plane()
    b.own(close(env, *got_b))

    got_b = b.gather_plane()
    got_a = a.gather_core(close(env, *got_a))
    work()
    (got_a,) = close(env, got_a)
    late[0](env, [a.mine, got_a])
    got_b = b.gather_core(close(env, *got_b))
    late[1](env)
    (got_b,) = close(env, got_b)
    return [b.mine, got_b]


def body(count, orbitals_zero, orbitals_one, correlation_zero, correlation_one, cotangent):
    me = slot_of(lax.axis_index("row")).astype(jnp.int32).reshape(1)
    env = dict(
        x0=orbitals_zero, x1=orbitals_one, s0=correlation_zero, s1=correlation_one, c=cotangent
    )

    def direct(part):
        def work(env):
            env[f"m{part}"] = affine(env["c"], env["s1"], part)
        return work

    def direct_and_turn(env):
        direct(2)(env)
        env["xh"], env["xl"] = turn(env["x0"])

    def cut_one(env):
        env["x1h"], env["x1l"] = cut(env["x1"])

    def middle(env, pieces):
        (env["mid"],) = first_part(
            me, SHARDS, pieces, env["x1h"], env["x1l"], [env["m0"], env["m1"], env["m2"]], (0, 1, 2, 3)
        )

    def column(env):
        env["col"] = column_product(env["xh"], env["xl"], env["mid"])

    keep, send, *parts = first_gram(me, SHARDS, env["x1"], env["c"])
    one = sum_chunks(
        count, env, (keep, send), lambda env: other_gram(me, SHARDS, *parts),
        [direct(0), direct(1), direct_and_turn, cut_one], [middle, column],
    )

    keep, send, env["mh"], env["ml"] = second_gram(
        me, SHARDS, one, env["x1h"], env["x1l"], env["mid"], env["xh"], env["xl"], env["col"]
    )

    def last_direct(part):
        def work(env):
            env[f"d{part}"] = affine_parts(env["mh"], env["ml"], env["s0"], part)
        return work

    def cut_zero(env):
        env["x0h"], env["x0l"] = cut(env["x0"])

    def three(name):
        return [env[f"{name}{part}"] for part in range(3)]

    def result(env, pieces):
        env["z"], env["symh"], env["syml"] = first_part(
            me, SHARDS, pieces, env["x0h"], env["x0l"], three("d"), (0,)
        )

    def rest(env):
        env["rest"] = other_part(
            env["x0h"], env["x0l"], env["symh"], env["syml"], three("d"), (1, 2, 3)
        )

    two = sum_chunks(
        count, env, (keep, send),
        lambda env: fourth_gram(me, SHARDS, env["xh"], env["xl"], env["mh"], env["ml"]),
        [last_direct(0), last_direct(1), last_direct(2), cut_zero], [result, rest],
    )
    return last_step(me, SHARDS, two, env["x0h"], env["x0l"], env["z"], env["rest"])


def solution(mesh):
    in_specs = (
        P(("kpt", "row"), None),
        P(("kpt", "row"), None),
        P("kpt", None),
        P("kpt", None),
        P(("kpt", "row"), None),
    )
    out_specs = P(("kpt", "row"), None)
    return jax.shard_map(
        functools.partial(body, mesh.shape["row"]),
        mesh=mesh, in_specs=in_specs, out_specs=out_specs, check_vma=False,
    )
```

```python
import functools
import jax
import jax.numpy as jnp
from jax import lax
from jax.experimental import pallas as pl
from jax.experimental.pallas import tpu as pltpu
from jax.sharding import PartitionSpec as P

F32 = jnp.float32
BF16 = jnp.bfloat16
B = 128
MIB = 1024 * 1024
WEIGHT = 10


def split(x):
    hi = x.astype(BF16)
    return hi, (x - hi.astype(F32)).astype(BF16)


def mm(a, b):
    (ah, al), (bh, bl) = a, b
    return jnp.dot(
        jnp.concatenate([ah, ah, al], axis=1),
        jnp.concatenate([bh, bl, bh], axis=0),
        preferred_element_type=F32,
    )


def call(kernel, name, out_shape, limit, products, arrays, **kw):
    size = 1024
    return pl.pallas_call(
        kernel,
        name=name,
        out_shape=out_shape,
        compiler_params=pltpu.CompilerParams(vmem_limit_bytes=limit * MIB),
        cost_estimate=pl.CostEstimate(
            flops=int(WEIGHT * 6 * products * size ** 3),
            bytes_accessed=int(WEIGHT * 4 * arrays * size * size),
            transcendentals=0,
        ),
        **kw,
    )


def struct(*shape, dtype=F32):
    return jax.ShapeDtypeStruct(shape, dtype)


SMEM = pl.BlockSpec(memory_space=pltpu.SMEM)
VMEM = pl.BlockSpec(memory_space=pltpu.VMEM)


def chunk_lines(size, chunk):
    half = size // B // 4
    return range(chunk * half, (chunk + 1) * half)


def line_blocks(size, i):
    n = size // B
    block = lambda k: slice(k * B, (k + 1) * B)
    return [(block(top), block(j)) for top in (i, n - 1 - i) for j in range(top + 1, n)]


def diagonal_blocks(size, i):
    n = size // B
    return [slice(k * B, (k + 1) * B) for k in (i, n - 1 - i)]


def part_rows(size, shards):
    return size // 4 // shards


def shard_rows(size, shards):
    return part_rows(size, shards) * (size // B) + 8


def places():
    row = lax.broadcasted_iota(jnp.int32, (B, B), 0)
    column = lax.broadcasted_iota(jnp.int32, (B, B), 1)
    return row, column


def pack(g, packed, keep_ref, send_ref, me, shards, chunk):
    size = g.shape[0]
    rows, height = part_rows(size, shards), shard_rows(size, shards)
    per = B // rows
    row, column = places()
    whole = lambda p, q: g[p, q] + g[q, p].T
    for line, i in enumerate(chunk_lines(size, chunk)):
        starts = [((line * per + s) ^ me) * height for s in range(per)]

        def put(at, s, value):
            start = pl.multiple_of(starts[s] + at, 8)
            packed[pl.ds(start, value.shape[0]), :] = value

        upper, lower = [whole(p, p) for p in diagonal_blocks(size, i)]
        for k, place in enumerate([None] + line_blocks(size, i)):
            block = whole(*place) if place else jnp.where(column >= row, upper, lower)
            for s in range(per):
                put(k * rows, s, block[s * rows:(s + 1) * rows])
        element = jnp.sum(jnp.where(column == row, lower, 0.0), axis=0, keepdims=True)
        for s in range(per):
            put(height - 8, s, jnp.broadcast_to(element, (8, B)))
    half = keep_ref.shape[0]
    keep_ref[...] = packed[:half]
    send_ref[...] = packed[half:]


def unpack(pieces, packed, hi, lo, me, shards, chunk):
    size = hi.shape[0]
    rows, height = part_rows(size, shards), shard_rows(size, shards)
    per = B // rows
    row, column = places()
    slot = 0
    for piece in pieces:
        for s in range(piece.shape[0] // height):
            at = pl.multiple_of((slot ^ me) * height, 8)
            packed[pl.ds(at, height), :] = piece[s * height:(s + 1) * height, :]
            slot += 1

    def put(p, q, block):
        hi[p, q], lo[p, q] = split(block)

    for line, i in enumerate(chunk_lines(size, chunk)):
        start = line * per * height

        def get(k):
            return jnp.concatenate(
                [
                    packed[start + s * height + k * rows:start + s * height + (k + 1) * rows, :]
                    for s in range(per)
                ],
                axis=0,
            )

        first, last = diagonal_blocks(size, i)
        block = get(0)
        turned = block.T
        element = packed[start + height - 8:start + height - 7, :]
        put(first, first, jnp.where(column >= row, block, turned))
        below = jnp.where(column < row, block, turned)
        put(last, last, jnp.where(column == row, jnp.broadcast_to(element, (B, B)), below))
        for k, (p, q) in enumerate(line_blocks(size, i)):
            block = get(k + 1)
            put(p, q, block)
            put(q, p, block.T)


def packed_scratch(size, shards):
    return pltpu.VMEM((shards * shard_rows(size, shards), B), F32)


def halves(size, shards):
    return [struct(shards // 2 * shard_rows(size, shards), B)] * 2


def outer_rows(ah, al, columns=slice(None)):
    q = ah.shape[0] // 4
    return [jnp.concatenate([x[:q, columns], x[3 * q:, columns]], axis=0) for x in (ah, al)]


def rest_shape(size):
    return struct(size // 4, size // 2)


def first_gram_kernel(
    shards, me_ref, a_hbm, b_hbm, keep_ref, send_ref, rest_ref, ah, al, bh, bl,
    a_buf, b_buf, sems, g, packed
):
    rows, size = a_buf.shape
    q = size // 4
    steps = sems.shape[1]
    tile = rows // steps

    def copies(step):
        r = slice(step * tile, (step + 1) * tile)
        return [
            pltpu.make_async_copy(src.at[r], dst.at[r], sems.at[k, step])
            for k, (src, dst) in enumerate([(a_hbm, a_buf), (b_hbm, b_buf)])
        ]

    def start(step):
        for copy in copies(step):
            copy.start()

    start(0)
    start(1)
    for step in range(steps):
        r = slice(step * tile, (step + 1) * tile)
        for copy in copies(step):
            copy.wait()
        if step + 2 < steps:
            start(step + 2)
        ah[:, r], al[:, r] = split(a_buf[r].T)
        bh[r], bl[r] = split(b_buf[r])
        left = mm((ah[:, r], al[:, r]), (bh[r, :q], bl[r, :q]))
        outer = mm(outer_rows(ah, al, r), (bh[r, q:], bl[r, q:]))
        if step:
            left += g[:, :q]
            outer += jnp.concatenate([g[:q, q:], g[3 * q:, q:]], axis=0)
        g[:, :q] = left
        g[:q, q:] = outer[:q]
        g[3 * q:, q:] = outer[q:]
    rest_ref[...] = g[3 * q:, q:3 * q]
    pack(g, packed, keep_ref, send_ref, me_ref[0], shards, 0)


def first_gram(me, shards, a, b):
    rows, size = a.shape
    hbm = pl.BlockSpec(memory_space=pltpu.HBM)
    return call(
        functools.partial(first_gram_kernel, shards), "first_gram",
        halves(size, shards) + [rest_shape(size)]
        + [struct(size, rows, dtype=BF16)] * 2 + [struct(rows, size, dtype=BF16)] * 2,
        43, 0.5, 4,
        in_specs=[SMEM, hbm, hbm],
        out_specs=[VMEM] * 7,
        scratch_shapes=[
            pltpu.VMEM((rows, size), F32), pltpu.VMEM((rows, size), F32),
            pltpu.SemaphoreType.DMA((2, 4)),
            pltpu.VMEM((size, size), F32), packed_scratch(size, shards),
        ],
    )(me, a, b)


def inner_kernel(shards, me_ref, rest_ref, ah, al, bh, bl, keep_ref, send_ref, g, packed):
    q = g.shape[0] // 4
    g[q:3 * q, q:] = mm((ah[q:3 * q, :], al[q:3 * q, :]), (bh[:, q:], bl[:, q:]))
    g[3 * q:, q:3 * q] = rest_ref[...]
    pack(g, packed, keep_ref, send_ref, me_ref[0], shards, 1)


def inner_gram(me, shards, rest, ah, al, bh, bl):
    size = ah.shape[0]
    return call(
        functools.partial(inner_kernel, shards), "inner_gram", halves(size, shards), 18, 0.4, 2,
        in_specs=[SMEM] + [VMEM] * 5,
        out_specs=[VMEM, VMEM],
        scratch_shapes=[pltpu.VMEM((size, size), F32), packed_scratch(size, shards)],
    )(me, rest, ah, al, bh, bl)


def tiles(count, tile, step):
    def body(t, _):
        step(pl.ds(pl.multiple_of(t * tile, tile), tile))
        return 0

    lax.fori_loop(0, count // tile, body, 0)


def affine_kernel(a_ref, b_ref, out_ref, hi, lo):
    hi[...], lo[...] = split(a_ref[...])

    def step(c):
        out_ref[:, c] = 1.5 * a_ref[:, c] - 0.5 * mm((hi[...], lo[...]), split(b_ref[:, c]))

    tiles(out_ref.shape[1], min(512, out_ref.shape[0]), step)


THIRDS = ((0, 4), (1, 4), (1, 2))


def row_part(part, rows, size):
    at, parts = THIRDS[part]
    return pl.BlockSpec((rows // parts, size), lambda r: (at, 0))


def affine(a, b, part):
    rows, size = a.shape
    height = rows // THIRDS[part][1]
    return call(
        affine_kernel, "affine", struct(height, size), 18, height / rows, 2,
        grid=(1,),
        in_specs=[row_part(part, rows, size), pl.BlockSpec((size, size), lambda r: (0, 0))],
        out_specs=pl.BlockSpec((height, size), lambda r: (0, 0)),
        scratch_shapes=[pltpu.VMEM((height, size), BF16)] * 2,
    )(a, b)


def affine_parts_kernel(ah, al, b_ref, out_ref):
    def step(c):
        product = mm((ah[...], al[...]), split(b_ref[:, c]))
        out_ref[:, c] = 1.5 * (ah[:, c].astype(F32) + al[:, c].astype(F32)) - 0.5 * product

    tiles(out_ref.shape[1], min(512, out_ref.shape[0]), step)


def affine_parts(ah, al, b, part):
    rows, size = ah.shape
    height = rows // THIRDS[part][1]
    return call(
        affine_parts_kernel, "affine_parts", struct(height, size), 18, height / rows, 2,
        grid=(1,),
        in_specs=[row_part(part, rows, size)] * 2
        + [pl.BlockSpec((size, size), lambda r: (0, 0))],
        out_specs=pl.BlockSpec((height, size), lambda r: (0, 0)),
    )(ah, al, b)


SPANS = (
    (((0, 4),), ((0, 1),), ((0, 1),), ((0, 1), (3, 4))),
    ((), ((1, 4),), ((1, 4),), ((1, 3),)),
)


def sym_product(ah, al, hi, lo, chunk, column, rows=slice(None)):
    q = hi.shape[0] // 4
    spans = [slice(k0 * q, k1 * q) for k0, k1 in SPANS[chunk][column]]
    c = slice(column * q, (column + 1) * q)
    a = [ref[rows, k] for ref in (ah, ah, al) for k in spans]
    b = [ref[k, c] for ref in (hi, lo, hi) for k in spans]
    return c, jnp.dot(
        jnp.concatenate(a, axis=1), jnp.concatenate(b, axis=0), preferred_element_type=F32
    )


def apply_first(base_refs, out_ref, ah, al, hi, lo, columns):
    q = hi.shape[0] // 4
    for column in columns:
        c, product = sym_product(ah, al, hi, lo, 0, column)
        out = slice(c.start - columns[0] * q, c.stop - columns[0] * q)
        at = 0
        for base_ref in base_refs:
            end = at + base_ref.shape[0]
            out_ref[at:end, out] = base_ref[:, c] - 0.5 * product[at:end]
            at = end


def sym_scratch(size, shards):
    return [pltpu.VMEM((size, size), BF16)] * 2 + [packed_scratch(size, shards)]


def first_part_kernel(shards, count, columns, me_ref, *refs):
    pieces, refs = refs[:count], refs[count:]
    ah, al, base_refs, (out_ref, hi, lo, packed) = refs[0], refs[1], refs[2:-4], refs[-4:]
    unpack(pieces, packed, hi, lo, me_ref[0], shards, 0)
    apply_first(base_refs, out_ref, ah, al, hi, lo, columns)


def first_part(me, shards, pieces, ah, al, base, columns):
    rows, size = ah.shape
    part = struct(size, size, dtype=BF16)
    more = len(columns) < 4
    scratch = sym_scratch(size, shards)
    return call(
        functools.partial(first_part_kernel, shards, len(pieces), columns), "first_part",
        [struct(rows, len(columns) * size // 4)] + [part, part] * more, 18, 0.5, 3,
        in_specs=[SMEM] + [VMEM] * (len(pieces) + 2 + len(base)),
        out_specs=[VMEM] * (1 + 2 * more),
        scratch_shapes=scratch[2 * more:],
    )(me, *pieces, ah, al, *base)


def other_part_kernel(columns, ah, al, hi, lo, *refs):
    apply_first(refs[:-1], refs[-1], ah, al, hi, lo, columns)


def other_part(ah, al, hi, lo, base, columns):
    rows, size = ah.shape
    return call(
        functools.partial(other_part_kernel, columns), "other_part",
        struct(rows, len(columns) * size // 4), 16, 0.25, 3,
        in_specs=[VMEM] * (4 + len(base)),
        out_specs=VMEM,
    )(ah, al, hi, lo, *base)


def column_kernel(xh, xl, mid_ref, col_ref):
    col_ref[...] = mm((xh[...], xl[...]), split(mid_ref[...]))


def column_product(xh, xl, mid):
    size, rows = xh.shape
    block = pl.BlockSpec((rows, size // 4), lambda r: (0, 0))
    whole = pl.BlockSpec((size, rows), lambda r: (0, 0))
    return call(
        column_kernel, "column_product", struct(size, size // 4), 16, 0.25, 2,
        grid=(1,), in_specs=[whole, whole, block], out_specs=block,
    )(xh, xl, mid)


def turn_kernel(x_ref, xh, xl):
    def step(r):
        xh[:, r], xl[:, r] = split(x_ref[r].T)

    tiles(x_ref.shape[0], 256, step)


def turn(x):
    part = struct(*x.shape[::-1], dtype=BF16)
    return call(
        turn_kernel, "turn", [part, part], 16, 0.1, 2, in_specs=[VMEM], out_specs=[VMEM] * 2
    )(x)


def cut_kernel(x_ref, hi, lo):
    def step(r):
        hi[r], lo[r] = split(x_ref[r])

    tiles(x_ref.shape[0], 128, step)


def cut(x):
    part = struct(*x.shape, dtype=BF16)
    return call(
        cut_kernel, "cut", [part, part], 16, 0.1, 2, in_specs=[VMEM], out_specs=[VMEM] * 2
    )(x)


def second_gram_kernel(shards, count, me_ref, *refs):
    pieces, refs = refs[:count], refs[count:]
    (ah, al, base_ref, xh, xl, col_ref), refs = refs[:6], refs[6:]
    keep_ref, send_ref, rest_ref, mh, ml, hi, lo, packed, g = refs
    size = g.shape[0]
    q = size // 4
    unpack(pieces, packed, hi, lo, me_ref[0], shards, 1)
    mh[:, :q], ml[:, :q] = split(base_ref[:, :q])
    for column in range(1, 4):
        c, product = sym_product(ah, al, hi, lo, 1, column)
        mid = base_ref[:, c] - 0.5 * product
        mh[:, c], ml[:, c] = split(mid)
    g[:, :q] = col_ref[...]
    outer = mm(outer_rows(xh, xl), (mh[:, q:], ml[:, q:]))
    g[:q, q:] = outer[:q]
    g[3 * q:, q:] = outer[q:]
    rest_ref[...] = outer[q:, :2 * q]
    pack(g, packed, keep_ref, send_ref, me_ref[0], shards, 0)


def second_gram(me, shards, pieces, ah, al, base, xh, xl, col):
    rows, size = ah.shape
    part = struct(rows, size, dtype=BF16)
    return call(
        functools.partial(second_gram_kernel, shards, len(pieces)), "second_gram",
        halves(size, shards) + [rest_shape(size), part, part], 20, 0.8, 5,
        in_specs=[SMEM] + [VMEM] * (len(pieces) + 6),
        out_specs=[VMEM] * 5,
        scratch_shapes=sym_scratch(size, shards) + [pltpu.VMEM((size, size), F32)],
    )(me, *pieces, ah, al, base, xh, xl, col)


def last_kernel(shards, count, me_ref, *refs):
    pieces = refs[:count]
    ah, al, z_ref, rest_ref, out_hbm, hi, lo, packed, out, sems = refs[count:]
    q = hi.shape[0] // 4
    copies = []

    def send(src, rows, c):
        copy = pltpu.make_async_copy(src, out_hbm.at[rows, c], sems.at[len(copies)])
        copy.start()
        copies.append(copy)

    count = out.shape[0]
    send(z_ref, slice(0, count), slice(0, q))
    unpack(pieces, packed, hi, lo, me_ref[0], shards, 1)
    for column in (1, 2, 3):
        parts = 2 if column == 3 else 1
        for part in range(parts):
            r = slice(part * count // parts, (part + 1) * count // parts)
            c, product = sym_product(ah, al, hi, lo, 1, column, r)
            out[r, c] = rest_ref[r, c.start - q:c.stop - q] - 0.5 * product
            send(out.at[r, c], r, c)
    for copy in copies:
        copy.wait()


def last_step(me, shards, pieces, ah, al, z, rest):
    rows, size = ah.shape
    return call(
        functools.partial(last_kernel, shards, len(pieces)), "last", struct(rows, size), 22, 0.5, 3,
        in_specs=[SMEM] + [VMEM] * (len(pieces) + 4),
        out_specs=pl.BlockSpec(memory_space=pltpu.HBM),
        scratch_shapes=sym_scratch(size, shards)
        + [pltpu.VMEM((rows, size), F32), pltpu.SemaphoreType.DMA((5,))],
    )(me, *pieces, ah, al, z, rest)


CORE = 1
PLANE = (2, 4, 6)
SHARDS = 2 * (1 + len(PLANE))


def slot_of(index):
    return (index % 2) * (SHARDS // 2) + (index // 2) % (SHARDS // 2)


class Sum:
    def __init__(self, count, keep, send):
        self.count, self.keep, self.send = count, keep, send

    def swap(self, x, offset):
        return lax.ppermute(x, "row", [(i, i ^ offset) for i in range(self.count)])

    def swaps(self, values):
        return [self.swap(x, offset) for x, offset in zip(values, PLANE)]

    def core(self):
        return self.swap(self.send, CORE)

    def plane(self, got):
        total = self.keep + got
        part = total.shape[0] // (1 + len(PLANE))
        self.keep, *sends = [total[k * part:(k + 1) * part] for k in range(1 + len(PLANE))]
        return self.swaps(sends)

    def own(self, got):
        self.keep = sum(got, self.keep)

    def exchange(self, offset):
        return self.swap(self.keep, offset)

    def gather_plane(self):
        return self.swaps([self.keep] * len(PLANE))

    def gather_core(self, got):
        self.mine = jnp.concatenate([self.keep, *got], axis=0)
        return self.swap(self.mine, CORE)


def close(env, *got):
    values = lax.optimization_barrier((*env.values(), *got[::-1]))
    env.update(zip(env, values))
    return values[len(env):][::-1]


def sum_chunks(count, env, first, second, works, late):
    beyond = [1 << s for s in range(3, count.bit_length() - 1)]
    works = list(works)

    def work():
        if works:
            works.pop(0)(env)

    a = Sum(count, *first)
    got_a = a.core()
    pair = second(env)
    got_a, *pair = close(env, got_a, *pair)
    b = Sum(count, *pair)

    got_a = a.plane(got_a)
    got_b = b.core()
    work()
    (got_b,) = close(env, got_b)

    got_b = b.plane(got_b)
    work()
    a.own(close(env, *got_a))

    for offset in beyond:
        got_a = a.exchange(offset)
        work()
        b.own(close(env, *got_b))
        got_b = [b.exchange(offset)]
        a.own(close(env, got_a))

    got_a = a.gather_plane()
    b.own(close(env, *got_b))

    got_b = b.gather_plane()
    got_a = a.gather_core(close(env, *got_a))
    work()
    (got_a,) = close(env, got_a)
    late[0](env, [a.mine, got_a])
    got_b = b.gather_core(close(env, *got_b))
    late[1](env)
    (got_b,) = close(env, got_b)
    return [b.mine, got_b]


def body(count, orbitals_zero, orbitals_one, correlation_zero, correlation_one, cotangent):
    me = slot_of(lax.axis_index("row")).astype(jnp.int32).reshape(1)
    env = dict(
        x0=orbitals_zero, x1=orbitals_one, s0=correlation_zero, s1=correlation_one, c=cotangent
    )

    def direct(part):
        def work(env):
            env[f"m{part}"] = affine(env["c"], env["s1"], part)
        return work

    def direct_and_turn(env):
        direct(2)(env)
        env["xh"], env["xl"] = turn(env["x0"])

    def cut_one(env):
        env["x1h"], env["x1l"] = cut(env["x1"])

    def middle(env, pieces):
        (env["mid"],) = first_part(
            me, SHARDS, pieces, env["x1h"], env["x1l"], [env["m0"], env["m1"], env["m2"]], (0, 1, 2, 3)
        )

    def column(env):
        env["col"] = column_product(env["xh"], env["xl"], env["mid"])

    keep, send, *parts = first_gram(me, SHARDS, env["x1"], env["c"])
    one = sum_chunks(
        count, env, (keep, send), lambda env: inner_gram(me, SHARDS, *parts),
        [direct(0), direct(1), direct_and_turn, cut_one], [middle, column],
    )

    keep, send, rest_two, env["mh"], env["ml"] = second_gram(
        me, SHARDS, one, env["x1h"], env["x1l"], env["mid"], env["xh"], env["xl"], env["col"]
    )

    def last_direct(part):
        def work(env):
            env[f"d{part}"] = affine_parts(env["mh"], env["ml"], env["s0"], part)
        return work

    def cut_zero(env):
        env["x0h"], env["x0l"] = cut(env["x0"])

    def three(name):
        return [env[f"{name}{part}"] for part in range(3)]

    def result(env, pieces):
        env["z"], env["symh"], env["syml"] = first_part(
            me, SHARDS, pieces, env["x0h"], env["x0l"], three("d"), (0,)
        )

    def rest(env):
        env["rest"] = other_part(
            env["x0h"], env["x0l"], env["symh"], env["syml"], three("d"), (1, 2, 3)
        )

    two = sum_chunks(
        count, env, (keep, send),
        lambda env: inner_gram(
            me, SHARDS, rest_two, env["xh"], env["xl"], env["mh"], env["ml"]
        ),
        [last_direct(0), last_direct(1), last_direct(2), cut_zero], [result, rest],
    )
    return last_step(me, SHARDS, two, env["x0h"], env["x0l"], env["z"], env["rest"])


def solution(mesh):
    in_specs = (
        P(("kpt", "row"), None),
        P(("kpt", "row"), None),
        P("kpt", None),
        P("kpt", None),
        P(("kpt", "row"), None),
    )
    out_specs = P(("kpt", "row"), None)
    return jax.shard_map(
        functools.partial(body, mesh.shape["row"]),
        mesh=mesh, in_specs=in_specs, out_specs=out_specs, check_vma=False,
    )
```

```python
import functools
import jax
import jax.numpy as jnp
from jax import lax
from jax.experimental import pallas as pl
from jax.experimental.pallas import tpu as pltpu
from jax.sharding import PartitionSpec as P

F32 = jnp.float32
BF16 = jnp.bfloat16
B = 128
MIB = 1024 * 1024
WEIGHT = 10


def split(x):
    hi = x.astype(BF16)
    return hi, (x - hi.astype(F32)).astype(BF16)


def mm(a, b):
    (ah, al), (bh, bl) = a, b
    return jnp.dot(
        jnp.concatenate([ah, ah, al], axis=1),
        jnp.concatenate([bh, bl, bh], axis=0),
        preferred_element_type=F32,
    )


def call(kernel, name, out_shape, limit, products, arrays, **kw):
    size = 1024
    return pl.pallas_call(
        kernel,
        name=name,
        out_shape=out_shape,
        compiler_params=pltpu.CompilerParams(vmem_limit_bytes=limit * MIB),
        cost_estimate=pl.CostEstimate(
            flops=int(WEIGHT * 6 * products * size ** 3),
            bytes_accessed=int(WEIGHT * 4 * arrays * size * size),
            transcendentals=0,
        ),
        **kw,
    )


def struct(*shape, dtype=F32):
    return jax.ShapeDtypeStruct(shape, dtype)


SMEM = pl.BlockSpec(memory_space=pltpu.SMEM)
VMEM = pl.BlockSpec(memory_space=pltpu.VMEM)


def chunk_lines(size, chunk):
    half = size // B // 4
    return range(chunk * half, (chunk + 1) * half)


def line_blocks(size, i):
    n = size // B
    block = lambda k: slice(k * B, (k + 1) * B)
    return [(block(top), block(j)) for top in (i, n - 1 - i) for j in range(top + 1, n)]


def diagonal_blocks(size, i):
    n = size // B
    return [slice(k * B, (k + 1) * B) for k in (i, n - 1 - i)]


def part_rows(size, shards):
    return size // 4 // shards


def shard_rows(size, shards):
    return part_rows(size, shards) * (size // B) + 8


def places():
    row = lax.broadcasted_iota(jnp.int32, (B, B), 0)
    column = lax.broadcasted_iota(jnp.int32, (B, B), 1)
    return row, column


def pack(g, packed, keep_ref, send_ref, me, shards, chunk):
    size = g.shape[0]
    rows, height = part_rows(size, shards), shard_rows(size, shards)
    per = B // rows
    row, column = places()
    whole = lambda p, q: g[p, q] + g[q, p].T
    for line, i in enumerate(chunk_lines(size, chunk)):
        starts = [((line * per + s) ^ me) * height for s in range(per)]

        def put(at, s, value):
            start = pl.multiple_of(starts[s] + at, 8)
            packed[pl.ds(start, value.shape[0]), :] = value

        upper, lower = [whole(p, p) for p in diagonal_blocks(size, i)]
        for k, place in enumerate([None] + line_blocks(size, i)):
            block = whole(*place) if place else jnp.where(column >= row, upper, lower)
            for s in range(per):
                put(k * rows, s, block[s * rows:(s + 1) * rows])
        element = jnp.sum(jnp.where(column == row, lower, 0.0), axis=0, keepdims=True)
        for s in range(per):
            put(height - 8, s, jnp.broadcast_to(element, (8, B)))
    half = keep_ref.shape[0]
    keep_ref[...] = packed[:half]
    send_ref[...] = packed[half:]


def unpack(pieces, packed, hi, lo, me, shards, chunk):
    size = hi.shape[0]
    rows, height = part_rows(size, shards), shard_rows(size, shards)
    per = B // rows
    row, column = places()
    slot = 0
    for piece in pieces:
        for s in range(piece.shape[0] // height):
            at = pl.multiple_of((slot ^ me) * height, 8)
            packed[pl.ds(at, height), :] = piece[s * height:(s + 1) * height, :]
            slot += 1

    def put(p, q, block):
        hi[p, q], lo[p, q] = split(block)

    for line, i in enumerate(chunk_lines(size, chunk)):
        start = line * per * height

        def get(k):
            return jnp.concatenate(
                [
                    packed[start + s * height + k * rows:start + s * height + (k + 1) * rows, :]
                    for s in range(per)
                ],
                axis=0,
            )

        first, last = diagonal_blocks(size, i)
        block = get(0)
        turned = block.T
        element = packed[start + height - 8:start + height - 7, :]
        put(first, first, jnp.where(column >= row, block, turned))
        below = jnp.where(column < row, block, turned)
        put(last, last, jnp.where(column == row, jnp.broadcast_to(element, (B, B)), below))
        for k, (p, q) in enumerate(line_blocks(size, i)):
            block = get(k + 1)
            put(p, q, block)
            put(q, p, block.T)


def packed_scratch(size, shards):
    return pltpu.VMEM((shards * shard_rows(size, shards), B), F32)


def halves(size, shards):
    return [struct(shards // 2 * shard_rows(size, shards), B)] * 2


def first_gram_kernel(
    shards, me_ref, a_hbm, b_hbm, keep_ref, send_ref, ah, al, bh, bl, a_buf, b_buf, sems, g, packed
):
    rows, size = a_buf.shape
    q = size // 4
    steps = sems.shape[1]
    tile = rows // steps

    def copies(step):
        r = slice(step * tile, (step + 1) * tile)
        return [
            pltpu.make_async_copy(src.at[r], dst.at[r], sems.at[k, step])
            for k, (src, dst) in enumerate([(a_hbm, a_buf), (b_hbm, b_buf)])
        ]

    def start(step):
        for copy in copies(step):
            copy.start()

    start(0)
    start(1)
    for step in range(steps):
        r = slice(step * tile, (step + 1) * tile)
        for copy in copies(step):
            copy.wait()
        if step + 2 < steps:
            start(step + 2)
        ah[:, r], al[:, r] = split(a_buf[r].T)
        bh[r], bl[r] = split(b_buf[r])
        for r0, r1, c0, c1 in [(0, q, 0, size), (q, size, 0, q), (3 * q, size, 3 * q, size)]:
            product = mm((ah[r0:r1, r], al[r0:r1, r]), (bh[r, c0:c1], bl[r, c0:c1]))
            if step:
                product += g[r0:r1, c0:c1]
            g[r0:r1, c0:c1] = product
    pack(g, packed, keep_ref, send_ref, me_ref[0], shards, 0)


def first_gram(me, shards, a, b):
    rows, size = a.shape
    hbm = pl.BlockSpec(memory_space=pltpu.HBM)
    return call(
        functools.partial(first_gram_kernel, shards), "first_gram",
        halves(size, shards) + [struct(size, rows, dtype=BF16)] * 2 + [struct(rows, size, dtype=BF16)] * 2,
        43, 0.5, 4,
        in_specs=[SMEM, hbm, hbm],
        out_specs=[VMEM] * 6,
        scratch_shapes=[
            pltpu.VMEM((rows, size), F32), pltpu.VMEM((rows, size), F32),
            pltpu.SemaphoreType.DMA((2, 4)),
            pltpu.VMEM((size, size), F32), packed_scratch(size, shards),
        ],
    )(me, a, b)


def lower_product(g, ah, al, bh, bl):
    size = g.shape[0]
    q = size // 4
    for r0, r1, c0, c1 in [(q, 3 * q, q, size), (3 * q, size, q, 3 * q)]:
        c = slice(c0 - q, c1 - q)
        g[r0:r1, c0:c1] = mm((ah[r0:r1, :], al[r0:r1, :]), (bh[:, c], bl[:, c]))


def other_gram_kernel(shards, me_ref, ah, al, bh, bl, keep_ref, send_ref, g, packed):
    q = g.shape[0] // 4
    lower_product(g, ah, al, bh[:, q:], bl[:, q:])
    pack(g, packed, keep_ref, send_ref, me_ref[0], shards, 1)


def other_gram(me, shards, ah, al, bh, bl):
    size = ah.shape[0]
    return call(
        functools.partial(other_gram_kernel, shards), "other_gram", halves(size, shards), 18, 0.5, 2,
        in_specs=[SMEM] + [VMEM] * 4,
        out_specs=[VMEM, VMEM],
        scratch_shapes=[pltpu.VMEM((size, size), F32), packed_scratch(size, shards)],
    )(me, ah, al, bh, bl)


def tiles(count, tile, step):
    def body(t, _):
        step(pl.ds(pl.multiple_of(t * tile, tile), tile))
        return 0

    lax.fori_loop(0, count // tile, body, 0)


def affine_kernel(a_ref, b_ref, out_ref, hi, lo):
    hi[...], lo[...] = split(a_ref[...])

    def step(c):
        out_ref[:, c] = 1.5 * a_ref[:, c] - 0.5 * mm((hi[...], lo[...]), split(b_ref[:, c]))

    tiles(out_ref.shape[1], min(512, out_ref.shape[0]), step)


THIRDS = ((0, 4), (1, 4), (1, 2))


def row_part(part, rows, size):
    at, parts = THIRDS[part]
    return pl.BlockSpec((rows // parts, size), lambda r: (at, 0))


def affine(a, b, part):
    rows, size = a.shape
    height = rows // THIRDS[part][1]
    return call(
        affine_kernel, "affine", struct(height, size), 18, height / rows, 2,
        grid=(1,),
        in_specs=[row_part(part, rows, size), pl.BlockSpec((size, size), lambda r: (0, 0))],
        out_specs=pl.BlockSpec((height, size), lambda r: (0, 0)),
        scratch_shapes=[pltpu.VMEM((height, size), BF16)] * 2,
    )(a, b)


def affine_parts_kernel(ah, al, b_ref, out_ref):
    def step(c):
        product = mm((ah[...], al[...]), split(b_ref[:, c]))
        out_ref[:, c] = 1.5 * (ah[:, c].astype(F32) + al[:, c].astype(F32)) - 0.5 * product

    tiles(out_ref.shape[1], min(512, out_ref.shape[0]), step)


def affine_parts(ah, al, b, part):
    rows, size = ah.shape
    height = rows // THIRDS[part][1]
    return call(
        affine_parts_kernel, "affine_parts", struct(height, size), 18, height / rows, 2,
        grid=(1,),
        in_specs=[row_part(part, rows, size)] * 2
        + [pl.BlockSpec((size, size), lambda r: (0, 0))],
        out_specs=pl.BlockSpec((height, size), lambda r: (0, 0)),
    )(ah, al, b)


SPANS = (
    (((0, 4),), ((0, 1),), ((0, 1),), ((0, 1), (3, 4))),
    ((), ((1, 4),), ((1, 4),), ((1, 3),)),
)


def sym_product(ah, al, hi, lo, chunk, column, rows=slice(None)):
    q = hi.shape[0] // 4
    spans = [slice(k0 * q, k1 * q) for k0, k1 in SPANS[chunk][column]]
    c = slice(column * q, (column + 1) * q)
    a = [ref[rows, k] for ref in (ah, ah, al) for k in spans]
    b = [ref[k, c] for ref in (hi, lo, hi) for k in spans]
    return c, jnp.dot(
        jnp.concatenate(a, axis=1), jnp.concatenate(b, axis=0), preferred_element_type=F32
    )


def apply_first(base_refs, out_ref, ah, al, hi, lo, columns):
    q = hi.shape[0] // 4
    for column in columns:
        c, product = sym_product(ah, al, hi, lo, 0, column)
        out = slice(c.start - columns[0] * q, c.stop - columns[0] * q)
        at = 0
        for base_ref in base_refs:
            end = at + base_ref.shape[0]
            out_ref[at:end, out] = base_ref[:, c] - 0.5 * product[at:end]
            at = end


def sym_scratch(size, shards):
    return [pltpu.VMEM((size, size), BF16)] * 2 + [packed_scratch(size, shards)]


def first_part_kernel(shards, count, columns, me_ref, *refs):
    pieces, refs = refs[:count], refs[count:]
    ah, al, base_refs, (out_ref, hi, lo, packed) = refs[0], refs[1], refs[2:-4], refs[-4:]
    unpack(pieces, packed, hi, lo, me_ref[0], shards, 0)
    apply_first(base_refs, out_ref, ah, al, hi, lo, columns)


def first_part(me, shards, pieces, ah, al, base, columns):
    rows, size = ah.shape
    part = struct(size, size, dtype=BF16)
    more = len(columns) < 4
    scratch = sym_scratch(size, shards)
    return call(
        functools.partial(first_part_kernel, shards, len(pieces), columns), "first_part",
        [struct(rows, len(columns) * size // 4)] + [part, part] * more, 18, 0.5, 3,
        in_specs=[SMEM] + [VMEM] * (len(pieces) + 2 + len(base)),
        out_specs=[VMEM] * (1 + 2 * more),
        scratch_shapes=scratch[2 * more:],
    )(me, *pieces, ah, al, *base)


def other_part_kernel(columns, ah, al, hi, lo, *refs):
    apply_first(refs[:-1], refs[-1], ah, al, hi, lo, columns)


def other_part(ah, al, hi, lo, base, columns):
    rows, size = ah.shape
    return call(
        functools.partial(other_part_kernel, columns), "other_part",
        struct(rows, len(columns) * size // 4), 16, 0.25, 3,
        in_specs=[VMEM] * (4 + len(base)),
        out_specs=VMEM,
    )(ah, al, hi, lo, *base)


def column_kernel(xh, xl, mid_ref, col_ref):
    col_ref[...] = mm((xh[...], xl[...]), split(mid_ref[...]))


def column_product(xh, xl, mid):
    size, rows = xh.shape
    block = pl.BlockSpec((rows, size // 4), lambda r: (0, 0))
    whole = pl.BlockSpec((size, rows), lambda r: (0, 0))
    return call(
        column_kernel, "column_product", struct(size, size // 4), 16, 0.25, 2,
        grid=(1,), in_specs=[whole, whole, block], out_specs=block,
    )(xh, xl, mid)


def turn_kernel(x_ref, xh, xl):
    def step(r):
        xh[:, r], xl[:, r] = split(x_ref[r].T)

    tiles(x_ref.shape[0], 256, step)


def turn(x):
    part = struct(*x.shape[::-1], dtype=BF16)
    return call(
        turn_kernel, "turn", [part, part], 16, 0.1, 2, in_specs=[VMEM], out_specs=[VMEM] * 2
    )(x)


def cut_kernel(x_ref, hi, lo):
    def step(r):
        hi[r], lo[r] = split(x_ref[r])

    tiles(x_ref.shape[0], 128, step)


def cut(x):
    part = struct(*x.shape, dtype=BF16)
    return call(
        cut_kernel, "cut", [part, part], 16, 0.1, 2, in_specs=[VMEM], out_specs=[VMEM] * 2
    )(x)


def second_gram_kernel(shards, count, me_ref, *refs):
    pieces, refs = refs[:count], refs[count:]
    (ah, al, base_ref, xh, xl, col_ref), refs = refs[:6], refs[6:]
    keep_ref, send_ref, mh, ml, hi, lo, packed, g = refs
    size = g.shape[0]
    q = size // 4
    unpack(pieces, packed, hi, lo, me_ref[0], shards, 1)
    mh[:, :q], ml[:, :q] = split(base_ref[:, :q])
    for column in range(1, 4):
        c, product = sym_product(ah, al, hi, lo, 1, column)
        mid = base_ref[:, c] - 0.5 * product
        mh[:, c], ml[:, c] = split(mid)
    g[:, :q] = col_ref[...]
    g[:q, q:] = mm((xh[:q, :], xl[:q, :]), (mh[:, q:], ml[:, q:]))
    g[3 * q:, 3 * q:] = mm((xh[3 * q:, :], xl[3 * q:, :]), (mh[:, 3 * q:], ml[:, 3 * q:]))
    pack(g, packed, keep_ref, send_ref, me_ref[0], shards, 0)


def second_gram(me, shards, pieces, ah, al, base, xh, xl, col):
    rows, size = ah.shape
    part = struct(rows, size, dtype=BF16)
    return call(
        functools.partial(second_gram_kernel, shards, len(pieces)), "second_gram",
        halves(size, shards) + [part, part], 20, 0.8, 5,
        in_specs=[SMEM] + [VMEM] * (len(pieces) + 6),
        out_specs=[VMEM] * 4,
        scratch_shapes=sym_scratch(size, shards) + [pltpu.VMEM((size, size), F32)],
    )(me, *pieces, ah, al, base, xh, xl, col)


def fourth_gram_kernel(shards, me_ref, xh, xl, mh, ml, keep_ref, send_ref, g, packed):
    q = g.shape[0] // 4
    lower_product(g, xh, xl, mh[:, q:], ml[:, q:])
    pack(g, packed, keep_ref, send_ref, me_ref[0], shards, 1)


def fourth_gram(me, shards, xh, xl, mh, ml):
    size = xh.shape[0]
    return call(
        functools.partial(fourth_gram_kernel, shards), "fourth_gram", halves(size, shards), 18, 0.5, 2,
        in_specs=[SMEM] + [VMEM] * 4,
        out_specs=[VMEM, VMEM],
        scratch_shapes=[pltpu.VMEM((size, size), F32), packed_scratch(size, shards)],
    )(me, xh, xl, mh, ml)


def last_kernel(shards, count, me_ref, *refs):
    pieces = refs[:count]
    ah, al, z_ref, rest_ref, out_hbm, hi, lo, packed, out, sems = refs[count:]
    q = hi.shape[0] // 4
    copies = []

    def send(src, rows, c):
        copy = pltpu.make_async_copy(src, out_hbm.at[rows, c], sems.at[len(copies)])
        copy.start()
        copies.append(copy)

    count = out.shape[0]
    send(z_ref, slice(0, count), slice(0, q))
    unpack(pieces, packed, hi, lo, me_ref[0], shards, 1)
    for column in (1, 2, 3):
        parts = 2 if column == 3 else 1
        for part in range(parts):
            r = slice(part * count // parts, (part + 1) * count // parts)
            c, product = sym_product(ah, al, hi, lo, 1, column, r)
            out[r, c] = rest_ref[r, c.start - q:c.stop - q] - 0.5 * product
            send(out.at[r, c], r, c)
    for copy in copies:
        copy.wait()


def last_step(me, shards, pieces, ah, al, z, rest):
    rows, size = ah.shape
    return call(
        functools.partial(last_kernel, shards, len(pieces)), "last", struct(rows, size), 22, 0.5, 3,
        in_specs=[SMEM] + [VMEM] * (len(pieces) + 4),
        out_specs=pl.BlockSpec(memory_space=pltpu.HBM),
        scratch_shapes=sym_scratch(size, shards)
        + [pltpu.VMEM((rows, size), F32), pltpu.SemaphoreType.DMA((5,))],
    )(me, *pieces, ah, al, z, rest)


CORE = 1
PLANE = (2, 4, 6)
SHARDS = 2 * (1 + len(PLANE))


def slot_of(index):
    return (index % 2) * (SHARDS // 2) + (index // 2) % (SHARDS // 2)


class Sum:
    def __init__(self, count, keep, send):
        self.count, self.keep, self.send = count, keep, send

    def swap(self, x, offset):
        return lax.ppermute(x, "row", [(i, i ^ offset) for i in range(self.count)])

    def swaps(self, values):
        return [self.swap(x, offset) for x, offset in zip(values, PLANE)]

    def core(self):
        return self.swap(self.send, CORE)

    def plane(self, got):
        total = self.keep + got
        part = total.shape[0] // (1 + len(PLANE))
        self.keep, *sends = [total[k * part:(k + 1) * part] for k in range(1 + len(PLANE))]
        return self.swaps(sends)

    def own(self, got):
        self.keep = sum(got, self.keep)

    def exchange(self, offset):
        return self.swap(self.keep, offset)

    def gather_plane(self):
        return self.swaps([self.keep] * len(PLANE))

    def gather_core(self, got):
        self.mine = jnp.concatenate([self.keep, *got], axis=0)
        return self.swap(self.mine, CORE)


def close(env, *got):
    values = lax.optimization_barrier((*env.values(), *got[::-1]))
    env.update(zip(env, values))
    return values[len(env):][::-1]


def sum_chunks(count, env, first, second, works, late):
    beyond = [1 << s for s in range(3, count.bit_length() - 1)]
    works = list(works)

    def work():
        if works:
            works.pop(0)(env)

    a = Sum(count, *first)
    got_a = a.core()
    pair = second(env)
    got_a, *pair = close(env, got_a, *pair)
    b = Sum(count, *pair)

    got_a = a.plane(got_a)
    got_b = b.core()
    work()
    (got_b,) = close(env, got_b)

    got_b = b.plane(got_b)[::-1]
    work()
    a.own(close(env, *got_a))

    for offset in beyond:
        got_a = a.exchange(offset)
        work()
        b.own(close(env, *got_b))
        got_b = [b.exchange(offset)]
        a.own(close(env, got_a))

    got_a = a.gather_plane()
    b.own(close(env, *got_b))

    got_b = b.gather_plane()[::-1]
    got_a = a.gather_core(close(env, *got_a))
    work()
    (got_a,) = close(env, got_a)
    late[0](env, [a.mine, got_a])
    got_b = b.gather_core(close(env, *got_b)[::-1])
    late[1](env)
    (got_b,) = close(env, got_b)
    return [b.mine, got_b]


def body(count, orbitals_zero, orbitals_one, correlation_zero, correlation_one, cotangent):
    me = slot_of(lax.axis_index("row")).astype(jnp.int32).reshape(1)
    env = dict(
        x0=orbitals_zero, x1=orbitals_one, s0=correlation_zero, s1=correlation_one, c=cotangent
    )

    def direct(part):
        def work(env):
            env[f"m{part}"] = affine(env["c"], env["s1"], part)
        return work

    def direct_and_turn(env):
        direct(2)(env)
        env["xh"], env["xl"] = turn(env["x0"])

    def cut_one(env):
        env["x1h"], env["x1l"] = cut(env["x1"])

    def middle(env, pieces):
        (env["mid"],) = first_part(
            me, SHARDS, pieces, env["x1h"], env["x1l"], [env["m0"], env["m1"], env["m2"]], (0, 1, 2, 3)
        )

    def column(env):
        env["col"] = column_product(env["xh"], env["xl"], env["mid"])

    keep, send, *parts = first_gram(me, SHARDS, env["x1"], env["c"])
    one = sum_chunks(
        count, env, (keep, send), lambda env: other_gram(me, SHARDS, *parts),
        [direct(0), direct(1), direct_and_turn, cut_one], [middle, column],
    )

    keep, send, env["mh"], env["ml"] = second_gram(
        me, SHARDS, one, env["x1h"], env["x1l"], env["mid"], env["xh"], env["xl"], env["col"]
    )

    def last_direct(part):
        def work(env):
            env[f"d{part}"] = affine_parts(env["mh"], env["ml"], env["s0"], part)
        return work

    def cut_zero(env):
        env["x0h"], env["x0l"] = cut(env["x0"])

    def three(name):
        return [env[f"{name}{part}"] for part in range(3)]

    def result(env, pieces):
        env["z"], env["symh"], env["syml"] = first_part(
            me, SHARDS, pieces, env["x0h"], env["x0l"], three("d"), (0,)
        )

    def rest(env):
        env["rest"] = other_part(
            env["x0h"], env["x0l"], env["symh"], env["syml"], three("d"), (1, 2, 3)
        )

    two = sum_chunks(
        count, env, (keep, send),
        lambda env: fourth_gram(me, SHARDS, env["xh"], env["xl"], env["mh"], env["ml"]),
        [last_direct(0), last_direct(1), last_direct(2), cut_zero], [result, rest],
    )
    return last_step(me, SHARDS, two, env["x0h"], env["x0l"], env["z"], env["rest"])


def solution(mesh):
    in_specs = (
        P(("kpt", "row"), None),
        P(("kpt", "row"), None),
        P("kpt", None),
        P("kpt", None),
        P(("kpt", "row"), None),
    )
    out_specs = P(("kpt", "row"), None)
    return jax.shard_map(
        functools.partial(body, mesh.shape["row"]),
        mesh=mesh, in_specs=in_specs, out_specs=out_specs, check_vma=False,
    )
```

```python
import functools
import jax
import jax.numpy as jnp
from jax import lax
from jax.experimental import pallas as pl
from jax.experimental.pallas import tpu as pltpu
from jax.sharding import PartitionSpec as P

F32 = jnp.float32
BF16 = jnp.bfloat16
B = 128
MIB = 1024 * 1024
WEIGHT = 10


def split(x):
    hi = x.astype(BF16)
    return hi, (x - hi.astype(F32)).astype(BF16)


def mm(a, b):
    (ah, al), (bh, bl) = a, b
    return jnp.dot(
        jnp.concatenate([ah, ah, al], axis=1),
        jnp.concatenate([bh, bl, bh], axis=0),
        preferred_element_type=F32,
    )


def call(kernel, name, out_shape, limit, products, arrays, **kw):
    size = 1024
    return pl.pallas_call(
        kernel,
        name=name,
        out_shape=out_shape,
        compiler_params=pltpu.CompilerParams(vmem_limit_bytes=limit * MIB),
        cost_estimate=pl.CostEstimate(
            flops=int(WEIGHT * 6 * products * size ** 3),
            bytes_accessed=int(WEIGHT * 4 * arrays * size * size),
            transcendentals=0,
        ),
        **kw,
    )


def struct(*shape, dtype=F32):
    return jax.ShapeDtypeStruct(shape, dtype)


SMEM = pl.BlockSpec(memory_space=pltpu.SMEM)
VMEM = pl.BlockSpec(memory_space=pltpu.VMEM)


def chunk_lines(size, chunk):
    half = size // B // 4
    return range(chunk * half, (chunk + 1) * half)


def line_blocks(size, i):
    n = size // B
    block = lambda k: slice(k * B, (k + 1) * B)
    return [(block(top), block(j)) for top in (i, n - 1 - i) for j in range(top + 1, n)]


def diagonal_blocks(size, i):
    n = size // B
    return [slice(k * B, (k + 1) * B) for k in (i, n - 1 - i)]


def part_rows(size, shards):
    return size // 4 // shards


def shard_rows(size, shards):
    return part_rows(size, shards) * (size // B) + 8


def places():
    row = lax.broadcasted_iota(jnp.int32, (B, B), 0)
    column = lax.broadcasted_iota(jnp.int32, (B, B), 1)
    return row, column


def pack(g, packed, keep_ref, send_ref, me, shards, chunk):
    size = g.shape[0]
    rows, height = part_rows(size, shards), shard_rows(size, shards)
    per = B // rows
    row, column = places()
    whole = lambda p, q: g[p, q] + g[q, p].T
    for line, i in enumerate(chunk_lines(size, chunk)):
        starts = [((line * per + s) ^ me) * height for s in range(per)]

        def put(at, s, value):
            start = pl.multiple_of(starts[s] + at, 8)
            packed[pl.ds(start, value.shape[0]), :] = value

        upper, lower = [whole(p, p) for p in diagonal_blocks(size, i)]
        for k, place in enumerate([None] + line_blocks(size, i)):
            block = whole(*place) if place else jnp.where(column >= row, upper, lower)
            for s in range(per):
                put(k * rows, s, block[s * rows:(s + 1) * rows])
        element = jnp.sum(jnp.where(column == row, lower, 0.0), axis=0, keepdims=True)
        for s in range(per):
            put(height - 8, s, jnp.broadcast_to(element, (8, B)))
    half = keep_ref.shape[0]
    keep_ref[...] = packed[:half]
    send_ref[...] = packed[half:]


def unpack(pieces, packed, hi, lo, me, shards, chunk):
    size = hi.shape[0]
    rows, height = part_rows(size, shards), shard_rows(size, shards)
    per = B // rows
    row, column = places()
    slot = 0
    for piece in pieces:
        for s in range(piece.shape[0] // height):
            at = pl.multiple_of((slot ^ me) * height, 8)
            packed[pl.ds(at, height), :] = piece[s * height:(s + 1) * height, :]
            slot += 1

    def put(p, q, block):
        hi[p, q], lo[p, q] = split(block)

    for line, i in enumerate(chunk_lines(size, chunk)):
        start = line * per * height

        def get(k):
            return jnp.concatenate(
                [
                    packed[start + s * height + k * rows:start + s * height + (k + 1) * rows, :]
                    for s in range(per)
                ],
                axis=0,
            )

        first, last = diagonal_blocks(size, i)
        block = get(0)
        turned = block.T
        element = packed[start + height - 8:start + height - 7, :]
        put(first, first, jnp.where(column >= row, block, turned))
        below = jnp.where(column < row, block, turned)
        put(last, last, jnp.where(column == row, jnp.broadcast_to(element, (B, B)), below))
        for k, (p, q) in enumerate(line_blocks(size, i)):
            block = get(k + 1)
            put(p, q, block)
            put(q, p, block.T)


def packed_scratch(size, shards):
    return pltpu.VMEM((shards * shard_rows(size, shards), B), F32)


def halves(size, shards):
    return [struct(shards // 2 * shard_rows(size, shards), B)] * 2


def first_gram_kernel(
    shards, me_ref, a_hbm, b_hbm, keep_ref, send_ref, ah, al, bh, bl, a_buf, b_buf, sems, g, packed
):
    rows, size = a_buf.shape
    q = size // 4
    steps = sems.shape[1]
    tile = rows // steps

    def copies(step):
        r = slice(step * tile, (step + 1) * tile)
        return [
            pltpu.make_async_copy(src.at[r], dst.at[r], sems.at[k, step])
            for k, (src, dst) in enumerate([(a_hbm, a_buf), (b_hbm, b_buf)])
        ]

    def start(step):
        for copy in copies(step):
            copy.start()

    start(0)
    start(1)
    for step in range(steps):
        r = slice(step * tile, (step + 1) * tile)
        for copy in copies(step):
            copy.wait()
        if step + 2 < steps:
            start(step + 2)
        ah[:, r], al[:, r] = split(a_buf[r].T)
        bh[r], bl[r] = split(b_buf[r])
        for r0, r1, c0, c1 in [(0, q, 0, size), (q, size, 0, q), (3 * q, size, 3 * q, size)]:
            product = mm((ah[r0:r1, r], al[r0:r1, r]), (bh[r, c0:c1], bl[r, c0:c1]))
            if step:
                product += g[r0:r1, c0:c1]
            g[r0:r1, c0:c1] = product
    pack(g, packed, keep_ref, send_ref, me_ref[0], shards, 0)


def first_gram(me, shards, a, b):
    rows, size = a.shape
    hbm = pl.BlockSpec(memory_space=pltpu.HBM)
    return call(
        functools.partial(first_gram_kernel, shards), "first_gram",
        halves(size, shards) + [struct(size, rows, dtype=BF16)] * 2 + [struct(rows, size, dtype=BF16)] * 2,
        43, 0.5, 4,
        in_specs=[SMEM, hbm, hbm],
        out_specs=[VMEM] * 6,
        scratch_shapes=[
            pltpu.VMEM((rows, size), F32), pltpu.VMEM((rows, size), F32),
            pltpu.SemaphoreType.DMA((2, 4)),
            pltpu.VMEM((size, size), F32), packed_scratch(size, shards),
        ],
    )(me, a, b)


def lower_product(g, ah, al, bh, bl):
    size = g.shape[0]
    q = size // 4
    for r0, r1, c0, c1 in [(q, 3 * q, q, size), (3 * q, size, q, 3 * q)]:
        c = slice(c0 - q, c1 - q)
        g[r0:r1, c0:c1] = mm((ah[r0:r1, :], al[r0:r1, :]), (bh[:, c], bl[:, c]))


def other_gram_kernel(shards, me_ref, ah, al, bh, bl, keep_ref, send_ref, g, packed):
    q = g.shape[0] // 4
    lower_product(g, ah, al, bh[:, q:], bl[:, q:])
    pack(g, packed, keep_ref, send_ref, me_ref[0], shards, 1)


def other_gram(me, shards, ah, al, bh, bl):
    size = ah.shape[0]
    return call(
        functools.partial(other_gram_kernel, shards), "other_gram", halves(size, shards), 18, 0.5, 2,
        in_specs=[SMEM] + [VMEM] * 4,
        out_specs=[VMEM, VMEM],
        scratch_shapes=[pltpu.VMEM((size, size), F32), packed_scratch(size, shards)],
    )(me, ah, al, bh, bl)


def tiles(count, tile, step):
    def body(t, _):
        step(pl.ds(pl.multiple_of(t * tile, tile), tile))
        return 0

    lax.fori_loop(0, count // tile, body, 0)


def row_part(part, rows):
    return slice(0, rows // 4) if part == 0 else slice(rows // 4, rows)


def affine_kernel(part, a_ref, b_ref, out_ref, hi, lo):
    r = row_part(part, a_ref.shape[0])
    hi[...], lo[...] = split(a_ref[r])

    def step(c):
        out_ref[:, c] = 1.5 * a_ref[r, c] - 0.5 * mm((hi[...], lo[...]), split(b_ref[:, c]))

    tiles(out_ref.shape[1], 256, step)


def affine(a, b, part):
    rows, size = a.shape
    height = rows // 4 if part == 0 else 3 * rows // 4
    return call(
        functools.partial(affine_kernel, part), "affine", struct(height, size), 18,
        height / rows, 2,
        in_specs=[VMEM, VMEM],
        out_specs=VMEM,
        scratch_shapes=[pltpu.VMEM((height, size), BF16)] * 2,
    )(a, b)


def affine_parts_kernel(part, ah, al, b_ref, out_ref):
    r = row_part(part, ah.shape[0])

    def step(c):
        product = mm((ah[r], al[r]), split(b_ref[:, c]))
        out_ref[:, c] = 1.5 * (ah[r, c].astype(F32) + al[r, c].astype(F32)) - 0.5 * product

    tiles(out_ref.shape[1], 256, step)


def affine_parts(ah, al, b, part):
    rows, size = ah.shape
    height = rows // 4 if part == 0 else 3 * rows // 4
    return call(
        functools.partial(affine_parts_kernel, part), "affine_parts", struct(height, size), 18,
        height / rows, 2,
        in_specs=[VMEM] * 3,
        out_specs=VMEM,
    )(ah, al, b)


SPANS = (
    (((0, 4),), ((0, 1),), ((0, 1),), ((0, 1), (3, 4))),
    ((), ((1, 4),), ((1, 4),), ((1, 3),)),
)


def sym_product(ah, al, hi, lo, chunk, column, rows=slice(None)):
    q = hi.shape[0] // 4
    spans = [slice(k0 * q, k1 * q) for k0, k1 in SPANS[chunk][column]]
    c = slice(column * q, (column + 1) * q)
    a = [ref[rows, k] for ref in (ah, ah, al) for k in spans]
    b = [ref[k, c] for ref in (hi, lo, hi) for k in spans]
    return c, jnp.dot(
        jnp.concatenate(a, axis=1), jnp.concatenate(b, axis=0), preferred_element_type=F32
    )


def apply_first(base_refs, out_ref, ah, al, hi, lo, columns):
    q = hi.shape[0] // 4
    for column in columns:
        c, product = sym_product(ah, al, hi, lo, 0, column)
        out = slice(c.start - columns[0] * q, c.stop - columns[0] * q)
        at = 0
        for base_ref in base_refs:
            end = at + base_ref.shape[0]
            out_ref[at:end, out] = base_ref[:, c] - 0.5 * product[at:end]
            at = end


def sym_scratch(size, shards):
    return [pltpu.VMEM((size, size), BF16)] * 2 + [packed_scratch(size, shards)]


def first_part_kernel(shards, count, columns, me_ref, *refs):
    pieces, refs = refs[:count], refs[count:]
    ah, al, base_refs, (out_ref, hi, lo, packed) = refs[0], refs[1], refs[2:-4], refs[-4:]
    unpack(pieces, packed, hi, lo, me_ref[0], shards, 0)
    apply_first(base_refs, out_ref, ah, al, hi, lo, columns)


def first_part(me, shards, pieces, ah, al, base, columns):
    rows, size = ah.shape
    part = struct(size, size, dtype=BF16)
    more = len(columns) < 4
    scratch = sym_scratch(size, shards)
    return call(
        functools.partial(first_part_kernel, shards, len(pieces), columns), "first_part",
        [struct(rows, len(columns) * size // 4)] + [part, part] * more, 18, 0.5, 3,
        in_specs=[SMEM] + [VMEM] * (len(pieces) + 2 + len(base)),
        out_specs=[VMEM] * (1 + 2 * more),
        scratch_shapes=scratch[2 * more:],
    )(me, *pieces, ah, al, *base)


def other_part_kernel(columns, ah, al, hi, lo, *refs):
    apply_first(refs[:-1], refs[-1], ah, al, hi, lo, columns)


def other_part(ah, al, hi, lo, base, columns):
    rows, size = ah.shape
    return call(
        functools.partial(other_part_kernel, columns), "other_part",
        struct(rows, len(columns) * size // 4), 16, 0.25, 3,
        in_specs=[VMEM] * (4 + len(base)),
        out_specs=VMEM,
    )(ah, al, hi, lo, *base)


def column_kernel(xh, xl, mid_ref, col_ref):
    col_ref[...] = mm((xh[...], xl[...]), split(mid_ref[...]))


def column_product(xh, xl, mid):
    size, rows = xh.shape
    block = pl.BlockSpec((rows, size // 4), lambda r: (0, 0))
    whole = pl.BlockSpec((size, rows), lambda r: (0, 0))
    return call(
        column_kernel, "column_product", struct(size, size // 4), 16, 0.25, 2,
        grid=(1,), in_specs=[whole, whole, block], out_specs=block,
    )(xh, xl, mid)


def turn_kernel(x_ref, xh, xl):
    def step(r):
        xh[:, r], xl[:, r] = split(x_ref[r].T)

    tiles(x_ref.shape[0], 256, step)


def turn(x):
    part = struct(*x.shape[::-1], dtype=BF16)
    return call(
        turn_kernel, "turn", [part, part], 16, 0.1, 2, in_specs=[VMEM], out_specs=[VMEM] * 2
    )(x)


def cut_kernel(which, x_ref, *out_refs):
    def step(r):
        parts = split(x_ref[r])
        for out_ref, k in zip(out_refs, which):
            out_ref[r] = parts[k]

    tiles(x_ref.shape[0], 128, step)


def cut(x, *which):
    count = len(which)
    return call(
        functools.partial(cut_kernel, which), "cut", [struct(*x.shape, dtype=BF16)] * count,
        16, 0.25, 2, in_specs=[VMEM], out_specs=[VMEM] * count,
    )(x)


def second_gram_kernel(shards, count, me_ref, *refs):
    pieces, refs = refs[:count], refs[count:]
    (ah, al, base_ref, xh, xl, col_ref), refs = refs[:6], refs[6:]
    keep_ref, send_ref, mh, ml, hi, lo, packed, g = refs
    size = g.shape[0]
    q = size // 4
    unpack(pieces, packed, hi, lo, me_ref[0], shards, 1)
    mh[:, :q], ml[:, :q] = split(base_ref[:, :q])
    for column in range(1, 4):
        c, product = sym_product(ah, al, hi, lo, 1, column)
        mid = base_ref[:, c] - 0.5 * product
        mh[:, c], ml[:, c] = split(mid)
    g[:, :q] = col_ref[...]
    g[:q, q:] = mm((xh[:q, :], xl[:q, :]), (mh[:, q:], ml[:, q:]))
    g[3 * q:, 3 * q:] = mm((xh[3 * q:, :], xl[3 * q:, :]), (mh[:, 3 * q:], ml[:, 3 * q:]))
    pack(g, packed, keep_ref, send_ref, me_ref[0], shards, 0)


def second_gram(me, shards, pieces, ah, al, base, xh, xl, col):
    rows, size = ah.shape
    part = struct(rows, size, dtype=BF16)
    return call(
        functools.partial(second_gram_kernel, shards, len(pieces)), "second_gram",
        halves(size, shards) + [part, part], 20, 0.8, 5,
        in_specs=[SMEM] + [VMEM] * (len(pieces) + 6),
        out_specs=[VMEM] * 4,
        scratch_shapes=sym_scratch(size, shards) + [pltpu.VMEM((size, size), F32)],
    )(me, *pieces, ah, al, base, xh, xl, col)


def fourth_gram_kernel(shards, me_ref, xh, xl, mh, ml, keep_ref, send_ref, g, packed):
    q = g.shape[0] // 4
    lower_product(g, xh, xl, mh[:, q:], ml[:, q:])
    pack(g, packed, keep_ref, send_ref, me_ref[0], shards, 1)


def fourth_gram(me, shards, xh, xl, mh, ml):
    size = xh.shape[0]
    return call(
        functools.partial(fourth_gram_kernel, shards), "fourth_gram", halves(size, shards), 18, 0.5, 2,
        in_specs=[SMEM] + [VMEM] * 4,
        out_specs=[VMEM, VMEM],
        scratch_shapes=[pltpu.VMEM((size, size), F32), packed_scratch(size, shards)],
    )(me, xh, xl, mh, ml)


def last_kernel(shards, count, me_ref, *refs):
    pieces = refs[:count]
    ah, al, z_ref, rest_ref, out_hbm, hi, lo, packed, out, sems = refs[count:]
    q = hi.shape[0] // 4
    copies = []

    def send(src, rows, c):
        copy = pltpu.make_async_copy(src, out_hbm.at[rows, c], sems.at[len(copies)])
        copy.start()
        copies.append(copy)

    count = out.shape[0]
    send(z_ref, slice(0, count), slice(0, q))
    unpack(pieces, packed, hi, lo, me_ref[0], shards, 1)
    for column in (1, 2, 3):
        parts = 2 if column == 3 else 1
        for part in range(parts):
            r = slice(part * count // parts, (part + 1) * count // parts)
            c, product = sym_product(ah, al, hi, lo, 1, column, r)
            out[r, c] = rest_ref[r, c.start - q:c.stop - q] - 0.5 * product
            send(out.at[r, c], r, c)
    for copy in copies:
        copy.wait()


def last_step(me, shards, pieces, ah, al, z, rest):
    rows, size = ah.shape
    return call(
        functools.partial(last_kernel, shards, len(pieces)), "last", struct(rows, size), 22, 0.5, 3,
        in_specs=[SMEM] + [VMEM] * (len(pieces) + 4),
        out_specs=pl.BlockSpec(memory_space=pltpu.HBM),
        scratch_shapes=sym_scratch(size, shards)
        + [pltpu.VMEM((rows, size), F32), pltpu.SemaphoreType.DMA((5,))],
    )(me, *pieces, ah, al, z, rest)


CORE = 1
PLANE = (2, 4, 6)
SHARDS = 2 * (1 + len(PLANE))


def slot_of(index):
    return (index % 2) * (SHARDS // 2) + (index // 2) % (SHARDS // 2)


class Sum:
    def __init__(self, count, keep, send):
        self.count, self.keep, self.send = count, keep, send

    def swap(self, x, offset):
        return lax.ppermute(x, "row", [(i, i ^ offset) for i in range(self.count)])

    def swaps(self, values):
        return [self.swap(x, offset) for x, offset in zip(values, PLANE)]

    def core(self):
        return self.swap(self.send, CORE)

    def plane(self, got):
        total = self.keep + got
        part = total.shape[0] // (1 + len(PLANE))
        self.keep, *sends = [total[k * part:(k + 1) * part] for k in range(1 + len(PLANE))]
        return self.swaps(sends)

    def own(self, got):
        self.keep = sum(got, self.keep)

    def exchange(self, offset):
        return self.swap(self.keep, offset)

    def gather_plane(self):
        return self.swaps([self.keep] * len(PLANE))

    def gather_core(self, got):
        self.mine = jnp.concatenate([self.keep, *got], axis=0)
        return self.swap(self.mine, CORE)


def close(env, *got):
    values = lax.optimization_barrier((*env.values(), *got[::-1]))
    env.update(zip(env, values))
    return values[len(env):][::-1]


def sum_chunks(count, env, first, second, works, late):
    beyond = [1 << s for s in range(3, count.bit_length() - 1)]
    works = list(works)

    def work():
        if works:
            works.pop(0)(env)

    a = Sum(count, *first)
    got_a = a.core()
    pair = second(env)
    got_a, *pair = close(env, got_a, *pair)
    b = Sum(count, *pair)

    got_a = a.plane(got_a)
    got_b = b.core()
    work()
    (got_b,) = close(env, got_b)

    got_b = b.plane(got_b)
    work()
    a.own(close(env, *got_a))

    for offset in beyond:
        got_a = a.exchange(offset)
        work()
        b.own(close(env, *got_b))
        got_b = [b.exchange(offset)]
        a.own(close(env, got_a))

    got_a = a.gather_plane()
    b.own(close(env, *got_b))

    got_b = b.gather_plane()
    got_a = a.gather_core(close(env, *got_a))
    work()
    (got_a,) = close(env, got_a)
    late[0](env, [a.mine, got_a])
    got_b = b.gather_core(close(env, *got_b))
    late[1](env)
    (got_b,) = close(env, got_b)
    return [b.mine, got_b]


def body(count, orbitals_zero, orbitals_one, correlation_zero, correlation_one, cotangent):
    me = slot_of(lax.axis_index("row")).astype(jnp.int32).reshape(1)
    env = dict(
        x0=orbitals_zero, x1=orbitals_one, s0=correlation_zero, s1=correlation_one, c=cotangent
    )

    def direct(part):
        def work(env):
            env[f"m{part}"] = affine(env["c"], env["s1"], part)
        return work

    def turned(env):
        env["xh"], env["xl"] = turn(env["x0"])

    def cut_one(env):
        env["x1h"], env["x1l"] = cut(env["x1"], 0, 1)

    def middle(env, pieces):
        (env["mid"],) = first_part(
            me, SHARDS, pieces, env["x1h"], env["x1l"], [env["m0"], env["m1"]], (0, 1, 2, 3)
        )

    def column(env):
        env["col"] = column_product(env["xh"], env["xl"], env["mid"])

    keep, send, *parts = first_gram(me, SHARDS, env["x1"], env["c"])
    one = sum_chunks(
        count, env, (keep, send), lambda env: other_gram(me, SHARDS, *parts),
        [direct(0), cut_one, direct(1), turned], [middle, column],
    )

    keep, send, env["mh"], env["ml"] = second_gram(
        me, SHARDS, one, env["x1h"], env["x1l"], env["mid"], env["xh"], env["xl"], env["col"]
    )

    def last_direct(part):
        def work(env):
            env[f"d{part}"] = affine_parts(env["mh"], env["ml"], env["s0"], part)
        return work

    def high(env):
        (env["x0h"],) = cut(env["x0"], 0)

    def low(env):
        (env["x0l"],) = cut(env["x0"], 1)

    def result(env, pieces):
        env["z"], env["symh"], env["syml"] = first_part(
            me, SHARDS, pieces, env["x0h"], env["x0l"], [env["d0"], env["d1"]], (0,)
        )

    def rest(env):
        env["rest"] = other_part(
            env["x0h"], env["x0l"], env["symh"], env["syml"], [env["d0"], env["d1"]], (1, 2, 3)
        )

    two = sum_chunks(
        count, env, (keep, send),
        lambda env: fourth_gram(me, SHARDS, env["xh"], env["xl"], env["mh"], env["ml"]),
        [last_direct(0), high, last_direct(1), low], [result, rest],
    )
    return last_step(me, SHARDS, two, env["x0h"], env["x0l"], env["z"], env["rest"])


def solution(mesh):
    in_specs = (
        P(("kpt", "row"), None),
        P(("kpt", "row"), None),
        P("kpt", None),
        P("kpt", None),
        P(("kpt", "row"), None),
    )
    out_specs = P(("kpt", "row"), None)
    return jax.shard_map(
        functools.partial(body, mesh.shape["row"]),
        mesh=mesh, in_specs=in_specs, out_specs=out_specs, check_vma=False,
    )
```

```python
import functools
import jax
import jax.numpy as jnp
from jax import lax
from jax.experimental import pallas as pl
from jax.experimental.pallas import tpu as pltpu
from jax.sharding import PartitionSpec as P

F32 = jnp.float32
BF16 = jnp.bfloat16
B = 128
MIB = 1024 * 1024
WEIGHT = 10


def split(x):
    hi = x.astype(BF16)
    return hi, (x - hi.astype(F32)).astype(BF16)


def mm(a, b):
    (ah, al), (bh, bl) = a, b
    return jnp.dot(
        jnp.concatenate([ah, ah, al], axis=1),
        jnp.concatenate([bh, bl, bh], axis=0),
        preferred_element_type=F32,
    )


def call(kernel, name, out_shape, limit, products, arrays, **kw):
    size = 1024
    return pl.pallas_call(
        kernel,
        name=name,
        out_shape=out_shape,
        compiler_params=pltpu.CompilerParams(vmem_limit_bytes=limit * MIB),
        cost_estimate=pl.CostEstimate(
            flops=int(WEIGHT * 6 * products * size ** 3),
            bytes_accessed=int(WEIGHT * 4 * arrays * size * size),
            transcendentals=0,
        ),
        **kw,
    )


def struct(*shape, dtype=F32):
    return jax.ShapeDtypeStruct(shape, dtype)


SMEM = pl.BlockSpec(memory_space=pltpu.SMEM)
VMEM = pl.BlockSpec(memory_space=pltpu.VMEM)


def chunk_lines(size, chunk):
    half = size // B // 4
    return range(chunk * half, (chunk + 1) * half)


def line_blocks(size, i):
    n = size // B
    block = lambda k: slice(k * B, (k + 1) * B)
    return [(block(top), block(j)) for top in (i, n - 1 - i) for j in range(top + 1, n)]


def diagonal_blocks(size, i):
    n = size // B
    return [slice(k * B, (k + 1) * B) for k in (i, n - 1 - i)]


def part_rows(size, shards):
    return size // 4 // shards


def shard_rows(size, shards):
    return part_rows(size, shards) * (size // B) + 8


def places():
    row = lax.broadcasted_iota(jnp.int32, (B, B), 0)
    column = lax.broadcasted_iota(jnp.int32, (B, B), 1)
    return row, column


def pack(g, packed, keep_ref, send_ref, me, shards, chunk):
    size = g.shape[0]
    rows, height = part_rows(size, shards), shard_rows(size, shards)
    per = B // rows
    row, column = places()
    whole = lambda p, q: g[p, q] + g[q, p].T
    for line, i in enumerate(chunk_lines(size, chunk)):
        starts = [((line * per + s) ^ me) * height for s in range(per)]

        def put(at, s, value):
            start = pl.multiple_of(starts[s] + at, 8)
            packed[pl.ds(start, value.shape[0]), :] = value

        upper, lower = [whole(p, p) for p in diagonal_blocks(size, i)]
        for k, place in enumerate([None] + line_blocks(size, i)):
            block = whole(*place) if place else jnp.where(column >= row, upper, lower)
            for s in range(per):
                put(k * rows, s, block[s * rows:(s + 1) * rows])
        element = jnp.sum(jnp.where(column == row, lower, 0.0), axis=0, keepdims=True)
        for s in range(per):
            put(height - 8, s, jnp.broadcast_to(element, (8, B)))
    half = keep_ref.shape[0]
    keep_ref[...] = packed[:half]
    send_ref[...] = packed[half:]


def unpack(pieces, packed, hi, lo, me, shards, chunk):
    size = hi.shape[0]
    rows, height = part_rows(size, shards), shard_rows(size, shards)
    per = B // rows
    row, column = places()
    slot = 0
    for piece in pieces:
        for s in range(piece.shape[0] // height):
            at = pl.multiple_of((slot ^ me) * height, 8)
            packed[pl.ds(at, height), :] = piece[s * height:(s + 1) * height, :]
            slot += 1

    def put(p, q, block):
        hi[p, q], lo[p, q] = split(block)

    for line, i in enumerate(chunk_lines(size, chunk)):
        start = line * per * height

        def get(k):
            return jnp.concatenate(
                [
                    packed[start + s * height + k * rows:start + s * height + (k + 1) * rows, :]
                    for s in range(per)
                ],
                axis=0,
            )

        first, last = diagonal_blocks(size, i)
        block = get(0)
        turned = block.T
        element = packed[start + height - 8:start + height - 7, :]
        put(first, first, jnp.where(column >= row, block, turned))
        below = jnp.where(column < row, block, turned)
        put(last, last, jnp.where(column == row, jnp.broadcast_to(element, (B, B)), below))
        for k, (p, q) in enumerate(line_blocks(size, i)):
            block = get(k + 1)
            put(p, q, block)
            put(q, p, block.T)


def packed_scratch(size, shards):
    return pltpu.VMEM((shards * shard_rows(size, shards), B), F32)


def halves(size, shards):
    return [struct(shards // 2 * shard_rows(size, shards), B)] * 2


def first_gram_kernel(
    shards, me_ref, a_hbm, b_hbm, keep_ref, send_ref, ah, al, bh, bl, a_buf, b_buf, sems, g, packed
):
    rows, size = a_buf.shape
    q = size // 4
    steps = sems.shape[1]
    tile = rows // steps

    def copies(step):
        r = slice(step * tile, (step + 1) * tile)
        return [
            pltpu.make_async_copy(src.at[r], dst.at[r], sems.at[k, step])
            for k, (src, dst) in enumerate([(a_hbm, a_buf), (b_hbm, b_buf)])
        ]

    def start(step):
        for copy in copies(step):
            copy.start()

    start(0)
    start(1)
    for step in range(steps):
        r = slice(step * tile, (step + 1) * tile)
        for copy in copies(step):
            copy.wait()
        if step + 2 < steps:
            start(step + 2)
        ah[:, r], al[:, r] = split(a_buf[r].T)
        bh[r], bl[r] = split(b_buf[r])
        for r0, r1, c0, c1 in [(0, q, 0, size), (q, size, 0, q), (3 * q, size, 3 * q, size)]:
            product = mm((ah[r0:r1, r], al[r0:r1, r]), (bh[r, c0:c1], bl[r, c0:c1]))
            if step:
                product += g[r0:r1, c0:c1]
            g[r0:r1, c0:c1] = product
    pack(g, packed, keep_ref, send_ref, me_ref[0], shards, 0)


def first_gram(me, shards, a, b):
    rows, size = a.shape
    hbm = pl.BlockSpec(memory_space=pltpu.HBM)
    return call(
        functools.partial(first_gram_kernel, shards), "first_gram",
        halves(size, shards) + [struct(size, rows, dtype=BF16)] * 2 + [struct(rows, size, dtype=BF16)] * 2,
        43, 0.5, 4,
        in_specs=[SMEM, hbm, hbm],
        out_specs=[VMEM] * 6,
        scratch_shapes=[
            pltpu.VMEM((rows, size), F32), pltpu.VMEM((rows, size), F32),
            pltpu.SemaphoreType.DMA((2, 4)),
            pltpu.VMEM((size, size), F32), packed_scratch(size, shards),
        ],
    )(me, a, b)


def lower_product(g, ah, al, bh, bl):
    size = g.shape[0]
    q = size // 4
    for r0, r1, c0, c1 in [(q, 3 * q, q, size), (3 * q, size, q, 3 * q)]:
        c = slice(c0 - q, c1 - q)
        g[r0:r1, c0:c1] = mm((ah[r0:r1, :], al[r0:r1, :]), (bh[:, c], bl[:, c]))


def other_gram_kernel(shards, me_ref, ah, al, bh, bl, keep_ref, send_ref, g, packed):
    q = g.shape[0] // 4
    lower_product(g, ah, al, bh[:, q:], bl[:, q:])
    pack(g, packed, keep_ref, send_ref, me_ref[0], shards, 1)


def other_gram(me, shards, ah, al, bh, bl):
    size = ah.shape[0]
    return call(
        functools.partial(other_gram_kernel, shards), "other_gram", halves(size, shards), 18, 0.5, 2,
        in_specs=[SMEM] + [VMEM] * 4,
        out_specs=[VMEM, VMEM],
        scratch_shapes=[pltpu.VMEM((size, size), F32), packed_scratch(size, shards)],
    )(me, ah, al, bh, bl)


def tiles(count, tile, step):
    def body(t, _):
        step(pl.ds(pl.multiple_of(t * tile, tile), tile))
        return 0

    lax.fori_loop(0, count // tile, body, 0)


def row_part(part, rows):
    return slice(0, rows // 4) if part == 0 else slice(rows // 4, rows)


def affine_kernel(part, a_ref, b_ref, out_ref, hi, lo):
    r = row_part(part, a_ref.shape[0])
    hi[...], lo[...] = split(a_ref[r])

    def step(c):
        out_ref[:, c] = 1.5 * a_ref[r, c] - 0.5 * mm((hi[...], lo[...]), split(b_ref[:, c]))

    tiles(out_ref.shape[1], 512 if part else 256, step)


def affine(a, b, part):
    rows, size = a.shape
    height = rows // 4 if part == 0 else 3 * rows // 4
    return call(
        functools.partial(affine_kernel, part), "affine", struct(height, size), 18,
        height / rows, 2,
        in_specs=[VMEM, VMEM],
        out_specs=VMEM,
        scratch_shapes=[pltpu.VMEM((height, size), BF16)] * 2,
    )(a, b)


def affine_parts_kernel(part, ah, al, b_ref, out_ref):
    r = row_part(part, ah.shape[0])

    def step(c):
        product = mm((ah[r], al[r]), split(b_ref[:, c]))
        out_ref[:, c] = 1.5 * (ah[r, c].astype(F32) + al[r, c].astype(F32)) - 0.5 * product

    tiles(out_ref.shape[1], 512 if part else 256, step)


def affine_parts(ah, al, b, part):
    rows, size = ah.shape
    height = rows // 4 if part == 0 else 3 * rows // 4
    return call(
        functools.partial(affine_parts_kernel, part), "affine_parts", struct(height, size), 18,
        height / rows, 2,
        in_specs=[VMEM] * 3,
        out_specs=VMEM,
    )(ah, al, b)


SPANS = (
    (((0, 4),), ((0, 1),), ((0, 1),), ((0, 1), (3, 4))),
    ((), ((1, 4),), ((1, 4),), ((1, 3),)),
)


def sym_product(ah, al, hi, lo, chunk, column, rows=slice(None)):
    q = hi.shape[0] // 4
    spans = [slice(k0 * q, k1 * q) for k0, k1 in SPANS[chunk][column]]
    c = slice(column * q, (column + 1) * q)
    a = [ref[rows, k] for ref in (ah, ah, al) for k in spans]
    b = [ref[k, c] for ref in (hi, lo, hi) for k in spans]
    return c, jnp.dot(
        jnp.concatenate(a, axis=1), jnp.concatenate(b, axis=0), preferred_element_type=F32
    )


def apply_first(base_refs, out_ref, ah, al, hi, lo, columns):
    q = hi.shape[0] // 4
    for column in columns:
        c, product = sym_product(ah, al, hi, lo, 0, column)
        out = slice(c.start - columns[0] * q, c.stop - columns[0] * q)
        at = 0
        for base_ref in base_refs:
            end = at + base_ref.shape[0]
            out_ref[at:end, out] = base_ref[:, c] - 0.5 * product[at:end]
            at = end


def sym_scratch(size, shards):
    return [pltpu.VMEM((size, size), BF16)] * 2 + [packed_scratch(size, shards)]


def first_part_kernel(shards, count, columns, me_ref, *refs):
    pieces, refs = refs[:count], refs[count:]
    ah, al, base_refs, (out_ref, hi, lo, packed) = refs[0], refs[1], refs[2:-4], refs[-4:]
    unpack(pieces, packed, hi, lo, me_ref[0], shards, 0)
    apply_first(base_refs, out_ref, ah, al, hi, lo, columns)


def first_part(me, shards, pieces, ah, al, base, columns):
    rows, size = ah.shape
    part = struct(size, size, dtype=BF16)
    more = len(columns) < 4
    scratch = sym_scratch(size, shards)
    return call(
        functools.partial(first_part_kernel, shards, len(pieces), columns), "first_part",
        [struct(rows, len(columns) * size // 4)] + [part, part] * more, 18, 0.5, 3,
        in_specs=[SMEM] + [VMEM] * (len(pieces) + 2 + len(base)),
        out_specs=[VMEM] * (1 + 2 * more),
        scratch_shapes=scratch[2 * more:],
    )(me, *pieces, ah, al, *base)


def other_part_kernel(columns, ah, al, hi, lo, *refs):
    apply_first(refs[:-1], refs[-1], ah, al, hi, lo, columns)


def other_part(ah, al, hi, lo, base, columns):
    rows, size = ah.shape
    return call(
        functools.partial(other_part_kernel, columns), "other_part",
        struct(rows, len(columns) * size // 4), 16, 0.25, 3,
        in_specs=[VMEM] * (4 + len(base)),
        out_specs=VMEM,
    )(ah, al, hi, lo, *base)


def column_kernel(xh, xl, mid_ref, col_ref):
    col_ref[...] = mm((xh[...], xl[...]), split(mid_ref[...]))


def column_product(xh, xl, mid):
    size, rows = xh.shape
    block = pl.BlockSpec((rows, size // 4), lambda r: (0, 0))
    whole = pl.BlockSpec((size, rows), lambda r: (0, 0))
    return call(
        column_kernel, "column_product", struct(size, size // 4), 16, 0.25, 2,
        grid=(1,), in_specs=[whole, whole, block], out_specs=block,
    )(xh, xl, mid)


def turn_kernel(x_ref, xh, xl):
    def step(r):
        xh[:, r], xl[:, r] = split(x_ref[r].T)

    tiles(x_ref.shape[0], 256, step)


def turn(x):
    part = struct(*x.shape[::-1], dtype=BF16)
    return call(
        turn_kernel, "turn", [part, part], 16, 0.1, 2, in_specs=[VMEM], out_specs=[VMEM] * 2
    )(x)


def cut_kernel(which, x_ref, *out_refs):
    def step(r):
        parts = split(x_ref[r])
        for out_ref, k in zip(out_refs, which):
            out_ref[r] = parts[k]

    tiles(x_ref.shape[0], 128, step)


def cut(x, *which):
    count = len(which)
    return call(
        functools.partial(cut_kernel, which), "cut", [struct(*x.shape, dtype=BF16)] * count,
        16, 0.25, 2, in_specs=[VMEM], out_specs=[VMEM] * count,
    )(x)


def second_gram_kernel(shards, count, me_ref, *refs):
    pieces, refs = refs[:count], refs[count:]
    (ah, al, base_ref, xh, xl, col_ref), refs = refs[:6], refs[6:]
    keep_ref, send_ref, mh, ml, hi, lo, packed, g = refs
    size = g.shape[0]
    q = size // 4
    unpack(pieces, packed, hi, lo, me_ref[0], shards, 1)
    mh[:, :q], ml[:, :q] = split(base_ref[:, :q])
    for column in range(1, 4):
        c, product = sym_product(ah, al, hi, lo, 1, column)
        mid = base_ref[:, c] - 0.5 * product
        mh[:, c], ml[:, c] = split(mid)
    g[:, :q] = col_ref[...]
    g[:q, q:] = mm((xh[:q, :], xl[:q, :]), (mh[:, q:], ml[:, q:]))
    g[3 * q:, 3 * q:] = mm((xh[3 * q:, :], xl[3 * q:, :]), (mh[:, 3 * q:], ml[:, 3 * q:]))
    pack(g, packed, keep_ref, send_ref, me_ref[0], shards, 0)


def second_gram(me, shards, pieces, ah, al, base, xh, xl, col):
    rows, size = ah.shape
    part = struct(rows, size, dtype=BF16)
    return call(
        functools.partial(second_gram_kernel, shards, len(pieces)), "second_gram",
        halves(size, shards) + [part, part], 20, 0.8, 5,
        in_specs=[SMEM] + [VMEM] * (len(pieces) + 6),
        out_specs=[VMEM] * 4,
        scratch_shapes=sym_scratch(size, shards) + [pltpu.VMEM((size, size), F32)],
    )(me, *pieces, ah, al, base, xh, xl, col)


def fourth_gram_kernel(shards, me_ref, xh, xl, mh, ml, keep_ref, send_ref, g, packed):
    q = g.shape[0] // 4
    lower_product(g, xh, xl, mh[:, q:], ml[:, q:])
    pack(g, packed, keep_ref, send_ref, me_ref[0], shards, 1)


def fourth_gram(me, shards, xh, xl, mh, ml):
    size = xh.shape[0]
    return call(
        functools.partial(fourth_gram_kernel, shards), "fourth_gram", halves(size, shards), 18, 0.5, 2,
        in_specs=[SMEM] + [VMEM] * 4,
        out_specs=[VMEM, VMEM],
        scratch_shapes=[pltpu.VMEM((size, size), F32), packed_scratch(size, shards)],
    )(me, xh, xl, mh, ml)


def last_kernel(shards, count, me_ref, *refs):
    pieces = refs[:count]
    ah, al, z_ref, rest_ref, out_hbm, hi, lo, packed, out, sems = refs[count:]
    q = hi.shape[0] // 4
    copies = []

    def send(src, rows, c):
        copy = pltpu.make_async_copy(src, out_hbm.at[rows, c], sems.at[len(copies)])
        copy.start()
        copies.append(copy)

    count = out.shape[0]
    send(z_ref, slice(0, count), slice(0, q))
    unpack(pieces, packed, hi, lo, me_ref[0], shards, 1)
    for column in (1, 2, 3):
        parts = 2 if column == 3 else 1
        for part in range(parts):
            r = slice(part * count // parts, (part + 1) * count // parts)
            c, product = sym_product(ah, al, hi, lo, 1, column, r)
            out[r, c] = rest_ref[r, c.start - q:c.stop - q] - 0.5 * product
            send(out.at[r, c], r, c)
    for copy in copies:
        copy.wait()


def last_step(me, shards, pieces, ah, al, z, rest):
    rows, size = ah.shape
    return call(
        functools.partial(last_kernel, shards, len(pieces)), "last", struct(rows, size), 22, 0.5, 3,
        in_specs=[SMEM] + [VMEM] * (len(pieces) + 4),
        out_specs=pl.BlockSpec(memory_space=pltpu.HBM),
        scratch_shapes=sym_scratch(size, shards)
        + [pltpu.VMEM((rows, size), F32), pltpu.SemaphoreType.DMA((5,))],
    )(me, *pieces, ah, al, z, rest)


CORE = 1
PLANE = (2, 4, 6)
SHARDS = 2 * (1 + len(PLANE))


def slot_of(index):
    return (index % 2) * (SHARDS // 2) + (index // 2) % (SHARDS // 2)


class Sum:
    def __init__(self, count, keep, send):
        self.count, self.keep, self.send = count, keep, send

    def swap(self, x, offset):
        return lax.ppermute(x, "row", [(i, i ^ offset) for i in range(self.count)])

    def swaps(self, values):
        return [self.swap(x, offset) for x, offset in zip(values, PLANE)]

    def core(self):
        return self.swap(self.send, CORE)

    def plane(self, got):
        total = self.keep + got
        part = total.shape[0] // (1 + len(PLANE))
        self.keep, *sends = [total[k * part:(k + 1) * part] for k in range(1 + len(PLANE))]
        return self.swaps(sends)

    def own(self, got):
        self.keep = sum(got, self.keep)

    def exchange(self, offset):
        return self.swap(self.keep, offset)

    def gather_plane(self):
        return self.swaps([self.keep] * len(PLANE))

    def gather_core(self, got):
        self.mine = jnp.concatenate([self.keep, *got], axis=0)
        return self.swap(self.mine, CORE)


def close(env, *got):
    values = lax.optimization_barrier((*env.values(), *got[::-1]))
    env.update(zip(env, values))
    return values[len(env):][::-1]


def sum_chunks(count, env, first, second, works, late):
    beyond = [1 << s for s in range(3, count.bit_length() - 1)]
    works = list(works)

    def work():
        if works:
            works.pop(0)(env)

    a = Sum(count, *first)
    got_a = a.core()
    pair = second(env)
    got_a, *pair = close(env, got_a, *pair)
    b = Sum(count, *pair)

    got_a = a.plane(got_a)
    got_b = b.core()
    work()
    (got_b,) = close(env, got_b)

    got_b = b.plane(got_b)[::-1]
    work()
    a.own(close(env, *got_a))

    for offset in beyond:
        got_a = a.exchange(offset)
        work()
        b.own(close(env, *got_b))
        got_b = [b.exchange(offset)]
        a.own(close(env, got_a))

    got_a = a.gather_plane()
    b.own(close(env, *got_b))

    got_b = b.gather_plane()
    got_a = a.gather_core(close(env, *got_a))
    work()
    (got_a,) = close(env, got_a)
    late[0](env, [a.mine, got_a])
    got_b = b.gather_core(close(env, *got_b))
    late[1](env)
    (got_b,) = close(env, got_b)
    return [b.mine, got_b]


def body(count, orbitals_zero, orbitals_one, correlation_zero, correlation_one, cotangent):
    me = slot_of(lax.axis_index("row")).astype(jnp.int32).reshape(1)
    env = dict(
        x0=orbitals_zero, x1=orbitals_one, s0=correlation_zero, s1=correlation_one, c=cotangent
    )

    def direct(part):
        def work(env):
            env[f"m{part}"] = affine(env["c"], env["s1"], part)
        return work

    def turned(env):
        env["xh"], env["xl"] = turn(env["x0"])

    def cut_one(env):
        env["x1h"], env["x1l"] = cut(env["x1"], 0, 1)

    def middle(env, pieces):
        (env["mid"],) = first_part(
            me, SHARDS, pieces, env["x1h"], env["x1l"], [env["m0"], env["m1"]], (0, 1, 2, 3)
        )

    def column(env):
        env["col"] = column_product(env["xh"], env["xl"], env["mid"])

    keep, send, *parts = first_gram(me, SHARDS, env["x1"], env["c"])
    one = sum_chunks(
        count, env, (keep, send), lambda env: other_gram(me, SHARDS, *parts),
        [direct(0), cut_one, direct(1), turned], [middle, column],
    )

    keep, send, env["mh"], env["ml"] = second_gram(
        me, SHARDS, one, env["x1h"], env["x1l"], env["mid"], env["xh"], env["xl"], env["col"]
    )

    def last_direct(part):
        def work(env):
            env[f"d{part}"] = affine_parts(env["mh"], env["ml"], env["s0"], part)
        return work

    def high(env):
        (env["x0h"],) = cut(env["x0"], 0)

    def low(env):
        (env["x0l"],) = cut(env["x0"], 1)

    def result(env, pieces):
        env["z"], env["symh"], env["syml"] = first_part(
            me, SHARDS, pieces, env["x0h"], env["x0l"], [env["d0"], env["d1"]], (0,)
        )

    def rest(env):
        env["rest"] = other_part(
            env["x0h"], env["x0l"], env["symh"], env["syml"], [env["d0"], env["d1"]], (1, 2, 3)
        )

    two = sum_chunks(
        count, env, (keep, send),
        lambda env: fourth_gram(me, SHARDS, env["xh"], env["xl"], env["mh"], env["ml"]),
        [last_direct(0), high, last_direct(1), low], [result, rest],
    )
    return last_step(me, SHARDS, two, env["x0h"], env["x0l"], env["z"], env["rest"])


def solution(mesh):
    in_specs = (
        P(("kpt", "row"), None),
        P(("kpt", "row"), None),
        P("kpt", None),
        P("kpt", None),
        P(("kpt", "row"), None),
    )
    out_specs = P(("kpt", "row"), None)
    return jax.shard_map(
        functools.partial(body, mesh.shape["row"]),
        mesh=mesh, in_specs=in_specs, out_specs=out_specs, check_vma=False,
    )
```

```python
import functools
import jax
import jax.numpy as jnp
from jax import lax
from jax.experimental import pallas as pl
from jax.experimental.pallas import tpu as pltpu
from jax.sharding import PartitionSpec as P

F32 = jnp.float32
BF16 = jnp.bfloat16
B = 128
MIB = 1024 * 1024
WEIGHT = 10


def split(x):
    hi = x.astype(BF16)
    return hi, (x - hi.astype(F32)).astype(BF16)


def mm(a, b):
    (ah, al), (bh, bl) = a, b
    return jnp.dot(
        jnp.concatenate([ah, ah, al], axis=1),
        jnp.concatenate([bh, bl, bh], axis=0),
        preferred_element_type=F32,
    )


def call(kernel, name, out_shape, limit, products, arrays, **kw):
    size = 1024
    return pl.pallas_call(
        kernel,
        name=name,
        out_shape=out_shape,
        compiler_params=pltpu.CompilerParams(vmem_limit_bytes=limit * MIB),
        cost_estimate=pl.CostEstimate(
            flops=int(WEIGHT * 6 * products * size ** 3),
            bytes_accessed=int(WEIGHT * 4 * arrays * size * size),
            transcendentals=0,
        ),
        **kw,
    )


def struct(*shape, dtype=F32):
    return jax.ShapeDtypeStruct(shape, dtype)


SMEM = pl.BlockSpec(memory_space=pltpu.SMEM)
VMEM = pl.BlockSpec(memory_space=pltpu.VMEM)


def chunk_lines(size, chunk):
    half = size // B // 4
    return range(chunk * half, (chunk + 1) * half)


def line_blocks(size, i):
    n = size // B
    block = lambda k: slice(k * B, (k + 1) * B)
    return [(block(top), block(j)) for top in (i, n - 1 - i) for j in range(top + 1, n)]


def diagonal_blocks(size, i):
    n = size // B
    return [slice(k * B, (k + 1) * B) for k in (i, n - 1 - i)]


def part_rows(size, shards):
    return size // 4 // shards


def shard_rows(size, shards):
    return part_rows(size, shards) * (size // B) + 8


def places():
    row = lax.broadcasted_iota(jnp.int32, (B, B), 0)
    column = lax.broadcasted_iota(jnp.int32, (B, B), 1)
    return row, column


def pack(g, packed, keep_ref, send_ref, me, shards, chunk):
    size = g.shape[0]
    rows, height = part_rows(size, shards), shard_rows(size, shards)
    per = B // rows
    row, column = places()
    whole = lambda p, q: g[p, q] + g[q, p].T
    for line, i in enumerate(chunk_lines(size, chunk)):
        starts = [((line * per + s) ^ me) * height for s in range(per)]

        def put(at, s, value):
            start = pl.multiple_of(starts[s] + at, 8)
            packed[pl.ds(start, value.shape[0]), :] = value

        upper, lower = [whole(p, p) for p in diagonal_blocks(size, i)]
        for k, place in enumerate([None] + line_blocks(size, i)):
            block = whole(*place) if place else jnp.where(column >= row, upper, lower)
            for s in range(per):
                put(k * rows, s, block[s * rows:(s + 1) * rows])
        element = jnp.sum(jnp.where(column == row, lower, 0.0), axis=0, keepdims=True)
        for s in range(per):
            put(height - 8, s, jnp.broadcast_to(element, (8, B)))
    half = keep_ref.shape[0]
    keep_ref[...] = packed[:half]
    send_ref[...] = packed[half:]


def unpack(pieces, packed, hi, lo, me, shards, chunk):
    size = hi.shape[0]
    rows, height = part_rows(size, shards), shard_rows(size, shards)
    per = B // rows
    row, column = places()
    slot = 0
    for piece in pieces:
        for s in range(piece.shape[0] // height):
            at = pl.multiple_of((slot ^ me) * height, 8)
            packed[pl.ds(at, height), :] = piece[s * height:(s + 1) * height, :]
            slot += 1

    def put(p, q, block):
        hi[p, q], lo[p, q] = split(block)

    for line, i in enumerate(chunk_lines(size, chunk)):
        start = line * per * height

        def get(k):
            return jnp.concatenate(
                [
                    packed[start + s * height + k * rows:start + s * height + (k + 1) * rows, :]
                    for s in range(per)
                ],
                axis=0,
            )

        first, last = diagonal_blocks(size, i)
        block = get(0)
        turned = block.T
        element = packed[start + height - 8:start + height - 7, :]
        put(first, first, jnp.where(column >= row, block, turned))
        below = jnp.where(column < row, block, turned)
        put(last, last, jnp.where(column == row, jnp.broadcast_to(element, (B, B)), below))
        for k, (p, q) in enumerate(line_blocks(size, i)):
            block = get(k + 1)
            put(p, q, block)
            put(q, p, block.T)


def packed_scratch(size, shards):
    return pltpu.VMEM((shards * shard_rows(size, shards), B), F32)


def halves(size, shards):
    return [struct(shards // 2 * shard_rows(size, shards), B)] * 2


def first_gram_kernel(
    shards, me_ref, a_hbm, b_hbm, keep_ref, send_ref, ah, al, bh, bl, a_buf, b_buf, sems, g, packed
):
    rows, size = a_buf.shape
    q = size // 4
    steps = sems.shape[1]
    tile = rows // steps

    def copies(step):
        r = slice(step * tile, (step + 1) * tile)
        return [
            pltpu.make_async_copy(src.at[r], dst.at[r], sems.at[k, step])
            for k, (src, dst) in enumerate([(a_hbm, a_buf), (b_hbm, b_buf)])
        ]

    def start(step):
        for copy in copies(step):
            copy.start()

    start(0)
    start(1)
    for step in range(steps):
        r = slice(step * tile, (step + 1) * tile)
        for copy in copies(step):
            copy.wait()
        if step + 2 < steps:
            start(step + 2)
        ah[:, r], al[:, r] = split(a_buf[r].T)
        bh[r], bl[r] = split(b_buf[r])
        for r0, r1, c0, c1 in [(0, q, 0, size), (q, size, 0, q), (3 * q, size, 3 * q, size)]:
            product = mm((ah[r0:r1, r], al[r0:r1, r]), (bh[r, c0:c1], bl[r, c0:c1]))
            if step:
                product += g[r0:r1, c0:c1]
            g[r0:r1, c0:c1] = product
    pack(g, packed, keep_ref, send_ref, me_ref[0], shards, 0)


def first_gram(me, shards, a, b):
    rows, size = a.shape
    hbm = pl.BlockSpec(memory_space=pltpu.HBM)
    return call(
        functools.partial(first_gram_kernel, shards), "first_gram",
        halves(size, shards) + [struct(size, rows, dtype=BF16)] * 2 + [struct(rows, size, dtype=BF16)] * 2,
        43, 0.5, 4,
        in_specs=[SMEM, hbm, hbm],
        out_specs=[VMEM] * 6,
        scratch_shapes=[
            pltpu.VMEM((rows, size), F32), pltpu.VMEM((rows, size), F32),
            pltpu.SemaphoreType.DMA((2, 4)),
            pltpu.VMEM((size, size), F32), packed_scratch(size, shards),
        ],
    )(me, a, b)


def lower_product(g, ah, al, bh, bl):
    size = g.shape[0]
    q = size // 4
    for r0, r1, c0, c1 in [(q, 3 * q, q, size), (3 * q, size, q, 3 * q)]:
        c = slice(c0 - q, c1 - q)
        g[r0:r1, c0:c1] = mm((ah[r0:r1, :], al[r0:r1, :]), (bh[:, c], bl[:, c]))


def other_gram_kernel(shards, me_ref, ah, al, bh, bl, keep_ref, send_ref, g, packed):
    q = g.shape[0] // 4
    lower_product(g, ah, al, bh[:, q:], bl[:, q:])
    pack(g, packed, keep_ref, send_ref, me_ref[0], shards, 1)


def other_gram(me, shards, ah, al, bh, bl):
    size = ah.shape[0]
    return call(
        functools.partial(other_gram_kernel, shards), "other_gram", halves(size, shards), 18, 0.5, 2,
        in_specs=[SMEM] + [VMEM] * 4,
        out_specs=[VMEM, VMEM],
        scratch_shapes=[pltpu.VMEM((size, size), F32), packed_scratch(size, shards)],
    )(me, ah, al, bh, bl)


def tiles(count, tile, step):
    def body(t, _):
        step(pl.ds(pl.multiple_of(t * tile, tile), tile))
        return 0

    lax.fori_loop(0, count // tile, body, 0)


def row_part(part, rows):
    return slice(0, rows // 4) if part == 0 else slice(rows // 4, rows)


def affine_kernel(part, a_ref, b_ref, out_ref, hi, lo):
    r = row_part(part, a_ref.shape[0])
    hi[...], lo[...] = split(a_ref[r])

    def step(c):
        out_ref[:, c] = 1.5 * a_ref[r, c] - 0.5 * mm((hi[...], lo[...]), split(b_ref[:, c]))

    tiles(out_ref.shape[1], 512 if part else 256, step)


def affine(a, b, part):
    rows, size = a.shape
    height = rows // 4 if part == 0 else 3 * rows // 4
    return call(
        functools.partial(affine_kernel, part), "affine", struct(height, size), 18,
        height / rows, 2,
        in_specs=[VMEM, VMEM],
        out_specs=VMEM,
        scratch_shapes=[pltpu.VMEM((height, size), BF16)] * 2,
    )(a, b)


def affine_parts_kernel(part, ah, al, b_ref, out_ref):
    r = row_part(part, ah.shape[0])

    def step(c):
        product = mm((ah[r], al[r]), split(b_ref[:, c]))
        out_ref[:, c] = 1.5 * (ah[r, c].astype(F32) + al[r, c].astype(F32)) - 0.5 * product

    tiles(out_ref.shape[1], 512 if part else 256, step)


def affine_parts(ah, al, b, part):
    rows, size = ah.shape
    height = rows // 4 if part == 0 else 3 * rows // 4
    return call(
        functools.partial(affine_parts_kernel, part), "affine_parts", struct(height, size), 18,
        height / rows, 2,
        in_specs=[VMEM] * 3,
        out_specs=VMEM,
    )(ah, al, b)


SPANS = (
    (((0, 4),), ((0, 1),), ((0, 1),), ((0, 1), (3, 4))),
    ((), ((1, 4),), ((1, 4),), ((1, 3),)),
)


def sym_product(ah, al, hi, lo, chunk, column, rows=slice(None)):
    q = hi.shape[0] // 4
    spans = [slice(k0 * q, k1 * q) for k0, k1 in SPANS[chunk][column]]
    c = slice(column * q, (column + 1) * q)
    a = [ref[rows, k] for ref in (ah, ah, al) for k in spans]
    b = [ref[k, c] for ref in (hi, lo, hi) for k in spans]
    return c, jnp.dot(
        jnp.concatenate(a, axis=1), jnp.concatenate(b, axis=0), preferred_element_type=F32
    )


def apply_first(base_refs, out_ref, ah, al, hi, lo, columns):
    q = hi.shape[0] // 4
    for column in columns:
        c, product = sym_product(ah, al, hi, lo, 0, column)
        out = slice(c.start - columns[0] * q, c.stop - columns[0] * q)
        at = 0
        for base_ref in base_refs:
            end = at + base_ref.shape[0]
            out_ref[at:end, out] = base_ref[:, c] - 0.5 * product[at:end]
            at = end


def sym_scratch(size, shards):
    return [pltpu.VMEM((size, size), BF16)] * 2 + [packed_scratch(size, shards)]


def first_part_kernel(shards, count, columns, me_ref, *refs):
    pieces, refs = refs[:count], refs[count:]
    ah, al, base_refs, (out_ref, hi, lo, packed) = refs[0], refs[1], refs[2:-4], refs[-4:]
    unpack(pieces, packed, hi, lo, me_ref[0], shards, 0)
    apply_first(base_refs, out_ref, ah, al, hi, lo, columns)


def first_part(me, shards, pieces, ah, al, base, columns):
    rows, size = ah.shape
    part = struct(size, size, dtype=BF16)
    more = len(columns) < 4
    scratch = sym_scratch(size, shards)
    return call(
        functools.partial(first_part_kernel, shards, len(pieces), columns), "first_part",
        [struct(rows, len(columns) * size // 4)] + [part, part] * more, 18, 0.5, 3,
        in_specs=[SMEM] + [VMEM] * (len(pieces) + 2 + len(base)),
        out_specs=[VMEM] * (1 + 2 * more),
        scratch_shapes=scratch[2 * more:],
    )(me, *pieces, ah, al, *base)


def other_part_kernel(columns, ah, al, hi, lo, *refs):
    apply_first(refs[:-1], refs[-1], ah, al, hi, lo, columns)


def other_part(ah, al, hi, lo, base, columns):
    rows, size = ah.shape
    return call(
        functools.partial(other_part_kernel, columns), "other_part",
        struct(rows, len(columns) * size // 4), 16, 0.25, 3,
        in_specs=[VMEM] * (4 + len(base)),
        out_specs=VMEM,
    )(ah, al, hi, lo, *base)


def column_kernel(xh, xl, mid_ref, col_ref):
    col_ref[...] = mm((xh[...], xl[...]), split(mid_ref[...]))


def column_product(xh, xl, mid):
    size, rows = xh.shape
    block = pl.BlockSpec((rows, size // 4), lambda r: (0, 0))
    whole = pl.BlockSpec((size, rows), lambda r: (0, 0))
    return call(
        column_kernel, "column_product", struct(size, size // 4), 16, 0.25, 2,
        grid=(1,), in_specs=[whole, whole, block], out_specs=block,
    )(xh, xl, mid)


def turn_kernel(x_ref, xh, xl):
    def step(r):
        xh[:, r], xl[:, r] = split(x_ref[r].T)

    tiles(x_ref.shape[0], 256, step)


def turn(x):
    part = struct(*x.shape[::-1], dtype=BF16)
    return call(
        turn_kernel, "turn", [part, part], 16, 0.1, 2, in_specs=[VMEM], out_specs=[VMEM] * 2
    )(x)


def cut_kernel(which, x_ref, *out_refs):
    def step(r):
        parts = split(x_ref[r])
        for out_ref, k in zip(out_refs, which):
            out_ref[r] = parts[k]

    tiles(x_ref.shape[0], 128, step)


def cut(x, *which):
    count = len(which)
    return call(
        functools.partial(cut_kernel, which), "cut", [struct(*x.shape, dtype=BF16)] * count,
        16, 0.25, 2, in_specs=[VMEM], out_specs=[VMEM] * count,
    )(x)


def second_gram_kernel(shards, count, me_ref, *refs):
    pieces, refs = refs[:count], refs[count:]
    (ah, al, base_ref, xh, xl, col_ref), refs = refs[:6], refs[6:]
    keep_ref, send_ref, mh, ml, hi, lo, packed, g = refs
    size = g.shape[0]
    q = size // 4
    unpack(pieces, packed, hi, lo, me_ref[0], shards, 1)
    mh[:, :q], ml[:, :q] = split(base_ref[:, :q])
    for column in range(1, 4):
        c, product = sym_product(ah, al, hi, lo, 1, column)
        mid = base_ref[:, c] - 0.5 * product
        mh[:, c], ml[:, c] = split(mid)
    g[:, :q] = col_ref[...]
    g[:q, q:] = mm((xh[:q, :], xl[:q, :]), (mh[:, q:], ml[:, q:]))
    g[3 * q:, 3 * q:] = mm((xh[3 * q:, :], xl[3 * q:, :]), (mh[:, 3 * q:], ml[:, 3 * q:]))
    pack(g, packed, keep_ref, send_ref, me_ref[0], shards, 0)


def second_gram(me, shards, pieces, ah, al, base, xh, xl, col):
    rows, size = ah.shape
    part = struct(rows, size, dtype=BF16)
    return call(
        functools.partial(second_gram_kernel, shards, len(pieces)), "second_gram",
        halves(size, shards) + [part, part], 20, 0.8, 5,
        in_specs=[SMEM] + [VMEM] * (len(pieces) + 6),
        out_specs=[VMEM] * 4,
        scratch_shapes=sym_scratch(size, shards) + [pltpu.VMEM((size, size), F32)],
    )(me, *pieces, ah, al, base, xh, xl, col)


def fourth_gram_kernel(shards, me_ref, xh, xl, mh, ml, keep_ref, send_ref, g, packed):
    q = g.shape[0] // 4
    lower_product(g, xh, xl, mh[:, q:], ml[:, q:])
    pack(g, packed, keep_ref, send_ref, me_ref[0], shards, 1)


def fourth_gram(me, shards, xh, xl, mh, ml):
    size = xh.shape[0]
    return call(
        functools.partial(fourth_gram_kernel, shards), "fourth_gram", halves(size, shards), 18, 0.5, 2,
        in_specs=[SMEM] + [VMEM] * 4,
        out_specs=[VMEM, VMEM],
        scratch_shapes=[pltpu.VMEM((size, size), F32), packed_scratch(size, shards)],
    )(me, xh, xl, mh, ml)


def last_kernel(shards, count, me_ref, *refs):
    pieces = refs[:count]
    ah, al, z_ref, rest_ref, out_hbm, hi, lo, packed, out, sems = refs[count:]
    q = hi.shape[0] // 4
    copies = []

    def send(src, rows, c):
        copy = pltpu.make_async_copy(src, out_hbm.at[rows, c], sems.at[len(copies)])
        copy.start()
        copies.append(copy)

    count = out.shape[0]
    send(z_ref, slice(0, count), slice(0, q))
    unpack(pieces, packed, hi, lo, me_ref[0], shards, 1)
    for column in (1, 2, 3):
        parts = 2 if column == 3 else 1
        for part in range(parts):
            r = slice(part * count // parts, (part + 1) * count // parts)
            c, product = sym_product(ah, al, hi, lo, 1, column, r)
            out[r, c] = rest_ref[r, c.start - q:c.stop - q] - 0.5 * product
            send(out.at[r, c], r, c)
    for copy in copies:
        copy.wait()


def last_step(me, shards, pieces, ah, al, z, rest):
    rows, size = ah.shape
    return call(
        functools.partial(last_kernel, shards, len(pieces)), "last", struct(rows, size), 22, 0.5, 3,
        in_specs=[SMEM] + [VMEM] * (len(pieces) + 4),
        out_specs=pl.BlockSpec(memory_space=pltpu.HBM),
        scratch_shapes=sym_scratch(size, shards)
        + [pltpu.VMEM((rows, size), F32), pltpu.SemaphoreType.DMA((5,))],
    )(me, *pieces, ah, al, z, rest)


CORE = 1
PLANE = (2, 4, 6)
SHARDS = 2 * (1 + len(PLANE))


def slot_of(index):
    return (index % 2) * (SHARDS // 2) + (index // 2) % (SHARDS // 2)


class Sum:
    def __init__(self, count, keep, send):
        self.count, self.keep, self.send = count, keep, send

    def swap(self, x, offset):
        return lax.ppermute(x, "row", [(i, i ^ offset) for i in range(self.count)])

    def swaps(self, values):
        return [self.swap(x, offset) for x, offset in zip(values, PLANE)]

    def core(self):
        return self.swap(self.send, CORE)

    def plane(self, got):
        total = self.keep + got
        part = total.shape[0] // (1 + len(PLANE))
        self.keep, *sends = [total[k * part:(k + 1) * part] for k in range(1 + len(PLANE))]
        return self.swaps(sends)

    def own(self, got):
        self.keep = sum(got, self.keep)

    def exchange(self, offset):
        return self.swap(self.keep, offset)

    def gather_plane(self):
        return self.swaps([self.keep] * len(PLANE))

    def gather_core(self, got):
        self.mine = jnp.concatenate([self.keep, *got], axis=0)
        return self.swap(self.mine, CORE)


def close(env, *got):
    values = lax.optimization_barrier((*env.values(), *got[::-1]))
    env.update(zip(env, values))
    return values[len(env):][::-1]


def sum_chunks(count, env, first, second, works, late):
    beyond = [1 << s for s in range(3, count.bit_length() - 1)]
    works = list(works)

    def work():
        if works:
            works.pop(0)(env)

    a = Sum(count, *first)
    got_a = a.core()
    pair = second(env)
    got_a, *pair = close(env, got_a, *pair)
    b = Sum(count, *pair)

    got_a = a.plane(got_a)
    got_b = b.core()
    work()
    (got_b,) = close(env, got_b)

    got_b = b.plane(got_b)[::-1]
    work()
    a.own(close(env, *got_a))

    for offset in beyond:
        got_a = a.exchange(offset)
        work()
        b.own(close(env, *got_b))
        got_b = [b.exchange(offset)]
        a.own(close(env, got_a))

    got_a = a.gather_plane()
    b.own(close(env, *got_b))

    got_b = b.gather_plane()[::-1]
    got_a = a.gather_core(close(env, *got_a))
    work()
    (got_a,) = close(env, got_a)
    late[0](env, [a.mine, got_a])
    got_b = b.gather_core(close(env, *got_b)[::-1])
    late[1](env)
    (got_b,) = close(env, got_b)
    return [b.mine, got_b]


def body(count, orbitals_zero, orbitals_one, correlation_zero, correlation_one, cotangent):
    me = slot_of(lax.axis_index("row")).astype(jnp.int32).reshape(1)
    env = dict(
        x0=orbitals_zero, x1=orbitals_one, s0=correlation_zero, s1=correlation_one, c=cotangent
    )

    def direct(part):
        def work(env):
            env[f"m{part}"] = affine(env["c"], env["s1"], part)
        return work

    def turned(env):
        env["xh"], env["xl"] = turn(env["x0"])

    def cut_one(env):
        env["x1h"], env["x1l"] = cut(env["x1"], 0, 1)

    def middle(env, pieces):
        (env["mid"],) = first_part(
            me, SHARDS, pieces, env["x1h"], env["x1l"], [env["m0"], env["m1"]], (0, 1, 2, 3)
        )

    def column(env):
        env["col"] = column_product(env["xh"], env["xl"], env["mid"])

    keep, send, *parts = first_gram(me, SHARDS, env["x1"], env["c"])
    one = sum_chunks(
        count, env, (keep, send), lambda env: other_gram(me, SHARDS, *parts),
        [direct(0), cut_one, direct(1), turned], [middle, column],
    )

    keep, send, env["mh"], env["ml"] = second_gram(
        me, SHARDS, one, env["x1h"], env["x1l"], env["mid"], env["xh"], env["xl"], env["col"]
    )

    def last_direct(part):
        def work(env):
            env[f"d{part}"] = affine_parts(env["mh"], env["ml"], env["s0"], part)
        return work

    def high(env):
        (env["x0h"],) = cut(env["x0"], 0)

    def low(env):
        (env["x0l"],) = cut(env["x0"], 1)

    def result(env, pieces):
        env["z"], env["symh"], env["syml"] = first_part(
            me, SHARDS, pieces, env["x0h"], env["x0l"], [env["d0"], env["d1"]], (0,)
        )

    def rest(env):
        env["rest"] = other_part(
            env["x0h"], env["x0l"], env["symh"], env["syml"], [env["d0"], env["d1"]], (1, 2, 3)
        )

    two = sum_chunks(
        count, env, (keep, send),
        lambda env: fourth_gram(me, SHARDS, env["xh"], env["xl"], env["mh"], env["ml"]),
        [last_direct(0), high, last_direct(1), low], [result, rest],
    )
    return last_step(me, SHARDS, two, env["x0h"], env["x0l"], env["z"], env["rest"])


def solution(mesh):
    in_specs = (
        P(("kpt", "row"), None),
        P(("kpt", "row"), None),
        P("kpt", None),
        P("kpt", None),
        P(("kpt", "row"), None),
    )
    out_specs = P(("kpt", "row"), None)
    return jax.shard_map(
        functools.partial(body, mesh.shape["row"]),
        mesh=mesh, in_specs=in_specs, out_specs=out_specs, check_vma=False,
    )
```

```python
import functools
import jax
import jax.numpy as jnp
from jax import lax
from jax.experimental import pallas as pl
from jax.experimental.pallas import tpu as pltpu
from jax.sharding import PartitionSpec as P

F32 = jnp.float32
BF16 = jnp.bfloat16
B = 128
MIB = 1024 * 1024
WEIGHT = 10


def split(x):
    hi = x.astype(BF16)
    return hi, (x - hi.astype(F32)).astype(BF16)


def mm(a, b):
    (ah, al), (bh, bl) = a, b
    return jnp.dot(
        jnp.concatenate([ah, ah, al], axis=1),
        jnp.concatenate([bh, bl, bh], axis=0),
        preferred_element_type=F32,
    )


def call(kernel, name, out_shape, limit, products, arrays, **kw):
    size = 1024
    return pl.pallas_call(
        kernel,
        name=name,
        out_shape=out_shape,
        compiler_params=pltpu.CompilerParams(vmem_limit_bytes=limit * MIB),
        cost_estimate=pl.CostEstimate(
            flops=int(WEIGHT * 6 * products * size ** 3),
            bytes_accessed=int(WEIGHT * 4 * arrays * size * size),
            transcendentals=0,
        ),
        **kw,
    )


def struct(*shape, dtype=F32):
    return jax.ShapeDtypeStruct(shape, dtype)


SMEM = pl.BlockSpec(memory_space=pltpu.SMEM)
VMEM = pl.BlockSpec(memory_space=pltpu.VMEM)


def chunk_lines(size, chunk):
    half = size // B // 4
    return range(chunk * half, (chunk + 1) * half)


def line_blocks(size, i):
    n = size // B
    block = lambda k: slice(k * B, (k + 1) * B)
    return [(block(top), block(j)) for top in (i, n - 1 - i) for j in range(top + 1, n)]


def diagonal_blocks(size, i):
    n = size // B
    return [slice(k * B, (k + 1) * B) for k in (i, n - 1 - i)]


def part_rows(size, shards):
    return size // 4 // shards


def shard_rows(size, shards):
    return part_rows(size, shards) * (size // B) + 8


def places():
    row = lax.broadcasted_iota(jnp.int32, (B, B), 0)
    column = lax.broadcasted_iota(jnp.int32, (B, B), 1)
    return row, column


def pack(g, packed, keep_ref, send_ref, me, shards, chunk):
    size = g.shape[0]
    rows, height = part_rows(size, shards), shard_rows(size, shards)
    per = B // rows
    row, column = places()
    whole = lambda p, q: g[p, q] + g[q, p].T
    for line, i in enumerate(chunk_lines(size, chunk)):
        starts = [((line * per + s) ^ me) * height for s in range(per)]

        def put(at, s, value):
            start = pl.multiple_of(starts[s] + at, 8)
            packed[pl.ds(start, value.shape[0]), :] = value

        upper, lower = [whole(p, p) for p in diagonal_blocks(size, i)]
        for k, place in enumerate([None] + line_blocks(size, i)):
            block = whole(*place) if place else jnp.where(column >= row, upper, lower)
            for s in range(per):
                put(k * rows, s, block[s * rows:(s + 1) * rows])
        element = jnp.sum(jnp.where(column == row, lower, 0.0), axis=0, keepdims=True)
        for s in range(per):
            put(height - 8, s, jnp.broadcast_to(element, (8, B)))
    half = keep_ref.shape[0]
    keep_ref[...] = packed[:half]
    send_ref[...] = packed[half:]


def unpack(pieces, packed, hi, lo, me, shards, chunk):
    size = hi.shape[0]
    rows, height = part_rows(size, shards), shard_rows(size, shards)
    per = B // rows
    row, column = places()
    slot = 0
    for piece in pieces:
        for s in range(piece.shape[0] // height):
            at = pl.multiple_of((slot ^ me) * height, 8)
            packed[pl.ds(at, height), :] = piece[s * height:(s + 1) * height, :]
            slot += 1

    def put(p, q, block):
        hi[p, q], lo[p, q] = split(block)

    for line, i in enumerate(chunk_lines(size, chunk)):
        start = line * per * height

        def get(k):
            return jnp.concatenate(
                [
                    packed[start + s * height + k * rows:start + s * height + (k + 1) * rows, :]
                    for s in range(per)
                ],
                axis=0,
            )

        first, last = diagonal_blocks(size, i)
        block = get(0)
        turned = block.T
        element = packed[start + height - 8:start + height - 7, :]
        put(first, first, jnp.where(column >= row, block, turned))
        below = jnp.where(column < row, block, turned)
        put(last, last, jnp.where(column == row, jnp.broadcast_to(element, (B, B)), below))
        for k, (p, q) in enumerate(line_blocks(size, i)):
            block = get(k + 1)
            put(p, q, block)
            put(q, p, block.T)


def packed_scratch(size, shards):
    return pltpu.VMEM((shards * shard_rows(size, shards), B), F32)


def halves(size, shards):
    return [struct(shards // 2 * shard_rows(size, shards), B)] * 2


def first_gram_kernel(
    shards, me_ref, a_hbm, b_hbm, keep_ref, send_ref, ah, al, bh, bl, a_buf, b_buf, sems, g, packed
):
    rows, size = a_buf.shape
    q = size // 4
    steps = sems.shape[1]
    tile = rows // steps

    def copies(step):
        r = slice(step * tile, (step + 1) * tile)
        return [
            pltpu.make_async_copy(src.at[r], dst.at[r], sems.at[k, step])
            for k, (src, dst) in enumerate([(a_hbm, a_buf), (b_hbm, b_buf)])
        ]

    def start(step):
        for copy in copies(step):
            copy.start()

    start(0)
    start(1)
    for step in range(steps):
        r = slice(step * tile, (step + 1) * tile)
        for copy in copies(step):
            copy.wait()
        if step + 2 < steps:
            start(step + 2)
        ah[:, r], al[:, r] = split(a_buf[r].T)
        bh[r], bl[r] = split(b_buf[r])
        for r0, r1, c0, c1 in [(0, q, 0, size), (q, size, 0, q), (3 * q, size, 3 * q, size)]:
            product = mm((ah[r0:r1, r], al[r0:r1, r]), (bh[r, c0:c1], bl[r, c0:c1]))
            if step:
                product += g[r0:r1, c0:c1]
            g[r0:r1, c0:c1] = product
    pack(g, packed, keep_ref, send_ref, me_ref[0], shards, 0)


def first_gram(me, shards, a, b):
    rows, size = a.shape
    hbm = pl.BlockSpec(memory_space=pltpu.HBM)
    return call(
        functools.partial(first_gram_kernel, shards), "first_gram",
        halves(size, shards) + [struct(size, rows, dtype=BF16)] * 2 + [struct(rows, size, dtype=BF16)] * 2,
        43, 0.5, 4,
        in_specs=[SMEM, hbm, hbm],
        out_specs=[VMEM] * 6,
        scratch_shapes=[
            pltpu.VMEM((rows, size), F32), pltpu.VMEM((rows, size), F32),
            pltpu.SemaphoreType.DMA((2, 4)),
            pltpu.VMEM((size, size), F32), packed_scratch(size, shards),
        ],
    )(me, a, b)


def lower_product(g, ah, al, bh, bl):
    size = g.shape[0]
    q = size // 4
    for r0, r1, c0, c1 in [(q, 3 * q, q, size), (3 * q, size, q, 3 * q)]:
        c = slice(c0 - q, c1 - q)
        g[r0:r1, c0:c1] = mm((ah[r0:r1, :], al[r0:r1, :]), (bh[:, c], bl[:, c]))


def other_gram_kernel(shards, me_ref, ah, al, bh, bl, keep_ref, send_ref, g, packed):
    q = g.shape[0] // 4
    lower_product(g, ah, al, bh[:, q:], bl[:, q:])
    pack(g, packed, keep_ref, send_ref, me_ref[0], shards, 1)


def other_gram(me, shards, ah, al, bh, bl):
    size = ah.shape[0]
    return call(
        functools.partial(other_gram_kernel, shards), "other_gram", halves(size, shards), 18, 0.5, 2,
        in_specs=[SMEM] + [VMEM] * 4,
        out_specs=[VMEM, VMEM],
        scratch_shapes=[pltpu.VMEM((size, size), F32), packed_scratch(size, shards)],
    )(me, ah, al, bh, bl)


def tiles(count, tile, step):
    def body(t, _):
        step(pl.ds(pl.multiple_of(t * tile, tile), tile))
        return 0

    lax.fori_loop(0, count // tile, body, 0)


def row_part(part, rows):
    return slice(0, rows // 4) if part == 0 else slice(rows // 4, rows)


def affine_kernel(part, a_ref, b_ref, out_ref, hi, lo):
    r = row_part(part, a_ref.shape[0])
    hi[...], lo[...] = split(a_ref[r])

    def step(c):
        out_ref[:, c] = 1.5 * a_ref[r, c] - 0.5 * mm((hi[...], lo[...]), split(b_ref[:, c]))

    tiles(out_ref.shape[1], 512 if part else 256, step)


def affine(a, b, part):
    rows, size = a.shape
    height = rows // 4 if part == 0 else 3 * rows // 4
    return call(
        functools.partial(affine_kernel, part), "affine", struct(height, size), 18,
        height / rows, 2,
        in_specs=[VMEM, VMEM],
        out_specs=VMEM,
        scratch_shapes=[pltpu.VMEM((height, size), BF16)] * 2,
    )(a, b)


def affine_parts_kernel(part, ah, al, b_ref, out_ref):
    r = row_part(part, ah.shape[0])

    def step(c):
        product = mm((ah[r], al[r]), split(b_ref[:, c]))
        out_ref[:, c] = 1.5 * (ah[r, c].astype(F32) + al[r, c].astype(F32)) - 0.5 * product

    tiles(out_ref.shape[1], 512 if part else 256, step)


def affine_parts(ah, al, b, part):
    rows, size = ah.shape
    height = rows // 4 if part == 0 else 3 * rows // 4
    return call(
        functools.partial(affine_parts_kernel, part), "affine_parts", struct(height, size), 18,
        height / rows, 2,
        in_specs=[VMEM] * 3,
        out_specs=VMEM,
    )(ah, al, b)


SPANS = (
    (((0, 4),), ((0, 1),), ((0, 1),), ((0, 1), (3, 4))),
    ((), ((1, 4),), ((1, 4),), ((1, 3),)),
)


def sym_product(ah, al, hi, lo, chunk, column, rows=slice(None)):
    q = hi.shape[0] // 4
    spans = [slice(k0 * q, k1 * q) for k0, k1 in SPANS[chunk][column]]
    c = slice(column * q, (column + 1) * q)
    a = [ref[rows, k] for ref in (ah, ah, al) for k in spans]
    b = [ref[k, c] for ref in (hi, lo, hi) for k in spans]
    return c, jnp.dot(
        jnp.concatenate(a, axis=1), jnp.concatenate(b, axis=0), preferred_element_type=F32
    )


def apply_first(base_refs, out_ref, ah, al, hi, lo, columns):
    q = hi.shape[0] // 4
    for column in columns:
        c, product = sym_product(ah, al, hi, lo, 0, column)
        out = slice(c.start - columns[0] * q, c.stop - columns[0] * q)
        at = 0
        for base_ref in base_refs:
            end = at + base_ref.shape[0]
            out_ref[at:end, out] = base_ref[:, c] - 0.5 * product[at:end]
            at = end


def sym_scratch(size, shards):
    return [pltpu.VMEM((size, size), BF16)] * 2 + [packed_scratch(size, shards)]


def first_part_kernel(shards, count, columns, me_ref, *refs):
    pieces, refs = refs[:count], refs[count:]
    ah, al, base_refs, (out_ref, hi, lo, packed) = refs[0], refs[1], refs[2:-4], refs[-4:]
    unpack(pieces, packed, hi, lo, me_ref[0], shards, 0)
    apply_first(base_refs, out_ref, ah, al, hi, lo, columns)


def first_part(me, shards, pieces, ah, al, base, columns):
    rows, size = ah.shape
    part = struct(size, size, dtype=BF16)
    more = len(columns) < 4
    scratch = sym_scratch(size, shards)
    return call(
        functools.partial(first_part_kernel, shards, len(pieces), columns), "first_part",
        [struct(rows, len(columns) * size // 4)] + [part, part] * more, 18, 0.5, 3,
        in_specs=[SMEM] + [VMEM] * (len(pieces) + 2 + len(base)),
        out_specs=[VMEM] * (1 + 2 * more),
        scratch_shapes=scratch[2 * more:],
    )(me, *pieces, ah, al, *base)


def other_part_kernel(columns, ah, al, hi, lo, *refs):
    apply_first(refs[:-1], refs[-1], ah, al, hi, lo, columns)


def other_part(ah, al, hi, lo, base, columns):
    rows, size = ah.shape
    return call(
        functools.partial(other_part_kernel, columns), "other_part",
        struct(rows, len(columns) * size // 4), 16, 0.25, 3,
        in_specs=[VMEM] * (4 + len(base)),
        out_specs=VMEM,
    )(ah, al, hi, lo, *base)


def column_kernel(xh, xl, mid_ref, col_ref):
    col_ref[...] = mm((xh[...], xl[...]), split(mid_ref[...]))


def column_product(xh, xl, mid):
    size, rows = xh.shape
    block = pl.BlockSpec((rows, size // 4), lambda r: (0, 0))
    whole = pl.BlockSpec((size, rows), lambda r: (0, 0))
    return call(
        column_kernel, "column_product", struct(size, size // 4), 16, 0.25, 2,
        grid=(1,), in_specs=[whole, whole, block], out_specs=block,
    )(xh, xl, mid)


def turn_kernel(x_ref, xh, xl):
    def step(r):
        xh[:, r], xl[:, r] = split(x_ref[r].T)

    tiles(x_ref.shape[0], 256, step)


def turn(x):
    part = struct(*x.shape[::-1], dtype=BF16)
    return call(
        turn_kernel, "turn", [part, part], 16, 0.1, 2, in_specs=[VMEM], out_specs=[VMEM] * 2
    )(x)


def cut_kernel(which, x_ref, *out_refs):
    def step(r):
        parts = split(x_ref[r])
        for out_ref, k in zip(out_refs, which):
            out_ref[r] = parts[k]

    tiles(x_ref.shape[0], 128, step)


def cut(x, *which):
    count = len(which)
    return call(
        functools.partial(cut_kernel, which), "cut", [struct(*x.shape, dtype=BF16)] * count,
        16, 0.25, 2, in_specs=[VMEM], out_specs=[VMEM] * count,
    )(x)


def second_gram_kernel(shards, count, me_ref, *refs):
    pieces, refs = refs[:count], refs[count:]
    (ah, al, base_ref, xh, xl, col_ref), refs = refs[:6], refs[6:]
    keep_ref, send_ref, mh, ml, hi, lo, packed, g = refs
    size = g.shape[0]
    q = size // 4
    unpack(pieces, packed, hi, lo, me_ref[0], shards, 1)
    mh[:, :q], ml[:, :q] = split(base_ref[:, :q])
    for column in range(1, 4):
        c, product = sym_product(ah, al, hi, lo, 1, column)
        mid = base_ref[:, c] - 0.5 * product
        mh[:, c], ml[:, c] = split(mid)
    g[:, :q] = col_ref[...]
    g[:q, q:] = mm((xh[:q, :], xl[:q, :]), (mh[:, q:], ml[:, q:]))
    g[3 * q:, 3 * q:] = mm((xh[3 * q:, :], xl[3 * q:, :]), (mh[:, 3 * q:], ml[:, 3 * q:]))
    pack(g, packed, keep_ref, send_ref, me_ref[0], shards, 0)


def second_gram(me, shards, pieces, ah, al, base, xh, xl, col):
    rows, size = ah.shape
    part = struct(rows, size, dtype=BF16)
    return call(
        functools.partial(second_gram_kernel, shards, len(pieces)), "second_gram",
        halves(size, shards) + [part, part], 20, 0.8, 5,
        in_specs=[SMEM] + [VMEM] * (len(pieces) + 6),
        out_specs=[VMEM] * 4,
        scratch_shapes=sym_scratch(size, shards) + [pltpu.VMEM((size, size), F32)],
    )(me, *pieces, ah, al, base, xh, xl, col)


def fourth_gram_kernel(shards, me_ref, xh, xl, mh, ml, keep_ref, send_ref, g, packed):
    q = g.shape[0] // 4
    lower_product(g, xh, xl, mh[:, q:], ml[:, q:])
    pack(g, packed, keep_ref, send_ref, me_ref[0], shards, 1)


def fourth_gram(me, shards, xh, xl, mh, ml):
    size = xh.shape[0]
    return call(
        functools.partial(fourth_gram_kernel, shards), "fourth_gram", halves(size, shards), 18, 0.5, 2,
        in_specs=[SMEM] + [VMEM] * 4,
        out_specs=[VMEM, VMEM],
        scratch_shapes=[pltpu.VMEM((size, size), F32), packed_scratch(size, shards)],
    )(me, xh, xl, mh, ml)


def last_kernel(shards, count, me_ref, *refs):
    pieces = refs[:count]
    ah, al, z_ref, rest_ref, out_hbm, hi, lo, packed, out, sems = refs[count:]
    q = hi.shape[0] // 4
    copies = []

    def send(src, rows, c):
        copy = pltpu.make_async_copy(src, out_hbm.at[rows, c], sems.at[len(copies)])
        copy.start()
        copies.append(copy)

    count = out.shape[0]
    send(z_ref, slice(0, count), slice(0, q))
    unpack(pieces, packed, hi, lo, me_ref[0], shards, 1)
    for column in (1, 2, 3):
        parts = 2 if column == 3 else 1
        for part in range(parts):
            r = slice(part * count // parts, (part + 1) * count // parts)
            c, product = sym_product(ah, al, hi, lo, 1, column, r)
            out[r, c] = rest_ref[r, c.start - q:c.stop - q] - 0.5 * product
            send(out.at[r, c], r, c)
    for copy in copies:
        copy.wait()


def last_step(me, shards, pieces, ah, al, z, rest):
    rows, size = ah.shape
    return call(
        functools.partial(last_kernel, shards, len(pieces)), "last", struct(rows, size), 22, 0.5, 3,
        in_specs=[SMEM] + [VMEM] * (len(pieces) + 4),
        out_specs=pl.BlockSpec(memory_space=pltpu.HBM),
        scratch_shapes=sym_scratch(size, shards)
        + [pltpu.VMEM((rows, size), F32), pltpu.SemaphoreType.DMA((5,))],
    )(me, *pieces, ah, al, z, rest)


CORE = 1
PLANE = (2, 4, 6)
SHARDS = 2 * (1 + len(PLANE))


def slot_of(index):
    return (index % 2) * (SHARDS // 2) + (index // 2) % (SHARDS // 2)


class Sum:
    def __init__(self, count, keep, send):
        self.count, self.keep, self.send = count, keep, send

    def swap(self, x, offset):
        return lax.ppermute(x, "row", [(i, i ^ offset) for i in range(self.count)])

    def swaps(self, values):
        return [self.swap(x, offset) for x, offset in zip(values, PLANE)]

    def core(self):
        return self.swap(self.send, CORE)

    def plane(self, got):
        total = self.keep + got
        part = total.shape[0] // (1 + len(PLANE))
        self.keep, *sends = [total[k * part:(k + 1) * part] for k in range(1 + len(PLANE))]
        return self.swaps(sends)

    def own(self, got):
        self.keep = sum(got, self.keep)

    def exchange(self, offset):
        return self.swap(self.keep, offset)

    def gather_plane(self):
        return self.swaps([self.keep] * len(PLANE))

    def gather_core(self, got):
        self.mine = jnp.concatenate([self.keep, *got], axis=0)
        return self.swap(self.mine, CORE)


def close(env, *got):
    values = lax.optimization_barrier((*env.values(), *got[::-1]))
    env.update(zip(env, values))
    return values[len(env):][::-1]


def sum_chunks(count, env, first, second, works, late):
    beyond = [1 << s for s in range(3, count.bit_length() - 1)]
    works = list(works)

    def work():
        if works:
            works.pop(0)(env)

    a = Sum(count, *first)
    got_a = a.core()
    pair = second(env)
    got_a, *pair = close(env, got_a, *pair)
    b = Sum(count, *pair)

    got_a = a.plane(got_a)
    got_b = b.core()
    work()
    (got_b,) = close(env, got_b)

    got_b = b.plane(got_b)[::-1]
    work()
    a.own(close(env, *got_a))

    for offset in beyond:
        got_a = a.exchange(offset)
        work()
        b.own(close(env, *got_b))
        got_b = [b.exchange(offset)]
        a.own(close(env, got_a))

    side_a, near_a = [a.swap(a.keep, offset) for offset in PLANE[:2]]
    (near_a,) = close(env, near_a)
    diagonal_a = a.swap(near_a, PLANE[0])
    b.own(close(env, *got_b))

    got_b = b.gather_plane()
    side_a, diagonal_a = close(env, side_a, diagonal_a)
    got_a = a.gather_core([side_a, near_a, diagonal_a])
    work()
    (got_a,) = close(env, got_a)
    late[0](env, [a.mine, got_a])
    got_b = b.gather_core(close(env, *got_b))
    late[1](env)
    (got_b,) = close(env, got_b)
    return [b.mine, got_b]


def body(count, orbitals_zero, orbitals_one, correlation_zero, correlation_one, cotangent):
    me = slot_of(lax.axis_index("row")).astype(jnp.int32).reshape(1)
    env = dict(
        x0=orbitals_zero, x1=orbitals_one, s0=correlation_zero, s1=correlation_one, c=cotangent
    )

    def direct(part):
        def work(env):
            env[f"m{part}"] = affine(env["c"], env["s1"], part)
        return work

    def turned(env):
        env["xh"], env["xl"] = turn(env["x0"])

    def cut_one(env):
        env["x1h"], env["x1l"] = cut(env["x1"], 0, 1)

    def middle(env, pieces):
        (env["mid"],) = first_part(
            me, SHARDS, pieces, env["x1h"], env["x1l"], [env["m0"], env["m1"]], (0, 1, 2, 3)
        )

    def column(env):
        env["col"] = column_product(env["xh"], env["xl"], env["mid"])

    keep, send, *parts = first_gram(me, SHARDS, env["x1"], env["c"])
    one = sum_chunks(
        count, env, (keep, send), lambda env: other_gram(me, SHARDS, *parts),
        [direct(0), cut_one, direct(1), turned], [middle, column],
    )

    keep, send, env["mh"], env["ml"] = second_gram(
        me, SHARDS, one, env["x1h"], env["x1l"], env["mid"], env["xh"], env["xl"], env["col"]
    )

    def last_direct(part):
        def work(env):
            env[f"d{part}"] = affine_parts(env["mh"], env["ml"], env["s0"], part)
        return work

    def high(env):
        (env["x0h"],) = cut(env["x0"], 0)

    def low(env):
        (env["x0l"],) = cut(env["x0"], 1)

    def result(env, pieces):
        env["z"], env["symh"], env["syml"] = first_part(
            me, SHARDS, pieces, env["x0h"], env["x0l"], [env["d0"], env["d1"]], (0,)
        )

    def rest(env):
        env["rest"] = other_part(
            env["x0h"], env["x0l"], env["symh"], env["syml"], [env["d0"], env["d1"]], (1, 2, 3)
        )

    two = sum_chunks(
        count, env, (keep, send),
        lambda env: fourth_gram(me, SHARDS, env["xh"], env["xl"], env["mh"], env["ml"]),
        [last_direct(0), high, last_direct(1), low], [result, rest],
    )
    return last_step(me, SHARDS, two, env["x0h"], env["x0l"], env["z"], env["rest"])


def solution(mesh):
    in_specs = (
        P(("kpt", "row"), None),
        P(("kpt", "row"), None),
        P("kpt", None),
        P("kpt", None),
        P(("kpt", "row"), None),
    )
    out_specs = P(("kpt", "row"), None)
    return jax.shard_map(
        functools.partial(body, mesh.shape["row"]),
        mesh=mesh, in_specs=in_specs, out_specs=out_specs, check_vma=False,
    )
```

```python
import functools
import jax
import jax.numpy as jnp
from jax import lax
from jax.experimental import pallas as pl
from jax.experimental.pallas import tpu as pltpu
from jax.sharding import PartitionSpec as P

F32 = jnp.float32
BF16 = jnp.bfloat16
B = 128
MIB = 1024 * 1024
WEIGHT = 10


def split(x):
    hi = x.astype(BF16)
    return hi, (x - hi.astype(F32)).astype(BF16)


def mm(a, b):
    (ah, al), (bh, bl) = a, b
    return jnp.dot(
        jnp.concatenate([ah, ah, al], axis=1),
        jnp.concatenate([bh, bl, bh], axis=0),
        preferred_element_type=F32,
    )


def call(kernel, name, out_shape, limit, products, arrays, **kw):
    size = 1024
    return pl.pallas_call(
        kernel,
        name=name,
        out_shape=out_shape,
        compiler_params=pltpu.CompilerParams(vmem_limit_bytes=limit * MIB),
        cost_estimate=pl.CostEstimate(
            flops=int(WEIGHT * 6 * products * size ** 3),
            bytes_accessed=int(WEIGHT * 4 * arrays * size * size),
            transcendentals=0,
        ),
        **kw,
    )


def struct(*shape, dtype=F32):
    return jax.ShapeDtypeStruct(shape, dtype)


SMEM = pl.BlockSpec(memory_space=pltpu.SMEM)
VMEM = pl.BlockSpec(memory_space=pltpu.VMEM)


def chunk_lines(size, chunk):
    half = size // B // 4
    return range(chunk * half, (chunk + 1) * half)


def line_blocks(size, i):
    n = size // B
    block = lambda k: slice(k * B, (k + 1) * B)
    return [(block(top), block(j)) for top in (i, n - 1 - i) for j in range(top + 1, n)]


def diagonal_blocks(size, i):
    n = size // B
    return [slice(k * B, (k + 1) * B) for k in (i, n - 1 - i)]


def part_rows(size, shards):
    return size // 4 // shards


def shard_rows(size, shards):
    return part_rows(size, shards) * (size // B) + 8


def places():
    row = lax.broadcasted_iota(jnp.int32, (B, B), 0)
    column = lax.broadcasted_iota(jnp.int32, (B, B), 1)
    return row, column


def pack(g, packed, keep_ref, send_ref, me, shards, chunk):
    size = g.shape[0]
    rows, height = part_rows(size, shards), shard_rows(size, shards)
    per = B // rows
    row, column = places()
    whole = lambda p, q: g[p, q] + g[q, p].T
    for line, i in enumerate(chunk_lines(size, chunk)):
        starts = [((line * per + s) ^ me) * height for s in range(per)]

        def put(at, s, value):
            start = pl.multiple_of(starts[s] + at, 8)
            packed[pl.ds(start, value.shape[0]), :] = value

        upper, lower = [whole(p, p) for p in diagonal_blocks(size, i)]
        for k, place in enumerate([None] + line_blocks(size, i)):
            block = whole(*place) if place else jnp.where(column >= row, upper, lower)
            for s in range(per):
                put(k * rows, s, block[s * rows:(s + 1) * rows])
        element = jnp.sum(jnp.where(column == row, lower, 0.0), axis=0, keepdims=True)
        for s in range(per):
            put(height - 8, s, jnp.broadcast_to(element, (8, B)))
    half = keep_ref.shape[0]
    keep_ref[...] = packed[:half]
    send_ref[...] = packed[half:]


def unpack(pieces, packed, hi, lo, me, shards, chunk):
    size = hi.shape[0]
    rows, height = part_rows(size, shards), shard_rows(size, shards)
    per = B // rows
    row, column = places()
    slot = 0
    for piece in pieces:
        for s in range(piece.shape[0] // height):
            at = pl.multiple_of((slot ^ me) * height, 8)
            packed[pl.ds(at, height), :] = piece[s * height:(s + 1) * height, :]
            slot += 1

    def put(p, q, block):
        hi[p, q], lo[p, q] = split(block)

    for line, i in enumerate(chunk_lines(size, chunk)):
        start = line * per * height

        def get(k):
            return jnp.concatenate(
                [
                    packed[start + s * height + k * rows:start + s * height + (k + 1) * rows, :]
                    for s in range(per)
                ],
                axis=0,
            )

        first, last = diagonal_blocks(size, i)
        block = get(0)
        turned = block.T
        element = packed[start + height - 8:start + height - 7, :]
        put(first, first, jnp.where(column >= row, block, turned))
        below = jnp.where(column < row, block, turned)
        put(last, last, jnp.where(column == row, jnp.broadcast_to(element, (B, B)), below))
        for k, (p, q) in enumerate(line_blocks(size, i)):
            block = get(k + 1)
            put(p, q, block)
            put(q, p, block.T)


def packed_scratch(size, shards):
    return pltpu.VMEM((shards * shard_rows(size, shards), B), F32)


def halves(size, shards):
    return [struct(shards // 2 * shard_rows(size, shards), B)] * 2


def first_gram_kernel(
    shards, me_ref, a_hbm, b_hbm, keep_ref, send_ref, ah, al, bh, bl, a_buf, b_buf, sems, g, packed
):
    rows, size = a_buf.shape
    q = size // 4
    steps = sems.shape[1]
    tile = rows // steps

    def copies(step):
        r = slice(step * tile, (step + 1) * tile)
        return [
            pltpu.make_async_copy(src.at[r], dst.at[r], sems.at[k, step])
            for k, (src, dst) in enumerate([(a_hbm, a_buf), (b_hbm, b_buf)])
        ]

    def start(step):
        for copy in copies(step):
            copy.start()

    start(0)
    start(1)
    for step in range(steps):
        r = slice(step * tile, (step + 1) * tile)
        for copy in copies(step):
            copy.wait()
        if step + 2 < steps:
            start(step + 2)
        ah[:, r], al[:, r] = split(a_buf[r].T)
        bh[r], bl[r] = split(b_buf[r])
    for r0, r1, c0, c1 in [(0, size, 0, q), (0, q, q, size), (3 * q, size, 3 * q, size)]:
        g[r0:r1, c0:c1] = mm((ah[r0:r1, :], al[r0:r1, :]), (bh[:, c0:c1], bl[:, c0:c1]))
    pack(g, packed, keep_ref, send_ref, me_ref[0], shards, 0)


def first_gram(me, shards, a, b):
    rows, size = a.shape
    hbm = pl.BlockSpec(memory_space=pltpu.HBM)
    return call(
        functools.partial(first_gram_kernel, shards), "first_gram",
        halves(size, shards) + [struct(size, rows, dtype=BF16)] * 2 + [struct(rows, size, dtype=BF16)] * 2,
        43, 0.5, 4,
        in_specs=[SMEM, hbm, hbm],
        out_specs=[VMEM] * 6,
        scratch_shapes=[
            pltpu.VMEM((rows, size), F32), pltpu.VMEM((rows, size), F32),
            pltpu.SemaphoreType.DMA((2, 4)),
            pltpu.VMEM((size, size), F32), packed_scratch(size, shards),
        ],
    )(me, a, b)


def lower_product(g, ah, al, bh, bl):
    size = g.shape[0]
    q = size // 4
    for r0, r1, c0, c1 in [(q, 3 * q, q, size), (3 * q, size, q, 3 * q)]:
        c = slice(c0 - q, c1 - q)
        g[r0:r1, c0:c1] = mm((ah[r0:r1, :], al[r0:r1, :]), (bh[:, c], bl[:, c]))


def other_gram_kernel(shards, me_ref, ah, al, bh, bl, keep_ref, send_ref, g, packed):
    q = g.shape[0] // 4
    lower_product(g, ah, al, bh[:, q:], bl[:, q:])
    pack(g, packed, keep_ref, send_ref, me_ref[0], shards, 1)


def other_gram(me, shards, ah, al, bh, bl):
    size = ah.shape[0]
    return call(
        functools.partial(other_gram_kernel, shards), "other_gram", halves(size, shards), 18, 0.5, 2,
        in_specs=[SMEM] + [VMEM] * 4,
        out_specs=[VMEM, VMEM],
        scratch_shapes=[pltpu.VMEM((size, size), F32), packed_scratch(size, shards)],
    )(me, ah, al, bh, bl)


def tiles(count, tile, step):
    def body(t, _):
        step(pl.ds(pl.multiple_of(t * tile, tile), tile))
        return 0

    lax.fori_loop(0, count // tile, body, 0)


def row_part(part, rows):
    return slice(0, rows // 4) if part == 0 else slice(rows // 4, rows)


def affine_kernel(part, a_ref, b_ref, out_ref, hi, lo):
    r = row_part(part, a_ref.shape[0])
    hi[...], lo[...] = split(a_ref[r])

    def step(c):
        out_ref[:, c] = 1.5 * a_ref[r, c] - 0.5 * mm((hi[...], lo[...]), split(b_ref[:, c]))

    tiles(out_ref.shape[1], 512 if part else 256, step)


def affine(a, b, part):
    rows, size = a.shape
    height = rows // 4 if part == 0 else 3 * rows // 4
    return call(
        functools.partial(affine_kernel, part), "affine", struct(height, size), 18,
        height / rows, 2,
        in_specs=[VMEM, VMEM],
        out_specs=VMEM,
        scratch_shapes=[pltpu.VMEM((height, size), BF16)] * 2,
    )(a, b)


def affine_parts_kernel(part, ah, al, b_ref, out_ref):
    r = row_part(part, ah.shape[0])

    def step(c):
        product = mm((ah[r], al[r]), split(b_ref[:, c]))
        out_ref[:, c] = 1.5 * (ah[r, c].astype(F32) + al[r, c].astype(F32)) - 0.5 * product

    tiles(out_ref.shape[1], 512 if part else 256, step)


def affine_parts(ah, al, b, part):
    rows, size = ah.shape
    height = rows // 4 if part == 0 else 3 * rows // 4
    return call(
        functools.partial(affine_parts_kernel, part), "affine_parts", struct(height, size), 18,
        height / rows, 2,
        in_specs=[VMEM] * 3,
        out_specs=VMEM,
    )(ah, al, b)


SPANS = (
    (((0, 4),), ((0, 1),), ((0, 1),), ((0, 1), (3, 4))),
    ((), ((1, 4),), ((1, 4),), ((1, 3),)),
)


def sym_product(ah, al, hi, lo, chunk, column, rows=slice(None)):
    q = hi.shape[0] // 4
    spans = [slice(k0 * q, k1 * q) for k0, k1 in SPANS[chunk][column]]
    c = slice(column * q, (column + 1) * q)
    a = [ref[rows, k] for ref in (ah, ah, al) for k in spans]
    b = [ref[k, c] for ref in (hi, lo, hi) for k in spans]
    return c, jnp.dot(
        jnp.concatenate(a, axis=1), jnp.concatenate(b, axis=0), preferred_element_type=F32
    )


def apply_first(base_refs, out_ref, ah, al, hi, lo, columns):
    q = hi.shape[0] // 4
    for column in columns:
        c, product = sym_product(ah, al, hi, lo, 0, column)
        out = slice(c.start - columns[0] * q, c.stop - columns[0] * q)
        at = 0
        for base_ref in base_refs:
            end = at + base_ref.shape[0]
            out_ref[at:end, out] = base_ref[:, c] - 0.5 * product[at:end]
            at = end


def sym_scratch(size, shards):
    return [pltpu.VMEM((size, size), BF16)] * 2 + [packed_scratch(size, shards)]


def first_part_kernel(shards, count, columns, me_ref, *refs):
    pieces, refs = refs[:count], refs[count:]
    ah, al, base_refs, (out_ref, hi, lo, packed) = refs[0], refs[1], refs[2:-4], refs[-4:]
    unpack(pieces, packed, hi, lo, me_ref[0], shards, 0)
    apply_first(base_refs, out_ref, ah, al, hi, lo, columns)


def first_part(me, shards, pieces, ah, al, base, columns):
    rows, size = ah.shape
    part = struct(size, size, dtype=BF16)
    more = len(columns) < 4
    scratch = sym_scratch(size, shards)
    return call(
        functools.partial(first_part_kernel, shards, len(pieces), columns), "first_part",
        [struct(rows, len(columns) * size // 4)] + [part, part] * more, 18, 0.5, 3,
        in_specs=[SMEM] + [VMEM] * (len(pieces) + 2 + len(base)),
        out_specs=[VMEM] * (1 + 2 * more),
        scratch_shapes=scratch[2 * more:],
    )(me, *pieces, ah, al, *base)


def other_part_kernel(columns, ah, al, hi, lo, *refs):
    apply_first(refs[:-1], refs[-1], ah, al, hi, lo, columns)


def other_part(ah, al, hi, lo, base, columns):
    rows, size = ah.shape
    return call(
        functools.partial(other_part_kernel, columns), "other_part",
        struct(rows, len(columns) * size // 4), 16, 0.25, 3,
        in_specs=[VMEM] * (4 + len(base)),
        out_specs=VMEM,
    )(ah, al, hi, lo, *base)


def column_kernel(xh, xl, mid_ref, col_ref):
    col_ref[...] = mm((xh[...], xl[...]), split(mid_ref[...]))


def column_product(xh, xl, mid):
    size, rows = xh.shape
    block = pl.BlockSpec((rows, size // 4), lambda r: (0, 0))
    whole = pl.BlockSpec((size, rows), lambda r: (0, 0))
    return call(
        column_kernel, "column_product", struct(size, size // 4), 16, 0.25, 2,
        grid=(1,), in_specs=[whole, whole, block], out_specs=block,
    )(xh, xl, mid)


def turn_kernel(x_ref, xh, xl):
    def step(r):
        xh[:, r], xl[:, r] = split(x_ref[r].T)

    tiles(x_ref.shape[0], 256, step)


def turn(x):
    part = struct(*x.shape[::-1], dtype=BF16)
    return call(
        turn_kernel, "turn", [part, part], 16, 0.1, 2, in_specs=[VMEM], out_specs=[VMEM] * 2
    )(x)


def cut_kernel(which, x_ref, *out_refs):
    def step(r):
        parts = split(x_ref[r])
        for out_ref, k in zip(out_refs, which):
            out_ref[r] = parts[k]

    tiles(x_ref.shape[0], 128, step)


def cut(x, *which):
    count = len(which)
    return call(
        functools.partial(cut_kernel, which), "cut", [struct(*x.shape, dtype=BF16)] * count,
        16, 0.25, 2, in_specs=[VMEM], out_specs=[VMEM] * count,
    )(x)


def second_gram_kernel(shards, count, me_ref, *refs):
    pieces, refs = refs[:count], refs[count:]
    (ah, al, base_ref, xh, xl, col_ref), refs = refs[:6], refs[6:]
    keep_ref, send_ref, mh, ml, hi, lo, packed, g = refs
    size = g.shape[0]
    q = size // 4
    unpack(pieces, packed, hi, lo, me_ref[0], shards, 1)
    mh[:, :q], ml[:, :q] = split(base_ref[:, :q])
    for column in range(1, 4):
        c, product = sym_product(ah, al, hi, lo, 1, column)
        mid = base_ref[:, c] - 0.5 * product
        mh[:, c], ml[:, c] = split(mid)
    g[:, :q] = col_ref[...]
    g[:q, q:] = mm((xh[:q, :], xl[:q, :]), (mh[:, q:], ml[:, q:]))
    g[3 * q:, 3 * q:] = mm((xh[3 * q:, :], xl[3 * q:, :]), (mh[:, 3 * q:], ml[:, 3 * q:]))
    pack(g, packed, keep_ref, send_ref, me_ref[0], shards, 0)


def second_gram(me, shards, pieces, ah, al, base, xh, xl, col):
    rows, size = ah.shape
    part = struct(rows, size, dtype=BF16)
    return call(
        functools.partial(second_gram_kernel, shards, len(pieces)), "second_gram",
        halves(size, shards) + [part, part], 20, 0.8, 5,
        in_specs=[SMEM] + [VMEM] * (len(pieces) + 6),
        out_specs=[VMEM] * 4,
        scratch_shapes=sym_scratch(size, shards) + [pltpu.VMEM((size, size), F32)],
    )(me, *pieces, ah, al, base, xh, xl, col)


def fourth_gram_kernel(shards, me_ref, xh, xl, mh, ml, keep_ref, send_ref, g, packed):
    q = g.shape[0] // 4
    lower_product(g, xh, xl, mh[:, q:], ml[:, q:])
    pack(g, packed, keep_ref, send_ref, me_ref[0], shards, 1)


def fourth_gram(me, shards, xh, xl, mh, ml):
    size = xh.shape[0]
    return call(
        functools.partial(fourth_gram_kernel, shards), "fourth_gram", halves(size, shards), 18, 0.5, 2,
        in_specs=[SMEM] + [VMEM] * 4,
        out_specs=[VMEM, VMEM],
        scratch_shapes=[pltpu.VMEM((size, size), F32), packed_scratch(size, shards)],
    )(me, xh, xl, mh, ml)


def last_kernel(shards, count, me_ref, *refs):
    pieces = refs[:count]
    ah, al, z_ref, rest_ref, out_hbm, hi, lo, packed, out, sems = refs[count:]
    q = hi.shape[0] // 4
    copies = []

    def send(src, rows, c):
        copy = pltpu.make_async_copy(src, out_hbm.at[rows, c], sems.at[len(copies)])
        copy.start()
        copies.append(copy)

    count = out.shape[0]
    send(z_ref, slice(0, count), slice(0, q))
    unpack(pieces, packed, hi, lo, me_ref[0], shards, 1)
    for column in (1, 2, 3):
        parts = 2 if column == 3 else 1
        for part in range(parts):
            r = slice(part * count // parts, (part + 1) * count // parts)
            c, product = sym_product(ah, al, hi, lo, 1, column, r)
            out[r, c] = rest_ref[r, c.start - q:c.stop - q] - 0.5 * product
            send(out.at[r, c], r, c)
    for copy in copies:
        copy.wait()


def last_step(me, shards, pieces, ah, al, z, rest):
    rows, size = ah.shape
    return call(
        functools.partial(last_kernel, shards, len(pieces)), "last", struct(rows, size), 22, 0.5, 3,
        in_specs=[SMEM] + [VMEM] * (len(pieces) + 4),
        out_specs=pl.BlockSpec(memory_space=pltpu.HBM),
        scratch_shapes=sym_scratch(size, shards)
        + [pltpu.VMEM((rows, size), F32), pltpu.SemaphoreType.DMA((5,))],
    )(me, *pieces, ah, al, z, rest)


CORE = 1
PLANE = (2, 4, 6)
SHARDS = 2 * (1 + len(PLANE))


def slot_of(index):
    return (index % 2) * (SHARDS // 2) + (index // 2) % (SHARDS // 2)


class Sum:
    def __init__(self, count, keep, send):
        self.count, self.keep, self.send = count, keep, send

    def swap(self, x, offset):
        return lax.ppermute(x, "row", [(i, i ^ offset) for i in range(self.count)])

    def swaps(self, values):
        return [self.swap(x, offset) for x, offset in zip(values, PLANE)]

    def core(self):
        return self.swap(self.send, CORE)

    def plane(self, got):
        total = self.keep + got
        part = total.shape[0] // (1 + len(PLANE))
        self.keep, *sends = [total[k * part:(k + 1) * part] for k in range(1 + len(PLANE))]
        return self.swaps(sends)

    def own(self, got):
        self.keep = sum(got, self.keep)

    def exchange(self, offset):
        return self.swap(self.keep, offset)

    def gather_plane(self):
        return self.swaps([self.keep] * len(PLANE))

    def gather_core(self, got):
        self.mine = jnp.concatenate([self.keep, *got], axis=0)
        return self.swap(self.mine, CORE)


def close(env, *got):
    values = lax.optimization_barrier((*env.values(), *got[::-1]))
    env.update(zip(env, values))
    return values[len(env):][::-1]


def sum_chunks(count, env, first, second, works, late):
    beyond = [1 << s for s in range(3, count.bit_length() - 1)]
    works = list(works)

    def work():
        if works:
            works.pop(0)(env)

    a = Sum(count, *first)
    got_a = a.core()
    pair = second(env)
    got_a, *pair = close(env, got_a, *pair)
    b = Sum(count, *pair)

    got_a = a.plane(got_a)
    got_b = b.core()
    work()
    (got_b,) = close(env, got_b)

    got_b = b.plane(got_b)[::-1]
    work()
    a.own(close(env, *got_a))

    for offset in beyond:
        got_a = a.exchange(offset)
        work()
        b.own(close(env, *got_b))
        got_b = [b.exchange(offset)]
        a.own(close(env, got_a))

    got_a = a.gather_plane()
    b.own(close(env, *got_b))

    got_b = b.gather_plane()
    got_a = a.gather_core(close(env, *got_a))
    work()
    (got_a,) = close(env, got_a)
    late[0](env, [a.mine, got_a])
    got_b = b.gather_core(close(env, *got_b))
    late[1](env)
    (got_b,) = close(env, got_b)
    return [b.mine, got_b]


def body(count, orbitals_zero, orbitals_one, correlation_zero, correlation_one, cotangent):
    me = slot_of(lax.axis_index("row")).astype(jnp.int32).reshape(1)
    env = dict(
        x0=orbitals_zero, x1=orbitals_one, s0=correlation_zero, s1=correlation_one, c=cotangent
    )

    def direct(part):
        def work(env):
            env[f"m{part}"] = affine(env["c"], env["s1"], part)
        return work

    def turned(env):
        env["xh"], env["xl"] = turn(env["x0"])

    def cut_one(env):
        env["x1h"], env["x1l"] = cut(env["x1"], 0, 1)

    def middle(env, pieces):
        (env["mid"],) = first_part(
            me, SHARDS, pieces, env["x1h"], env["x1l"], [env["m0"], env["m1"]], (0, 1, 2, 3)
        )

    def column(env):
        env["col"] = column_product(env["xh"], env["xl"], env["mid"])

    keep, send, *parts = first_gram(me, SHARDS, env["x1"], env["c"])
    one = sum_chunks(
        count, env, (keep, send), lambda env: other_gram(me, SHARDS, *parts),
        [direct(0), cut_one, direct(1), turned], [middle, column],
    )

    keep, send, env["mh"], env["ml"] = second_gram(
        me, SHARDS, one, env["x1h"], env["x1l"], env["mid"], env["xh"], env["xl"], env["col"]
    )

    def last_direct(part):
        def work(env):
            env[f"d{part}"] = affine_parts(env["mh"], env["ml"], env["s0"], part)
        return work

    def high(env):
        (env["x0h"],) = cut(env["x0"], 0)

    def low(env):
        (env["x0l"],) = cut(env["x0"], 1)

    def result(env, pieces):
        env["z"], env["symh"], env["syml"] = first_part(
            me, SHARDS, pieces, env["x0h"], env["x0l"], [env["d0"], env["d1"]], (0,)
        )

    def rest(env):
        env["rest"] = other_part(
            env["x0h"], env["x0l"], env["symh"], env["syml"], [env["d0"], env["d1"]], (1, 2, 3)
        )

    two = sum_chunks(
        count, env, (keep, send),
        lambda env: fourth_gram(me, SHARDS, env["xh"], env["xl"], env["mh"], env["ml"]),
        [last_direct(0), high, last_direct(1), low], [result, rest],
    )
    return last_step(me, SHARDS, two, env["x0h"], env["x0l"], env["z"], env["rest"])


def solution(mesh):
    in_specs = (
        P(("kpt", "row"), None),
        P(("kpt", "row"), None),
        P("kpt", None),
        P("kpt", None),
        P(("kpt", "row"), None),
    )
    out_specs = P(("kpt", "row"), None)
    return jax.shard_map(
        functools.partial(body, mesh.shape["row"]),
        mesh=mesh, in_specs=in_specs, out_specs=out_specs, check_vma=False,
    )
```
